32 devices in a mesh: fsdp: 4 (over y, x), blk: 8 (over z, core).
Axes of the slice: x: 2, y: 2, z: 4, core: 2. Of those that a mesh axis runs over, the one named last changes fastest.
Arguments:
- tokens: bfloat16 [12288, 1152], P(('fsdp', 'blk')), may hold values from -6 to 6
- timesteps: int32 [4, 8], P('fsdp'), may hold values from 0 to 999
- segment_ids: int32 [4, 3072], P('fsdp'), may hold values from 0 to 7, as said below
- head_mask: int32 [4, 8, 16], P('fsdp'), may hold values 0 or 1
- chan_mask: int32 [4, 8, 4608], P('fsdp'), may hold values 0 or 1
- token_mask: int32 [12288], P(('fsdp', 'blk')), may hold values 0 or 1
- w_temb: bfloat16 [256, 1152], P('fsdp'), may hold values from -0.375 to 0.375
- w_ada: bfloat16 [1152, 6912], P('fsdp'), may hold values from -0.1875 to 0.1875
- w_qkv: bfloat16 [1152, 3456], P('fsdp'), may hold values from -0.25 to 0.25
- w_out: bfloat16 [1152, 1152], P('fsdp'), may hold values from -1 to 1
- w_fc1: bfloat16 [1152, 4608], P('fsdp'), may hold values from -0.1875 to 0.1875
- w_fc2: bfloat16 [4608, 1152], P('fsdp'), may hold values from -0.1875 to 0.1875
- cotangent: bfloat16 [12288, 1152], P(('fsdp', 'blk')), may hold values from -6 to 6
Outputs:
- result: bfloat16 [12288, 1152], P(('fsdp', 'blk'))
- grad_tokens: bfloat16 [12288, 1152], P(('fsdp', 'blk'))
- grad_temb: float32 [256, 1152], P('fsdp')
- grad_ada: float32 [1152, 6912], P('fsdp')
- grad_qkv: float32 [1152, 3456], P('fsdp')
- grad_out: float32 [1152, 1152], P('fsdp')
- grad_fc1: float32 [1152, 4608], P('fsdp')
- grad_fc2: float32 [4608, 1152], P('fsdp')
The draws below stay inside these ranges and needn't reach their ends.
Inputs may be any that keep to these rules, and one draw needn't show every extreme that they name: `segment_ids`: in each stream slot 0 holds 1024 tokens, every other slot below 7 holds 1024, 256 or no tokens, and slot 7 holds the remaining padding tokens, at least 128 of them; each slot's tokens are spread over the devices of blk as evenly as possible, their counts on two devices differing by at most one.
All inputs are finite; a program needn't handle non-finite values. No bound on the sum of `head_mask` or of `chan_mask` or of `token_mask` on one device may be relied on, other than what follows from the above.
Results may differ from the reference program's by a relative error of at most 0.022.
Values may be sent and summed in bfloat16 or wider, within the bound.
A program may use at most 256 MiB of HBM per device.

```python
import math
import jax
import jax.numpy as jnp
from jax import lax

HEADS = 16
HEAD_DIM = 72
FF = 4608
FREQ = 256
ITEMS = 8
IMG_BIG = 1024
IMG_SMALL = 256
TOK_DEV = 384
D = 1152
GROUP_TOK = 3072
GROUPS = 4
TOKENS = 12288
N_BLK = 8


def draw_segment_ids(key, part):
    key = jax.random.fold_in(key, 11)
    key_kind, key_place = jax.random.split(key)
    kinds = jax.random.randint(key_kind, (GROUPS, ITEMS - 1), 0, 3)
    wanted = jnp.where(kinds == 2, IMG_BIG, jnp.where(kinds == 1, IMG_SMALL, 0)).astype(jnp.int32)
    wanted = wanted.at[:, 0].set(IMG_BIG)
    room = GROUP_TOK - IMG_SMALL // 2

    def accept(total, size):
        taken = jnp.where(total + size <= room, size, 0).astype(jnp.int32)
        return (total + taken, taken)
    _, taken = lax.scan(accept, jnp.zeros((GROUPS,), jnp.int32), wanted.T)
    taken = taken.T
    padding = GROUP_TOK - jnp.sum(taken, axis=1, keepdims=True)
    sizes_all = jnp.concatenate([taken, padding], axis=1).astype(jnp.int32)
    ends = jnp.cumsum(sizes_all, axis=1).astype(jnp.int32)
    order = lax.iota(jnp.int32, GROUP_TOK)
    sorted_ids = jnp.sum((order[None, :, None] >= ends[:, None, :]).astype(jnp.int32), axis=2)
    blocks = GROUP_TOK // TOK_DEV
    spread = jnp.transpose(sorted_ids.reshape(GROUPS, TOK_DEV, blocks), (0, 2, 1))
    noise = jax.random.randint(key_place, (GROUPS, blocks, TOK_DEV), 0, 1048576) * TOK_DEV + lax.iota(jnp.int32, TOK_DEV)[None, None, :]
    ranks = jnp.argsort(noise, axis=2)
    placed = jnp.take_along_axis(spread, ranks, axis=2)
    return placed.reshape(GROUPS, GROUP_TOK).astype(jnp.int32)


def plant(drawn, rng, smallest, high):
    dims = drawn.shape
    place = [jax.random.randint(jax.random.fold_in(rng, axis), (), 0, dims[axis]) for axis in range(len(dims))]
    drawn = drawn.at[tuple(place)].set(smallest)
    longest = dims.index(max(dims))
    place[longest] = (place[longest] + 1) % dims[longest]
    return drawn.at[tuple(place)].set(high)


def level_of(key, dims, shards, least, largest):
    gain = 1.0
    for axis_at, parts in shards:
        steps = jax.random.uniform(jax.random.fold_in(jax.random.fold_in(key, 6), axis_at), (parts,), jnp.float32, least / len(shards), largest / len(shards))
        gain = gain * jnp.repeat(jnp.exp(steps), dims[axis_at] // parts).reshape((-1,) + (1,) * (len(dims) - 1 - axis_at))
    return gain


def scatter_about(key, extent, scale, limit, cuts=(), kind=jnp.bfloat16):
    drawn = scale * jax.random.normal(key, extent, jnp.float32)
    if cuts:
        drawn = drawn * level_of(key, extent, cuts, -0.22, 0.18)
    return jnp.clip(drawn, -limit, limit).astype(kind)


def setup_inputs(seed: int = 0) -> dict:
    splits = jax.random.split(jax.random.key(seed), 14)
    return {
        "tokens": scatter_about(splits[0], (TOKENS, D), 1.0, 6.0, ((0, 32),)),
        "timesteps": plant(jax.random.randint(splits[1], (GROUPS, ITEMS), 0, 1000), jax.random.fold_in(splits[1], 1), 0, 999).astype(jnp.int32),
        "segment_ids": draw_segment_ids(jax.random.fold_in(splits[13], 71), 0),
        "head_mask": plant((jax.random.randint(splits[3], (GROUPS, ITEMS, HEADS), 0, 4) < 3).astype(jnp.int32), jax.random.fold_in(splits[3], 1), 0, 1),
        "chan_mask": plant((jax.random.randint(splits[4], (GROUPS, ITEMS, FF), 0, 4) < 3).astype(jnp.int32), jax.random.fold_in(splits[4], 1), 0, 1),
        "token_mask": plant((jax.random.randint(splits[5], (TOKENS,), 0, 4) < 3).astype(jnp.int32), jax.random.fold_in(splits[5], 1), 0, 1),
        "w_temb": scatter_about(splits[6], (FREQ, D), FREQ ** -0.5, 0.375, ((0, 4),)),
        "w_ada": scatter_about(splits[7], (D, 6 * D), D ** -0.5, 0.1875, ((0, 4),)),
        "w_qkv": scatter_about(splits[8], (D, 3 * D), (D // 2) ** -0.5, 0.25, ((0, 4),)),
        "w_out": scatter_about(splits[9], (D, D), (D // 32) ** -0.5, 1.0, ((0, 4),)),
        "w_fc1": scatter_about(splits[10], (D, FF), D ** -0.5, 0.1875, ((0, 4),)),
        "w_fc2": scatter_about(splits[11], (FF, D), (FF // 4) ** -0.5, 0.1875, ((0, 4),)),
        "cotangent": scatter_about(splits[12], (TOKENS, D), 1.0, 6.0, ((0, 32),)),
    }


@jax.custom_vjp
def low(v):
    return lax.optimization_barrier(v.astype(jnp.bfloat16)).astype(jnp.float32)

@jax.custom_vjp
def low_back(v):
    return v

def low_keep(v):
    return (low(v), None)

def low_pass(kept, grad):
    return (grad,)

def back_keep(v):
    return (v, None)

def back_low(kept, grad):
    return (low(grad),)
low.defvjp(low_keep, low_pass)
low_back.defvjp(back_keep, back_low)
HIGH = lax.Precision.HIGHEST
NEG = -1e+30

def frequencies(steps):
    half = FREQ // 2
    ladder = jnp.exp(-math.log(10000.0) * jnp.arange(half, dtype=jnp.float32) / half)
    angles = steps.astype(jnp.float32)[..., None] * ladder
    return jnp.concatenate([jnp.cos(angles), jnp.sin(angles)], axis=-1)

def silu_fn(values):
    return values / (1.0 + jnp.exp(-values))

def gelu_tanh(values):
    return 0.5 * values * (1.0 + jnp.tanh(0.7978845608028654 * (values + 0.044715 * values * values * values)))

def norm_mod(values, shift_by, scale_by):
    center = values - lax.optimization_barrier(jnp.mean(values, axis=-1, keepdims=True))
    spread = lax.optimization_barrier(jnp.mean(center * center, axis=-1, keepdims=True))
    return center * lax.rsqrt(spread + 1e-06) * (1.0 + scale_by) + shift_by

def group_forward(weights, tokens, modulation, owners, head_mask, chan_mask, token_mask):
    w_qkv, w_out, w_fc1, w_fc2 = weights
    owners = owners.astype(jnp.int32)
    picker = (owners[:, None] == jnp.arange(ITEMS, dtype=jnp.int32)[None, :]).astype(jnp.float32)
    per_token = jnp.dot(picker, modulation, precision=HIGH)
    shift_one, scale_one, gate_one, shift_two, scale_two, gate_two = jnp.split(per_token, 6, axis=1)
    normed = norm_mod(tokens, shift_one, scale_one)
    packed = low_back(low(jnp.dot(low(normed), w_qkv, precision=HIGH)))
    queries, keys, values = jnp.split(packed, 3, axis=1)
    key_heads = keys.reshape(GROUP_TOK, HEADS, HEAD_DIM)
    value_heads = values.reshape(GROUP_TOK, HEADS, HEAD_DIM)
    score_scale = 1.0 / math.sqrt(HEAD_DIM)

    def attend(block):
        query_block, block_items = block
        scores = low_back(jnp.einsum('qhd,khd->hqk', query_block, key_heads, precision=HIGH) * score_scale)
        same = block_items[:, None] == owners[None, :]
        masked = jnp.where(same[None], scores, NEG)
        top = lax.optimization_barrier(jnp.max(masked, axis=2, keepdims=True))
        raised = jnp.exp(masked - top)
        probs = raised / lax.optimization_barrier(jnp.sum(raised, axis=2, keepdims=True))
        return jnp.einsum('hqk,khd->qhd', low(probs), value_heads, precision=HIGH)
    attended = lax.map(jax.checkpoint(attend), (queries.reshape(N_BLK, TOK_DEV, HEADS, HEAD_DIM), owners.reshape(N_BLK, TOK_DEV)))
    attended = attended.reshape(GROUP_TOK, HEADS, HEAD_DIM)
    head_keep = jnp.dot(picker, head_mask.astype(jnp.float32), precision=HIGH)
    masked_rows = low_back(low((attended * head_keep[:, :, None]).reshape(GROUP_TOK, D)))
    attn_branch = low_back(jnp.dot(masked_rows, w_out, precision=HIGH))
    middle = tokens + gate_one * attn_branch
    normed_two = norm_mod(middle, shift_two, scale_two)
    hidden_pre = low_back(jnp.dot(low(normed_two), w_fc1, precision=HIGH))
    channel_keep = jnp.dot(picker, chan_mask.astype(jnp.float32), precision=HIGH) * token_mask.astype(jnp.float32)[:, None]
    hidden = low(gelu_tanh(hidden_pre) * channel_keep)
    mlp_branch = low_back(jnp.dot(hidden, w_fc2, precision=HIGH))
    return middle + gate_two * mlp_branch

def full_forward(timesteps, segment_ids, head_mask, chan_mask, token_mask):

    def forward(tokens, w_temb, w_ada, w_qkv, w_out, w_fc1, w_fc2):
        spectrum = low(frequencies(timesteps))
        condition = jnp.einsum('gif,fd->gid', spectrum, w_temb, precision=HIGH)
        modulation = low_back(jnp.einsum('gid,de->gie', low(silu_fn(condition)), w_ada, precision=HIGH))

        def one_group(carry, group):
            return (carry, group_forward((w_qkv, w_out, w_fc1, w_fc2), *group))
        groups = (tokens.reshape(GROUPS, GROUP_TOK, D), modulation, segment_ids, head_mask, chan_mask, token_mask.reshape(GROUPS, GROUP_TOK))
        _, outputs = lax.scan(one_group, jnp.zeros((), jnp.float32), groups)
        return outputs.reshape(TOKENS, D)
    return forward

def reference(tokens, timesteps, segment_ids, head_mask, chan_mask, token_mask, w_temb, w_ada, w_qkv, w_out, w_fc1, w_fc2, cotangent):
    forward = full_forward(timesteps, segment_ids, head_mask, chan_mask, token_mask)
    floats = tuple((array.astype(jnp.float32) for array in (tokens, w_temb, w_ada, w_qkv, w_out, w_fc1, w_fc2)))
    result, pull = jax.vjp(forward, *floats)
    grads = pull(cotangent.astype(jnp.float32))
    return (result.astype(jnp.bfloat16), grads[0].astype(jnp.bfloat16), grads[1], grads[2], grads[3], grads[4], grads[5], grads[6])
```

```python
import functools
import math

import jax
import jax.numpy as jnp
from jax import lax
from jax.experimental import pallas as pl
from jax.experimental.pallas import tpu as pltpu
from jax.sharding import PartitionSpec as P

HIGH = lax.Precision.HIGHEST
BF16 = jnp.bfloat16
F32 = jnp.float32
I32 = jnp.int32
LANES = 128
BLOCK = 256
NEG = -1e30
LOG2E = 1.4426950408889634

VMEM = pl.BlockSpec(memory_space=pltpu.VMEM)
SMEM = pl.BlockSpec(memory_space=pltpu.SMEM)
ANY = pl.BlockSpec(memory_space=pl.ANY)


def shape(dims, kind=BF16):
    return jax.ShapeDtypeStruct(tuple(dims), kind)


def run(name, body, ins, outs, scratch=(), flops=0, vmem=48, **more):
    moved = sum(a.size * a.dtype.itemsize for _, a in ins)
    moved += sum(math.prod(o.shape) * jnp.dtype(o.dtype).itemsize for _, o in outs)
    return pl.pallas_call(
        body,
        out_shape=[o for _, o in outs],
        in_specs=[s for s, _ in ins],
        out_specs=[s for s, _ in outs],
        scratch_shapes=list(scratch),
        compiler_params=pltpu.CompilerParams(vmem_limit_bytes=vmem << 20),
        cost_estimate=pl.CostEstimate(flops=flops, bytes_accessed=moved, transcendentals=0),
        name=name,
        **more,
    )(*[a for _, a in ins])


def swap(array, axis, by):
    size = lax.axis_size(axis)
    return lax.ppermute(array, axis, [(i, i ^ by) for i in range(size)])


def after(array, *others):
    return lax.optimization_barrier((array,) + others)[0]


def nn(left, right):
    return lax.dot_general(left, right, (((1,), (0,)), ((), ())), preferred_element_type=F32)


def nt(left, right):
    return lax.dot_general(left, right, (((1,), (1,)), ((), ())), preferred_element_type=F32)


def tn(left, right):
    return lax.dot_general(left, right, (((0,), (0,)), ((), ())), preferred_element_type=F32)


def each(count, step):
    def one(index, carry):
        step(index)
        return carry

    lax.fori_loop(0, count, one, 0)


def normal(values):
    center = values - jnp.mean(values, axis=-1, keepdims=True)
    scale = lax.rsqrt(jnp.mean(center * center, axis=-1, keepdims=True) + 1e-06)
    return center * scale, scale


def normal_back(grad, normed, scale):
    along = jnp.mean(grad * normed, axis=-1, keepdims=True)
    return scale * (grad - jnp.mean(grad, axis=-1, keepdims=True) - normed * along)


def sort_body(width, items_ref, keep_ref, x_ref, c_ref, xs_ref, cs_ref, hot_ref, info_ref, perm_ref):
    count = items_ref.shape[1]
    slots = hot_ref.shape[0]
    items = items_ref[...]
    slot = lax.broadcasted_iota(I32, (slots, count), 0)
    hot = (items == slot).astype(F32)
    start = jnp.sum((items < slot).astype(F32), axis=1, keepdims=True)
    end = start + jnp.sum(hot, axis=1, keepdims=True)
    row = lax.broadcasted_iota(I32, (count, count), 0)
    col = lax.broadcasted_iota(I32, (count, count), 1)
    rank = nn(hot.astype(BF16), (row <= col).astype(BF16))
    place = jnp.sum(hot * (start + rank), axis=0, keepdims=True) - 1.0
    perm = (row.astype(F32) == place).astype(BF16)
    perm_ref[...] = perm
    xs_ref[...] = nn(perm, x_ref[...]).astype(BF16)
    cs_ref[...] = nn(perm, c_ref[...]).astype(BF16)
    keep = jnp.broadcast_to(keep_ref[...].astype(F32), (slots, count)).astype(BF16)
    kept = nt(keep, perm)
    at = lax.broadcasted_iota(I32, (slots, count), 1).astype(F32)
    hot_ref[...] = kept * ((at >= start) & (at < end)).astype(F32)
    head = (lax.broadcasted_iota(I32, (slots, LANES), 1) * width).astype(F32)
    own = ((head >= start) & (head < end)).astype(F32)
    which = lax.broadcasted_iota(I32, (slots, LANES), 0).astype(F32)
    info_ref[0:1, :] = jnp.sum(own * which, axis=0, keepdims=True).astype(I32)
    info_ref[1:2, :] = (jnp.sum(own * start, axis=0, keepdims=True) / width).astype(I32)
    info_ref[2:3, :] = (jnp.sum(own * end, axis=0, keepdims=True) / width).astype(I32)
    info_ref[3:8, :] = jnp.zeros((5, LANES), I32)


def pick_heads_body(own, size, ids_ref, w_ref, o_ref):
    width = w_ref.shape[1] // 3
    first = ids_ref[1] * (own * size)
    row = lax.broadcasted_iota(I32, (width, LANES), 0)
    col = lax.broadcasted_iota(I32, (width, LANES), 1)
    for head in range(own):
        mark = (row == first + head * size + col) & (col < size)
        pick = mark.astype(F32).astype(BF16)
        for part in range(3):
            at = (part * own + head) * LANES
            o_ref[:, at : at + LANES] = nn(
                w_ref[:, part * width : (part + 1) * width], pick
            ).astype(BF16)


def pick_half_body(parts, ids_ref, w_ref, o_ref):
    half = w_ref.shape[1] // parts // 2
    for core in range(2):

        @pl.when(ids_ref[2] == core)
        def _():
            for part in range(parts):
                at = (2 * part + core) * half
                o_ref[:, part * half : (part + 1) * half] = w_ref[:, at : at + half]


def fetch(pairs, sems):
    copies = []
    for index, (source, target) in enumerate(pairs):
        copy = pltpu.make_async_copy(source, target, sems.at[index])
        copy.start()
        copies.append(copy)
    return copies


def first_body(chips, plan, ids_ref, info_ref, mod_ref, *refs):
    n_x = 2 + 4 * (chips - 1)
    x_refs, refs = refs[:n_x], refs[n_x:]
    w_refs, (h_ref, o_ref, x_all, w_all, sems) = refs[: len(plan)], refs[len(plan) :]
    width = x_refs[0].shape[1]
    f, b, c = ids_ref[0], ids_ref[1], ids_ref[2]
    z = b // 2
    u = pl.program_id(0)

    @pl.when(u == 0)
    def _():
        rows = plan[-1][2]
        todo = [(None, x_refs[0], x_all.at[b]), (None, x_refs[1], x_all.at[b + 1 - 2 * c])]
        for s in range(1, chips):
            left, right = (z - s) * 2, (z + s) * 2
            at = 2 + 4 * (s - 1)
            todo.append((z >= s, x_refs[at], x_all.at[jnp.maximum(left, 0) + c]))
            todo.append((z >= s, x_refs[at + 1], x_all.at[jnp.maximum(left, 0) + 1 - c]))
            capped = jnp.minimum(right, 2 * chips - 2)
            todo.append((z + s < chips, x_refs[at + 2], x_all.at[capped + c]))
            todo.append((z + s < chips, x_refs[at + 3], x_all.at[capped + 1 - c]))
        for ref, (k, start, _) in zip(w_refs, plan):
            at = pl.multiple_of(lax.bitwise_xor(f, k) * rows + start, 16)
            todo.append((None, ref, w_all.at[pl.ds(at, ref.shape[0])]))
        for phase in range(2):
            for index, (when, source, target) in enumerate(todo):
                copy = pltpu.make_async_copy(source, target, sems.at[index])
                act = copy.wait if phase else copy.start
                if when is None:
                    act()
                else:
                    pl.when(when)(act)

    slot = info_ref[0, u]
    shift = mod_ref[pl.ds(slot, 1), 0:width]
    scale = mod_ref[pl.ds(slot, 1), width : 2 * width]
    rows = BLOCK // (2 * chips)
    part = x_all[:, pl.ds(pl.multiple_of(u * rows, rows), rows), :]
    values = part.reshape(BLOCK, width).astype(F32)
    normed, _ = normal(values)
    low = (normed * (1.0 + scale) + shift).astype(BF16)
    h_ref[0] = low
    o_ref[0] = nn(low, w_all[...]).astype(BF16)


def exchange_lanes(tiles, width):
    tiles = list(tiles)
    count = len(tiles)
    group = lax.broadcasted_iota(I32, tiles[0].shape, 1) // width
    half = count // 2
    while half:
        low = (group // half) % 2 == 0
        fresh = list(tiles)
        for i in range(count):
            if (i // half) % 2 == 0:
                a, d = tiles[i], tiles[i + half]
                fresh[i] = jnp.where(low, a, pltpu.roll(d, half * width, 1))
                fresh[i + half] = jnp.where(low, pltpu.roll(a, LANES - half * width, 1), d)
        tiles = fresh
        half //= 2
    return tiles


def attend_body(own, size, blocks, ids_ref, info_ref, mask_ref, qkv_ref, o_ref, lse_ref, *refs):
    outs, (held,) = refs[:blocks], refs[blocks:]
    units = qkv_ref.shape[0]
    width = BLOCK // blocks
    b = ids_ref[1]
    scale = LOG2E / math.sqrt(size)
    pad = -size % 16

    def one_unit(u):
        queries = [qkv_ref[u, :, h * LANES : (h + 1) * LANES] for h in range(own)]

        def one_block(j, carry):
            fresh = []
            for h in range(own):
                top, total, acc = carry[h]
                keys = qkv_ref[j, :, (own + h) * LANES : (own + h + 1) * LANES]
                at = (2 * own + h) * LANES
                values = qkv_ref[j, :, at : at + LANES]
                scores = nt(keys, queries[h]) * scale
                new_top = jnp.maximum(top, jnp.max(scores, axis=0, keepdims=True))
                probs = jnp.exp2(scores - new_top)
                decay = jnp.exp2(top - new_top)
                total = total * decay + jnp.sum(probs, axis=0, keepdims=True)
                acc = acc * decay + tn(values, probs.astype(BF16))
                fresh.append((new_top, total, acc))
            return tuple(fresh)

        start = tuple(
            (
                jnp.full((1, BLOCK), NEG, F32),
                jnp.zeros((1, BLOCK), F32),
                jnp.zeros((LANES, BLOCK), F32),
            )
            for _ in range(own)
        )
        done = lax.fori_loop(info_ref[1, u], info_ref[2, u], one_block, start)
        slot = info_ref[0, u]
        rows = []
        for h in range(own):
            top, total, acc = done[h]
            keep = mask_ref[slot, b * own + h].astype(F32)
            rows.append((acc * (keep / total))[0:size])
            lse_ref[u, h : h + 1, :] = top + jnp.log2(total)
        held[u] = jnp.concatenate(rows, axis=0) if own > 1 else rows[0]
        o_ref[u] = held[u].astype(BF16)

    each(units, one_unit)
    groups = LANES // width
    for g in range(units // groups):
        for e in range(blocks // groups):
            tiles = [
                held[groups * g + i, :, e * LANES : (e + 1) * LANES] for i in range(groups)
            ]
            for j, tile in enumerate(exchange_lanes(tiles, width)):
                device = groups * e + j
                for k in range(blocks):

                    @pl.when(lax.bitwise_xor(b, k) == device)
                    def _():
                        outs[k][:, g * LANES : (g + 1) * LANES] = tile.astype(BF16)


def attend_back_body(own, size, blocks, ids_ref, info_ref, mask_ref, qkv_ref, o_ref, lse_ref, *refs):
    pieces, (d_ref, given, up, delta, d_q, d_k, d_v) = refs[:blocks], refs[blocks:]
    units = qkv_ref.shape[0]
    width = BLOCK // blocks
    b = ids_ref[1]
    factor = 1.0 / math.sqrt(size)
    scale = LOG2E * factor
    for k in range(blocks):
        given[lax.bitwise_xor(b, k)] = pieces[k][...]
    up[...] = jnp.zeros_like(up)
    groups = LANES // width
    for g in range(units // groups):
        for e in range(blocks // groups):
            tiles = [
                given[groups * e + j, :, g * LANES : (g + 1) * LANES].astype(F32)
                for j in range(groups)
            ]
            for i, tile in enumerate(exchange_lanes(tiles, width)):
                unit = groups * g + i
                slot = info_ref[0, unit]
                for h in range(own):
                    keep = mask_ref[slot, b * own + h].astype(F32)
                    kept = tile[h * size : (h + 1) * size] * keep
                    up[unit, h, 0:size, e * LANES : (e + 1) * LANES] = kept.astype(BF16)
                    mine = o_ref[unit, h * size : (h + 1) * size, e * LANES : (e + 1) * LANES]
                    delta[unit, h : h + 1, e * LANES : (e + 1) * LANES] = jnp.sum(
                        kept * mine.astype(F32), axis=0, keepdims=True
                    )
    d_q[...] = jnp.zeros_like(d_q)

    def one_unit(j):
        d_k[...] = jnp.zeros_like(d_k)
        d_v[...] = jnp.zeros_like(d_v)
        keys = [qkv_ref[j, :, (own + h) * LANES : (own + h + 1) * LANES] for h in range(own)]
        turned = [keys[h].astype(F32).T.astype(BF16) for h in range(own)]

        def one_block(i, carry):
            for h in range(own):
                queries = qkv_ref[i, :, h * LANES : (h + 1) * LANES]
                at = (2 * own + h) * LANES
                values = qkv_ref[j, :, at : at + LANES]
                scores = nt(keys[h], queries) * scale
                probs = jnp.exp2(scores - lse_ref[i, h : h + 1, :])
                d_probs = nn(values, up[i, h])
                d_scores = (probs * (d_probs - delta[i, h : h + 1, :])).astype(BF16)
                d_k[h] += nn(d_scores, queries)
                d_v[h] += nt(probs.astype(BF16), up[i, h])
                d_q[i, h] += nn(turned[h], d_scores)
            return carry

        lax.fori_loop(info_ref[1, j], info_ref[2, j], one_block, 0)
        for h in range(own):
            at = (own + h) * LANES
            d_ref[j, :, at : at + LANES] = (d_k[h] * factor).astype(BF16)
            at = (2 * own + h) * LANES
            d_ref[j, :, at : at + LANES] = d_v[h].astype(BF16)

    each(units, one_unit)

    def turn(i):
        for h in range(own):
            d_ref[i, :, h * LANES : (h + 1) * LANES] = (d_q[i, h].T * factor).astype(BF16)

    each(units, turn)


def early_body(width, info_ref, mod_ref, c_ref, o_ref):
    size = c_ref.shape[1]

    def one(u):
        rows = pl.ds(pl.multiple_of(u * width, width), width)
        gate = mod_ref[pl.ds(info_ref[0, u], 1), 5 * size : 6 * size]
        o_ref[rows, :] = (c_ref[rows, :].astype(F32) * gate).astype(BF16)

    each(c_ref.shape[0] // width, one)


def project_body(width, blocks, ids_ref, info_ref, mod_ref, x_ref, *refs):
    om_refs, refs = refs[:blocks], refs[blocks:]
    w_refs, refs = refs[:-8], refs[-8:]
    attn_ref, x1_ref, h_ref, om_ref, w_ref, om_all, w_all, sems = refs
    f, b, c = ids_ref[0], ids_ref[1], ids_ref[2]
    size = x_ref.shape[1]
    copies = fetch(
        [(om_refs[k], om_all.at[lax.bitwise_xor(b, k)]) for k in range(blocks)]
        + [
            (ref, w_all.at[2 * lax.bitwise_xor(f, i // 2) + lax.bitwise_xor(c, i % 2)])
            for i, ref in enumerate(w_refs)
        ],
        sems,
    )
    for copy in copies:
        copy.wait()
    om = om_all[...].reshape(size, x_ref.shape[0])
    weight = w_all[...].reshape(size, size)
    om_ref[...] = om
    w_ref[...] = weight
    attn_ref[...] = tn(om, weight)

    def one(u):
        rows = pl.ds(pl.multiple_of(u * width, width), width)
        slot = info_ref[0, u]
        gate, shift, scale = [
            mod_ref[pl.ds(slot, 1), i * size : (i + 1) * size] for i in (2, 3, 4)
        ]
        middle = x_ref[rows, :].astype(F32) + gate * attn_ref[rows, :]
        x1_ref[rows, :] = middle
        normed, _ = normal(middle)
        h_ref[rows, :] = (normed * (1.0 + scale) + shift).astype(BF16)

    each(x_ref.shape[0] // width, one)


def ff_body(plan1, plan2, outs1, outs2, step, ids_ref, hot_m, hot_o, chan_ref, *refs):
    n1, n2 = len(plan1), len(plan2)
    rows_refs, refs = refs[:4], refs[4:]
    w1_refs, w2_refs, refs = refs[:n1], refs[n1 : n1 + n2], refs[n1 + n2 :]
    mlp_m, mlp_o, dh_m, dh_o = refs[:4]
    g1_refs, refs = refs[4 : 4 + len(outs1)], refs[4 + len(outs1) :]
    g2_refs, refs = refs[: len(outs2)], refs[len(outs2) :]
    w1, w2, h, dm, turned, hid_s, du_s, mlp, dh, g1, g2, sems = refs
    f = ids_ref[0]
    total = h.shape[0]
    count = total // 2
    f_size, size = w2.shape
    row1, row2 = plan1[-1][2], plan2[-1][2]
    shards = size // row1

    def placed(refs, plan, rows, target):
        for ref, (k, start, _) in zip(refs, plan):
            at = pl.multiple_of(lax.bitwise_xor(f, k) * rows + start, 16)
            yield ref, target.at[pl.ds(at, ref.shape[0])]

    copies = fetch(
        [
            (rows_refs[0], h.at[0:count]),
            (rows_refs[1], h.at[count:total]),
            (rows_refs[2], dm.at[0:count]),
            (rows_refs[3], dm.at[count:total]),
        ]
        + list(placed(w1_refs, plan1, row1, w1))
        + list(placed(w2_refs, plan2, row2, w2)),
        sems,
    )
    for copy in copies:
        copy.wait()
    for at in range(0, total, LANES):
        turned[:, at : at + LANES] = h[at : at + LANES, :].astype(F32).T.astype(BF16)
    mlp[...] = jnp.zeros_like(mlp)
    dh[...] = jnp.zeros_like(dh)
    hots = [hot_m[...].astype(BF16), hot_o[...].astype(BF16)]

    def one(index):
        cols = pl.ds(pl.multiple_of(index * step, step), step)
        up = w1[:, cols]
        down = w2[cols, :]
        chan = chan_ref[:, cols].astype(F32).astype(BF16)
        for side in range(2):
            rows = slice(side * count, (side + 1) * count)
            keep = tn(hots[side], chan)
            pre = nn(h[rows, :], up)
            inner = pre * pre
            bent = jnp.tanh(0.7978845608028654 * (pre + 0.044715 * inner * pre))
            half = 0.5 * (1.0 + bent)
            hid = (pre * half * keep).astype(BF16)
            slope = half + (0.5 * 0.7978845608028654) * pre * (1.0 - bent * bent) * (
                1.0 + (3.0 * 0.044715) * inner
            )
            back = nt(dm[rows, :], down)
            du = (slope * back * keep).astype(BF16)
            hid_s[rows, :] = hid
            du_s[rows, :] = du
            mlp[rows, :] += nn(hid, down)
            dh[rows, :] += nt(du, up)
        g1[:, cols] = nn(turned[...], du_s[...]).astype(BF16)
        g2[cols, :] = tn(hid_s[...], dm[...]).astype(BF16)

    each(f_size // step, one)
    mlp_m[...] = mlp[0:count, :]
    mlp_o[...] = mlp[count:total, :].astype(BF16)
    dh_m[...] = dh[0:count, :]
    dh_o[...] = dh[count:total, :].astype(BF16)

    def leave(refs, outs, rows, source):
        for ref, (ks, start, height) in zip(refs, outs):
            for i, k in enumerate(ks):
                at = pl.multiple_of(lax.bitwise_xor(f, k) * rows + start, 16)
                yield source.at[pl.ds(at, height)], ref.at[i]

    copies = fetch(
        list(leave(g1_refs, outs1, row1, g1)) + list(leave(g2_refs, outs2, row2, g2)), sems
    )
    for copy in copies:
        copy.wait()


def middle_body(
    width, blocks, ids_ref, info_ref, mod_ref, x1_ref, c_ref, dh_ref, got_ref, w_ref, *refs
):
    outs, (dx_ref, da_ref, sum_ref) = refs[:blocks], refs[blocks:]
    b = ids_ref[1]
    count, size = x1_ref.shape
    part = size // blocks
    sum_ref[...] = jnp.zeros_like(sum_ref)

    def one(u):
        rows = pl.ds(pl.multiple_of(u * width, width), width)
        slot = info_ref[0, u]
        gate = mod_ref[pl.ds(slot, 1), 2 * size : 3 * size]
        scale = mod_ref[pl.ds(slot, 1), 4 * size : 5 * size]
        normed, spread = normal(x1_ref[rows, :])
        grad = dh_ref[rows, :] + got_ref[rows, :].astype(F32)
        sum_ref[pl.ds(slot, 1), 0:size] += jnp.sum(grad, axis=0, keepdims=True)
        sum_ref[pl.ds(slot, 1), size : 2 * size] += jnp.sum(grad * normed, axis=0, keepdims=True)
        dx = c_ref[rows, :].astype(F32) + normal_back(grad * (1.0 + scale), normed, spread)
        dx_ref[rows, :] = dx
        da_ref[rows, :] = (dx * gate).astype(BF16)

    each(count // width, one)
    for k in range(blocks):
        outs[k][...] = nt(w_ref[lax.bitwise_xor(b, k)], da_ref[...]).astype(BF16)


def result_body(
    width, shards, ids_ref, info_ref, mod_ref, x1_ref, c_ref, mlp_ref, got_ref, attn_ref, dx_ref,
    da_ref, om_ref, perm_ref, r_ref, sum_ref, mine_ref, other_ref, held, grad,
):
    f, c = ids_ref[0], ids_ref[2]
    count, size = x1_ref.shape
    sum_ref[...] = jnp.zeros_like(sum_ref)

    def one(u):
        rows = pl.ds(pl.multiple_of(u * width, width), width)
        slot = info_ref[0, u]
        gate = mod_ref[pl.ds(slot, 1), 5 * size : 6 * size]
        mlp = mlp_ref[rows, :] + got_ref[rows, :].astype(F32)
        held[rows, :] = (x1_ref[rows, :] + gate * mlp).astype(BF16)
        sum_ref[pl.ds(slot, 1), 0:size] += jnp.sum(
            dx_ref[rows, :] * attn_ref[rows, :], axis=0, keepdims=True
        )
        sum_ref[pl.ds(slot, 1), size : 2 * size] += jnp.sum(
            c_ref[rows, :].astype(F32) * mlp, axis=0, keepdims=True
        )

    each(count // width, one)
    r_ref[...] = tn(perm_ref[...], held[...]).astype(BF16)
    grad[...] = nn(om_ref[...], da_ref[...]).astype(BF16).reshape(grad.shape)
    for k in range(shards):
        base = 2 * lax.bitwise_xor(f, k)
        mine_ref[k] = grad[base + c]
        other_ref[k] = grad[base + 1 - c]


def qkv_back_body(plan, outs, blocks, ids_ref, h_ref, d_ref, w_ref, *refs):
    n = len(outs)
    dh_ref, g_refs, (acc, low, sems) = refs[0], refs[1 : 1 + n], refs[1 + n :]
    f = ids_ref[0]
    step = pl.program_id(0)
    per, _, size = h_ref.shape
    rows = plan[-1][2]
    width = BLOCK // blocks
    for i in range(per):
        piece = nt(d_ref[i], w_ref[...]).astype(BF16)
        dh_ref[:, i] = piece.reshape(blocks, width, size)
    part = tn(h_ref[...].reshape(per * BLOCK, size), d_ref[...].reshape(per * BLOCK, -1))

    @pl.when(step == 0)
    def _():
        acc[...] = part

    @pl.when(step > 0)
    def _():
        acc[...] += part

    @pl.when(step == pl.num_programs(0) - 1)
    def _():
        low[...] = acc[...].astype(BF16)
        todo = []
        for ref, (ks, start, height) in zip(g_refs, outs):
            for i, k in enumerate(ks):
                at = pl.multiple_of(lax.bitwise_xor(f, k) * rows + start, 16)
                todo.append((low.at[pl.ds(at, height)], ref.at[i]))
        for copy in fetch(todo, sems):
            copy.wait()


def last_body(width, info_ref, mod_ref, x_ref, dx_ref, dh_ref, perm_ref, o_ref, sum_ref, held):
    count, size = x_ref.shape
    sum_ref[...] = jnp.zeros_like(sum_ref)

    def one(u):
        rows = pl.ds(pl.multiple_of(u * width, width), width)
        slot = info_ref[0, u]
        scale = mod_ref[pl.ds(slot, 1), size : 2 * size]
        normed, spread = normal(x_ref[rows, :].astype(F32))
        grad = dh_ref[rows, :].astype(F32)
        sum_ref[pl.ds(slot, 1), 0:size] += jnp.sum(grad, axis=0, keepdims=True)
        sum_ref[pl.ds(slot, 1), size : 2 * size] += jnp.sum(grad * normed, axis=0, keepdims=True)
        dx = dx_ref[rows, :] + normal_back(grad * (1.0 + scale), normed, spread)
        held[rows, :] = dx.astype(BF16)

    each(count // width, one)
    o_ref[...] = tn(perm_ref[...], held[...]).astype(BF16)


def gather_plan(shards, rows):
    if shards == 4:
        half = rows // 2
        return [(0, 0, rows), (1, 0, rows), (2, 0, rows), (3, 0, rows), (3, half, rows)]
    return [(k, 0, rows) for k in range(shards)]


def gather_rows(own, shards):
    if shards == 4:
        half = own.shape[0] // 2
        one, two = swap(own, "fsdp", 1), swap(own, "fsdp", 2)
        top, low = swap(one[:half], "fsdp", 2), swap(two[half:], "fsdp", 1)
        return [own, one, two, top, low]
    return [own] + [swap(own, "fsdp", k) for k in range(1, shards)]


def reduce_plan(shards, rows):
    if shards == 4:
        half = rows // 2
        return [
            ((0, 2), 0, half),
            ((1, 3), 0, half),
            ((0, 1), half, half),
            ((2, 3), half, half),
        ]
    return [(tuple(range(shards)), 0, rows)]


def add(left, right):
    return (left.astype(F32) + right.astype(F32)).astype(BF16)


def reduce_rows(pieces, shards):
    if shards == 4:
        keep_a, send_a, keep_b, send_b = pieces
        sum_a = add(keep_a, swap(send_a, "fsdp", 1))
        sum_b = add(keep_b, swap(send_b, "fsdp", 2))
        return (
            add(sum_a[0], swap(sum_a[1], "fsdp", 2)),
            add(sum_b[0], swap(sum_b[1], "fsdp", 1)),
        )
    (pieces,) = pieces
    total = pieces[0]
    for k in range(1, shards):
        total = add(total, swap(pieces[k], "fsdp", k))
    half = total.shape[0] // 2
    return total[:half], total[half:]


def sum_chips(pair, chips):
    one, two = pair
    if chips == 4:
        even = (lax.axis_index("blk") // 2) % 2 == 0
        send, keep = jnp.where(even, two, one), jnp.where(even, one, two)
        part = add(keep, swap(send, "blk", 2))
        part = add(part, swap(part, "blk", 4))
        other = swap(part, "blk", 2)
        return jnp.where(even, part, other), jnp.where(even, other, part)
    groups = [[2 * i + core for i in range(chips)] for core in range(2)]
    both = lax.psum(jnp.concatenate([one, two]), "blk", axis_index_groups=groups)
    return both[: one.shape[0]], both[one.shape[0] :]


def line_gather(own, chips):
    out = []
    behind = ahead = own
    for s in range(1, chips):
        first, last = 2 * (s - 1), 2 * (chips - 1)
        behind = lax.ppermute(behind, "blk", [(i, i + 2) for i in range(first, last)])
        ahead = lax.ppermute(ahead, "blk", [(i + 2, i) for i in range(last - first)])
        out += [behind, swap(behind, "blk", 1), ahead, swap(ahead, "blk", 1)]
    return out


def both_cores(array):
    other = swap(array, "blk", 1)
    first = lax.axis_index("blk") % 2 == 0
    return jnp.where(first, array, other), jnp.where(first, other, array)


def on_device(
    tokens,
    timesteps,
    segment_ids,
    head_mask,
    chan_mask,
    token_mask,
    w_temb,
    w_ada,
    w_qkv,
    w_out,
    w_fc1,
    w_fc2,
    cotangent,
):
    count, size = tokens.shape
    slots, heads = head_mask.shape[1:]
    head_size = size // heads
    shards, blocks = lax.axis_size("fsdp"), lax.axis_size("blk")
    chips = blocks // 2
    f, b = lax.axis_index("fsdp"), lax.axis_index("blk")
    c = b % 2
    width = BLOCK // blocks
    units = count // width
    own = heads // blocks
    wide = 3 * own * LANES
    hidden = w_fc1.shape[1]
    half = hidden // 2
    ids = jnp.stack([f, b, c]).astype(I32)

    items = lax.dynamic_slice_in_dim(segment_ids, b * count, count, axis=1)
    x_s, c_s, hot, info, perm = run(
        "sort_tokens",
        functools.partial(sort_body, width),
        [(VMEM, items), (VMEM, token_mask[None, :]), (VMEM, tokens), (VMEM, cotangent)],
        [
            (VMEM, shape((count, size))),
            (VMEM, shape((count, size))),
            (VMEM, shape((slots, count), F32)),
            (VMEM, shape((8, LANES), I32)),
            (VMEM, shape((count, count))),
        ],
    )

    rows = w_temb.shape[0]
    entries = rows * shards
    index = jnp.concatenate([(f ^ k) * rows + lax.iota(I32, rows) for k in range(shards)])
    ladder = jnp.exp(
        -math.log(10000.0) * (index % (entries // 2)).astype(F32) / (entries // 2)
    )
    steps = jnp.concatenate(
        [timesteps[0]] + [swap(timesteps, "fsdp", k)[0] for k in range(1, shards)]
    )
    angles = steps.astype(F32)[:, None] * ladder[None, :]
    spectrum = jnp.where(index[None, :] < entries // 2, jnp.cos(angles), jnp.sin(angles))
    spectrum = spectrum.astype(BF16)
    temb = jnp.concatenate([w_temb] + [swap(w_temb, "fsdp", k) for k in range(1, shards)])
    ada_rows = w_ada.shape[0]
    condition = lax.dynamic_slice_in_dim(nn(spectrum, temb), f * ada_rows, ada_rows, axis=1)
    lifted, silu_pull = jax.vjp(lambda v: v / (1.0 + jnp.exp(-v)), condition)
    lifted = lifted.astype(BF16)
    partial = nn(lifted, w_ada).reshape(shards, slots, -1)
    mod = partial[0]
    for k in range(1, shards):
        mod = mod + swap(partial[k], "fsdp", k)

    x_parts = [x_s, swap(x_s, "blk", 1)] + line_gather(x_s, chips)

    (w_heads,) = run(
        "pick_heads",
        functools.partial(pick_heads_body, own, head_size),
        [(SMEM, ids), (VMEM, w_qkv)],
        [(VMEM, shape((w_qkv.shape[0], wide)))],
    )
    (w_fc1_half,) = run(
        "pick_half",
        functools.partial(pick_half_body, shards),
        [(SMEM, ids), (VMEM, w_fc1)],
        [(VMEM, shape((w_fc1.shape[0], half)))],
    )
    plan_qkv = gather_plan(shards, w_heads.shape[0])
    qkv_parts = gather_rows(w_heads, shards)
    out_rows = w_out.shape[0] // 2
    w_out_half = lax.dynamic_slice_in_dim(w_out, c * out_rows, out_rows)
    w_out_other = lax.dynamic_slice_in_dim(w_out, (1 - c) * out_rows, out_rows)
    w_out_half = after(w_out_half, qkv_parts[1])
    got = [swap(w_out_half, "fsdp", k) for k in range(1, shards)]
    out_parts = [w_out_half, w_out_other]
    for piece in got:
        out_parts += [piece, swap(piece, "blk", 1)]
    plan1 = gather_plan(shards, w_fc1_half.shape[0])
    fc1_parts = gather_rows(after(w_fc1_half, got[0], got[1]), shards)
    fc2_rows = w_fc2.shape[0] // 2
    w_fc2_half = lax.dynamic_slice_in_dim(w_fc2, c * fc2_rows, fc2_rows)
    plan2 = gather_plan(shards, fc2_rows)
    fc2_parts = gather_rows(after(w_fc2_half, fc1_parts[1], fc1_parts[2]), shards)

    (dm,) = run(
        "grad_mlp",
        functools.partial(early_body, width),
        [(SMEM, info), (VMEM, mod), (VMEM, c_s)],
        [(VMEM, shape((count, size)))],
    )
    dm_other = swap(dm, "blk", 1)
    hot_other = swap(hot, "blk", 1)

    whole = pl.BlockSpec(memory_space=pltpu.VMEM)
    n_copies = len(x_parts) + len(plan_qkv)
    normed, qkv = run(
        "norm_qkv",
        functools.partial(first_body, chips, plan_qkv),
        [(SMEM, ids), (SMEM, info), (whole, mod)]
        + [(ANY, part) for part in x_parts]
        + [(ANY, part) for part in qkv_parts],
        [
            (pl.BlockSpec((1, BLOCK, size), lambda u: (u, 0, 0)), shape((units, BLOCK, size))),
            (pl.BlockSpec((1, BLOCK, wide), lambda u: (u, 0, 0)), shape((units, BLOCK, wide))),
        ],
        [
            pltpu.VMEM((blocks, count, size), BF16),
            pltpu.VMEM((size, wide), BF16),
            pltpu.SemaphoreType.DMA((n_copies,)),
        ],
        flops=2 * units * BLOCK * size * wide,
        grid=(units,),
    )

    mask = head_mask[0]
    narrow = own * head_size
    outs = run(
        "attend",
        functools.partial(attend_body, own, head_size, blocks),
        [(SMEM, ids), (SMEM, info), (SMEM, mask), (VMEM, qkv)],
        [
            (VMEM, shape((units, narrow, BLOCK))),
            (VMEM, shape((units, 8, BLOCK), F32)),
        ]
        + [(VMEM, shape((narrow, count)))] * blocks,
        [pltpu.VMEM((units, narrow, BLOCK), F32)],
        flops=2 * units * units * BLOCK * BLOCK * wide // 3,
    )
    held, lse, pieces = outs[0], outs[1], outs[2:]
    om_parts = [pieces[0]] + [swap(pieces[k], "blk", k) for k in range(1, blocks)]

    attn, x1, h2, om, w_out_all = run(
        "project",
        functools.partial(project_body, width, blocks),
        [(SMEM, ids), (SMEM, info), (VMEM, mod), (VMEM, x_s)]
        + [(ANY, part) for part in om_parts]
        + [(ANY, part) for part in out_parts],
        [
            (VMEM, shape((count, size), F32)),
            (VMEM, shape((count, size), F32)),
            (VMEM, shape((count, size))),
            (VMEM, shape((size, count))),
            (VMEM, shape((size, size))),
        ],
        [
            pltpu.VMEM((blocks, narrow, count), BF16),
            pltpu.VMEM((2 * shards, out_rows, size), BF16),
            pltpu.SemaphoreType.DMA((blocks + 2 * shards,)),
        ],
        flops=2 * count * size * size,
    )
    h2_other = swap(h2, "blk", 1)

    outs1 = reduce_plan(shards, w_fc1_half.shape[0])
    outs2 = reduce_plan(shards, fc2_rows)
    chan = chan_mask[0].reshape(slots, shards, 2, half // shards)
    chan = lax.dynamic_slice_in_dim(chan, c, 1, axis=2).reshape(slots, half)
    n_sems = max(
        4 + len(plan1) + len(plan2),
        sum(len(ks) for ks, _, _ in outs1) + sum(len(ks) for ks, _, _ in outs2),
    )
    outs = run(
        "feed_forward",
        functools.partial(ff_body, plan1, plan2, outs1, outs2, 256),
        [(SMEM, ids), (VMEM, hot), (VMEM, hot_other), (VMEM, chan)]
        + [(ANY, a) for a in (h2, h2_other, dm, dm_other)]
        + [(ANY, a) for a in fc1_parts]
        + [(ANY, a) for a in fc2_parts],
        [
            (VMEM, shape((count, size), F32)),
            (VMEM, shape((count, size))),
            (VMEM, shape((count, size), F32)),
            (VMEM, shape((count, size))),
        ]
        + [(ANY, shape((len(ks), height, half))) for ks, _, height in outs1]
        + [(ANY, shape((len(ks), height, size))) for ks, _, height in outs2],
        [
            pltpu.VMEM((size, half), BF16),
            pltpu.VMEM((half, size), BF16),
            pltpu.VMEM((2 * count, size), BF16),
            pltpu.VMEM((2 * count, size), BF16),
            pltpu.VMEM((size, 2 * count), BF16),
            pltpu.VMEM((2 * count, 256), BF16),
            pltpu.VMEM((2 * count, 256), BF16),
            pltpu.VMEM((2 * count, size), F32),
            pltpu.VMEM((2 * count, size), F32),
            pltpu.VMEM((size, half), BF16),
            pltpu.VMEM((half, size), BF16),
            pltpu.SemaphoreType.DMA((n_sems,)),
        ],
        flops=6 * 2 * 2 * count * size * half,
        vmem=60,
    )
    mlp, mlp_send, dh2, dh2_send = outs[:4]
    g1_parts, g2_parts = outs[4 : 4 + len(outs1)], outs[4 + len(outs1) :]
    dh2_got = swap(dh2_send, "blk", 1)
    mlp_got = swap(mlp_send, "blk", 1)

    outs = run(
        "middle_back",
        functools.partial(middle_body, width, blocks),
        [(SMEM, ids), (SMEM, info), (VMEM, mod), (VMEM, x1), (VMEM, c_s), (VMEM, dh2)]
        + [(VMEM, dh2_got), (VMEM, w_out_all.reshape(blocks, narrow, size))],
        [(VMEM, shape((narrow, count)))] * blocks
        + [
            (VMEM, shape((count, size), F32)),
            (VMEM, shape((count, size))),
            (VMEM, shape((slots, 2 * size), F32)),
        ],
        flops=2 * count * size * size,
    )
    pieces, (dx1, d_attn, sums_two) = outs[:blocks], outs[blocks:]
    up_parts = [pieces[0]] + [swap(pieces[k], "blk", k) for k in range(1, blocks)]

    result, sums_gate, g_out, g_out_send = run(
        "result",
        functools.partial(result_body, width, shards),
        [(SMEM, ids), (SMEM, info)]
        + [(VMEM, a) for a in (mod, x1, c_s, mlp, mlp_got, attn, dx1, d_attn, om, perm)],
        [
            (VMEM, shape((count, size))),
            (VMEM, shape((slots, 2 * size), F32)),
            (VMEM, shape((shards, out_rows, size))),
            (VMEM, shape((shards, out_rows, size))),
        ],
        [pltpu.VMEM((count, size), BF16), pltpu.VMEM((2 * shards, out_rows, size), BF16)],
        flops=2 * count * size * size,
    )
    g_out = add(g_out, swap(g_out_send, "blk", 1))

    (d_qkv,) = run(
        "attend_back",
        functools.partial(attend_back_body, own, head_size, blocks),
        [(SMEM, ids), (SMEM, info), (SMEM, mask)]
        + [(VMEM, a) for a in (qkv, held, lse)]
        + [(VMEM, a) for a in up_parts],
        [(VMEM, shape((units, BLOCK, wide)))],
        [
            pltpu.VMEM((blocks, narrow, count), BF16),
            pltpu.VMEM((units, own, LANES, BLOCK), BF16),
            pltpu.VMEM((units, 8, BLOCK), F32),
            pltpu.VMEM((units, own, LANES, BLOCK), F32),
            pltpu.VMEM((own, BLOCK, LANES), F32),
            pltpu.VMEM((own, BLOCK, LANES), F32),
        ],
        flops=5 * units * units * BLOCK * BLOCK * wide // 3,
    )
    w_heads_all = jnp.zeros((size, wide), BF16)
    for part, (k, start, rows_in) in zip(qkv_parts, plan_qkv):
        w_heads_all = lax.dynamic_update_slice_in_dim(
            w_heads_all, part, (f ^ k) * rows_in + start, axis=0
        )
    per = 4
    outs_qkv = reduce_plan(shards, w_heads.shape[0])
    outs = run(
        "qkv_back",
        functools.partial(qkv_back_body, plan_qkv, outs_qkv, blocks),
        [
            (SMEM, ids),
            (pl.BlockSpec((per, BLOCK, size), lambda i: (i, 0, 0)), normed),
            (pl.BlockSpec((per, BLOCK, wide), lambda i: (i, 0, 0)), d_qkv),
            (whole, w_heads_all),
        ],
        [
            (
                pl.BlockSpec((blocks, per, width, size), lambda i: (0, i, 0, 0)),
                shape((blocks, units, width, size)),
            )
        ]
        + [(ANY, shape((len(ks), height, wide))) for ks, _, height in outs_qkv],
        [
            pltpu.VMEM((size, wide), F32),
            pltpu.VMEM((size, wide), BF16),
            pltpu.SemaphoreType.DMA((2 * shards,)),
        ],
        flops=4 * units * BLOCK * size * wide,
        grid=(units // per,),
    )
    d_normed, gq_parts = outs[0], outs[1:]
    d_normed = lax.psum_scatter(
        d_normed.reshape(blocks * count, size), "blk", scatter_dimension=0, tiled=True
    )
    grad_tokens, sums_one = run(
        "first_back",
        functools.partial(last_body, width),
        [(SMEM, info)] + [(VMEM, a) for a in (mod, x_s, dx1, d_normed, perm)],
        [(VMEM, shape((count, size))), (VMEM, shape((slots, 2 * size), F32))],
        [pltpu.VMEM((count, size), BF16)],
    )

    def over_stream(sums):
        low = sums.astype(BF16)
        total = low.astype(F32)
        for k in (1, 2, 4, 8, 16):
            if k < blocks:
                total = total + swap(total, "blk", k)
        low = total.astype(BF16)
        return jnp.concatenate([low] + [swap(low, "fsdp", k) for k in range(1, shards)])

    gate_all, two_all, one_all = over_stream(sums_gate), over_stream(sums_two), over_stream(sums_one)
    d_mod = jnp.concatenate(
        [one_all, gate_all[:, :size], two_all, gate_all[:, size:]], axis=1
    )
    grad_ada = tn(lifted, d_mod)
    (d_condition,) = silu_pull(nt(d_mod, w_ada))
    d_all = jnp.zeros((shards * slots, size), F32)
    for k in range(shards):
        piece = d_condition if k == 0 else swap(d_condition, "fsdp", k)
        piece = piece.reshape(shards, slots, ada_rows)
        piece = jnp.concatenate([piece[r ^ k] for r in range(shards)])
        d_all = lax.dynamic_update_slice_in_dim(d_all, piece, (f ^ k) * ada_rows, axis=1)
    grad_temb = lax.dot_general(
        spectrum[:, :rows].astype(F32), d_all, (((0,), (0,)), ((), ())), precision=HIGH
    )

    g1_one, g1_two = sum_chips(reduce_rows(g1_parts, shards), chips)
    g2_one, g2_two = sum_chips(reduce_rows(g2_parts, shards), chips)
    if shards == 4:
        cut = out_rows // 2
        pieces = [
            jnp.stack([g_out[0, :cut], g_out[2, :cut]]),
            jnp.stack([g_out[1, :cut], g_out[3, :cut]]),
            g_out[0:2, cut:],
            g_out[2:4, cut:],
        ]
    else:
        pieces = [g_out]
    o_one, o_two = sum_chips(reduce_rows(pieces, shards), chips)
    first, second = both_cores(jnp.concatenate([o_one, o_two]))
    grad_out = jnp.concatenate([first, second]).astype(F32)
    first, second = both_cores(jnp.concatenate([g2_one, g2_two]))
    grad_fc2 = jnp.concatenate([first, second]).astype(F32)
    first, second = both_cores(jnp.concatenate([g1_one, g1_two]))
    part = half // shards
    grad_fc1 = jnp.concatenate(
        [side[:, i * part : (i + 1) * part] for i in range(shards) for side in (first, second)],
        axis=1,
    ).astype(F32)
    gq = lax.all_gather(jnp.concatenate(reduce_rows(gq_parts, shards)), "blk", axis=0)
    gq = gq.reshape(blocks, -1, 3, own, LANES)[..., :head_size]
    grad_qkv = jnp.transpose(gq, (1, 2, 0, 3, 4)).reshape(w_qkv.shape).astype(F32)
    return (
        result,
        grad_tokens,
        grad_temb,
        grad_ada,
        grad_qkv,
        grad_out,
        grad_fc1,
        grad_fc2,
    )


def solution(mesh):
    placed = (
        P(("fsdp", "blk"), None),
        P("fsdp", None),
        P("fsdp", None),
        P("fsdp", None, None),
        P("fsdp", None, None),
        P(("fsdp", "blk")),
        P("fsdp", None),
        P("fsdp", None),
        P("fsdp", None),
        P("fsdp", None),
        P("fsdp", None),
        P("fsdp", None),
        P(("fsdp", "blk"), None),
    )
    return jax.shard_map(
        on_device,
        mesh=mesh,
        in_specs=placed,
        out_specs=(
            P(("fsdp", "blk"), None),
            P(("fsdp", "blk"), None),
            P("fsdp", None),
            P("fsdp", None),
            P("fsdp", None),
            P("fsdp", None),
            P("fsdp", None),
            P("fsdp", None),
        ),
        check_vma=False,
    )
```

```python
import functools
import math

import jax
import jax.numpy as jnp
from jax import lax
from jax.experimental import pallas as pl
from jax.experimental.pallas import tpu as pltpu
from jax.sharding import PartitionSpec as P

HIGH = lax.Precision.HIGHEST
BF16 = jnp.bfloat16
F32 = jnp.float32
I32 = jnp.int32
LANES = 128
BLOCK = 256
NEG = -1e30
LOG2E = 1.4426950408889634

VMEM = pl.BlockSpec(memory_space=pltpu.VMEM)
SMEM = pl.BlockSpec(memory_space=pltpu.SMEM)
ANY = pl.BlockSpec(memory_space=pl.ANY)


def shape(dims, kind=BF16):
    return jax.ShapeDtypeStruct(tuple(dims), kind)


def run(name, body, ins, outs, scratch=(), flops=0, vmem=48, collective=None, **more):
    moved = sum(a.size * a.dtype.itemsize for _, a in ins)
    moved += sum(math.prod(o.shape) * jnp.dtype(o.dtype).itemsize for _, o in outs)
    return pl.pallas_call(
        body,
        out_shape=[o for _, o in outs],
        in_specs=[s for s, _ in ins],
        out_specs=[s for s, _ in outs],
        scratch_shapes=list(scratch),
        compiler_params=pltpu.CompilerParams(
            vmem_limit_bytes=vmem << 20,
            collective_id=collective,
            has_side_effects=collective is not None,
        ),
        cost_estimate=pl.CostEstimate(flops=flops, bytes_accessed=moved, transcendentals=0),
        name=name,
        **more,
    )(*[a for _, a in ins])


def swap(array, axis, by):
    size = lax.axis_size(axis)
    return lax.ppermute(array, axis, [(i, i ^ by) for i in range(size)])


def after(array, *others):
    return lax.optimization_barrier((array,) + others)[0]


def frequencies(steps, entries):
    half = entries // 2
    ladder = jnp.exp(-math.log(10000.0) * lax.iota(jnp.int32, half) / half)
    angles = steps.astype(F32)[:, None] * ladder[None, :]
    return jnp.concatenate([jnp.cos(angles), jnp.sin(angles)], axis=1)


def nn(left, right):
    return lax.dot_general(left, right, (((1,), (0,)), ((), ())), preferred_element_type=F32)


def nt(left, right):
    return lax.dot_general(left, right, (((1,), (1,)), ((), ())), preferred_element_type=F32)


def tn(left, right):
    return lax.dot_general(left, right, (((0,), (0,)), ((), ())), preferred_element_type=F32)


def each(count, step, group=1):
    if count % group:
        group = 1

    def one(index, carry):
        for i in range(group):
            step(index * group + i)
        return carry

    lax.fori_loop(0, count // group, one, 0)


def normal(values):
    center = values - jnp.mean(values, axis=-1, keepdims=True)
    scale = lax.rsqrt(jnp.mean(center * center, axis=-1, keepdims=True) + 1e-06)
    return center * scale, scale


def normal_back(grad, normed, scale):
    along = jnp.mean(grad * normed, axis=-1, keepdims=True)
    return scale * (grad - jnp.mean(grad, axis=-1, keepdims=True) - normed * along)


def flip(index, by):
    bit = 1
    while bit <= by:
        if by & bit:
            index = index + bit * (1 - 2 * ((index // bit) % 2))
        bit *= 2
    return index


def fetch(pairs, sems, first=0):
    copies = []
    for index, (source, target) in enumerate(pairs, first):
        copy = pltpu.make_async_copy(source, target, sems.at[index])
        copy.start()
        copies.append(copy)
    return copies


class Routes:
    def __init__(self, sent, got):
        self.sent, self.got, self.known, self.started = sent, got, {}, []

    def slot(self, name):
        return self.known.setdefault(name, len(self.known))

    def copy(self, name, source, target, to):
        slot = self.slot(name)
        return pltpu.make_async_remote_copy(
            src_ref=source,
            dst_ref=target,
            send_sem=self.sent.at[slot],
            recv_sem=self.got.at[slot],
            device_id=to,
            device_id_type=pl.DeviceIdType.MESH,
        )

    def start(self, name, source, target, to, when=None):
        def make():
            return self.copy(name, source, target, to)

        self.started.append((make, when))
        if when is None:
            make().start()
        else:
            pl.when(when)(lambda: make().start())

    def arrive(self, name, target, when=None):
        def wait():
            b = lax.axis_index("blk")
            self.copy(name, target, target, {"blk": b + 1 - 2 * (b % 2)}).wait_recv()

        if when is None:
            wait()
        else:
            pl.when(when)(wait)

    def finish(self):
        for make, when in self.started:
            if when is None:
                make().wait_send()
            else:
                pl.when(when)(lambda make=make: make().wait_send())


def greet(shards, chips):
    f, b = lax.axis_index("fsdp"), lax.axis_index("blk")
    z, c = b // 2, b % 2
    barrier = pltpu.get_barrier_semaphore()

    def signal(to):
        pl.semaphore_signal(barrier, inc=1, device_id=to, device_id_type=pl.DeviceIdType.MESH)

    for k in range(1, shards):
        signal({"fsdp": flip(f, k)})
    signal({"blk": b + 1 - 2 * c})
    pl.when(z > 0)(lambda: signal({"blk": b - 2}))
    pl.when(z < chips - 1)(lambda: signal({"blk": b + 2}))
    ends = (z == 0).astype(I32) + (z == chips - 1).astype(I32)
    pl.semaphore_wait(barrier, shards + 2 - ends)


def pick_half_body(parts, ids_ref, w1_ref, w2_ref, o_ref):
    rows, hidden = w1_ref.shape
    half = hidden // parts // 2
    size = o_ref.shape[1]
    down = w2_ref.shape[0] // 2
    blocks = hidden // 2 // size
    for core in range(2):

        @pl.when(ids_ref[2] == core)
        def _():
            picked = jnp.concatenate(
                [
                    w1_ref[:, (2 * part + core) * half : (2 * part + core + 1) * half]
                    for part in range(parts)
                ],
                axis=1,
            )
            for block in range(blocks):
                o_ref[block * rows : (block + 1) * rows, :] = picked[
                    :, block * size : (block + 1) * size
                ]
            o_ref[blocks * rows :, :] = w2_ref[core * down : (core + 1) * down, :]


def front_body(
    shards, chips, heads, items_ref, keep_ref, x_ref, c_ref, spec_ref, temb_ref, ada_ref, qkvw_ref,
    outw_ref, xs_ref, cs_ref, hot_ref, info_ref, perm_ref, mod_ref, cond_ref, low_ref, dm_ref, h_ref,
    qkv_ref, wh_ref, wo_ref, x_all, spec_all, temb_all, part_own, part_got, hots, dms, wh_all, wo_all,
    h_all, ada_s, qkvw_s, local, sent, got,
):
    f, b = lax.axis_index("fsdp"), lax.axis_index("blk")
    z, c = b // 2, b % 2
    blocks = 2 * chips
    pair = b + 1 - 2 * c
    width = BLOCK // blocks
    count, size = x_ref.shape
    units = count // width
    own = heads // blocks
    head_size = size // heads
    slots = spec_ref.shape[0]
    routes = Routes(sent, got)
    inside = fetch(
        [(ada_ref, ada_s), (qkvw_ref, qkvw_s), (outw_ref, wo_all.at[f])], local, units
    )
    greet(shards, chips)

    spec_all[f] = spec_ref[...]
    temb_all[f] = temb_ref[...]
    for k in range(1, shards):
        to = {"fsdp": flip(f, k)}
        routes.start(("spec", k), spec_ref, spec_all.at[f], to)
        routes.start(("temb", k), temb_ref, temb_all.at[f], to)

    items = items_ref[...]
    slot = lax.broadcasted_iota(I32, (slots, count), 0)
    hot = (items == slot).astype(F32)
    start = jnp.sum((items < slot).astype(F32), axis=1, keepdims=True)
    end = start + jnp.sum(hot, axis=1, keepdims=True)
    row = lax.broadcasted_iota(I32, (count, count), 0)
    col = lax.broadcasted_iota(I32, (count, count), 1)
    rank = nn(hot.astype(BF16), (row <= col).astype(BF16))
    place = jnp.sum(hot * (start + rank), axis=0, keepdims=True) - 1.0
    perm = (row.astype(F32) == place).astype(BF16)
    perm_ref[...] = perm
    x_s = nn(perm, x_ref[...]).astype(BF16)
    xs_ref[...] = x_s
    x_all[b] = x_s

    def line(side, s, send):
        away = s - 1 if send else s
        chip = z - away if side == 0 else z + away
        ahead = z + 1 < chips if side == 0 else z > 0
        known = z >= away if side == 0 else z + away < chips
        when = known & ahead if send else known
        return chip * 2 + c, {"blk": b + 2 if side == 0 else b - 2}, when

    def send_on(s):
        for side in range(2):
            device, to, when = line(side, s, True)
            routes.start(("line", side, s), x_all.at[device], x_all.at[device], to, when)

    send_on(1)
    routes.start("pair", x_all.at[b], x_all.at[b], {"blk": pair})
    cs_ref[...] = nn(perm, c_ref[...]).astype(BF16)
    keep = jnp.broadcast_to(keep_ref[...].astype(F32), (slots, count)).astype(BF16)
    kept = nt(keep, perm)
    at = lax.broadcasted_iota(I32, (slots, count), 1).astype(F32)
    hots[0] = kept * ((at >= start) & (at < end)).astype(F32)
    first = (lax.broadcasted_iota(I32, (slots, LANES), 1) * width).astype(F32)
    mine = ((first >= start) & (first < end)).astype(F32)
    which = lax.broadcasted_iota(I32, (slots, LANES), 0).astype(F32)
    info_ref[0:1, :] = jnp.sum(mine * which, axis=0, keepdims=True).astype(I32)
    info_ref[1:2, :] = (jnp.sum(mine * start, axis=0, keepdims=True) / width).astype(I32)
    info_ref[2:3, :] = (jnp.sum(mine * end, axis=0, keepdims=True) / width).astype(I32)
    info_ref[3:8, :] = jnp.zeros((5, LANES), I32)

    for k in range(1, shards):
        other = flip(f, k)
        routes.arrive(("spec", k), spec_all.at[other])
        routes.arrive(("temb", k), temb_all.at[other])
    spectra = spec_all[...].reshape(shards * slots, -1).astype(BF16)
    condition = nn(spectra, temb_all[...].reshape(-1, size))
    rows = ada_ref.shape[0]
    for shard in range(shards):

        @pl.when(f == shard)
        def _():
            cond_ref[...] = condition[:, shard * rows : (shard + 1) * rows]

    values = cond_ref[...]
    lifted = (values / (1.0 + jnp.exp(-values))).astype(BF16)
    low_ref[...] = lifted
    inside[0].wait()
    part_own[...] = nn(lifted, ada_s[...]).reshape(part_own.shape)
    for k in range(1, shards):
        other = flip(f, k)
        routes.start(("part", k), part_own.at[other], part_got.at[f], {"fsdp": other})

    rows = qkvw_ref.shape[0]
    inside[1].wait()
    row = lax.broadcasted_iota(I32, (size, LANES), 0)
    col = lax.broadcasted_iota(I32, (size, LANES), 1)
    picked = []
    for head in range(own):
        mark = (row == (b * own + head) * head_size + col) & (col < head_size)
        picked.append(mark.astype(F32).astype(BF16))
    for part in range(3):
        for head in range(own):
            at = (part * own + head) * LANES
            wh_all[f, :, at : at + LANES] = nn(
                qkvw_s[:, part * size : (part + 1) * size], picked[head]
            ).astype(BF16)
    if shards == 4:
        for k in (1, 2):
            routes.start(("head", k), wh_all.at[f], wh_all.at[f], {"fsdp": flip(f, k)})
    else:
        for k in range(1, shards):
            routes.start(("head", k), wh_all.at[f], wh_all.at[f], {"fsdp": flip(f, k)})

    def take(s):
        for side in range(2):
            device, _, when = line(side, s, False)
            routes.arrive(("line", side, s), x_all.at[device], when)
            if s + 1 < chips:
                device, to, onward = line(side, s + 1, True)
                routes.start(
                    ("line", side, s + 1), x_all.at[device], x_all.at[device], to, onward
                )
            device, _, when = line(side, s, False)
            routes.start(
                ("pair", side, s), x_all.at[device], x_all.at[device], {"blk": pair}, when
            )

    take(1)
    if shards == 4:
        half = rows // 2
        for k, low in ((1, 0), (2, half)):
            routes.arrive(("head", k), wh_all.at[flip(f, k)])
            part = wh_all.at[flip(f, k), low : low + half]
            routes.start(("head", 3, k), part, part, {"fsdp": flip(f, 3 - k)})

    for k in range(1, shards):
        routes.start(("out", k), outw_ref.at[c], wo_all.at[f, c], {"fsdp": flip(f, k)})

    total = part_own[f]
    for k in range(1, shards):
        other = flip(f, k)
        routes.arrive(("part", k), part_got.at[other])
        total = total + part_got[other]
    mod_ref[...] = lax.dot_general(
        mine[:, : mod_ref.shape[0]], total, (((0,), (0,)), ((), ())), precision=HIGH,
        preferred_element_type=F32,
    )

    def early(u):
        rows = pl.ds(pl.multiple_of(u * width, width), width)
        gate = mod_ref[pl.ds(u, 1), 5 * size : 6 * size]
        dms[0, rows, :] = (cs_ref[rows, :].astype(F32) * gate).astype(BF16)

    each(units, early)
    routes.start("dm", dms.at[0], dms.at[1], {"blk": pair})
    routes.start("hot", hots.at[0], hots.at[1], {"blk": pair})

    if shards == 4:
        half = rows // 2
        routes.arrive(("head", 3, 1), wh_all.at[flip(f, 3), 0:half])
        routes.arrive(("head", 3, 2), wh_all.at[flip(f, 3), half:rows])
    else:
        for k in range(1, shards):
            routes.arrive(("head", k), wh_all.at[flip(f, k)])
    wh_ref[...] = wh_all[...].reshape(wh_ref.shape)

    def block(device):
        at = pl.ds(pl.multiple_of(device * width, width), width)

        def one(u):
            shift = mod_ref[pl.ds(u, 1), 0:size]
            scale = mod_ref[pl.ds(u, 1), size : 2 * size]
            part = x_all[device, pl.ds(pl.multiple_of(u * width, width), width), :]
            normed, _ = normal(part.astype(F32))
            low = (normed * (1.0 + scale) + shift).astype(BF16)
            h_all[pl.ds(pl.multiple_of(u * width, width), width), :] = low

        each(units, one, 3)
        copies = fetch(
            [
                (h_all.at[u * width : (u + 1) * width], h_ref.at[u, at])
                for u in range(units)
            ],
            local,
        )
        found = nn(h_all[...], wh_ref[...]).astype(BF16)
        qkv_ref[:, at, :] = found.reshape(units, width, found.shape[1])
        for copy in copies:
            copy.wait()

    routes.arrive("pair", x_all.at[pair])
    each(2, lambda core: block(z * 2 + core))

    def work(s):
        for side in range(2):
            device, _, when = line(side, s, False)
            routes.arrive(("pair", side, s), x_all.at[device + 1 - 2 * c], when)

        def pick(q):
            chip = z - s + 2 * s * (q // 2)

            @pl.when((chip >= 0) & (chip < chips))
            def _():
                block(chip * 2 + q % 2)

        each(4, pick)

    for s in range(2, chips):
        take(s)
        if s == 2:
            for k in range(1, shards):
                other = flip(f, k)
                routes.arrive(("out", k), wo_all.at[other, c])
                routes.start(
                    ("pair out", k), wo_all.at[other, c], wo_all.at[other, c], {"blk": pair}
                )
        work(s - 1)
    work(chips - 1)
    inside[2].wait()
    for k in range(1, shards):
        routes.arrive(("pair out", k), wo_all.at[flip(f, k), 1 - c])
    routes.arrive("dm", dms.at[1])
    routes.arrive("hot", hots.at[1])
    routes.finish()
    copies = fetch([(wo_all, wo_ref), (dms, dm_ref), (hots, hot_ref)], local)
    for copy in copies:
        copy.wait()


def exchange_lanes(tiles, width):
    tiles = list(tiles)
    count = len(tiles)
    group = lax.broadcasted_iota(I32, tiles[0].shape, 1) // width
    half = count // 2
    while half:
        low = (group // half) % 2 == 0
        fresh = list(tiles)
        for i in range(count):
            if (i // half) % 2 == 0:
                a, d = tiles[i], tiles[i + half]
                fresh[i] = jnp.where(low, a, pltpu.roll(d, half * width, 1))
                fresh[i + half] = jnp.where(low, pltpu.roll(a, LANES - half * width, 1), d)
        tiles = fresh
        half //= 2
    return tiles


def attend_body(own, size, blocks, ids_ref, info_ref, mask_ref, qkv_ref, o_ref, lse_ref, *refs):
    outs, (held,) = refs[:blocks], refs[blocks:]
    units = qkv_ref.shape[0]
    width = BLOCK // blocks
    b = ids_ref[1]
    scale = LOG2E / math.sqrt(size)
    pad = -size % 16

    def one_unit(u):
        queries = [qkv_ref[u, :, h * LANES : (h + 1) * LANES] for h in range(own)]

        def one_block(j, carry):
            fresh = []
            for h in range(own):
                top, total, acc = carry[h]
                keys = qkv_ref[j, :, (own + h) * LANES : (own + h + 1) * LANES]
                at = (2 * own + h) * LANES
                values = qkv_ref[j, :, at : at + LANES]
                scores = nt(keys, queries[h]) * scale
                new_top = jnp.maximum(top, jnp.max(scores, axis=0, keepdims=True))
                probs = jnp.exp2(scores - new_top)
                decay = jnp.exp2(top - new_top)
                total = total * decay + jnp.sum(probs, axis=0, keepdims=True)
                acc = acc * decay + tn(values, probs.astype(BF16))
                fresh.append((new_top, total, acc))
            return tuple(fresh)

        start = tuple(
            (
                jnp.full((1, BLOCK), NEG, F32),
                jnp.zeros((1, BLOCK), F32),
                jnp.zeros((LANES, BLOCK), F32),
            )
            for _ in range(own)
        )
        done = lax.fori_loop(info_ref[1, u], info_ref[2, u], one_block, start)
        slot = info_ref[0, u]
        rows = []
        for h in range(own):
            top, total, acc = done[h]
            keep = mask_ref[slot, b * own + h].astype(F32)
            rows.append((acc * (keep / total))[0:size])
            lse_ref[u, h : h + 1, :] = top + jnp.log2(total)
        held[u] = jnp.concatenate(rows, axis=0) if own > 1 else rows[0]
        o_ref[u] = held[u].astype(BF16)

    each(units, one_unit)
    groups = LANES // width
    for g in range(units // groups):
        for e in range(blocks // groups):
            tiles = [
                held[groups * g + i, :, e * LANES : (e + 1) * LANES] for i in range(groups)
            ]
            for j, tile in enumerate(exchange_lanes(tiles, width)):
                device = groups * e + j
                for k in range(blocks):

                    @pl.when(lax.bitwise_xor(b, k) == device)
                    def _():
                        outs[k][:, g * LANES : (g + 1) * LANES] = tile.astype(BF16)


def attend_back_body(own, size, blocks, ids_ref, info_ref, mask_ref, qkv_ref, o_ref, lse_ref, *refs):
    pieces, (d_ref, given, up, delta, d_q, d_k, d_v) = refs[:blocks], refs[blocks:]
    units = qkv_ref.shape[0]
    width = BLOCK // blocks
    b = ids_ref[1]
    factor = 1.0 / math.sqrt(size)
    scale = LOG2E * factor
    for k in range(blocks):
        given[lax.bitwise_xor(b, k)] = pieces[k][...]
    up[...] = jnp.zeros_like(up)
    groups = LANES // width
    for g in range(units // groups):
        for e in range(blocks // groups):
            tiles = [
                given[groups * e + j, :, g * LANES : (g + 1) * LANES].astype(F32)
                for j in range(groups)
            ]
            for i, tile in enumerate(exchange_lanes(tiles, width)):
                unit = groups * g + i
                slot = info_ref[0, unit]
                for h in range(own):
                    keep = mask_ref[slot, b * own + h].astype(F32)
                    kept = tile[h * size : (h + 1) * size] * keep
                    up[unit, h, 0:size, e * LANES : (e + 1) * LANES] = kept.astype(BF16)
                    mine = o_ref[unit, h * size : (h + 1) * size, e * LANES : (e + 1) * LANES]
                    delta[unit, h : h + 1, e * LANES : (e + 1) * LANES] = jnp.sum(
                        kept * mine.astype(F32), axis=0, keepdims=True
                    )
    d_q[...] = jnp.zeros_like(d_q)

    def one_unit(j):
        d_k[...] = jnp.zeros_like(d_k)
        d_v[...] = jnp.zeros_like(d_v)
        keys = [qkv_ref[j, :, (own + h) * LANES : (own + h + 1) * LANES] for h in range(own)]
        turned = [keys[h].astype(F32).T.astype(BF16) for h in range(own)]

        def one_block(i, carry):
            for h in range(own):
                queries = qkv_ref[i, :, h * LANES : (h + 1) * LANES]
                at = (2 * own + h) * LANES
                values = qkv_ref[j, :, at : at + LANES]
                scores = nt(keys[h], queries) * scale
                probs = jnp.exp2(scores - lse_ref[i, h : h + 1, :])
                d_probs = nn(values, up[i, h])
                d_scores = (probs * (d_probs - delta[i, h : h + 1, :])).astype(BF16)
                d_k[h] += nn(d_scores, queries)
                d_v[h] += nt(probs.astype(BF16), up[i, h])
                d_q[i, h] += nn(turned[h], d_scores)
            return carry

        lax.fori_loop(info_ref[1, j], info_ref[2, j], one_block, 0)
        for h in range(own):
            at = (own + h) * LANES
            d_ref[j, :, at : at + LANES] = (d_k[h] * factor).astype(BF16)
            at = (2 * own + h) * LANES
            d_ref[j, :, at : at + LANES] = d_v[h].astype(BF16)

    each(units, one_unit)

    def turn(i):
        for h in range(own):
            d_ref[i, :, h * LANES : (h + 1) * LANES] = (d_q[i, h].T * factor).astype(BF16)

    each(units, turn)


def project_body(width, blocks, ids_ref, mod_ref, x_ref, w_ref, *refs):
    om_refs, refs = refs[:blocks], refs[blocks:]
    attn_ref, x1_ref, h_ref, om_ref, om_all, sems = refs
    b = ids_ref[1]
    size = x_ref.shape[1]
    copies = fetch(
        [(om_refs[k], om_all.at[lax.bitwise_xor(b, k)]) for k in range(blocks)], sems
    )
    for copy in copies:
        copy.wait()
    om = om_all[...].reshape(size, x_ref.shape[0])
    om_ref[...] = om
    weight = w_ref[...]
    attn_ref[...] = tn(om, weight)

    def one(u):
        rows = pl.ds(pl.multiple_of(u * width, width), width)
        gate, shift, scale = [mod_ref[pl.ds(u, 1), i * size : (i + 1) * size] for i in (2, 3, 4)]
        middle = x_ref[rows, :].astype(F32) + gate * attn_ref[rows, :]
        x1_ref[rows, :] = middle
        normed, _ = normal(middle)
        h_ref[rows, :] = (normed * (1.0 + scale) + shift).astype(BF16)

    each(x_ref.shape[0] // width, one)


def ff_body(shards, step, hot_ref, chan_ref, h_m, h_o, dm_ref, w_ref, *refs):
    mlp_m, mlp_o, dh_m, dh_o, g_ref, w1, w2, h, dm, turned, hid_s, du_s, mlp, dh, g1, g2, sems = refs
    total = h.shape[0]
    count = total // 2
    f_size, size = w2.shape
    blocks = f_size // size
    row1, row2 = size // shards, f_size // shards

    def placed(rows, one, two):
        for shard in range(shards):
            for block in range(blocks):
                yield (
                    rows.at[shard, block * row1 : (block + 1) * row1],
                    one.at[shard * row1 : (shard + 1) * row1, block * size : (block + 1) * size],
                )
            yield rows.at[shard, blocks * row1 :], two.at[shard * row2 : (shard + 1) * row2]

    copies = fetch(
        [
            (h_m, h.at[0:count]),
            (h_o, h.at[count:total]),
            (dm_ref.at[0], dm.at[0:count]),
            (dm_ref.at[1], dm.at[count:total]),
        ]
        + list(placed(w_ref, w1, w2)),
        sems,
    )
    for copy in copies:
        copy.wait()
    for at in range(0, total, LANES):
        turned[:, at : at + LANES] = h[at : at + LANES, :].astype(F32).T.astype(BF16)
    mlp[...] = jnp.zeros_like(mlp)
    dh[...] = jnp.zeros_like(dh)
    hots = [hot_ref[side].astype(BF16) for side in range(2)]

    def one(index):
        cols = pl.ds(pl.multiple_of(index * step, step), step)
        up = w1[:, cols]
        down = w2[cols, :]
        chan = chan_ref[:, cols].astype(F32).astype(BF16)
        for side in range(2):
            rows = slice(side * count, (side + 1) * count)
            keep = tn(hots[side], chan)
            pre = nn(h[rows, :], up)
            inner = pre * pre
            bent = jnp.tanh(0.7978845608028654 * (pre + 0.044715 * inner * pre))
            half = 0.5 * (1.0 + bent)
            hid = (pre * half * keep).astype(BF16)
            slope = half + (0.5 * 0.7978845608028654) * pre * (1.0 - bent * bent) * (
                1.0 + (3.0 * 0.044715) * inner
            )
            back = nt(dm[rows, :], down)
            du = (slope * back * keep).astype(BF16)
            hid_s[rows, :] = hid
            du_s[rows, :] = du
            mlp[rows, :] += nn(hid, down)
            dh[rows, :] += nt(du, up)
        g1[:, cols] = nn(turned[...], du_s[...]).astype(BF16)
        g2[cols, :] = tn(hid_s[...], dm[...]).astype(BF16)

    each(f_size // step, one)
    mlp_m[...] = mlp[0:count, :]
    mlp_o[...] = mlp[count:total, :].astype(BF16)
    dh_m[...] = dh[0:count, :]
    dh_o[...] = dh[count:total, :].astype(BF16)

    for copy in fetch([(found, rows) for rows, found in placed(g_ref, g1, g2)], sems):
        copy.wait()


def middle_body(
    width, blocks, ids_ref, info_ref, mod_ref, x1_ref, c_ref, dh_ref, got_ref, w_ref, *refs
):
    outs, (dx_ref, da_ref, sum_ref) = refs[:blocks], refs[blocks:]
    b = ids_ref[1]
    count, size = x1_ref.shape
    part = size // blocks
    sum_ref[...] = jnp.zeros_like(sum_ref)

    def one(u):
        rows = pl.ds(pl.multiple_of(u * width, width), width)
        slot = info_ref[0, u]
        gate = mod_ref[pl.ds(u, 1), 2 * size : 3 * size]
        scale = mod_ref[pl.ds(u, 1), 4 * size : 5 * size]
        normed, spread = normal(x1_ref[rows, :])
        grad = dh_ref[rows, :] + got_ref[rows, :].astype(F32)
        sum_ref[pl.ds(slot, 1), 0:size] += jnp.sum(grad, axis=0, keepdims=True)
        sum_ref[pl.ds(slot, 1), size : 2 * size] += jnp.sum(grad * normed, axis=0, keepdims=True)
        dx = c_ref[rows, :].astype(F32) + normal_back(grad * (1.0 + scale), normed, spread)
        dx_ref[rows, :] = dx
        da_ref[rows, :] = (dx * gate).astype(BF16)

    each(count // width, one)
    for k in range(blocks):
        outs[k][...] = nt(w_ref[lax.bitwise_xor(b, k)], da_ref[...]).astype(BF16)


def result_body(
    width, shards, ids_ref, info_ref, mod_ref, x1_ref, c_ref, mlp_ref, got_ref, attn_ref, dx_ref,
    da_ref, om_ref, perm_ref, r_ref, sum_ref, mine_ref, other_ref, held, grad,
):
    f, c = ids_ref[0], ids_ref[2]
    count, size = x1_ref.shape
    sum_ref[...] = jnp.zeros_like(sum_ref)

    def one(u):
        rows = pl.ds(pl.multiple_of(u * width, width), width)
        slot = info_ref[0, u]
        gate = mod_ref[pl.ds(u, 1), 5 * size : 6 * size]
        mlp = mlp_ref[rows, :] + got_ref[rows, :].astype(F32)
        held[rows, :] = (x1_ref[rows, :] + gate * mlp).astype(BF16)
        sum_ref[pl.ds(slot, 1), 0:size] += jnp.sum(
            dx_ref[rows, :] * attn_ref[rows, :], axis=0, keepdims=True
        )
        sum_ref[pl.ds(slot, 1), size : 2 * size] += jnp.sum(
            c_ref[rows, :].astype(F32) * mlp, axis=0, keepdims=True
        )

    each(count // width, one)
    r_ref[...] = tn(perm_ref[...], held[...]).astype(BF16)
    grad[...] = nn(om_ref[...], da_ref[...]).astype(BF16).reshape(grad.shape)
    for k in range(shards):
        base = 2 * lax.bitwise_xor(f, k)
        mine_ref[k] = grad[base + c]
        other_ref[k] = grad[base + 1 - c]


def qkv_back_body(rows, outs, blocks, ids_ref, h_ref, d_ref, w_ref, *refs):
    n = len(outs)
    dh_ref, g_refs, (acc, low, sems) = refs[0], refs[1 : 1 + n], refs[1 + n :]
    f = ids_ref[0]
    step = pl.program_id(0)
    per, _, size = h_ref.shape
    width = BLOCK // blocks
    for i in range(per):
        piece = nt(d_ref[i], w_ref[...]).astype(BF16)
        dh_ref[:, i] = piece.reshape(blocks, width, size)
    part = tn(h_ref[...].reshape(per * BLOCK, size), d_ref[...].reshape(per * BLOCK, -1))

    @pl.when(step == 0)
    def _():
        acc[...] = part

    @pl.when(step > 0)
    def _():
        acc[...] += part

    @pl.when(step == pl.num_programs(0) - 1)
    def _():
        low[...] = acc[...].astype(BF16)
        todo = []
        for ref, (ks, start, height) in zip(g_refs, outs):
            for i, k in enumerate(ks):
                at = pl.multiple_of(lax.bitwise_xor(f, k) * rows + start, 16)
                todo.append((low.at[pl.ds(at, height)], ref.at[i]))
        for copy in fetch(todo, sems):
            copy.wait()


def last_body(width, info_ref, mod_ref, x_ref, dx_ref, dh_ref, perm_ref, o_ref, sum_ref, held):
    count, size = x_ref.shape
    sum_ref[...] = jnp.zeros_like(sum_ref)

    def one(u):
        rows = pl.ds(pl.multiple_of(u * width, width), width)
        slot = info_ref[0, u]
        scale = mod_ref[pl.ds(u, 1), size : 2 * size]
        normed, spread = normal(x_ref[rows, :].astype(F32))
        grad = dh_ref[rows, :].astype(F32)
        sum_ref[pl.ds(slot, 1), 0:size] += jnp.sum(grad, axis=0, keepdims=True)
        sum_ref[pl.ds(slot, 1), size : 2 * size] += jnp.sum(grad * normed, axis=0, keepdims=True)
        dx = dx_ref[rows, :] + normal_back(grad * (1.0 + scale), normed, spread)
        held[rows, :] = dx.astype(BF16)

    each(count // width, one)
    o_ref[...] = tn(perm_ref[...], held[...]).astype(BF16)


def reduce_plan(shards, rows):
    if shards == 4:
        half = rows // 2
        return [
            ((0, 2), 0, half),
            ((1, 3), 0, half),
            ((0, 1), half, half),
            ((2, 3), half, half),
        ]
    return [(tuple(range(shards)), 0, rows)]


def add(left, right):
    return (left.astype(F32) + right.astype(F32)).astype(BF16)


def reduce_rows(pieces, shards):
    if shards == 4:
        keep_a, send_a, keep_b, send_b = pieces
        sum_a = add(keep_a, swap(send_a, "fsdp", 1))
        sum_b = add(keep_b, swap(send_b, "fsdp", 2))
        return (
            add(sum_a[0], swap(sum_a[1], "fsdp", 2)),
            add(sum_b[0], swap(sum_b[1], "fsdp", 1)),
        )
    (pieces,) = pieces
    total = pieces[0]
    for k in range(1, shards):
        total = add(total, swap(pieces[k], "fsdp", k))
    half = total.shape[0] // 2
    return total[:half], total[half:]


def sum_chips(pair, chips):
    one, two = pair
    if chips == 4:
        even = (lax.axis_index("blk") // 2) % 2 == 0
        send, keep = jnp.where(even, two, one), jnp.where(even, one, two)
        part = add(keep, swap(send, "blk", 2))
        part = add(part, swap(part, "blk", 4))
        other = swap(part, "blk", 2)
        return jnp.where(even, part, other), jnp.where(even, other, part)
    groups = [[2 * i + core for i in range(chips)] for core in range(2)]
    both = lax.psum(jnp.concatenate([one, two]), "blk", axis_index_groups=groups)
    return both[: one.shape[0]], both[one.shape[0] :]


def both_cores(array):
    other = swap(array, "blk", 1)
    first = lax.axis_index("blk") % 2 == 0
    return jnp.where(first, array, other), jnp.where(first, other, array)


def on_device(
    tokens,
    timesteps,
    segment_ids,
    head_mask,
    chan_mask,
    token_mask,
    w_temb,
    w_ada,
    w_qkv,
    w_out,
    w_fc1,
    w_fc2,
    cotangent,
):
    count, size = tokens.shape
    slots, heads = head_mask.shape[1:]
    head_size = size // heads
    shards, blocks = lax.axis_size("fsdp"), lax.axis_size("blk")
    chips = blocks // 2
    f, b = lax.axis_index("fsdp"), lax.axis_index("blk")
    c = b % 2
    width = BLOCK // blocks
    units = count // width
    own = heads // blocks
    wide = 3 * own * LANES
    hidden = w_fc1.shape[1]
    half = hidden // 2
    ids = jnp.stack([f, b, c]).astype(I32)

    fc_rows = (half // size) * w_fc1.shape[0] + w_fc2.shape[0] // 2
    (fc_own,) = run(
        "pick_half",
        functools.partial(pick_half_body, shards),
        [(SMEM, ids), (VMEM, w_fc1), (VMEM, w_fc2)],
        [(VMEM, shape((fc_rows, size)))],
    )
    fc_all = lax.all_gather(fc_own, "fsdp", axis=0, tiled=True).reshape(shards, fc_rows, size)

    items = lax.dynamic_slice_in_dim(segment_ids, b * count, count, axis=1)
    rows = w_temb.shape[0]
    entries = rows * shards
    spectrum = frequencies(timesteps[0], entries).astype(BF16).astype(F32)
    out_rows = w_out.shape[0] // 2
    ada_rows, wider = w_ada.shape
    padded = -(-units // 8) * 8
    n_copies = 8 * shards + 4 * chips + 8
    outs = run(
        "front",
        functools.partial(front_body, shards, chips, heads),
        [
            (VMEM, a)
            for a in (items, token_mask[None, :], tokens, cotangent, spectrum, w_temb)
        ]
        + [(ANY, a) for a in (w_ada, w_qkv, w_out.reshape(2, out_rows, size))],
        [
            (VMEM, shape((count, size))),
            (VMEM, shape((count, size))),
            (ANY, shape((2, slots, count), F32)),
            (VMEM, shape((8, LANES), I32)),
            (VMEM, shape((count, count))),
            (VMEM, shape((padded, wider), F32)),
            (VMEM, shape((shards * slots, ada_rows), F32)),
            (VMEM, shape((shards * slots, ada_rows))),
            (ANY, shape((2, count, size))),
            (ANY, shape((units, BLOCK, size))),
            (VMEM, shape((units, BLOCK, wide))),
            (VMEM, shape((size, wide))),
            (ANY, shape((shards, 2, out_rows, size))),
        ],
        [
            pltpu.VMEM((blocks, count, size), BF16),
            pltpu.VMEM((shards, slots, entries), F32),
            pltpu.VMEM((shards, rows, size), BF16),
            pltpu.VMEM((shards, slots, wider), F32),
            pltpu.VMEM((shards, slots, wider), F32),
            pltpu.VMEM((2, slots, count), F32),
            pltpu.VMEM((2, count, size), BF16),
            pltpu.VMEM((shards, w_qkv.shape[0], wide), BF16),
            pltpu.VMEM((shards, 2, out_rows, size), BF16),
            pltpu.VMEM((count, size), BF16),
            pltpu.VMEM(w_ada.shape, BF16),
            pltpu.VMEM(w_qkv.shape, BF16),
            pltpu.SemaphoreType.DMA((units + 3,)),
            pltpu.SemaphoreType.DMA((n_copies,)),
            pltpu.SemaphoreType.DMA((n_copies,)),
        ],
        flops=2 * units * BLOCK * size * wide,
        vmem=60,
        collective=0,
    )
    x_s, c_s, hots, info, perm, mod, condition, lifted, dms, normed, qkv, w_heads, w_out_all = outs
    w_out_all = w_out_all.reshape(size, size)

    mask = head_mask[0]
    narrow = own * head_size
    outs = run(
        "attend",
        functools.partial(attend_body, own, head_size, blocks),
        [(SMEM, ids), (SMEM, info), (SMEM, mask), (VMEM, qkv)],
        [
            (VMEM, shape((units, narrow, BLOCK))),
            (VMEM, shape((units, 8, BLOCK), F32)),
        ]
        + [(VMEM, shape((narrow, count)))] * blocks,
        [pltpu.VMEM((units, narrow, BLOCK), F32)],
        flops=2 * units * units * BLOCK * BLOCK * wide // 3,
    )
    held, lse, pieces = outs[0], outs[1], outs[2:]
    om_parts = [pieces[0]] + [swap(pieces[k], "blk", k) for k in range(1, blocks)]

    attn, x1, h2, om = run(
        "project",
        functools.partial(project_body, width, blocks),
        [(SMEM, ids), (VMEM, mod), (VMEM, x_s), (VMEM, w_out_all)]
        + [(ANY, part) for part in om_parts],
        [
            (VMEM, shape((count, size), F32)),
            (VMEM, shape((count, size), F32)),
            (VMEM, shape((count, size))),
            (VMEM, shape((size, count))),
        ],
        [
            pltpu.VMEM((blocks, narrow, count), BF16),
            pltpu.SemaphoreType.DMA((blocks,)),
        ],
        flops=2 * count * size * size,
    )
    h2_other = swap(h2, "blk", 1)

    chan = chan_mask[0].reshape(slots, shards, 2, half // shards)
    chan = lax.dynamic_slice_in_dim(chan, c, 1, axis=2).reshape(slots, half)
    n_sems = 4 + shards * (half // size + 1)
    mlp, mlp_send, dh2, dh2_send, g_fc = run(
        "feed_forward",
        functools.partial(ff_body, shards, 256),
        [(VMEM, hots), (VMEM, chan)] + [(ANY, a) for a in (h2, h2_other, dms, fc_all)],
        [
            (VMEM, shape((count, size), F32)),
            (VMEM, shape((count, size))),
            (VMEM, shape((count, size), F32)),
            (VMEM, shape((count, size))),
            (ANY, shape((shards, fc_rows, size))),
        ],
        [
            pltpu.VMEM((size, half), BF16),
            pltpu.VMEM((half, size), BF16),
            pltpu.VMEM((2 * count, size), BF16),
            pltpu.VMEM((2 * count, size), BF16),
            pltpu.VMEM((size, 2 * count), BF16),
            pltpu.VMEM((2 * count, 256), BF16),
            pltpu.VMEM((2 * count, 256), BF16),
            pltpu.VMEM((2 * count, size), F32),
            pltpu.VMEM((2 * count, size), F32),
            pltpu.VMEM((size, half), BF16),
            pltpu.VMEM((half, size), BF16),
            pltpu.SemaphoreType.DMA((n_sems,)),
        ],
        flops=6 * 2 * 2 * count * size * half,
        vmem=60,
    )
    g_fc = lax.psum_scatter(
        g_fc.reshape(shards * fc_rows, size), "fsdp", scatter_dimension=0, tiled=True
    )
    dh2_got = swap(dh2_send, "blk", 1)
    mlp_got = swap(mlp_send, "blk", 1)

    outs = run(
        "middle_back",
        functools.partial(middle_body, width, blocks),
        [(SMEM, ids), (SMEM, info), (VMEM, mod), (VMEM, x1), (VMEM, c_s), (VMEM, dh2)]
        + [(VMEM, dh2_got), (VMEM, w_out_all.reshape(blocks, narrow, size))],
        [(VMEM, shape((narrow, count)))] * blocks
        + [
            (VMEM, shape((count, size), F32)),
            (VMEM, shape((count, size))),
            (VMEM, shape((slots, 2 * size), F32)),
        ],
        flops=2 * count * size * size,
    )
    pieces, (dx1, d_attn, sums_two) = outs[:blocks], outs[blocks:]
    up_parts = [pieces[0]] + [swap(pieces[k], "blk", k) for k in range(1, blocks)]

    result, sums_gate, g_out, g_out_send = run(
        "result",
        functools.partial(result_body, width, shards),
        [(SMEM, ids), (SMEM, info)]
        + [(VMEM, a) for a in (mod, x1, c_s, mlp, mlp_got, attn, dx1, d_attn, om, perm)],
        [
            (VMEM, shape((count, size))),
            (VMEM, shape((slots, 2 * size), F32)),
            (VMEM, shape((shards, out_rows, size))),
            (VMEM, shape((shards, out_rows, size))),
        ],
        [pltpu.VMEM((count, size), BF16), pltpu.VMEM((2 * shards, out_rows, size), BF16)],
        flops=2 * count * size * size,
    )
    g_out = add(g_out, swap(g_out_send, "blk", 1))

    (d_qkv,) = run(
        "attend_back",
        functools.partial(attend_back_body, own, head_size, blocks),
        [(SMEM, ids), (SMEM, info), (SMEM, mask)]
        + [(VMEM, a) for a in (qkv, held, lse)]
        + [(VMEM, a) for a in up_parts],
        [(VMEM, shape((units, BLOCK, wide)))],
        [
            pltpu.VMEM((blocks, narrow, count), BF16),
            pltpu.VMEM((units, own, LANES, BLOCK), BF16),
            pltpu.VMEM((units, 8, BLOCK), F32),
            pltpu.VMEM((units, own, LANES, BLOCK), F32),
            pltpu.VMEM((own, BLOCK, LANES), F32),
            pltpu.VMEM((own, BLOCK, LANES), F32),
        ],
        flops=5 * units * units * BLOCK * BLOCK * wide // 3,
    )
    per = 4
    rows_qkv = w_qkv.shape[0]
    outs_qkv = reduce_plan(shards, rows_qkv)
    outs = run(
        "qkv_back",
        functools.partial(qkv_back_body, rows_qkv, outs_qkv, blocks),
        [
            (SMEM, ids),
            (pl.BlockSpec((per, BLOCK, size), lambda i: (i, 0, 0)), normed),
            (pl.BlockSpec((per, BLOCK, wide), lambda i: (i, 0, 0)), d_qkv),
            (VMEM, w_heads),
        ],
        [
            (
                pl.BlockSpec((blocks, per, width, size), lambda i: (0, i, 0, 0)),
                shape((blocks, units, width, size)),
            )
        ]
        + [(ANY, shape((len(ks), height, wide))) for ks, _, height in outs_qkv],
        [
            pltpu.VMEM((size, wide), F32),
            pltpu.VMEM((size, wide), BF16),
            pltpu.SemaphoreType.DMA((2 * shards,)),
        ],
        flops=4 * units * BLOCK * size * wide,
        grid=(units // per,),
    )
    d_normed, gq_parts = outs[0], outs[1:]
    d_normed = lax.psum_scatter(
        d_normed.reshape(blocks * count, size), "blk", scatter_dimension=0, tiled=True
    )
    grad_tokens, sums_one = run(
        "first_back",
        functools.partial(last_body, width),
        [(SMEM, info)] + [(VMEM, a) for a in (mod, x_s, dx1, d_normed, perm)],
        [(VMEM, shape((count, size))), (VMEM, shape((slots, 2 * size), F32))],
        [pltpu.VMEM((count, size), BF16)],
    )

    def over_stream(sums):
        low = sums.astype(BF16)
        total = low.astype(F32)
        for k in (1, 2, 4, 8, 16):
            if k < blocks:
                total = total + swap(total, "blk", k)
        low = total.astype(BF16)
        return lax.all_gather(low, "fsdp", axis=0, tiled=True)

    gate_all, two_all, one_all = over_stream(sums_gate), over_stream(sums_two), over_stream(sums_one)
    d_mod = jnp.concatenate(
        [one_all, gate_all[:, :size], two_all, gate_all[:, size:]], axis=1
    )
    grad_ada = tn(lifted, d_mod)
    _, silu_pull = jax.vjp(lambda v: v / (1.0 + jnp.exp(-v)), condition)
    (d_condition,) = silu_pull(nt(d_mod, w_ada))
    d_all = lax.all_gather(d_condition, "fsdp", axis=1, tiled=True)
    steps = lax.all_gather(timesteps, "fsdp", axis=0, tiled=True)
    spectra = frequencies(steps.reshape(-1), entries).astype(BF16).astype(F32)
    grad_temb = lax.dot_general(
        lax.dynamic_slice_in_dim(spectra, f * rows, rows, axis=1),
        d_all,
        (((0,), (0,)), ((), ())),
        precision=HIGH,
    )

    cut = fc_rows - w_fc2.shape[0] // 2
    g1, g2 = sum_chips((g_fc[:cut], g_fc[cut:]), chips)
    if shards == 4:
        cut = out_rows // 2
        pieces = [
            jnp.stack([g_out[0, :cut], g_out[2, :cut]]),
            jnp.stack([g_out[1, :cut], g_out[3, :cut]]),
            g_out[0:2, cut:],
            g_out[2:4, cut:],
        ]
    else:
        pieces = [g_out]
    o_one, o_two = sum_chips(reduce_rows(pieces, shards), chips)
    first, second = both_cores(jnp.concatenate([o_one, o_two]))
    grad_out = jnp.concatenate([first, second]).astype(F32)
    first, second = both_cores(g2)
    grad_fc2 = jnp.concatenate([first, second]).astype(F32)
    first, second = both_cores(
        jnp.concatenate(jnp.split(g1, half // size, axis=0), axis=1)
    )
    part = half // shards
    grad_fc1 = jnp.concatenate(
        [side[:, i * part : (i + 1) * part] for i in range(shards) for side in (first, second)],
        axis=1,
    ).astype(F32)
    gq = lax.all_gather(jnp.concatenate(reduce_rows(gq_parts, shards)), "blk", axis=0)
    gq = gq.reshape(blocks, -1, 3, own, LANES)[..., :head_size]
    grad_qkv = jnp.transpose(gq, (1, 2, 0, 3, 4)).reshape(w_qkv.shape).astype(F32)
    return (
        result,
        grad_tokens,
        grad_temb,
        grad_ada,
        grad_qkv,
        grad_out,
        grad_fc1,
        grad_fc2,
    )


def solution(mesh):
    placed = (
        P(("fsdp", "blk"), None),
        P("fsdp", None),
        P("fsdp", None),
        P("fsdp", None, None),
        P("fsdp", None, None),
        P(("fsdp", "blk")),
        P("fsdp", None),
        P("fsdp", None),
        P("fsdp", None),
        P("fsdp", None),
        P("fsdp", None),
        P("fsdp", None),
        P(("fsdp", "blk"), None),
    )
    return jax.shard_map(
        on_device,
        mesh=mesh,
        in_specs=placed,
        out_specs=(
            P(("fsdp", "blk"), None),
            P(("fsdp", "blk"), None),
            P("fsdp", None),
            P("fsdp", None),
            P("fsdp", None),
            P("fsdp", None),
            P("fsdp", None),
            P("fsdp", None),
        ),
        check_vma=False,
    )
```

```python
import functools
import math

import jax
import jax.numpy as jnp
from jax import lax
from jax.experimental import pallas as pl
from jax.experimental.pallas import tpu as pltpu
from jax.sharding import PartitionSpec as P

HIGH = lax.Precision.HIGHEST
BF16 = jnp.bfloat16
F32 = jnp.float32
I32 = jnp.int32
LANES = 128
BLOCK = 256
NEG = -1e30
LOG2E = 1.4426950408889634

VMEM = pl.BlockSpec(memory_space=pltpu.VMEM)
SMEM = pl.BlockSpec(memory_space=pltpu.SMEM)
ANY = pl.BlockSpec(memory_space=pl.ANY)


def shape(dims, kind=BF16):
    return jax.ShapeDtypeStruct(tuple(dims), kind)


def run(name, body, ins, outs, scratch=(), flops=0, vmem=48, collective=None, **more):
    moved = sum(a.size * a.dtype.itemsize for _, a in ins)
    moved += sum(math.prod(o.shape) * jnp.dtype(o.dtype).itemsize for _, o in outs)
    return pl.pallas_call(
        body,
        out_shape=[o for _, o in outs],
        in_specs=[s for s, _ in ins],
        out_specs=[s for s, _ in outs],
        scratch_shapes=list(scratch),
        compiler_params=pltpu.CompilerParams(
            vmem_limit_bytes=vmem << 20,
            collective_id=collective,
            has_side_effects=collective is not None,
        ),
        cost_estimate=pl.CostEstimate(flops=flops, bytes_accessed=moved, transcendentals=0),
        name=name,
        **more,
    )(*[a for _, a in ins])


def swap(array, axis, by):
    size = lax.axis_size(axis)
    return lax.ppermute(array, axis, [(i, i ^ by) for i in range(size)])


def frequencies(steps, entries):
    half = entries // 2
    ladder = jnp.exp(-math.log(10000.0) * lax.iota(jnp.int32, half) / half)
    angles = steps.astype(F32)[:, None] * ladder[None, :]
    return jnp.concatenate([jnp.cos(angles), jnp.sin(angles)], axis=1)


def nn(left, right):
    return lax.dot_general(left, right, (((1,), (0,)), ((), ())), preferred_element_type=F32)


def nt(left, right):
    return lax.dot_general(left, right, (((1,), (1,)), ((), ())), preferred_element_type=F32)


def tn(left, right):
    return lax.dot_general(left, right, (((0,), (0,)), ((), ())), preferred_element_type=F32)


def each(count, step, group=1):
    if count % group:
        group = 1

    def one(index, carry):
        for i in range(group):
            step(index * group + i)
        return carry

    lax.fori_loop(0, count // group, one, 0)


def normal(values):
    center = values - jnp.mean(values, axis=-1, keepdims=True)
    scale = lax.rsqrt(jnp.mean(center * center, axis=-1, keepdims=True) + 1e-06)
    return center * scale, scale


def normal_back(grad, normed, scale):
    along = jnp.mean(grad * normed, axis=-1, keepdims=True)
    return scale * (grad - jnp.mean(grad, axis=-1, keepdims=True) - normed * along)


def flip(index, by):
    bit = 1
    while bit <= by:
        if by & bit:
            index = index + bit * (1 - 2 * ((index // bit) % 2))
        bit *= 2
    return index


def fetch(pairs, sems, first=0):
    copies = []
    for index, (source, target) in enumerate(pairs, first):
        copy = pltpu.make_async_copy(source, target, sems.at[index])
        copy.start()
        copies.append(copy)
    return copies


class Routes:
    def __init__(self, sent, got):
        self.sent, self.got, self.known, self.started = sent, got, {}, []

    def slot(self, name):
        return self.known.setdefault(name, len(self.known))

    def copy(self, name, source, target, to, landed=None):
        return pltpu.make_async_remote_copy(
            src_ref=source,
            dst_ref=target,
            send_sem=self.sent.at[self.slot(name)],
            recv_sem=self.got.at[self.slot(landed or name)],
            device_id=to,
            device_id_type=pl.DeviceIdType.MESH,
        )

    def start(self, name, source, target, to, when=None, landed=None):
        def make():
            return self.copy(name, source, target, to, landed)

        self.started.append((make, when))
        if when is None:
            make().start()
        else:
            pl.when(when)(lambda: make().start())

    def arrive(self, name, target, when=None):
        def wait():
            b = lax.axis_index("blk")
            self.copy(name, target, target, {"blk": b + 1 - 2 * (b % 2)}).wait_recv()

        if when is None:
            wait()
        else:
            pl.when(when)(wait)

    def finish(self):
        for make, when in self.started:
            if when is None:
                make().wait_send()
            else:
                pl.when(when)(lambda make=make: make().wait_send())


def greet(shards, chips):
    f, b = lax.axis_index("fsdp"), lax.axis_index("blk")
    z, c = b // 2, b % 2
    barrier = pltpu.get_barrier_semaphore()

    def signal(to):
        pl.semaphore_signal(barrier, inc=1, device_id=to, device_id_type=pl.DeviceIdType.MESH)

    for k in range(1, shards):
        signal({"fsdp": flip(f, k)})
    signal({"blk": b + 1 - 2 * c})
    pl.when(z > 0)(lambda: signal({"blk": b - 2}))
    pl.when(z < chips - 1)(lambda: signal({"blk": b + 2}))
    ends = (z == 0).astype(I32) + (z == chips - 1).astype(I32)
    pl.semaphore_wait(barrier, shards + 2 - ends)


def pick_half_body(parts, ids_ref, w1_ref, w2_ref, o_ref):
    rows, hidden = w1_ref.shape
    half = hidden // parts // 2
    size = o_ref.shape[1]
    down = w2_ref.shape[0] // 2
    blocks = hidden // 2 // size
    for core in range(2):

        @pl.when(ids_ref[2] == core)
        def _():
            picked = jnp.concatenate(
                [
                    w1_ref[:, (2 * part + core) * half : (2 * part + core + 1) * half]
                    for part in range(parts)
                ],
                axis=1,
            )
            for block in range(blocks):
                o_ref[block * rows : (block + 1) * rows, :] = picked[
                    :, block * size : (block + 1) * size
                ]
            o_ref[blocks * rows :, :] = w2_ref[core * down : (core + 1) * down, :]


def front_body(
    shards, chips, heads, items_ref, keep_ref, x_ref, c_ref, spec_ref, temb_ref, ada_ref, qkvw_ref,
    outw_ref, xs_ref, cs_ref, hot_ref, info_ref, mark_ref, perm_ref, mod_ref, cond_ref, low_ref, wave_ref, dm_ref, h_ref,
    qkv_ref, wh_ref, wo_ref, x_all, spec_all, temb_all, part_own, part_got, hots, dms, wh_all, wo_all,
    h_all, ada_s, qkvw_s, local, sent, got,
):
    f, b = lax.axis_index("fsdp"), lax.axis_index("blk")
    z, c = b // 2, b % 2
    blocks = 2 * chips
    pair = b + 1 - 2 * c
    width = BLOCK // blocks
    count, size = x_ref.shape
    units = count // width
    own = heads // blocks
    head_size = size // heads
    slots = spec_ref.shape[0]
    routes = Routes(sent, got)
    inside = fetch(
        [(ada_ref, ada_s), (qkvw_ref, qkvw_s), (outw_ref, wo_all.at[f])], local, units
    )
    greet(shards, chips)

    spec_all[f] = spec_ref[...]
    temb_all[f] = temb_ref[...]
    for k in range(1, shards):
        to = {"fsdp": flip(f, k)}
        routes.start(("spec", k), spec_ref, spec_all.at[f], to)
        routes.start(("temb", k), temb_ref, temb_all.at[f], to)

    items = items_ref[...]
    slot = lax.broadcasted_iota(I32, (slots, count), 0)
    hot = (items == slot).astype(F32)
    start = jnp.sum((items < slot).astype(F32), axis=1, keepdims=True)
    end = start + jnp.sum(hot, axis=1, keepdims=True)
    row = lax.broadcasted_iota(I32, (count, count), 0)
    col = lax.broadcasted_iota(I32, (count, count), 1)
    rank = nn(hot.astype(BF16), (row <= col).astype(BF16))
    place = jnp.sum(hot * (start + rank), axis=0, keepdims=True) - 1.0
    perm = (row.astype(F32) == place).astype(BF16)
    perm_ref[...] = perm
    x_s = nn(perm, x_ref[...]).astype(BF16)
    xs_ref[...] = x_s
    x_all[b] = x_s

    def line(side, s, send):
        away = s - 1 if send else s
        chip = z - away if side == 0 else z + away
        ahead = z + 1 < chips if side == 0 else z > 0
        known = z >= away if side == 0 else z + away < chips
        when = known & ahead if send else known
        return chip * 2 + c, {"blk": b + 2 if side == 0 else b - 2}, when

    def send_on(s):
        for side in range(2):
            device, to, when = line(side, s, True)
            routes.start(("line", side, s), x_all.at[device], x_all.at[device], to, when)

    send_on(1)
    routes.start("pair", x_all.at[b], x_all.at[b], {"blk": pair})
    cs_ref[...] = nn(perm, c_ref[...]).astype(BF16)
    keep = jnp.broadcast_to(keep_ref[...].astype(F32), (slots, count)).astype(BF16)
    kept = nt(keep, perm)
    at = lax.broadcasted_iota(I32, (slots, count), 1).astype(F32)
    hots[0] = kept * ((at >= start) & (at < end)).astype(F32)
    first = (lax.broadcasted_iota(I32, (slots, LANES), 1) * width).astype(F32)
    mine = ((first >= start) & (first < end)).astype(F32)
    mark_ref[...] = mine
    which = lax.broadcasted_iota(I32, (slots, LANES), 0).astype(F32)
    info_ref[0:1, :] = jnp.sum(mine * which, axis=0, keepdims=True).astype(I32)
    info_ref[1:2, :] = (jnp.sum(mine * start, axis=0, keepdims=True) / width).astype(I32)
    info_ref[2:3, :] = (jnp.sum(mine * end, axis=0, keepdims=True) / width).astype(I32)
    info_ref[3:8, :] = jnp.zeros((5, LANES), I32)

    for k in range(1, shards):
        other = flip(f, k)
        routes.arrive(("spec", k), spec_all.at[other])
        routes.arrive(("temb", k), temb_all.at[other])
    spectra = spec_all[...].reshape(shards * slots, -1).astype(BF16)
    condition = nn(spectra, temb_all[...].reshape(-1, size))
    rows = ada_ref.shape[0]
    for shard in range(shards):

        @pl.when(f == shard)
        def _():
            cond_ref[...] = condition[:, shard * rows : (shard + 1) * rows]
            freqs = temb_ref.shape[0]
            wave_ref[...] = spectra[:, shard * freqs : (shard + 1) * freqs].astype(F32)

    values = cond_ref[...]
    lifted = (values / (1.0 + jnp.exp(-values))).astype(BF16)
    low_ref[...] = lifted
    inside[0].wait()
    part_own[...] = nn(lifted, ada_s[...]).reshape(part_own.shape)
    for k in range(1, shards):
        other = flip(f, k)
        routes.start(("part", k), part_own.at[other], part_got.at[f], {"fsdp": other})

    rows = qkvw_ref.shape[0]
    inside[1].wait()
    row = lax.broadcasted_iota(I32, (size, LANES), 0)
    col = lax.broadcasted_iota(I32, (size, LANES), 1)
    picked = []
    for head in range(own):
        mark = (row == (b * own + head) * head_size + col) & (col < head_size)
        picked.append(mark.astype(F32).astype(BF16))
    for part in range(3):
        for head in range(own):
            at = (part * own + head) * LANES
            wh_all[f, :, at : at + LANES] = nn(
                qkvw_s[:, part * size : (part + 1) * size], picked[head]
            ).astype(BF16)
    if shards == 4:
        for k in (1, 2):
            routes.start(("head", k), wh_all.at[f], wh_all.at[f], {"fsdp": flip(f, k)})
    else:
        for k in range(1, shards):
            routes.start(("head", k), wh_all.at[f], wh_all.at[f], {"fsdp": flip(f, k)})

    def take(s):
        for side in range(2):
            device, _, when = line(side, s, False)
            routes.arrive(("line", side, s), x_all.at[device], when)
            if s + 1 < chips:
                device, to, onward = line(side, s + 1, True)
                routes.start(
                    ("line", side, s + 1), x_all.at[device], x_all.at[device], to, onward
                )
            device, _, when = line(side, s, False)
            routes.start(
                ("pair", side, s), x_all.at[device], x_all.at[device], {"blk": pair}, when
            )

    take(1)
    if shards == 4:
        half = rows // 2
        for k, low in ((1, 0), (2, half)):
            routes.arrive(("head", k), wh_all.at[flip(f, k)])
            part = wh_all.at[flip(f, k), low : low + half]
            routes.start(("head", 3, k), part, part, {"fsdp": flip(f, 3 - k)})

    for k in range(1, shards):
        routes.start(("out", k), outw_ref.at[c], wo_all.at[f, c], {"fsdp": flip(f, k)})

    total = part_own[f]
    for k in range(1, shards):
        other = flip(f, k)
        routes.arrive(("part", k), part_got.at[other])
        total = total + part_got[other]
    mod_ref[...] = lax.dot_general(
        mine[:, : mod_ref.shape[0]], total, (((0,), (0,)), ((), ())), precision=HIGH,
        preferred_element_type=F32,
    )

    def early(u):
        rows = pl.ds(pl.multiple_of(u * width, width), width)
        gate = mod_ref[pl.ds(u, 1), 5 * size : 6 * size]
        dms[0, rows, :] = (cs_ref[rows, :].astype(F32) * gate).astype(BF16)

    each(units, early)
    routes.start("dm", dms.at[0], dms.at[1], {"blk": pair})
    routes.start("hot", hots.at[0], hots.at[1], {"blk": pair})

    if shards == 4:
        half = rows // 2
        routes.arrive(("head", 3, 1), wh_all.at[flip(f, 3), 0:half])
        routes.arrive(("head", 3, 2), wh_all.at[flip(f, 3), half:rows])
    else:
        for k in range(1, shards):
            routes.arrive(("head", k), wh_all.at[flip(f, k)])
    wh_ref[...] = wh_all[...].reshape(wh_ref.shape)

    def block(device):
        at = pl.ds(pl.multiple_of(device * width, width), width)

        def one(u):
            shift = mod_ref[pl.ds(u, 1), 0:size]
            scale = mod_ref[pl.ds(u, 1), size : 2 * size]
            part = x_all[device, pl.ds(pl.multiple_of(u * width, width), width), :]
            normed, _ = normal(part.astype(F32))
            low = (normed * (1.0 + scale) + shift).astype(BF16)
            h_all[pl.ds(pl.multiple_of(u * width, width), width), :] = low

        each(units, one, 3)
        copies = fetch(
            [
                (h_all.at[u * width : (u + 1) * width], h_ref.at[u, at])
                for u in range(units)
            ],
            local,
        )
        found = nn(h_all[...], wh_ref[...]).astype(BF16)
        qkv_ref[:, at, :] = found.reshape(units, width, found.shape[1])
        for copy in copies:
            copy.wait()

    routes.arrive("pair", x_all.at[pair])
    each(2, lambda core: block(z * 2 + core))

    def work(s):
        for side in range(2):
            device, _, when = line(side, s, False)
            routes.arrive(("pair", side, s), x_all.at[device + 1 - 2 * c], when)

        def pick(q):
            chip = z - s + 2 * s * (q // 2)

            @pl.when((chip >= 0) & (chip < chips))
            def _():
                block(chip * 2 + q % 2)

        each(4, pick)

    for s in range(2, chips):
        take(s)
        if s == 2:
            for k in range(1, shards):
                other = flip(f, k)
                routes.arrive(("out", k), wo_all.at[other, c])
                routes.start(
                    ("pair out", k), wo_all.at[other, c], wo_all.at[other, c], {"blk": pair}
                )
        work(s - 1)
    work(chips - 1)
    inside[2].wait()
    for k in range(1, shards):
        routes.arrive(("pair out", k), wo_all.at[flip(f, k), 1 - c])
    routes.arrive("dm", dms.at[1])
    routes.arrive("hot", hots.at[1])
    routes.finish()
    copies = fetch([(wo_all, wo_ref), (dms, dm_ref), (hots, hot_ref)], local)
    for copy in copies:
        copy.wait()


def exchange_lanes(tiles, width):
    tiles = list(tiles)
    count = len(tiles)
    group = lax.broadcasted_iota(I32, tiles[0].shape, 1) // width
    half = count // 2
    while half:
        low = (group // half) % 2 == 0
        fresh = list(tiles)
        for i in range(count):
            if (i // half) % 2 == 0:
                a, d = tiles[i], tiles[i + half]
                fresh[i] = jnp.where(low, a, pltpu.roll(d, half * width, 1))
                fresh[i + half] = jnp.where(low, pltpu.roll(a, LANES - half * width, 1), d)
        tiles = fresh
        half //= 2
    return tiles


def attend_body(own, size, blocks, ids_ref, info_ref, mask_ref, qkv_ref, o_ref, lse_ref, *refs):
    outs, (held,) = refs[:blocks], refs[blocks:]
    units = qkv_ref.shape[0]
    width = BLOCK // blocks
    b = ids_ref[1]
    scale = LOG2E / math.sqrt(size)
    pad = -size % 16

    def one_unit(u):
        queries = [qkv_ref[u, :, h * LANES : (h + 1) * LANES] for h in range(own)]

        def one_block(j, carry):
            fresh = []
            for h in range(own):
                top, total, acc = carry[h]
                keys = qkv_ref[j, :, (own + h) * LANES : (own + h + 1) * LANES]
                at = (2 * own + h) * LANES
                values = qkv_ref[j, :, at : at + LANES]
                scores = nt(keys, queries[h]) * scale
                new_top = jnp.maximum(top, jnp.max(scores, axis=0, keepdims=True))
                probs = jnp.exp2(scores - new_top)
                decay = jnp.exp2(top - new_top)
                total = total * decay + jnp.sum(probs, axis=0, keepdims=True)
                acc = acc * decay + tn(values, probs.astype(BF16))
                fresh.append((new_top, total, acc))
            return tuple(fresh)

        start = tuple(
            (
                jnp.full((1, BLOCK), NEG, F32),
                jnp.zeros((1, BLOCK), F32),
                jnp.zeros((LANES, BLOCK), F32),
            )
            for _ in range(own)
        )
        done = lax.fori_loop(info_ref[1, u], info_ref[2, u], one_block, start)
        slot = info_ref[0, u]
        rows = []
        for h in range(own):
            top, total, acc = done[h]
            keep = mask_ref[slot, b * own + h].astype(F32)
            rows.append((acc * (keep / total))[0:size])
            lse_ref[u, h : h + 1, :] = top + jnp.log2(total)
        held[u] = jnp.concatenate(rows, axis=0) if own > 1 else rows[0]
        o_ref[u] = held[u].astype(BF16)

    each(units, one_unit)
    groups = LANES // width
    for g in range(units // groups):
        for e in range(blocks // groups):
            tiles = [
                held[groups * g + i, :, e * LANES : (e + 1) * LANES] for i in range(groups)
            ]
            for j, tile in enumerate(exchange_lanes(tiles, width)):
                device = groups * e + j
                for k in range(blocks):

                    @pl.when(lax.bitwise_xor(b, k) == device)
                    def _():
                        outs[k][:, g * LANES : (g + 1) * LANES] = tile.astype(BF16)


def attend_back_body(own, size, blocks, ids_ref, info_ref, mask_ref, qkv_ref, o_ref, lse_ref, *refs):
    pieces, (d_ref, given, up, delta, d_q, d_k, d_v) = refs[:blocks], refs[blocks:]
    units = qkv_ref.shape[0]
    width = BLOCK // blocks
    b = ids_ref[1]
    factor = 1.0 / math.sqrt(size)
    scale = LOG2E * factor
    for k in range(blocks):
        given[lax.bitwise_xor(b, k)] = pieces[k][...]
    up[...] = jnp.zeros_like(up)
    groups = LANES // width
    for g in range(units // groups):
        for e in range(blocks // groups):
            tiles = [
                given[groups * e + j, :, g * LANES : (g + 1) * LANES].astype(F32)
                for j in range(groups)
            ]
            for i, tile in enumerate(exchange_lanes(tiles, width)):
                unit = groups * g + i
                slot = info_ref[0, unit]
                for h in range(own):
                    keep = mask_ref[slot, b * own + h].astype(F32)
                    kept = tile[h * size : (h + 1) * size] * keep
                    up[unit, h, 0:size, e * LANES : (e + 1) * LANES] = kept.astype(BF16)
                    mine = o_ref[unit, h * size : (h + 1) * size, e * LANES : (e + 1) * LANES]
                    delta[unit, h : h + 1, e * LANES : (e + 1) * LANES] = jnp.sum(
                        kept * mine.astype(F32), axis=0, keepdims=True
                    )
    d_q[...] = jnp.zeros_like(d_q)

    def one_unit(j):
        d_k[...] = jnp.zeros_like(d_k)
        d_v[...] = jnp.zeros_like(d_v)
        keys = [qkv_ref[j, :, (own + h) * LANES : (own + h + 1) * LANES] for h in range(own)]
        turned = [keys[h].astype(F32).T.astype(BF16) for h in range(own)]

        def one_block(i, carry):
            for h in range(own):
                queries = qkv_ref[i, :, h * LANES : (h + 1) * LANES]
                at = (2 * own + h) * LANES
                values = qkv_ref[j, :, at : at + LANES]
                scores = nt(keys[h], queries) * scale
                probs = jnp.exp2(scores - lse_ref[i, h : h + 1, :])
                d_probs = nn(values, up[i, h])
                d_scores = (probs * (d_probs - delta[i, h : h + 1, :])).astype(BF16)
                d_k[h] += nn(d_scores, queries)
                d_v[h] += nt(probs.astype(BF16), up[i, h])
                d_q[i, h] += nn(turned[h], d_scores)
            return carry

        lax.fori_loop(info_ref[1, j], info_ref[2, j], one_block, 0)
        for h in range(own):
            at = (own + h) * LANES
            d_ref[j, :, at : at + LANES] = (d_k[h] * factor).astype(BF16)
            at = (2 * own + h) * LANES
            d_ref[j, :, at : at + LANES] = d_v[h].astype(BF16)

    each(units, one_unit)

    def turn(i):
        for h in range(own):
            d_ref[i, :, h * LANES : (h + 1) * LANES] = (d_q[i, h].T * factor).astype(BF16)

    each(units, turn)


def project_body(width, blocks, ids_ref, mod_ref, x_ref, w_ref, *refs):
    om_refs, refs = refs[:blocks], refs[blocks:]
    attn_ref, x1_ref, h_ref, om_ref, om_all, sems = refs
    b = ids_ref[1]
    size = x_ref.shape[1]
    copies = fetch(
        [(om_refs[k], om_all.at[lax.bitwise_xor(b, k)]) for k in range(blocks)], sems
    )
    for copy in copies:
        copy.wait()
    om = om_all[...].reshape(size, x_ref.shape[0])
    om_ref[...] = om
    weight = w_ref[...]
    attn_ref[...] = tn(om, weight)

    def one(u):
        rows = pl.ds(pl.multiple_of(u * width, width), width)
        gate, shift, scale = [mod_ref[pl.ds(u, 1), i * size : (i + 1) * size] for i in (2, 3, 4)]
        middle = x_ref[rows, :].astype(F32) + gate * attn_ref[rows, :]
        x1_ref[rows, :] = middle
        normed, _ = normal(middle)
        h_ref[rows, :] = (normed * (1.0 + scale) + shift).astype(BF16)

    each(x_ref.shape[0] // width, one)


def ff_body(shards, step, hot_ref, chan_ref, h_m, h_o, dm_ref, w_ref, *refs):
    mlp_m, mlp_o, dh_m, dh_o, g_ref, w1, w2, h, dm, turned, hid_s, du_s, mlp, dh, g1, g2, sems = refs
    total = h.shape[0]
    count = total // 2
    f_size, size = w2.shape
    blocks = f_size // size
    row1, row2 = size // shards, f_size // shards

    def placed(rows, one, two):
        for shard in range(shards):
            for block in range(blocks):
                yield (
                    rows.at[shard, block * row1 : (block + 1) * row1],
                    one.at[shard * row1 : (shard + 1) * row1, block * size : (block + 1) * size],
                )
            yield rows.at[shard, blocks * row1 :], two.at[shard * row2 : (shard + 1) * row2]

    copies = fetch(
        [
            (h_m, h.at[0:count]),
            (h_o, h.at[count:total]),
            (dm_ref.at[0], dm.at[0:count]),
            (dm_ref.at[1], dm.at[count:total]),
        ]
        + list(placed(w_ref, w1, w2)),
        sems,
    )
    for copy in copies:
        copy.wait()
    for at in range(0, total, LANES):
        turned[:, at : at + LANES] = h[at : at + LANES, :].astype(F32).T.astype(BF16)
    mlp[...] = jnp.zeros_like(mlp)
    dh[...] = jnp.zeros_like(dh)
    hots = [hot_ref[side].astype(BF16) for side in range(2)]

    def one(index):
        cols = pl.ds(pl.multiple_of(index * step, step), step)
        up = w1[:, cols]
        down = w2[cols, :]
        chan = chan_ref[:, cols].astype(F32).astype(BF16)
        for side in range(2):
            rows = slice(side * count, (side + 1) * count)
            keep = tn(hots[side], chan)
            pre = nn(h[rows, :], up)
            inner = pre * pre
            bent = jnp.tanh(0.7978845608028654 * (pre + 0.044715 * inner * pre))
            half = 0.5 * (1.0 + bent)
            hid = (pre * half * keep).astype(BF16)
            slope = half + (0.5 * 0.7978845608028654) * pre * (1.0 - bent * bent) * (
                1.0 + (3.0 * 0.044715) * inner
            )
            back = nt(dm[rows, :], down)
            du = (slope * back * keep).astype(BF16)
            hid_s[rows, :] = hid
            du_s[rows, :] = du
            mlp[rows, :] += nn(hid, down)
            dh[rows, :] += nt(du, up)
        g1[:, cols] = nn(turned[...], du_s[...]).astype(BF16)
        g2[cols, :] = tn(hid_s[...], dm[...]).astype(BF16)

    each(f_size // step, one)
    mlp_m[...] = mlp[0:count, :]
    mlp_o[...] = mlp[count:total, :].astype(BF16)
    dh_m[...] = dh[0:count, :]
    dh_o[...] = dh[count:total, :].astype(BF16)

    for copy in fetch([(found, rows) for rows, found in placed(g_ref, g1, g2)], sems):
        copy.wait()


def middle_body(
    width, blocks, ids_ref, info_ref, mod_ref, x1_ref, c_ref, dh_ref, got_ref, w_ref, *refs
):
    outs, (dx_ref, da_ref, sum_ref) = refs[:blocks], refs[blocks:]
    b = ids_ref[1]
    count, size = x1_ref.shape
    part = size // blocks
    sum_ref[...] = jnp.zeros_like(sum_ref)

    def one(u):
        rows = pl.ds(pl.multiple_of(u * width, width), width)
        slot = info_ref[0, u]
        gate = mod_ref[pl.ds(u, 1), 2 * size : 3 * size]
        scale = mod_ref[pl.ds(u, 1), 4 * size : 5 * size]
        normed, spread = normal(x1_ref[rows, :])
        grad = dh_ref[rows, :] + got_ref[rows, :].astype(F32)
        sum_ref[pl.ds(slot, 1), 0:size] += jnp.sum(grad, axis=0, keepdims=True)
        sum_ref[pl.ds(slot, 1), size : 2 * size] += jnp.sum(grad * normed, axis=0, keepdims=True)
        dx = c_ref[rows, :].astype(F32) + normal_back(grad * (1.0 + scale), normed, spread)
        dx_ref[rows, :] = dx
        da_ref[rows, :] = (dx * gate).astype(BF16)

    each(count // width, one)
    for k in range(blocks):
        outs[k][...] = nt(w_ref[lax.bitwise_xor(b, k)], da_ref[...]).astype(BF16)


def result_body(
    width, shards, ids_ref, info_ref, mod_ref, x1_ref, c_ref, mlp_ref, got_ref, attn_ref, dx_ref,
    da_ref, om_ref, perm_ref, r_ref, sum_ref, mine_ref, other_ref, held, grad,
):
    f, c = ids_ref[0], ids_ref[2]
    count, size = x1_ref.shape
    sum_ref[...] = jnp.zeros_like(sum_ref)

    def one(u):
        rows = pl.ds(pl.multiple_of(u * width, width), width)
        slot = info_ref[0, u]
        gate = mod_ref[pl.ds(u, 1), 5 * size : 6 * size]
        mlp = mlp_ref[rows, :] + got_ref[rows, :].astype(F32)
        held[rows, :] = (x1_ref[rows, :] + gate * mlp).astype(BF16)
        sum_ref[pl.ds(slot, 1), 0:size] += jnp.sum(
            dx_ref[rows, :] * attn_ref[rows, :], axis=0, keepdims=True
        )
        sum_ref[pl.ds(slot, 1), size : 2 * size] += jnp.sum(
            c_ref[rows, :].astype(F32) * mlp, axis=0, keepdims=True
        )

    each(count // width, one)
    r_ref[...] = tn(perm_ref[...], held[...]).astype(BF16)
    grad[...] = nn(om_ref[...], da_ref[...]).astype(BF16).reshape(grad.shape)
    for k in range(shards):
        base = 2 * lax.bitwise_xor(f, k)
        mine_ref[k] = grad[base + c]
        other_ref[k] = grad[base + 1 - c]


def stream_back_body(
    shards, chips, heads, per, h_ref, gs_ref, d_ref, wh_ref, mod_ref, mine_ref, x_ref, dx_ref, perm_ref,
    gm_ref, o_ref, sum_ref, g_ref, go_ref, give, take, keep, came, h_s, acc, low, others, out_in, out_low,
    out_got, total, held, by_unit, local, sent, got,
):
    f, b = lax.axis_index("fsdp"), lax.axis_index("blk")
    z, c = b // 2, b % 2
    pair = b + 1 - 2 * c
    width = BLOCK // (2 * chips)
    units = d_ref.shape[0]
    count, size = x_ref.shape
    wide = wh_ref.shape[1]
    own = heads // (2 * chips)
    head_size = size // heads
    rows = low.shape[1]
    steps = units // per
    routes = Routes(sent, got)

    def load(i):
        return pltpu.make_async_copy(
            h_ref.at[pl.ds(i * per, per)], h_s.at[i % 2], local.at[i % 2]
        )

    load(0).start()
    greet(shards, chips)
    routes.start("out", gs_ref, out_in, {"blk": pair})

    def partial(device, target):
        at = pl.ds(pl.multiple_of(device * width, width), width)
        grads = d_ref[:, at, :].reshape(count, wide)
        for col in range(0, size, 3 * LANES):
            target[:, col : col + 3 * LANES] = nt(
                grads, wh_ref[col : col + 3 * LANES, :]
            ).astype(BF16)

    def route(side, t):
        if side == 0:
            chip = chips - 1 - t
            return chip, z < chip, z > 0
        return t, z > t, z < chips - 1

    def onward(side, t, chip, when):
        if side == 0:
            slot, to = chip, b + 2
        else:
            slot, to = chip + (chips - chip) * (z - 1 == chip).astype(I32), b - 2
        routes.start(("sum", side, t), keep.at[chip], came.at[slot], {"blk": to}, when)

    def join(chip, slot=None):
        value = keep[chip].astype(F32) + take[chip].astype(F32)
        if slot is not None:
            value = value + came[slot].astype(F32)
        keep[chip] = value.astype(BF16)

    for t in range(chips - 1):
        for side in range(2):
            chip, passes, inside = route(side, t)

            @pl.when(passes)
            def _():
                partial(chip * 2 + 1 - c, give.at[chip])

            routes.start(("pair", side, t), give.at[chip], take.at[chip], {"blk": pair}, passes)

            @pl.when(passes)
            def _():
                partial(chip * 2 + c, keep.at[chip])

            first = passes & jnp.logical_not(inside)
            routes.arrive(("pair", side, t), take.at[chip], first)

            pl.when(first)(lambda: join(chip))
            onward(side, t, chip, first)

    partial(z * 2 + 1 - c, give.at[z])
    routes.start(("pair", "own"), give.at[z], take.at[z], {"blk": pair})
    partial(z * 2 + c, keep.at[z])

    def gather(i):
        if i + 1 < steps:
            load(i + 1).start()
        load(i).wait()
        part = tn(
            h_s[i % 2].reshape(per * BLOCK, size),
            d_ref[i * per : (i + 1) * per].reshape(per * BLOCK, wide),
        )
        if i:
            acc[...] += part
        else:
            acc[...] = part

    for t in range(max(chips - 1, steps)):
        if t < steps:
            gather(t)
        if t == steps - 1:
            packed = jnp.concatenate(
                [acc[:, i * LANES : i * LANES + head_size] for i in range(3 * own)], axis=1
            )
            low[...] = packed.astype(BF16).reshape(low.shape)
            for k in range(1, shards):
                other = flip(f, k)
                routes.start(("grad", k), low.at[other], others.at[k], {"fsdp": other})
        if t == 0:
            routes.arrive("out", out_in)
            out_low[...] = (gm_ref[...].astype(F32) + out_in[...].astype(F32)).astype(BF16)
            for k in range(1, shards):
                routes.start(("out", k), out_low.at[k], out_got.at[k], {"fsdp": flip(f, k)})
        if t >= chips - 1:
            continue
        for near, side in ((True, 0), (True, 1), (False, 1), (False, 0)):
            chip, passes, inside = route(side, t)
            when = passes & inside & ((z < chips // 2) == near)
            routes.arrive(("pair", side, t), take.at[chip], when)
            routes.arrive(("sum", side, t), came.at[chip], when)
            pl.when(when)(lambda: join(chip, chip))
            onward(side, t, chip, when)

    grad, grad_out = low[f].astype(F32), out_low[0].astype(F32)
    for k in range(1, shards):
        routes.arrive(("grad", k), others.at[k])
        grad = grad + others[k].astype(F32)
        routes.arrive(("out", k), out_got.at[k])
        grad_out = grad_out + out_got[k].astype(F32)
    g_ref[...] = grad.astype(BF16)
    go_ref[...] = grad_out.astype(BF16)

    routes.arrive(("pair", "own"), take.at[z])
    total[...] = keep[z].astype(F32) + take[z].astype(F32)
    for t in range(chips - 1):
        for side in range(2):
            chip, _, inside = route(side, t)
            slot = chip if side == 0 else chips
            here = (z == chip) & inside
            routes.arrive(("sum", side, t), came.at[slot], here)

            @pl.when(here)
            def _():
                total[...] += came[slot].astype(F32)

    by_unit[...] = jnp.zeros_like(by_unit)

    def one(u):
        rows = pl.ds(pl.multiple_of(u * width, width), width)
        scale = mod_ref[pl.ds(u, 1), size : 2 * size]
        normed, spread = normal(x_ref[rows, :].astype(F32))
        grad = total[rows, :]
        by_unit[pl.ds(u, 1), 0:size] = jnp.sum(grad, axis=0, keepdims=True)
        by_unit[pl.ds(u, 1), size : 2 * size] = jnp.sum(grad * normed, axis=0, keepdims=True)
        dx = dx_ref[rows, :] + normal_back(grad * (1.0 + scale), normed, spread)
        held[rows, :] = dx.astype(BF16)

    each(units, one, 3)
    o_ref[...] = tn(perm_ref[...], held[...]).astype(BF16)
    sum_ref[...] = lax.dot_general(
        mine_ref[:, : by_unit.shape[0]], by_unit[...], (((1,), (0,)), ((), ())), precision=HIGH,
        preferred_element_type=F32,
    )
    routes.finish()


def finish_body(
    shards, chips, fc_ref, ada_ref, go_ref, gq_ref, one_ref, two_ref, gate_ref, cond_ref, tot_ref, gqa_ref,
    dm_ref, dc_ref, mine, up, inner_in, result, other, gq_all, sum_own, sum_pair, sums, mods, conds, ada_s,
    local, sent, got,
):
    f, b = lax.axis_index("fsdp"), lax.axis_index("blk")
    z, c = b // 2, b % 2
    pair = b + 1 - 2 * c
    count = mine.shape[0]
    slots, wider = sum_own.shape
    size = wider // 6
    routes = Routes(sent, got)
    loads = fetch([(fc_ref, mine.at[0 : count - 1]), (ada_ref, ada_s)], local)
    greet(shards, chips)

    sum_own[:, 0 : 2 * size] = one_ref[...]
    sum_own[:, 2 * size : 3 * size] = gate_ref[:, 0:size]
    sum_own[:, 3 * size : 5 * size] = two_ref[...]
    sum_own[:, 5 * size : 6 * size] = gate_ref[:, size : 2 * size]
    routes.start("sum", sum_own, sum_pair, {"blk": pair})
    gq_all[b] = gq_ref[...]

    def line(side, s, send):
        away = s - 1 if send else s
        chip = z - away if side == 0 else z + away
        ahead = z + 1 < chips if side == 0 else z > 0
        known = z >= away if side == 0 else z + away < chips
        return chip, {"blk": b + 2 if side == 0 else b - 2}, known & ahead if send else known

    def send(name, s, place):
        for side in range(2):
            chip, to, when = line(side, s, True)
            routes.start((name, side, s), place(chip), place(chip), to, when)

    def take(name, s, place):
        for side in range(2):
            chip, _, when = line(side, s, False)
            routes.arrive((name, side, s), place(chip), when)
        if s + 1 < chips:
            send(name, s + 1, place)

    def head(chip):
        return gq_all.at[chip * 2 + c]

    send("head", 1, head)
    routes.start("head pair", gq_all.at[b], gq_all.at[b], {"blk": pair})

    half = chips // 2
    right = z // half
    inner, outer = {"blk": b + 2 - 4 * right}, {"blk": b - 2 + 4 * right}
    ends = (z > 0) & (z < chips - 1)
    middle = (z == half - 1) | (z == half)
    edge = jnp.logical_not(middle)

    def inward(i, when):
        routes.start(("up", i), mine.at[i], up.at[i], inner, when & edge)
        routes.start(("across", i), mine.at[i], inner_in.at[i], inner, when & middle, ("in", i))

    routes.arrive("sum", sum_pair)
    sums[z] = (sum_own[...] + sum_pair[...]).astype(BF16).astype(F32)
    send("small", 1, lambda chip: sums.at[chip])
    mine[count - 1] = go_ref[...]
    loads[0].wait()
    ahead = min(3, count)
    for i in range(ahead):
        inward(i, jnp.logical_not(ends))

    def combine():
        total = sums[0]
        for chip in range(1, chips):
            total = total + sums[chip]
        mods[f] = total.astype(BF16).astype(F32)
        for k in range(1, shards):
            routes.start(("mod", k), mods.at[f], mods.at[f], {"fsdp": flip(f, k)})

    def condition():
        for k in range(1, shards):
            routes.arrive(("mod", k), mods.at[flip(f, k)])
        dm_ref[...] = mods[...]
        loads[1].wait()
        grad = nt(mods[...].reshape(shards * slots, wider).astype(BF16), ada_s[...])
        values = cond_ref[...]
        gate = 1.0 / (1.0 + jnp.exp(-values))
        conds[f] = grad * (gate + values * gate * (1.0 - gate))
        for k in range(1, shards):
            routes.start(("cond", k), conds.at[f], conds.at[f], {"fsdp": flip(f, k)})

    def conditions():
        for k in range(1, shards):
            routes.arrive(("cond", k), conds.at[flip(f, k)])
        dc_ref[...] = conds[...]

    jobs = []
    for s in range(1, chips):
        jobs.append(lambda s=s: take("small", s, lambda chip: sums.at[chip]))
    jobs += [combine, condition, conditions]
    heads = [lambda s=s: take("head", s, head) for s in range(1, chips)]

    def forward(i):
        routes.arrive(("up", i), up.at[i], ends)

        @pl.when(ends)
        def _():
            mine[i] = (mine[i].astype(F32) + up[i].astype(F32)).astype(BF16)

        inward(i, ends)
        if i + ahead < count:
            inward(i + ahead, jnp.logical_not(ends))

    def back(i):
        routes.arrive(("in", i), inner_in.at[i])

        @pl.when(middle)
        def _():
            result[i] = (mine[i].astype(F32) + inner_in[i].astype(F32)).astype(BF16)

        @pl.when(edge)
        def _():
            result[i] = inner_in[i]

        routes.start(("down", i), result.at[i], inner_in.at[i], outer, ends, ("in", i))
        routes.start(("pair", i), result.at[i], other.at[i], {"blk": pair})

    for i in range(count + 1):
        if i < count:
            forward(i)
        if i:
            back(i - 1)
            if jobs and i > 1:
                jobs.pop(0)()
            if heads and i % 2 == 1 and i > 2:
                heads.pop(0)()
    for job in jobs + heads:
        job()
    for s in range(1, chips):
        for side in range(2):
            chip, _, when = line(side, s, False)
            routes.start(("head pair", side, s), head(chip), head(chip), {"blk": pair}, when)
    copies = fetch([(result, tot_ref.at[c])], local)
    for i in range(count):
        routes.arrive(("pair", i), other.at[i])
    copies += fetch([(other, tot_ref.at[1 - c])], local, 1)
    routes.arrive("head pair", gq_all.at[pair])
    for s in range(1, chips):
        for side in range(2):
            chip, _, when = line(side, s, False)
            routes.arrive(("head pair", side, s), gq_all.at[chip * 2 + 1 - c], when)
    copies += fetch([(gq_all, gqa_ref)], local, 2)
    routes.finish()
    for copy in copies:
        copy.wait()


def unfold_body(
    shards, low_ref, wave_ref, dm_ref, dc_ref, tot_ref, gq_ref, temb_ref, ada_ref, qkv_ref, out_ref,
    fc1_ref, fc2_ref, ada_s, qkv_s, out_s, fc1_s, fc2_s, sems,
):
    _, count, rows, size = tot_ref.shape
    slots = dm_ref.shape[1]
    copies = []

    def leave(source, target):
        copy = pltpu.make_async_copy(source, target, sems.at[len(copies)])
        copy.start()
        copies.append(copy)

    hidden = fc1_s.shape[1]
    part = hidden // shards // 2
    height = fc1_s.shape[0]
    blocks = hidden // 2 // size
    per = height // rows
    for core in range(2):
        for i in range(blocks * per):
            piece = tot_ref[core, i].astype(F32)
            block, at = i // per, (i % per) * rows
            for j in range(size // part):
                column = (block * (size // part) + j) * 2 * part + core * part
                fc1_s[at : at + rows, column : column + part] = piece[:, j * part : (j + 1) * part]
        rest = count - 1 - blocks * per
        for i in range(rest):
            at = (core * rest + i) * rows
            fc2_s[at : at + rows, :] = tot_ref[core, blocks * per + i].astype(F32)
        out_s[core * rows : (core + 1) * rows, :] = tot_ref[core, count - 1].astype(F32)
    leave(fc1_s, fc1_ref)
    leave(fc2_s, fc2_ref)
    leave(out_s, out_ref)
    devices, _, packed = gq_ref.shape
    narrow = packed // 3
    for p in range(3):
        for i in range(devices):
            at = p * size + i * narrow
            qkv_s[:, at : at + narrow] = gq_ref[i, :, p * narrow : (p + 1) * narrow].astype(F32)
    leave(qkv_s, qkv_ref)
    grads = dm_ref[...].reshape(shards * slots, -1).astype(BF16)
    ada_s[...] = tn(low_ref[...], grads)
    leave(ada_s, ada_ref)
    step = dc_ref.shape[2]
    for i in range(shards):
        temb_ref[:, i * step : (i + 1) * step] = lax.dot_general(
            wave_ref[...], dc_ref[i], (((0,), (0,)), ((), ())), precision=HIGH,
            preferred_element_type=F32,
        )
    for copy in copies:
        copy.wait()


def on_device(
    tokens,
    timesteps,
    segment_ids,
    head_mask,
    chan_mask,
    token_mask,
    w_temb,
    w_ada,
    w_qkv,
    w_out,
    w_fc1,
    w_fc2,
    cotangent,
):
    count, size = tokens.shape
    slots, heads = head_mask.shape[1:]
    head_size = size // heads
    shards, blocks = lax.axis_size("fsdp"), lax.axis_size("blk")
    chips = blocks // 2
    f, b = lax.axis_index("fsdp"), lax.axis_index("blk")
    c = b % 2
    width = BLOCK // blocks
    units = count // width
    own = heads // blocks
    wide = 3 * own * LANES
    hidden = w_fc1.shape[1]
    half = hidden // 2
    ids = jnp.stack([f, b, c]).astype(I32)

    fc_rows = (half // size) * w_fc1.shape[0] + w_fc2.shape[0] // 2
    (fc_own,) = run(
        "pick_half",
        functools.partial(pick_half_body, shards),
        [(SMEM, ids), (VMEM, w_fc1), (VMEM, w_fc2)],
        [(VMEM, shape((fc_rows, size)))],
    )
    fc_all = lax.all_gather(fc_own, "fsdp", axis=0, tiled=True).reshape(shards, fc_rows, size)

    items = lax.dynamic_slice_in_dim(segment_ids, b * count, count, axis=1)
    rows = w_temb.shape[0]
    entries = rows * shards
    spectrum = frequencies(timesteps[0], entries).astype(BF16).astype(F32)
    out_rows = w_out.shape[0] // 2
    ada_rows, wider = w_ada.shape
    padded = -(-units // 8) * 8
    n_copies = 8 * shards + 4 * chips + 8
    outs = run(
        "front",
        functools.partial(front_body, shards, chips, heads),
        [
            (VMEM, a)
            for a in (items, token_mask[None, :], tokens, cotangent, spectrum, w_temb)
        ]
        + [(ANY, a) for a in (w_ada, w_qkv, w_out.reshape(2, out_rows, size))],
        [
            (VMEM, shape((count, size))),
            (VMEM, shape((count, size))),
            (ANY, shape((2, slots, count), F32)),
            (VMEM, shape((8, LANES), I32)),
            (VMEM, shape((slots, LANES), F32)),
            (VMEM, shape((count, count))),
            (VMEM, shape((padded, wider), F32)),
            (VMEM, shape((shards * slots, ada_rows), F32)),
            (VMEM, shape((shards * slots, ada_rows))),
            (VMEM, shape((shards * slots, rows), F32)),
            (ANY, shape((2, count, size))),
            (ANY, shape((units, BLOCK, size))),
            (VMEM, shape((units, BLOCK, wide))),
            (VMEM, shape((size, wide))),
            (ANY, shape((shards, 2, out_rows, size))),
        ],
        [
            pltpu.VMEM((blocks, count, size), BF16),
            pltpu.VMEM((shards, slots, entries), F32),
            pltpu.VMEM((shards, rows, size), BF16),
            pltpu.VMEM((shards, slots, wider), F32),
            pltpu.VMEM((shards, slots, wider), F32),
            pltpu.VMEM((2, slots, count), F32),
            pltpu.VMEM((2, count, size), BF16),
            pltpu.VMEM((shards, w_qkv.shape[0], wide), BF16),
            pltpu.VMEM((shards, 2, out_rows, size), BF16),
            pltpu.VMEM((count, size), BF16),
            pltpu.VMEM(w_ada.shape, BF16),
            pltpu.VMEM(w_qkv.shape, BF16),
            pltpu.SemaphoreType.DMA((units + 3,)),
            pltpu.SemaphoreType.DMA((n_copies,)),
            pltpu.SemaphoreType.DMA((n_copies,)),
        ],
        flops=2 * units * BLOCK * size * wide,
        vmem=60,
        collective=0,
    )
    x_s, c_s, hots, info, mark, perm, mod, condition, lifted, waves, dms, normed, qkv, w_heads, w_out_all = outs
    w_out_all = w_out_all.reshape(size, size)

    mask = head_mask[0]
    narrow = own * head_size
    outs = run(
        "attend",
        functools.partial(attend_body, own, head_size, blocks),
        [(SMEM, ids), (SMEM, info), (SMEM, mask), (VMEM, qkv)],
        [
            (VMEM, shape((units, narrow, BLOCK))),
            (VMEM, shape((units, 8, BLOCK), F32)),
        ]
        + [(VMEM, shape((narrow, count)))] * blocks,
        [pltpu.VMEM((units, narrow, BLOCK), F32)],
        flops=2 * units * units * BLOCK * BLOCK * wide // 3,
    )
    held, lse, pieces = outs[0], outs[1], outs[2:]
    om_parts = [pieces[0]] + [swap(pieces[k], "blk", k) for k in range(1, blocks)]

    attn, x1, h2, om = run(
        "project",
        functools.partial(project_body, width, blocks),
        [(SMEM, ids), (VMEM, mod), (VMEM, x_s), (VMEM, w_out_all)]
        + [(ANY, part) for part in om_parts],
        [
            (VMEM, shape((count, size), F32)),
            (VMEM, shape((count, size), F32)),
            (VMEM, shape((count, size))),
            (VMEM, shape((size, count))),
        ],
        [
            pltpu.VMEM((blocks, narrow, count), BF16),
            pltpu.SemaphoreType.DMA((blocks,)),
        ],
        flops=2 * count * size * size,
    )
    h2_other = swap(h2, "blk", 1)

    chan = chan_mask[0].reshape(slots, shards, 2, half // shards)
    chan = lax.dynamic_slice_in_dim(chan, c, 1, axis=2).reshape(slots, half)
    n_sems = 4 + shards * (half // size + 1)
    mlp, mlp_send, dh2, dh2_send, g_fc = run(
        "feed_forward",
        functools.partial(ff_body, shards, 256),
        [(VMEM, hots), (VMEM, chan)] + [(ANY, a) for a in (h2, h2_other, dms, fc_all)],
        [
            (VMEM, shape((count, size), F32)),
            (VMEM, shape((count, size))),
            (VMEM, shape((count, size), F32)),
            (VMEM, shape((count, size))),
            (ANY, shape((shards, fc_rows, size))),
        ],
        [
            pltpu.VMEM((size, half), BF16),
            pltpu.VMEM((half, size), BF16),
            pltpu.VMEM((2 * count, size), BF16),
            pltpu.VMEM((2 * count, size), BF16),
            pltpu.VMEM((size, 2 * count), BF16),
            pltpu.VMEM((2 * count, 256), BF16),
            pltpu.VMEM((2 * count, 256), BF16),
            pltpu.VMEM((2 * count, size), F32),
            pltpu.VMEM((2 * count, size), F32),
            pltpu.VMEM((size, half), BF16),
            pltpu.VMEM((half, size), BF16),
            pltpu.SemaphoreType.DMA((n_sems,)),
        ],
        flops=6 * 2 * 2 * count * size * half,
        vmem=60,
    )
    g_fc = lax.psum_scatter(
        g_fc.reshape(shards * fc_rows, size), "fsdp", scatter_dimension=0, tiled=True
    )
    dh2_got = swap(dh2_send, "blk", 1)
    mlp_got = swap(mlp_send, "blk", 1)

    outs = run(
        "middle_back",
        functools.partial(middle_body, width, blocks),
        [(SMEM, ids), (SMEM, info), (VMEM, mod), (VMEM, x1), (VMEM, c_s), (VMEM, dh2)]
        + [(VMEM, dh2_got), (VMEM, w_out_all.reshape(blocks, narrow, size))],
        [(VMEM, shape((narrow, count)))] * blocks
        + [
            (VMEM, shape((count, size), F32)),
            (VMEM, shape((count, size))),
            (VMEM, shape((slots, 2 * size), F32)),
        ],
        flops=2 * count * size * size,
    )
    pieces, (dx1, d_attn, sums_two) = outs[:blocks], outs[blocks:]
    up_parts = [pieces[0]] + [swap(pieces[k], "blk", k) for k in range(1, blocks)]

    result, sums_gate, g_out, g_out_send = run(
        "result",
        functools.partial(result_body, width, shards),
        [(SMEM, ids), (SMEM, info)]
        + [(VMEM, a) for a in (mod, x1, c_s, mlp, mlp_got, attn, dx1, d_attn, om, perm)],
        [
            (VMEM, shape((count, size))),
            (VMEM, shape((slots, 2 * size), F32)),
            (VMEM, shape((shards, out_rows, size))),
            (VMEM, shape((shards, out_rows, size))),
        ],
        [pltpu.VMEM((count, size), BF16), pltpu.VMEM((2 * shards, out_rows, size), BF16)],
        flops=2 * count * size * size,
    )

    (d_qkv,) = run(
        "attend_back",
        functools.partial(attend_back_body, own, head_size, blocks),
        [(SMEM, ids), (SMEM, info), (SMEM, mask)]
        + [(VMEM, a) for a in (qkv, held, lse)]
        + [(VMEM, a) for a in up_parts],
        [(VMEM, shape((units, BLOCK, wide)))],
        [
            pltpu.VMEM((blocks, narrow, count), BF16),
            pltpu.VMEM((units, own, LANES, BLOCK), BF16),
            pltpu.VMEM((units, 8, BLOCK), F32),
            pltpu.VMEM((units, own, LANES, BLOCK), F32),
            pltpu.VMEM((own, BLOCK, LANES), F32),
            pltpu.VMEM((own, BLOCK, LANES), F32),
        ],
        flops=5 * units * units * BLOCK * BLOCK * wide // 3,
    )
    per = 4 if units % 4 == 0 else 1
    rows_qkv = w_qkv.shape[0]
    n_copies = 4 * chips + 2 * shards + 4
    grad_tokens, sums_one, g_qkv, g_out = run(
        "stream_back",
        functools.partial(stream_back_body, shards, chips, heads, per),
        [(ANY, normed), (ANY, g_out_send)]
        + [(VMEM, a) for a in (d_qkv, w_heads, mod, mark, x_s, dx1, perm, g_out)],
        [
            (VMEM, shape((count, size))),
            (VMEM, shape((slots, 2 * size), F32)),
            (VMEM, shape((rows_qkv, 3 * narrow))),
            (VMEM, shape((out_rows, size))),
        ],
        [
            pltpu.VMEM((chips, count, size), BF16),
            pltpu.VMEM((chips, count, size), BF16),
            pltpu.VMEM((chips, count, size), BF16),
            pltpu.VMEM((chips + 1, count, size), BF16),
            pltpu.VMEM((2, per, BLOCK, size), BF16),
            pltpu.VMEM((size, wide), F32),
            pltpu.VMEM((shards, rows_qkv, 3 * narrow), BF16),
            pltpu.VMEM((shards, rows_qkv, 3 * narrow), BF16),
            pltpu.VMEM((shards, out_rows, size), BF16),
            pltpu.VMEM((shards, out_rows, size), BF16),
            pltpu.VMEM((shards, out_rows, size), BF16),
            pltpu.VMEM((count, size), F32),
            pltpu.VMEM((count, size), BF16),
            pltpu.VMEM((padded, 2 * size), F32),
            pltpu.SemaphoreType.DMA((2,)),
            pltpu.SemaphoreType.DMA((n_copies,)),
            pltpu.SemaphoreType.DMA((n_copies,)),
        ],
        flops=4 * units * BLOCK * size * wide,
        vmem=60,
        collective=1,
    )

    pieces = fc_rows // out_rows
    n_copies = 5 * pieces + 10 + 6 * chips + 2 * shards
    totals, g_qkv, d_mod, d_cond = run(
        "finish",
        functools.partial(finish_body, shards, chips),
        [(ANY, g_fc.reshape(pieces, out_rows, size)), (ANY, w_ada)]
        + [(VMEM, a) for a in (g_out, g_qkv, sums_one, sums_two, sums_gate, condition)],
        [
            (ANY, shape((2, pieces + 1, out_rows, size))),
            (ANY, shape((blocks, rows_qkv, 3 * narrow))),
            (VMEM, shape((shards, slots, wider), F32)),
            (VMEM, shape((shards, shards * slots, ada_rows), F32)),
        ],
        [pltpu.VMEM((pieces + 1, out_rows, size), BF16)] * 5
        + [
            pltpu.VMEM((blocks, rows_qkv, 3 * narrow), BF16),
            pltpu.VMEM((slots, wider), F32),
            pltpu.VMEM((slots, wider), F32),
            pltpu.VMEM((chips, slots, wider), F32),
            pltpu.VMEM((shards, slots, wider), F32),
            pltpu.VMEM((shards, shards * slots, ada_rows), F32),
            pltpu.VMEM(w_ada.shape, BF16),
            pltpu.SemaphoreType.DMA((3,)),
            pltpu.SemaphoreType.DMA((n_copies,)),
            pltpu.SemaphoreType.DMA((n_copies,)),
        ],
        vmem=60,
        collective=2,
    )
    grad_temb, grad_ada, grad_qkv, grad_out, grad_fc1, grad_fc2 = run(
        "unfold",
        functools.partial(unfold_body, shards),
        [(VMEM, a) for a in (lifted, waves, d_mod, d_cond, totals, g_qkv)],
        [
            (VMEM, shape(w_temb.shape, F32)),
            (ANY, shape(w_ada.shape, F32)),
            (ANY, shape(w_qkv.shape, F32)),
            (ANY, shape(w_out.shape, F32)),
            (ANY, shape(w_fc1.shape, F32)),
            (ANY, shape(w_fc2.shape, F32)),
        ],
        [
            pltpu.VMEM(a.shape, F32) for a in (w_ada, w_qkv, w_out, w_fc1, w_fc2)
        ]
        + [pltpu.SemaphoreType.DMA((5,))],
        vmem=60,
    )
    return (
        result,
        grad_tokens,
        grad_temb,
        grad_ada,
        grad_qkv,
        grad_out,
        grad_fc1,
        grad_fc2,
    )


def solution(mesh):
    placed = (
        P(("fsdp", "blk"), None),
        P("fsdp", None),
        P("fsdp", None),
        P("fsdp", None, None),
        P("fsdp", None, None),
        P(("fsdp", "blk")),
        P("fsdp", None),
        P("fsdp", None),
        P("fsdp", None),
        P("fsdp", None),
        P("fsdp", None),
        P("fsdp", None),
        P(("fsdp", "blk"), None),
    )
    return jax.shard_map(
        on_device,
        mesh=mesh,
        in_specs=placed,
        out_specs=(
            P(("fsdp", "blk"), None),
            P(("fsdp", "blk"), None),
            P("fsdp", None),
            P("fsdp", None),
            P("fsdp", None),
            P("fsdp", None),
            P("fsdp", None),
            P("fsdp", None),
        ),
        check_vma=False,
    )
```

```python
import functools
import math

import jax
import jax.numpy as jnp
from jax import lax
from jax.experimental import pallas as pl
from jax.experimental.pallas import tpu as pltpu
from jax.sharding import PartitionSpec as P

HIGH = lax.Precision.HIGHEST
BF16 = jnp.bfloat16
F32 = jnp.float32
I32 = jnp.int32
LANES = 128
BLOCK = 256
NEG = -1e30
LOG2E = 1.4426950408889634

VMEM = pl.BlockSpec(memory_space=pltpu.VMEM)
SMEM = pl.BlockSpec(memory_space=pltpu.SMEM)
ANY = pl.BlockSpec(memory_space=pl.ANY)


def shape(dims, kind=BF16):
    return jax.ShapeDtypeStruct(tuple(dims), kind)


def run(name, body, ins, outs, scratch=(), flops=0, vmem=48, collective=None, **more):
    moved = sum(a.size * a.dtype.itemsize for _, a in ins)
    moved += sum(math.prod(o.shape) * jnp.dtype(o.dtype).itemsize for _, o in outs)
    return pl.pallas_call(
        body,
        out_shape=[o for _, o in outs],
        in_specs=[s for s, _ in ins],
        out_specs=[s for s, _ in outs],
        scratch_shapes=list(scratch),
        compiler_params=pltpu.CompilerParams(
            vmem_limit_bytes=vmem << 20,
            collective_id=collective,
            has_side_effects=collective is not None,
        ),
        cost_estimate=pl.CostEstimate(flops=flops, bytes_accessed=moved, transcendentals=0),
        name=name,
        **more,
    )(*[a for _, a in ins])


def swap(array, axis, by):
    size = lax.axis_size(axis)
    return lax.ppermute(array, axis, [(i, i ^ by) for i in range(size)])


def frequencies(steps, entries):
    half = entries // 2
    ladder = jnp.exp(-math.log(10000.0) * lax.iota(jnp.int32, half) / half)
    angles = steps.astype(F32)[:, None] * ladder[None, :]
    return jnp.concatenate([jnp.cos(angles), jnp.sin(angles)], axis=1)


def nn(left, right):
    return lax.dot_general(left, right, (((1,), (0,)), ((), ())), preferred_element_type=F32)


def nt(left, right):
    return lax.dot_general(left, right, (((1,), (1,)), ((), ())), preferred_element_type=F32)


def tn(left, right):
    return lax.dot_general(left, right, (((0,), (0,)), ((), ())), preferred_element_type=F32)


def each(count, step, group=1):
    if count % group:
        group = 1

    def one(index, carry):
        for i in range(group):
            step(index * group + i)
        return carry

    lax.fori_loop(0, count // group, one, 0)


def normal(values):
    center = values - jnp.mean(values, axis=-1, keepdims=True)
    scale = lax.rsqrt(jnp.mean(center * center, axis=-1, keepdims=True) + 1e-06)
    return center * scale, scale


def normal_back(grad, normed, scale):
    along = jnp.mean(grad * normed, axis=-1, keepdims=True)
    return scale * (grad - jnp.mean(grad, axis=-1, keepdims=True) - normed * along)


def flip(index, by):
    bit = 1
    while bit <= by:
        if by & bit:
            index = index + bit * (1 - 2 * ((index // bit) % 2))
        bit *= 2
    return index


def fetch(pairs, sems, first=0):
    copies = []
    for index, (source, target) in enumerate(pairs, first):
        copy = pltpu.make_async_copy(source, target, sems.at[index])
        copy.start()
        copies.append(copy)
    return copies


class Routes:
    def __init__(self, sent, got):
        self.sent, self.got, self.known, self.started = sent, got, {}, []

    def slot(self, name):
        return self.known.setdefault(name, len(self.known))

    def copy(self, name, source, target, to, landed=None):
        return pltpu.make_async_remote_copy(
            src_ref=source,
            dst_ref=target,
            send_sem=self.sent.at[self.slot(name)],
            recv_sem=self.got.at[self.slot(landed or name)],
            device_id=to,
            device_id_type=pl.DeviceIdType.MESH,
        )

    def start(self, name, source, target, to, when=None, landed=None):
        def make():
            return self.copy(name, source, target, to, landed)

        self.started.append((make, when))
        if when is None:
            make().start()
        else:
            pl.when(when)(lambda: make().start())

    def arrive(self, name, target, when=None):
        def wait():
            b = lax.axis_index("blk")
            self.copy(name, target, target, {"blk": b + 1 - 2 * (b % 2)}).wait_recv()

        if when is None:
            wait()
        else:
            pl.when(when)(wait)

    def finish(self):
        for make, when in self.started:
            if when is None:
                make().wait_send()
            else:
                pl.when(when)(lambda make=make: make().wait_send())


def greet(shards, chips):
    f, b = lax.axis_index("fsdp"), lax.axis_index("blk")
    z, c = b // 2, b % 2
    barrier = pltpu.get_barrier_semaphore()

    def signal(to):
        pl.semaphore_signal(barrier, inc=1, device_id=to, device_id_type=pl.DeviceIdType.MESH)

    for k in range(1, shards):
        signal({"fsdp": flip(f, k)})
    signal({"blk": b + 1 - 2 * c})
    pl.when(z > 0)(lambda: signal({"blk": b - 2}))
    pl.when(z < chips - 1)(lambda: signal({"blk": b + 2}))
    ends = (z == 0).astype(I32) + (z == chips - 1).astype(I32)
    pl.semaphore_wait(barrier, shards + 2 - ends)


def pick_half_body(parts, ids_ref, w1_ref, w2_ref, o_ref):
    rows, hidden = w1_ref.shape
    half = hidden // parts // 2
    size = o_ref.shape[1]
    down = w2_ref.shape[0] // 2
    blocks = hidden // 2 // size
    for core in range(2):

        @pl.when(ids_ref[2] == core)
        def _():
            picked = jnp.concatenate(
                [
                    w1_ref[:, (2 * part + core) * half : (2 * part + core + 1) * half]
                    for part in range(parts)
                ],
                axis=1,
            )
            for block in range(blocks):
                o_ref[block * rows : (block + 1) * rows, :] = picked[
                    :, block * size : (block + 1) * size
                ]
            o_ref[blocks * rows :, :] = w2_ref[core * down : (core + 1) * down, :]


def front_body(
    shards, chips, heads, items_ref, keep_ref, x_ref, c_ref, spec_ref, temb_ref, ada_ref, qkvw_ref,
    outw_ref, xs_ref, cs_ref, hot_ref, info_ref, mark_ref, perm_ref, mod_ref, cond_ref, low_ref, wave_ref, dm_ref, h_ref,
    qkv_ref, wh_ref, wo_ref, x_all, spec_all, temb_all, part_own, part_got, hots, dms, wh_all, wo_all,
    h_all, ada_s, qkvw_s, local, sent, got,
):
    f, b = lax.axis_index("fsdp"), lax.axis_index("blk")
    z, c = b // 2, b % 2
    blocks = 2 * chips
    pair = b + 1 - 2 * c
    width = BLOCK // blocks
    count, size = x_ref.shape
    units = count // width
    own = heads // blocks
    head_size = size // heads
    slots = spec_ref.shape[0]
    routes = Routes(sent, got)
    inside = fetch(
        [(ada_ref, ada_s), (qkvw_ref, qkvw_s), (outw_ref, wo_all.at[f])], local, units
    )
    greet(shards, chips)

    spec_all[f] = spec_ref[...]
    temb_all[f] = temb_ref[...]
    for k in range(1, shards):
        to = {"fsdp": flip(f, k)}
        routes.start(("spec", k), spec_ref, spec_all.at[f], to)
        routes.start(("temb", k), temb_ref, temb_all.at[f], to)

    items = items_ref[...]
    slot = lax.broadcasted_iota(I32, (slots, count), 0)
    hot = (items == slot).astype(F32)
    start = jnp.sum((items < slot).astype(F32), axis=1, keepdims=True)
    end = start + jnp.sum(hot, axis=1, keepdims=True)
    row = lax.broadcasted_iota(I32, (count, count), 0)
    col = lax.broadcasted_iota(I32, (count, count), 1)
    rank = nn(hot.astype(BF16), (row <= col).astype(BF16))
    place = jnp.sum(hot * (start + rank), axis=0, keepdims=True) - 1.0
    perm = (row.astype(F32) == place).astype(BF16)
    perm_ref[...] = perm
    x_s = nn(perm, x_ref[...]).astype(BF16)
    xs_ref[...] = x_s
    x_all[b] = x_s

    def line(side, s, send):
        away = s - 1 if send else s
        chip = z - away if side == 0 else z + away
        ahead = z + 1 < chips if side == 0 else z > 0
        known = z >= away if side == 0 else z + away < chips
        when = known & ahead if send else known
        return chip * 2 + c, {"blk": b + 2 if side == 0 else b - 2}, when

    def send_on(s):
        for side in range(2):
            device, to, when = line(side, s, True)
            routes.start(("line", side, s), x_all.at[device], x_all.at[device], to, when)

    send_on(1)
    routes.start("pair", x_all.at[b], x_all.at[b], {"blk": pair})
    cs_ref[...] = nn(perm, c_ref[...]).astype(BF16)
    keep = jnp.broadcast_to(keep_ref[...].astype(F32), (slots, count)).astype(BF16)
    kept = nt(keep, perm)
    at = lax.broadcasted_iota(I32, (slots, count), 1).astype(F32)
    hots[0] = kept * ((at >= start) & (at < end)).astype(F32)
    first = (lax.broadcasted_iota(I32, (slots, LANES), 1) * width).astype(F32)
    mine = ((first >= start) & (first < end)).astype(F32)
    mark_ref[...] = mine
    which = lax.broadcasted_iota(I32, (slots, LANES), 0).astype(F32)
    info_ref[0:1, :] = jnp.sum(mine * which, axis=0, keepdims=True).astype(I32)
    info_ref[1:2, :] = (jnp.sum(mine * start, axis=0, keepdims=True) / width).astype(I32)
    info_ref[2:3, :] = (jnp.sum(mine * end, axis=0, keepdims=True) / width).astype(I32)
    info_ref[3:8, :] = jnp.zeros((5, LANES), I32)

    for k in range(1, shards):
        other = flip(f, k)
        routes.arrive(("spec", k), spec_all.at[other])
        routes.arrive(("temb", k), temb_all.at[other])
    spectra = spec_all[...].reshape(shards * slots, -1).astype(BF16)
    condition = nn(spectra, temb_all[...].reshape(-1, size))
    rows = ada_ref.shape[0]
    for shard in range(shards):

        @pl.when(f == shard)
        def _():
            cond_ref[...] = condition[:, shard * rows : (shard + 1) * rows]
            freqs = temb_ref.shape[0]
            wave_ref[...] = spectra[:, shard * freqs : (shard + 1) * freqs].astype(F32)

    values = cond_ref[...]
    lifted = (values / (1.0 + jnp.exp(-values))).astype(BF16)
    low_ref[...] = lifted
    inside[0].wait()
    part_own[...] = nn(lifted, ada_s[...]).reshape(part_own.shape)
    for k in range(1, shards):
        other = flip(f, k)
        routes.start(("part", k), part_own.at[other], part_got.at[f], {"fsdp": other})

    rows = qkvw_ref.shape[0]
    inside[1].wait()
    row = lax.broadcasted_iota(I32, (size, LANES), 0)
    col = lax.broadcasted_iota(I32, (size, LANES), 1)
    picked = []
    for head in range(own):
        mark = (row == (b * own + head) * head_size + col) & (col < head_size)
        picked.append(mark.astype(F32).astype(BF16))
    for part in range(3):
        for head in range(own):
            at = (part * own + head) * LANES
            wh_all[f, :, at : at + LANES] = nn(
                qkvw_s[:, part * size : (part + 1) * size], picked[head]
            ).astype(BF16)
    if shards == 4:
        for k in (1, 2):
            routes.start(("head", k), wh_all.at[f], wh_all.at[f], {"fsdp": flip(f, k)})
    else:
        for k in range(1, shards):
            routes.start(("head", k), wh_all.at[f], wh_all.at[f], {"fsdp": flip(f, k)})

    def take(s):
        for side in range(2):
            device, _, when = line(side, s, False)
            routes.arrive(("line", side, s), x_all.at[device], when)
            if s + 1 < chips:
                device, to, onward = line(side, s + 1, True)
                routes.start(
                    ("line", side, s + 1), x_all.at[device], x_all.at[device], to, onward
                )
            device, _, when = line(side, s, False)
            routes.start(
                ("pair", side, s), x_all.at[device], x_all.at[device], {"blk": pair}, when
            )

    take(1)
    if shards == 4:
        half = rows // 2
        for k, low in ((1, 0), (2, half)):
            routes.arrive(("head", k), wh_all.at[flip(f, k)])
            part = wh_all.at[flip(f, k), low : low + half]
            routes.start(("head", 3, k), part, part, {"fsdp": flip(f, 3 - k)})

    for k in range(1, shards):
        routes.start(("out", k), outw_ref.at[c], wo_all.at[f, c], {"fsdp": flip(f, k)})

    total = part_own[f]
    for k in range(1, shards):
        other = flip(f, k)
        routes.arrive(("part", k), part_got.at[other])
        total = total + part_got[other]
    mod_ref[...] = lax.dot_general(
        mine[:, : mod_ref.shape[0]], total, (((0,), (0,)), ((), ())), precision=HIGH,
        preferred_element_type=F32,
    )

    def early(u):
        rows = pl.ds(pl.multiple_of(u * width, width), width)
        gate = mod_ref[pl.ds(u, 1), 5 * size : 6 * size]
        dms[0, rows, :] = (cs_ref[rows, :].astype(F32) * gate).astype(BF16)

    each(units, early)
    routes.start("dm", dms.at[0], dms.at[1], {"blk": pair})
    routes.start("hot", hots.at[0], hots.at[1], {"blk": pair})

    if shards == 4:
        half = rows // 2
        routes.arrive(("head", 3, 1), wh_all.at[flip(f, 3), 0:half])
        routes.arrive(("head", 3, 2), wh_all.at[flip(f, 3), half:rows])
    else:
        for k in range(1, shards):
            routes.arrive(("head", k), wh_all.at[flip(f, k)])
    wh_ref[...] = wh_all[...].reshape(wh_ref.shape)

    def block(device):
        at = pl.ds(pl.multiple_of(device * width, width), width)

        def one(u):
            shift = mod_ref[pl.ds(u, 1), 0:size]
            scale = mod_ref[pl.ds(u, 1), size : 2 * size]
            part = x_all[device, pl.ds(pl.multiple_of(u * width, width), width), :]
            normed, _ = normal(part.astype(F32))
            low = (normed * (1.0 + scale) + shift).astype(BF16)
            h_all[pl.ds(pl.multiple_of(u * width, width), width), :] = low

        each(units, one, 3)
        copies = fetch(
            [
                (h_all.at[u * width : (u + 1) * width], h_ref.at[u, at])
                for u in range(units)
            ],
            local,
        )
        found = nn(h_all[...], wh_ref[...]).astype(BF16)
        qkv_ref[:, at, :] = found.reshape(units, width, found.shape[1])
        for copy in copies:
            copy.wait()

    routes.arrive("pair", x_all.at[pair])
    each(2, lambda core: block(z * 2 + core))

    def work(s):
        for side in range(2):
            device, _, when = line(side, s, False)
            routes.arrive(("pair", side, s), x_all.at[device + 1 - 2 * c], when)

        def pick(q):
            chip = z - s + 2 * s * (q // 2)

            @pl.when((chip >= 0) & (chip < chips))
            def _():
                block(chip * 2 + q % 2)

        each(4, pick)

    for s in range(2, chips):
        take(s)
        if s == 2:
            for k in range(1, shards):
                other = flip(f, k)
                routes.arrive(("out", k), wo_all.at[other, c])
                routes.start(
                    ("pair out", k), wo_all.at[other, c], wo_all.at[other, c], {"blk": pair}
                )
        work(s - 1)
    work(chips - 1)
    inside[2].wait()
    for k in range(1, shards):
        routes.arrive(("pair out", k), wo_all.at[flip(f, k), 1 - c])
    routes.arrive("dm", dms.at[1])
    routes.arrive("hot", hots.at[1])
    routes.finish()
    copies = fetch([(wo_all, wo_ref), (dms, dm_ref), (hots, hot_ref)], local)
    for copy in copies:
        copy.wait()


def exchange_lanes(tiles, width):
    tiles = list(tiles)
    count = len(tiles)
    group = lax.broadcasted_iota(I32, tiles[0].shape, 1) // width
    half = count // 2
    while half:
        low = (group // half) % 2 == 0
        fresh = list(tiles)
        for i in range(count):
            if (i // half) % 2 == 0:
                a, d = tiles[i], tiles[i + half]
                fresh[i] = jnp.where(low, a, pltpu.roll(d, half * width, 1))
                fresh[i + half] = jnp.where(low, pltpu.roll(a, LANES - half * width, 1), d)
        tiles = fresh
        half //= 2
    return tiles


def in_groups(first, last, sizes, step, carry):
    for size in sizes:
        count = (last - first) // size

        def one(index, carry, first=first, size=size):
            return step(first + index * size, size, carry)

        carry = lax.fori_loop(0, count, one, carry)
        first = first + count * size
    return carry


def attend_body(own, size, blocks, ids_ref, info_ref, mask_ref, qkv_ref, o_ref, lse_ref, *refs):
    outs, (held, turned, placed) = refs[:blocks], refs[blocks:]
    units = qkv_ref.shape[0]
    width = BLOCK // blocks
    b = ids_ref[1]
    scale = LOG2E / math.sqrt(size)
    tall = turned.shape[2]

    def turn(j):
        for h in range(own):
            at = (2 * own + h) * LANES
            values = qkv_ref[j, :, at : at + LANES].astype(F32).T
            turned[j, h] = values[0:tall].astype(BF16)

    each(units, turn, 2)

    def one_unit(u):
        queries = [qkv_ref[u, :, h * LANES : (h + 1) * LANES] for h in range(own)]

        def some_blocks(j, count, carry):
            fresh = []
            for h in range(own):
                top, total, acc = carry[h]
                keys = qkv_ref[pl.ds(j, count), :, (own + h) * LANES : (own + h + 1) * LANES]
                scores = nt(keys.reshape(count * BLOCK, LANES), queries[h]) * scale
                new_top = jnp.maximum(top, jnp.max(scores, axis=0, keepdims=True))
                probs = jnp.exp2(scores - new_top)
                decay = jnp.exp2(top - new_top)
                total = total * decay + jnp.sum(probs, axis=0, keepdims=True)
                acc = acc * decay
                low = probs.astype(BF16)
                for i in range(count):
                    acc = acc + nn(turned[j + i, h], low[i * BLOCK : (i + 1) * BLOCK])
                fresh.append((new_top, total, acc))
            return tuple(fresh)

        start = tuple(
            (
                jnp.full((1, BLOCK), NEG, F32),
                jnp.zeros((1, BLOCK), F32),
                jnp.zeros((tall, BLOCK), F32),
            )
            for _ in range(own)
        )
        done = in_groups(info_ref[1, u], info_ref[2, u], (4, 2, 1), some_blocks, start)
        slot = info_ref[0, u]
        rows = []
        for h in range(own):
            top, total, acc = done[h]
            keep = mask_ref[slot, b * own + h].astype(F32)
            rows.append((acc * (keep / total))[0:size])
            lse_ref[u, h : h + 1, :] = top + jnp.log2(total)
        held[u] = jnp.concatenate(rows, axis=0) if own > 1 else rows[0]
        o_ref[u] = held[u].astype(BF16)

    each(units, one_unit)
    groups = LANES // width
    for g in range(units // groups):
        for e in range(blocks // groups):
            tiles = [
                held[groups * g + i, :, e * LANES : (e + 1) * LANES] for i in range(groups)
            ]
            for j, tile in enumerate(exchange_lanes(tiles, width)):
                placed[groups * e + j, :, g * LANES : (g + 1) * LANES] = tile.astype(BF16)
    for k in range(blocks):
        outs[k][...] = placed[lax.bitwise_xor(b, k)]


def attend_back_body(own, size, blocks, ids_ref, info_ref, mask_ref, qkv_ref, o_ref, lse_ref, *refs):
    pieces, (d_ref, given, up, delta, d_q, d_k, d_v) = refs[:blocks], refs[blocks:]
    units = qkv_ref.shape[0]
    width = BLOCK // blocks
    b = ids_ref[1]
    factor = 1.0 / math.sqrt(size)
    scale = LOG2E * factor
    for k in range(blocks):
        given[lax.bitwise_xor(b, k)] = pieces[k][...]
    up[...] = jnp.zeros_like(up)
    groups = LANES // width
    for g in range(units // groups):
        for e in range(blocks // groups):
            tiles = [
                given[groups * e + j, :, g * LANES : (g + 1) * LANES].astype(F32)
                for j in range(groups)
            ]
            for i, tile in enumerate(exchange_lanes(tiles, width)):
                unit = groups * g + i
                slot = info_ref[0, unit]
                for h in range(own):
                    keep = mask_ref[slot, b * own + h].astype(F32)
                    kept = tile[h * size : (h + 1) * size] * keep
                    up[unit, h, 0:size, e * LANES : (e + 1) * LANES] = kept.astype(BF16)
                    mine = o_ref[unit, h * size : (h + 1) * size, e * LANES : (e + 1) * LANES]
                    delta[unit, h : h + 1, e * LANES : (e + 1) * LANES] = jnp.sum(
                        kept * mine.astype(F32), axis=0, keepdims=True
                    )
    d_q[...] = jnp.zeros_like(d_q)

    def one_unit(j):
        d_k[...] = jnp.zeros_like(d_k)
        d_v[...] = jnp.zeros_like(d_v)
        keys = [qkv_ref[j, :, (own + h) * LANES : (own + h + 1) * LANES] for h in range(own)]
        turned = [keys[h].astype(F32).T.astype(BF16) for h in range(own)]

        def some_blocks(i, count, carry):
            for h in range(own):
                at = (2 * own + h) * LANES
                values = qkv_ref[j, :, at : at + LANES]
                sum_k = sum_v = 0.0
                for n in range(count):
                    queries = qkv_ref[i + n, :, h * LANES : (h + 1) * LANES]
                    scores = nt(keys[h], queries) * scale
                    probs = jnp.exp2(scores - lse_ref[i + n, h : h + 1, :])
                    d_probs = nn(values, up[i + n, h])
                    d_scores = (probs * (d_probs - delta[i + n, h : h + 1, :])).astype(BF16)
                    sum_k = sum_k + nn(d_scores, queries)
                    sum_v = sum_v + nt(probs.astype(BF16), up[i + n, h])
                    d_q[i + n, h] += nn(turned[h], d_scores)
                d_k[h] += sum_k
                d_v[h] += sum_v
            return carry

        in_groups(info_ref[1, j], info_ref[2, j], (4, 2, 1), some_blocks, 0)
        for h in range(own):
            at = (own + h) * LANES
            d_ref[j, :, at : at + LANES] = (d_k[h] * factor).astype(BF16)
            at = (2 * own + h) * LANES
            d_ref[j, :, at : at + LANES] = d_v[h].astype(BF16)

    each(units, one_unit)

    def turn(i):
        for h in range(own):
            d_ref[i, :, h * LANES : (h + 1) * LANES] = (d_q[i, h].T * factor).astype(BF16)

    each(units, turn)


def project_body(width, blocks, ids_ref, mod_ref, x_ref, w_ref, *refs):
    om_refs, refs = refs[:blocks], refs[blocks:]
    attn_ref, x1_ref, h_ref, om_ref, om_all, sems = refs
    b = ids_ref[1]
    size = x_ref.shape[1]
    copies = fetch(
        [(om_refs[k], om_all.at[lax.bitwise_xor(b, k)]) for k in range(blocks)], sems
    )
    for copy in copies:
        copy.wait()
    om = om_all[...].reshape(size, x_ref.shape[0])
    om_ref[...] = om
    weight = w_ref[...]
    attn_ref[...] = tn(om, weight)

    def one(u):
        rows = pl.ds(pl.multiple_of(u * width, width), width)
        gate, shift, scale = [mod_ref[pl.ds(u, 1), i * size : (i + 1) * size] for i in (2, 3, 4)]
        middle = x_ref[rows, :].astype(F32) + gate * attn_ref[rows, :]
        x1_ref[rows, :] = middle
        normed, _ = normal(middle)
        h_ref[rows, :] = (normed * (1.0 + scale) + shift).astype(BF16)

    each(x_ref.shape[0] // width, one)


def ff_body(shards, step, sides, hot_ref, chan_ref, h_m, h_o, dm_ref, w_ref, *refs):
    mlp_m, mlp_o, dh_m, dh_o, g_ref, w1, w2, h, dm, turned, hid_s, du_s, mlp, dh, g1, g2, sems = refs
    total = h.shape[0]
    count = total // 2
    f_size, size = w2.shape
    blocks = f_size // size
    row1, row2 = size // shards, f_size // shards

    def up_part(ref, shard, low, high):
        block = low // size
        return ref.at[
            shard, block * row1 : (block + 1) * row1, low - block * size : high - block * size
        ]

    def down_part(ref, shard, low, high):
        at = blocks * row1 - shard * row2
        return ref.at[shard, at + low : at + high]

    def chunk(index):
        low, high = index * step, (index + 1) * step
        cols = [
            (max(low, i * size), min(high, (i + 1) * size))
            for i in range(blocks)
            if max(low, i * size) < min(high, (i + 1) * size)
        ]
        rows = [
            (i, max(low, i * row2), min(high, (i + 1) * row2))
            for i in range(shards)
            if max(low, i * row2) < min(high, (i + 1) * row2)
        ]
        return cols, rows

    used = [0]

    def begin(pairs):
        copies = fetch(pairs, sems, used[0])
        used[0] += len(copies)
        return copies

    waits = [
        begin(
            [
                (h_m, h.at[0:count]),
                (h_o, h.at[count:total]),
                (dm_ref.at[0], dm.at[0:count]),
                (dm_ref.at[1], dm.at[count:total]),
            ]
        )
    ]
    chunks = f_size // step
    for index in range(chunks):
        cols, rows = chunk(index)
        pairs = [
            (up_part(w_ref, shard, lo, hi), w1.at[shard * row1 : (shard + 1) * row1, lo:hi])
            for shard in range(shards)
            for lo, hi in cols
        ]
        pairs += [(down_part(w_ref, shard, lo, hi), w2.at[lo:hi]) for shard, lo, hi in rows]
        waits.append(begin(pairs))
    for copy in waits[0]:
        copy.wait()
    for at in range(0, total, LANES):
        turned[:, at : at + LANES] = h[at : at + LANES, :].astype(F32).T.astype(BF16)
    hots = jnp.concatenate([hot_ref[side] for side in range(2)], axis=1).astype(BF16)
    left = []
    for index in range(chunks):
        for copy in waits[index + 1]:
            copy.wait()
        cols = slice(index * step, (index + 1) * step)
        up = w1[:, cols]
        down = w2[cols, :]
        chan = chan_ref[:, cols].astype(F32).astype(BF16)
        for side in range(sides):
            rows = slice(side * total // sides, (side + 1) * total // sides)
            keep = tn(hots[:, rows], chan)
            pre = nn(h[rows, :], up)
            inner = pre * pre
            bent = jnp.tanh(0.7978845608028654 * (pre + 0.044715 * inner * pre))
            half = 0.5 * (1.0 + bent)
            hid = (pre * half * keep).astype(BF16)
            slope = half + (0.5 * 0.7978845608028654) * pre * (1.0 - bent * bent) * (
                1.0 + (3.0 * 0.044715) * inner
            )
            back = nt(dm[rows, :], down)
            du = (slope * back * keep).astype(BF16)
            hid_s[rows, :] = hid
            du_s[rows, :] = du
            if index:
                mlp[rows, :] += nn(hid, down)
                dh[rows, :] += nt(du, up)
            else:
                mlp[rows, :] = nn(hid, down)
                dh[rows, :] = nt(du, up)
        g1[:, cols] = nn(turned[...], du_s[...]).astype(BF16)
        g2[cols, :] = tn(hid_s[...], dm[...]).astype(BF16)
        parts, rows = chunk(index)
        pairs = [
            (g1.at[shard * row1 : (shard + 1) * row1, lo:hi], up_part(g_ref, shard, lo, hi))
            for shard in range(shards)
            for lo, hi in parts
        ]
        pairs += [(g2.at[lo:hi], down_part(g_ref, shard, lo, hi)) for shard, lo, hi in rows]
        left += begin(pairs)
    mlp_m[...] = mlp[0:count, :]
    mlp_o[...] = mlp[count:total, :].astype(BF16)
    dh_m[...] = dh[0:count, :]
    dh_o[...] = dh[count:total, :].astype(BF16)
    for copy in left:
        copy.wait()


def middle_body(
    width, blocks, ids_ref, info_ref, mod_ref, x1_ref, c_ref, dh_ref, got_ref, w_ref, *refs
):
    outs, (dx_ref, da_ref, sum_ref) = refs[:blocks], refs[blocks:]
    b = ids_ref[1]
    count, size = x1_ref.shape
    part = size // blocks
    sum_ref[...] = jnp.zeros_like(sum_ref)

    def one(u):
        rows = pl.ds(pl.multiple_of(u * width, width), width)
        slot = info_ref[0, u]
        gate = mod_ref[pl.ds(u, 1), 2 * size : 3 * size]
        scale = mod_ref[pl.ds(u, 1), 4 * size : 5 * size]
        normed, spread = normal(x1_ref[rows, :])
        grad = dh_ref[rows, :] + got_ref[rows, :].astype(F32)
        sum_ref[pl.ds(slot, 1), 0:size] += jnp.sum(grad, axis=0, keepdims=True)
        sum_ref[pl.ds(slot, 1), size : 2 * size] += jnp.sum(grad * normed, axis=0, keepdims=True)
        dx = c_ref[rows, :].astype(F32) + normal_back(grad * (1.0 + scale), normed, spread)
        dx_ref[rows, :] = dx
        da_ref[rows, :] = (dx * gate).astype(BF16)

    each(count // width, one)
    for k in range(blocks):
        outs[k][...] = nt(w_ref[lax.bitwise_xor(b, k)], da_ref[...]).astype(BF16)


def result_body(
    width, shards, ids_ref, info_ref, mod_ref, x1_ref, c_ref, mlp_ref, got_ref, attn_ref, dx_ref,
    da_ref, om_ref, perm_ref, r_ref, sum_ref, mine_ref, other_ref, held, grad,
):
    f, c = ids_ref[0], ids_ref[2]
    count, size = x1_ref.shape
    sum_ref[...] = jnp.zeros_like(sum_ref)

    def one(u):
        rows = pl.ds(pl.multiple_of(u * width, width), width)
        slot = info_ref[0, u]
        gate = mod_ref[pl.ds(u, 1), 5 * size : 6 * size]
        mlp = mlp_ref[rows, :] + got_ref[rows, :].astype(F32)
        held[rows, :] = (x1_ref[rows, :] + gate * mlp).astype(BF16)
        sum_ref[pl.ds(slot, 1), 0:size] += jnp.sum(
            dx_ref[rows, :] * attn_ref[rows, :], axis=0, keepdims=True
        )
        sum_ref[pl.ds(slot, 1), size : 2 * size] += jnp.sum(
            c_ref[rows, :].astype(F32) * mlp, axis=0, keepdims=True
        )

    each(count // width, one)
    r_ref[...] = tn(perm_ref[...], held[...]).astype(BF16)
    grad[...] = nn(om_ref[...], da_ref[...]).astype(BF16).reshape(grad.shape)
    for k in range(shards):
        base = 2 * lax.bitwise_xor(f, k)
        mine_ref[k] = grad[base + c]
        other_ref[k] = grad[base + 1 - c]


def stream_back_body(
    shards, chips, heads, per, h_ref, gs_ref, d_ref, wh_ref, mod_ref, mine_ref, x_ref, dx_ref, perm_ref,
    gm_ref, o_ref, sum_ref, g_ref, go_ref, give, take, keep, came, h_s, acc, low, others, out_in, out_low,
    out_got, total, held, by_unit, local, sent, got,
):
    f, b = lax.axis_index("fsdp"), lax.axis_index("blk")
    z, c = b // 2, b % 2
    pair = b + 1 - 2 * c
    width = BLOCK // (2 * chips)
    units = d_ref.shape[0]
    count, size = x_ref.shape
    wide = wh_ref.shape[1]
    own = heads // (2 * chips)
    head_size = size // heads
    rows = low.shape[1]
    steps = units // per
    routes = Routes(sent, got)

    def load(i):
        return pltpu.make_async_copy(
            h_ref.at[pl.ds(i * per, per)], h_s.at[i % 2], local.at[i % 2]
        )

    load(0).start()
    greet(shards, chips)
    routes.start("out", gs_ref, out_in, {"blk": pair})

    def partial(device, target):
        at = pl.ds(pl.multiple_of(device * width, width), width)
        grads = d_ref[:, at, :].reshape(count, wide)
        for col in range(0, size, 3 * LANES):
            target[:, col : col + 3 * LANES] = nt(
                grads, wh_ref[col : col + 3 * LANES, :]
            ).astype(BF16)

    def route(side, t):
        if side == 0:
            chip = chips - 1 - t
            return chip, z < chip, z > 0
        return t, z > t, z < chips - 1

    def onward(side, t, chip, when):
        if side == 0:
            slot, to = chip, b + 2
        else:
            slot, to = chip + (chips - chip) * (z - 1 == chip).astype(I32), b - 2
        routes.start(("sum", side, t), keep.at[chip], came.at[slot], {"blk": to}, when)

    def join(chip, slot=None):
        value = keep[chip].astype(F32) + take[chip].astype(F32)
        if slot is not None:
            value = value + came[slot].astype(F32)
        keep[chip] = value.astype(BF16)

    for t in range(chips - 1):
        for side in range(2):
            chip, passes, inside = route(side, t)

            @pl.when(passes)
            def _():
                partial(chip * 2 + 1 - c, give.at[chip])

            routes.start(("pair", side, t), give.at[chip], take.at[chip], {"blk": pair}, passes)

            @pl.when(passes)
            def _():
                partial(chip * 2 + c, keep.at[chip])

            first = passes & jnp.logical_not(inside)
            routes.arrive(("pair", side, t), take.at[chip], first)

            pl.when(first)(lambda: join(chip))
            onward(side, t, chip, first)

    partial(z * 2 + 1 - c, give.at[z])
    routes.start(("pair", "own"), give.at[z], take.at[z], {"blk": pair})
    partial(z * 2 + c, keep.at[z])

    def gather(i):
        if i + 1 < steps:
            load(i + 1).start()
        load(i).wait()
        part = tn(
            h_s[i % 2].reshape(per * BLOCK, size),
            d_ref[i * per : (i + 1) * per].reshape(per * BLOCK, wide),
        )
        if i:
            acc[...] += part
        else:
            acc[...] = part

    for t in range(max(chips - 1, steps)):
        if t < steps:
            gather(t)
        if t == steps - 1:
            packed = jnp.concatenate(
                [acc[:, i * LANES : i * LANES + head_size] for i in range(3 * own)], axis=1
            )
            low[...] = packed.astype(BF16).reshape(low.shape)
            for k in range(1, shards):
                other = flip(f, k)
                routes.start(("grad", k), low.at[other], others.at[k], {"fsdp": other})
        if t == 0:
            routes.arrive("out", out_in)
            out_low[...] = (gm_ref[...].astype(F32) + out_in[...].astype(F32)).astype(BF16)
            for k in range(1, shards):
                routes.start(("out", k), out_low.at[k], out_got.at[k], {"fsdp": flip(f, k)})
        if t >= chips - 1:
            continue
        for near, side in ((True, 0), (True, 1), (False, 1), (False, 0)):
            chip, passes, inside = route(side, t)
            when = passes & inside & ((z < chips // 2) == near)
            routes.arrive(("pair", side, t), take.at[chip], when)
            routes.arrive(("sum", side, t), came.at[chip], when)
            pl.when(when)(lambda: join(chip, chip))
            onward(side, t, chip, when)

    grad, grad_out = low[f].astype(F32), out_low[0].astype(F32)
    for k in range(1, shards):
        routes.arrive(("grad", k), others.at[k])
        grad = grad + others[k].astype(F32)
        routes.arrive(("out", k), out_got.at[k])
        grad_out = grad_out + out_got[k].astype(F32)
    g_ref[...] = grad.astype(BF16)
    go_ref[...] = grad_out.astype(BF16)

    routes.arrive(("pair", "own"), take.at[z])
    total[...] = keep[z].astype(F32) + take[z].astype(F32)
    for t in range(chips - 1):
        for side in range(2):
            chip, _, inside = route(side, t)
            slot = chip if side == 0 else chips
            here = (z == chip) & inside
            routes.arrive(("sum", side, t), came.at[slot], here)

            @pl.when(here)
            def _():
                total[...] += came[slot].astype(F32)

    by_unit[...] = jnp.zeros_like(by_unit)

    def one(u):
        rows = pl.ds(pl.multiple_of(u * width, width), width)
        scale = mod_ref[pl.ds(u, 1), size : 2 * size]
        normed, spread = normal(x_ref[rows, :].astype(F32))
        grad = total[rows, :]
        by_unit[pl.ds(u, 1), 0:size] = jnp.sum(grad, axis=0, keepdims=True)
        by_unit[pl.ds(u, 1), size : 2 * size] = jnp.sum(grad * normed, axis=0, keepdims=True)
        dx = dx_ref[rows, :] + normal_back(grad * (1.0 + scale), normed, spread)
        held[rows, :] = dx.astype(BF16)

    each(units, one, 3)
    o_ref[...] = tn(perm_ref[...], held[...]).astype(BF16)
    sum_ref[...] = lax.dot_general(
        mine_ref[:, : by_unit.shape[0]], by_unit[...], (((1,), (0,)), ((), ())), precision=HIGH,
        preferred_element_type=F32,
    )
    routes.finish()


def finish_body(
    shards, chips, fc_ref, ada_ref, go_ref, gq_ref, one_ref, two_ref, gate_ref, cond_ref, tot_ref, gqa_ref,
    dm_ref, dc_ref, mine, up, inner_in, result, other, gq_all, sum_own, sum_pair, small, mods, conds, ada_s,
    local, sent, got,
):
    f, b = lax.axis_index("fsdp"), lax.axis_index("blk")
    z, c = b // 2, b % 2
    pair = b + 1 - 2 * c
    count = mine.shape[0]
    slots, wider = sum_own.shape
    size = wider // 6
    routes = Routes(sent, got)
    loads = fetch([(fc_ref, mine.at[0 : count - 1]), (ada_ref, ada_s)], local)
    greet(shards, chips)

    sum_own[:, 0 : 2 * size] = one_ref[...]
    sum_own[:, 2 * size : 3 * size] = gate_ref[:, 0:size]
    sum_own[:, 3 * size : 5 * size] = two_ref[...]
    sum_own[:, 5 * size : 6 * size] = gate_ref[:, size : 2 * size]
    routes.start("sum", sum_own, sum_pair, {"blk": pair})
    gq_all[b] = gq_ref[...]

    def line(side, s, send):
        away = s - 1 if send else s
        chip = z - away if side == 0 else z + away
        ahead = z + 1 < chips if side == 0 else z > 0
        known = z >= away if side == 0 else z + away < chips
        return chip, {"blk": b + 2 if side == 0 else b - 2}, known & ahead if send else known

    def send(name, s, place):
        for side in range(2):
            chip, to, when = line(side, s, True)
            routes.start((name, side, s), place(chip), place(chip), to, when)

    def take(name, s, place):
        for side in range(2):
            chip, _, when = line(side, s, False)
            routes.arrive((name, side, s), place(chip), when)
        if s + 1 < chips:
            send(name, s + 1, place)

    def head(chip):
        return gq_all.at[chip * 2 + c]

    send("head", 1, head)
    routes.start("head pair", gq_all.at[b], gq_all.at[b], {"blk": pair})

    half = chips // 2
    right = z // half
    inner, outer = {"blk": b + 2 - 4 * right}, {"blk": b - 2 + 4 * right}
    ends = (z > 0) & (z < chips - 1)
    middle = (z == half - 1) | (z == half)
    edge = jnp.logical_not(middle)

    parts = [[small.at[i] for i in range(4)]]
    parts += [[ref.at[i] for ref in (mine, up, inner_in, result)] for i in range(count)]
    count += 1

    def inward(i, when):
        own, above, within, _ = parts[i]
        routes.start(("up", i), own, above, inner, when & edge)
        routes.start(("across", i), own, within, inner, when & middle, ("in", i))

    mine[count - 2] = go_ref[...]
    routes.arrive("sum", sum_pair)
    total = sum_own[...] + sum_pair[...]
    small[0] = jnp.concatenate(
        [total[:, : 3 * size], total[:, 3 * size :]], axis=0
    ).astype(BF16)
    ahead = min(4, count)
    inward(0, jnp.logical_not(ends))
    loads[0].wait()
    for i in range(1, ahead):
        inward(i, jnp.logical_not(ends))

    def combine():
        mods[f, :, : 3 * size] = small[3, 0:slots].astype(F32)
        mods[f, :, 3 * size :] = small[3, slots : 2 * slots].astype(F32)
        for k in range(1, shards):
            routes.start(("mod", k), mods.at[f], mods.at[f], {"fsdp": flip(f, k)})

    def condition():
        for k in range(1, shards):
            routes.arrive(("mod", k), mods.at[flip(f, k)])
        dm_ref[...] = mods[...]
        loads[1].wait()
        grad = nt(mods[...].reshape(shards * slots, wider).astype(BF16), ada_s[...])
        values = cond_ref[...]
        gate = 1.0 / (1.0 + jnp.exp(-values))
        conds[f] = grad * (gate + values * gate * (1.0 - gate))
        for k in range(1, shards):
            routes.start(("cond", k), conds.at[f], conds.at[f], {"fsdp": flip(f, k)})

    def conditions():
        for k in range(1, shards):
            routes.arrive(("cond", k), conds.at[flip(f, k)])
        dc_ref[...] = conds[...]

    jobs = [combine, condition, conditions]
    heads = [lambda s=s: take("head", s, head) for s in range(1, chips)]

    def forward(i):
        own, above, _, _ = parts[i]
        routes.arrive(("up", i), above, ends)

        @pl.when(ends)
        def _():
            own[...] = (own[...].astype(F32) + above[...].astype(F32)).astype(BF16)

        inward(i, ends)
        if i + ahead < count:
            inward(i + ahead, jnp.logical_not(ends))

    def back(i):
        own, _, within, full = parts[i]
        routes.arrive(("in", i), within)

        @pl.when(middle)
        def _():
            full[...] = (own[...].astype(F32) + within[...].astype(F32)).astype(BF16)

        @pl.when(edge)
        def _():
            full[...] = within[...]

        routes.start(("down", i), full, within, outer, ends, ("in", i))
        if i:
            routes.start(("pair", i - 1), full, other.at[i - 1], {"blk": pair})

    for i in range(count + 1):
        if i < count:
            forward(i)
        if i:
            back(i - 1)
            if jobs and i % 2 == 1:
                jobs.pop(0)()
            if heads and i % 2 == 0 and i > 2:
                heads.pop(0)()
    for job in jobs + heads:
        job()
    for s in range(1, chips):
        for side in range(2):
            chip, _, when = line(side, s, False)
            routes.start(("head pair", side, s), head(chip), head(chip), {"blk": pair}, when)
    copies = fetch([(result, tot_ref.at[c])], local)
    for i in range(count - 1):
        routes.arrive(("pair", i), other.at[i])
    copies += fetch([(other, tot_ref.at[1 - c])], local, 1)
    routes.arrive("head pair", gq_all.at[pair])
    for s in range(1, chips):
        for side in range(2):
            chip, _, when = line(side, s, False)
            routes.arrive(("head pair", side, s), gq_all.at[chip * 2 + 1 - c], when)
    copies += fetch([(gq_all, gqa_ref)], local, 2)
    routes.finish()
    for copy in copies:
        copy.wait()


def unfold_body(
    shards, low_ref, wave_ref, dm_ref, dc_ref, tot_ref, gq_ref, temb_ref, ada_ref, qkv_ref, out_ref,
    fc1_ref, fc2_ref, ada_s, qkv_s, out_s, fc1_s, fc2_s, sems,
):
    _, count, rows, size = tot_ref.shape
    slots = dm_ref.shape[1]
    copies = []

    def leave(source, target):
        copy = pltpu.make_async_copy(source, target, sems.at[len(copies)])
        copy.start()
        copies.append(copy)

    hidden = fc1_s.shape[1]
    part = hidden // shards // 2
    height = fc1_s.shape[0]
    blocks = hidden // 2 // size
    per = height // rows
    for core in range(2):
        for i in range(blocks * per):
            piece = tot_ref[core, i].astype(F32)
            block, at = i // per, (i % per) * rows
            for j in range(size // part):
                column = (block * (size // part) + j) * 2 * part + core * part
                fc1_s[at : at + rows, column : column + part] = piece[:, j * part : (j + 1) * part]
        rest = count - 1 - blocks * per
        for i in range(rest):
            at = (core * rest + i) * rows
            fc2_s[at : at + rows, :] = tot_ref[core, blocks * per + i].astype(F32)
        out_s[core * rows : (core + 1) * rows, :] = tot_ref[core, count - 1].astype(F32)
    leave(fc1_s, fc1_ref)
    leave(fc2_s, fc2_ref)
    leave(out_s, out_ref)
    devices, _, packed = gq_ref.shape
    narrow = packed // 3
    for p in range(3):
        for i in range(devices):
            at = p * size + i * narrow
            qkv_s[:, at : at + narrow] = gq_ref[i, :, p * narrow : (p + 1) * narrow].astype(F32)
    leave(qkv_s, qkv_ref)
    grads = dm_ref[...].reshape(shards * slots, -1).astype(BF16)
    ada_s[...] = tn(low_ref[...], grads)
    leave(ada_s, ada_ref)
    step = dc_ref.shape[2]
    for i in range(shards):
        temb_ref[:, i * step : (i + 1) * step] = lax.dot_general(
            wave_ref[...], dc_ref[i], (((0,), (0,)), ((), ())), precision=HIGH,
            preferred_element_type=F32,
        )
    for copy in copies:
        copy.wait()


def on_device(
    tokens,
    timesteps,
    segment_ids,
    head_mask,
    chan_mask,
    token_mask,
    w_temb,
    w_ada,
    w_qkv,
    w_out,
    w_fc1,
    w_fc2,
    cotangent,
):
    count, size = tokens.shape
    slots, heads = head_mask.shape[1:]
    head_size = size // heads
    shards, blocks = lax.axis_size("fsdp"), lax.axis_size("blk")
    chips = blocks // 2
    f, b = lax.axis_index("fsdp"), lax.axis_index("blk")
    c = b % 2
    width = BLOCK // blocks
    units = count // width
    own = heads // blocks
    wide = 3 * own * LANES
    hidden = w_fc1.shape[1]
    half = hidden // 2
    ids = jnp.stack([f, b, c]).astype(I32)

    fc_rows = (half // size) * w_fc1.shape[0] + w_fc2.shape[0] // 2
    (fc_own,) = run(
        "pick_half",
        functools.partial(pick_half_body, shards),
        [(SMEM, ids), (VMEM, w_fc1), (VMEM, w_fc2)],
        [(VMEM, shape((fc_rows, size)))],
    )
    fc_all = lax.all_gather(fc_own, "fsdp", axis=0, tiled=True).reshape(shards, fc_rows, size)

    items = lax.dynamic_slice_in_dim(segment_ids, b * count, count, axis=1)
    rows = w_temb.shape[0]
    entries = rows * shards
    spectrum = frequencies(timesteps[0], entries).astype(BF16).astype(F32)
    out_rows = w_out.shape[0] // 2
    ada_rows, wider = w_ada.shape
    padded = -(-units // 8) * 8
    n_copies = 8 * shards + 4 * chips + 8
    outs = run(
        "front",
        functools.partial(front_body, shards, chips, heads),
        [
            (VMEM, a)
            for a in (items, token_mask[None, :], tokens, cotangent, spectrum, w_temb)
        ]
        + [(ANY, a) for a in (w_ada, w_qkv, w_out.reshape(2, out_rows, size))],
        [
            (VMEM, shape((count, size))),
            (VMEM, shape((count, size))),
            (ANY, shape((2, slots, count), F32)),
            (VMEM, shape((8, LANES), I32)),
            (VMEM, shape((slots, LANES), F32)),
            (VMEM, shape((count, count))),
            (VMEM, shape((padded, wider), F32)),
            (VMEM, shape((shards * slots, ada_rows), F32)),
            (VMEM, shape((shards * slots, ada_rows))),
            (VMEM, shape((shards * slots, rows), F32)),
            (ANY, shape((2, count, size))),
            (ANY, shape((units, BLOCK, size))),
            (VMEM, shape((units, BLOCK, wide))),
            (VMEM, shape((size, wide))),
            (ANY, shape((shards, 2, out_rows, size))),
        ],
        [
            pltpu.VMEM((blocks, count, size), BF16),
            pltpu.VMEM((shards, slots, entries), F32),
            pltpu.VMEM((shards, rows, size), BF16),
            pltpu.VMEM((shards, slots, wider), F32),
            pltpu.VMEM((shards, slots, wider), F32),
            pltpu.VMEM((2, slots, count), F32),
            pltpu.VMEM((2, count, size), BF16),
            pltpu.VMEM((shards, w_qkv.shape[0], wide), BF16),
            pltpu.VMEM((shards, 2, out_rows, size), BF16),
            pltpu.VMEM((count, size), BF16),
            pltpu.VMEM(w_ada.shape, BF16),
            pltpu.VMEM(w_qkv.shape, BF16),
            pltpu.SemaphoreType.DMA((units + 3,)),
            pltpu.SemaphoreType.DMA((n_copies,)),
            pltpu.SemaphoreType.DMA((n_copies,)),
        ],
        flops=2 * units * BLOCK * size * wide,
        vmem=60,
        collective=0,
    )
    x_s, c_s, hots, info, mark, perm, mod, condition, lifted, waves, dms, normed, qkv, w_heads, w_out_all = outs
    w_out_all = w_out_all.reshape(size, size)

    mask = head_mask[0]
    narrow = own * head_size
    outs = run(
        "attend",
        functools.partial(attend_body, own, head_size, blocks),
        [(SMEM, ids), (SMEM, info), (SMEM, mask), (VMEM, qkv)],
        [
            (VMEM, shape((units, narrow, BLOCK))),
            (VMEM, shape((units, 8, BLOCK), F32)),
        ]
        + [(VMEM, shape((narrow, count)))] * blocks,
        [
            pltpu.VMEM((units, narrow, BLOCK), F32),
            pltpu.VMEM((units, own, -(-head_size // 16) * 16, BLOCK), BF16),
            pltpu.VMEM((blocks, narrow, count), BF16),
        ],
        flops=2 * units * units * BLOCK * BLOCK * wide // 3,
    )
    held, lse, pieces = outs[0], outs[1], outs[2:]
    om_parts = [pieces[0]] + [swap(pieces[k], "blk", k) for k in range(1, blocks)]

    attn, x1, h2, om = run(
        "project",
        functools.partial(project_body, width, blocks),
        [(SMEM, ids), (VMEM, mod), (VMEM, x_s), (VMEM, w_out_all)]
        + [(ANY, part) for part in om_parts],
        [
            (VMEM, shape((count, size), F32)),
            (VMEM, shape((count, size), F32)),
            (VMEM, shape((count, size))),
            (VMEM, shape((size, count))),
        ],
        [
            pltpu.VMEM((blocks, narrow, count), BF16),
            pltpu.SemaphoreType.DMA((blocks,)),
        ],
        flops=2 * count * size * size,
    )
    h2_other = swap(h2, "blk", 1)

    chan = chan_mask[0].reshape(slots, shards, 2, half // shards)
    chan = lax.dynamic_slice_in_dim(chan, c, 1, axis=2).reshape(slots, half)
    ff_step = 768
    n_sems = 4 + 4 * shards * (half // ff_step + 1)
    mlp, mlp_send, dh2, dh2_send, g_fc = run(
        "feed_forward",
        functools.partial(ff_body, shards, ff_step, 2),
        [(VMEM, hots), (VMEM, chan)] + [(ANY, a) for a in (h2, h2_other, dms, fc_all)],
        [
            (VMEM, shape((count, size), F32)),
            (VMEM, shape((count, size))),
            (VMEM, shape((count, size), F32)),
            (VMEM, shape((count, size))),
            (ANY, shape((shards, fc_rows, size))),
        ],
        [
            pltpu.VMEM((size, half), BF16),
            pltpu.VMEM((half, size), BF16),
            pltpu.VMEM((2 * count, size), BF16),
            pltpu.VMEM((2 * count, size), BF16),
            pltpu.VMEM((size, 2 * count), BF16),
            pltpu.VMEM((2 * count, ff_step), BF16),
            pltpu.VMEM((2 * count, ff_step), BF16),
            pltpu.VMEM((2 * count, size), F32),
            pltpu.VMEM((2 * count, size), F32),
            pltpu.VMEM((size, half), BF16),
            pltpu.VMEM((half, size), BF16),
            pltpu.SemaphoreType.DMA((n_sems,)),
        ],
        flops=6 * 2 * 2 * count * size * half,
        vmem=60,
    )
    g_fc = lax.psum_scatter(
        g_fc.reshape(shards * fc_rows, size), "fsdp", scatter_dimension=0, tiled=True
    )
    dh2_got = swap(dh2_send, "blk", 1)
    mlp_got = swap(mlp_send, "blk", 1)

    outs = run(
        "middle_back",
        functools.partial(middle_body, width, blocks),
        [(SMEM, ids), (SMEM, info), (VMEM, mod), (VMEM, x1), (VMEM, c_s), (VMEM, dh2)]
        + [(VMEM, dh2_got), (VMEM, w_out_all.reshape(blocks, narrow, size))],
        [(VMEM, shape((narrow, count)))] * blocks
        + [
            (VMEM, shape((count, size), F32)),
            (VMEM, shape((count, size))),
            (VMEM, shape((slots, 2 * size), F32)),
        ],
        flops=2 * count * size * size,
    )
    pieces, (dx1, d_attn, sums_two) = outs[:blocks], outs[blocks:]
    up_parts = [pieces[0]] + [swap(pieces[k], "blk", k) for k in range(1, blocks)]

    result, sums_gate, g_out, g_out_send = run(
        "result",
        functools.partial(result_body, width, shards),
        [(SMEM, ids), (SMEM, info)]
        + [(VMEM, a) for a in (mod, x1, c_s, mlp, mlp_got, attn, dx1, d_attn, om, perm)],
        [
            (VMEM, shape((count, size))),
            (VMEM, shape((slots, 2 * size), F32)),
            (VMEM, shape((shards, out_rows, size))),
            (VMEM, shape((shards, out_rows, size))),
        ],
        [pltpu.VMEM((count, size), BF16), pltpu.VMEM((2 * shards, out_rows, size), BF16)],
        flops=2 * count * size * size,
    )

    (d_qkv,) = run(
        "attend_back",
        functools.partial(attend_back_body, own, head_size, blocks),
        [(SMEM, ids), (SMEM, info), (SMEM, mask)]
        + [(VMEM, a) for a in (qkv, held, lse)]
        + [(VMEM, a) for a in up_parts],
        [(VMEM, shape((units, BLOCK, wide)))],
        [
            pltpu.VMEM((blocks, narrow, count), BF16),
            pltpu.VMEM((units, own, LANES, BLOCK), BF16),
            pltpu.VMEM((units, 8, BLOCK), F32),
            pltpu.VMEM((units, own, LANES, BLOCK), F32),
            pltpu.VMEM((own, BLOCK, LANES), F32),
            pltpu.VMEM((own, BLOCK, LANES), F32),
        ],
        flops=5 * units * units * BLOCK * BLOCK * wide // 3,
    )
    per = 4 if units % 4 == 0 else 1
    rows_qkv = w_qkv.shape[0]
    n_copies = 4 * chips + 2 * shards + 4
    grad_tokens, sums_one, g_qkv, g_out = run(
        "stream_back",
        functools.partial(stream_back_body, shards, chips, heads, per),
        [(ANY, normed), (ANY, g_out_send)]
        + [(VMEM, a) for a in (d_qkv, w_heads, mod, mark, x_s, dx1, perm, g_out)],
        [
            (VMEM, shape((count, size))),
            (VMEM, shape((slots, 2 * size), F32)),
            (VMEM, shape((rows_qkv, 3 * narrow))),
            (VMEM, shape((out_rows, size))),
        ],
        [
            pltpu.VMEM((chips, count, size), BF16),
            pltpu.VMEM((chips, count, size), BF16),
            pltpu.VMEM((chips, count, size), BF16),
            pltpu.VMEM((chips + 1, count, size), BF16),
            pltpu.VMEM((2, per, BLOCK, size), BF16),
            pltpu.VMEM((size, wide), F32),
            pltpu.VMEM((shards, rows_qkv, 3 * narrow), BF16),
            pltpu.VMEM((shards, rows_qkv, 3 * narrow), BF16),
            pltpu.VMEM((shards, out_rows, size), BF16),
            pltpu.VMEM((shards, out_rows, size), BF16),
            pltpu.VMEM((shards, out_rows, size), BF16),
            pltpu.VMEM((count, size), F32),
            pltpu.VMEM((count, size), BF16),
            pltpu.VMEM((padded, 2 * size), F32),
            pltpu.SemaphoreType.DMA((2,)),
            pltpu.SemaphoreType.DMA((n_copies,)),
            pltpu.SemaphoreType.DMA((n_copies,)),
        ],
        flops=4 * units * BLOCK * size * wide,
        vmem=60,
        collective=1,
    )

    pieces = fc_rows // out_rows
    n_copies = 5 * pieces + 16 + 4 * chips + 2 * shards
    totals, g_qkv, d_mod, d_cond = run(
        "finish",
        functools.partial(finish_body, shards, chips),
        [(ANY, g_fc.reshape(pieces, out_rows, size)), (ANY, w_ada)]
        + [(VMEM, a) for a in (g_out, g_qkv, sums_one, sums_two, sums_gate, condition)],
        [
            (ANY, shape((2, pieces + 1, out_rows, size))),
            (ANY, shape((blocks, rows_qkv, 3 * narrow))),
            (VMEM, shape((shards, slots, wider), F32)),
            (VMEM, shape((shards, shards * slots, ada_rows), F32)),
        ],
        [pltpu.VMEM((pieces + 1, out_rows, size), BF16)] * 5
        + [
            pltpu.VMEM((blocks, rows_qkv, 3 * narrow), BF16),
            pltpu.VMEM((slots, wider), F32),
            pltpu.VMEM((slots, wider), F32),
            pltpu.VMEM((4, 2 * slots, wider // 2), BF16),
            pltpu.VMEM((shards, slots, wider), F32),
            pltpu.VMEM((shards, shards * slots, ada_rows), F32),
            pltpu.VMEM(w_ada.shape, BF16),
            pltpu.SemaphoreType.DMA((3,)),
            pltpu.SemaphoreType.DMA((n_copies,)),
            pltpu.SemaphoreType.DMA((n_copies,)),
        ],
        vmem=60,
        collective=2,
    )
    grad_temb, grad_ada, grad_qkv, grad_out, grad_fc1, grad_fc2 = run(
        "unfold",
        functools.partial(unfold_body, shards),
        [(VMEM, a) for a in (lifted, waves, d_mod, d_cond, totals, g_qkv)],
        [
            (VMEM, shape(w_temb.shape, F32)),
            (ANY, shape(w_ada.shape, F32)),
            (ANY, shape(w_qkv.shape, F32)),
            (ANY, shape(w_out.shape, F32)),
            (ANY, shape(w_fc1.shape, F32)),
            (ANY, shape(w_fc2.shape, F32)),
        ],
        [
            pltpu.VMEM(a.shape, F32) for a in (w_ada, w_qkv, w_out, w_fc1, w_fc2)
        ]
        + [pltpu.SemaphoreType.DMA((5,))],
        vmem=60,
    )
    return (
        result,
        grad_tokens,
        grad_temb,
        grad_ada,
        grad_qkv,
        grad_out,
        grad_fc1,
        grad_fc2,
    )


def solution(mesh):
    placed = (
        P(("fsdp", "blk"), None),
        P("fsdp", None),
        P("fsdp", None),
        P("fsdp", None, None),
        P("fsdp", None, None),
        P(("fsdp", "blk")),
        P("fsdp", None),
        P("fsdp", None),
        P("fsdp", None),
        P("fsdp", None),
        P("fsdp", None),
        P("fsdp", None),
        P(("fsdp", "blk"), None),
    )
    return jax.shard_map(
        on_device,
        mesh=mesh,
        in_specs=placed,
        out_specs=(
            P(("fsdp", "blk"), None),
            P(("fsdp", "blk"), None),
            P("fsdp", None),
            P("fsdp", None),
            P("fsdp", None),
            P("fsdp", None),
            P("fsdp", None),
            P("fsdp", None),
        ),
        check_vma=False,
    )
```

```python
import functools
import math

import jax
import jax.numpy as jnp
from jax import lax
from jax.experimental import pallas as pl
from jax.experimental.pallas import tpu as pltpu
from jax.sharding import PartitionSpec as P

HIGH = lax.Precision.HIGHEST
BF16 = jnp.bfloat16
F32 = jnp.float32
I32 = jnp.int32
LANES = 128
BLOCK = 256
NEG = -1e30
LOG2E = 1.4426950408889634

VMEM = pl.BlockSpec(memory_space=pltpu.VMEM)
SMEM = pl.BlockSpec(memory_space=pltpu.SMEM)
ANY = pl.BlockSpec(memory_space=pl.ANY)


def shape(dims, kind=BF16):
    return jax.ShapeDtypeStruct(tuple(dims), kind)


def run(name, body, ins, outs, scratch=(), flops=0, vmem=48, collective=None, **more):
    moved = sum(a.size * a.dtype.itemsize for _, a in ins)
    moved += sum(math.prod(o.shape) * jnp.dtype(o.dtype).itemsize for _, o in outs)
    return pl.pallas_call(
        body,
        out_shape=[o for _, o in outs],
        in_specs=[s for s, _ in ins],
        out_specs=[s for s, _ in outs],
        scratch_shapes=list(scratch),
        compiler_params=pltpu.CompilerParams(
            vmem_limit_bytes=vmem << 20,
            collective_id=collective,
            has_side_effects=collective is not None,
        ),
        cost_estimate=pl.CostEstimate(flops=flops, bytes_accessed=moved, transcendentals=0),
        name=name,
        **more,
    )(*[a for _, a in ins])


def swap(array, axis, by):
    size = lax.axis_size(axis)
    return lax.ppermute(array, axis, [(i, i ^ by) for i in range(size)])


def frequencies(steps, entries):
    half = entries // 2
    ladder = jnp.exp(-math.log(10000.0) * lax.iota(jnp.int32, half) / half)
    angles = steps.astype(F32)[:, None] * ladder[None, :]
    return jnp.concatenate([jnp.cos(angles), jnp.sin(angles)], axis=1)


def nn(left, right):
    return lax.dot_general(left, right, (((1,), (0,)), ((), ())), preferred_element_type=F32)


def nt(left, right):
    return lax.dot_general(left, right, (((1,), (1,)), ((), ())), preferred_element_type=F32)


def tn(left, right):
    return lax.dot_general(left, right, (((0,), (0,)), ((), ())), preferred_element_type=F32)


def each(count, step, group=1):
    if count % group:
        group = 1

    def one(index, carry):
        for i in range(group):
            step(index * group + i)
        return carry

    lax.fori_loop(0, count // group, one, 0)


def normal(values):
    center = values - jnp.mean(values, axis=-1, keepdims=True)
    scale = lax.rsqrt(jnp.mean(center * center, axis=-1, keepdims=True) + 1e-06)
    return center * scale, scale


def normal_back(grad, normed, scale):
    along = jnp.mean(grad * normed, axis=-1, keepdims=True)
    return scale * (grad - jnp.mean(grad, axis=-1, keepdims=True) - normed * along)


def flip(index, by):
    bit = 1
    while bit <= by:
        if by & bit:
            index = index + bit * (1 - 2 * ((index // bit) % 2))
        bit *= 2
    return index


def fetch(pairs, sems, first=0):
    copies = []
    for index, (source, target) in enumerate(pairs, first):
        copy = pltpu.make_async_copy(source, target, sems.at[index])
        copy.start()
        copies.append(copy)
    return copies


class Routes:
    def __init__(self, sent, got):
        self.sent, self.got, self.known, self.started = sent, got, {}, []

    def slot(self, name):
        return self.known.setdefault(name, len(self.known))

    def copy(self, name, source, target, to, landed=None):
        return pltpu.make_async_remote_copy(
            src_ref=source,
            dst_ref=target,
            send_sem=self.sent.at[self.slot(name)],
            recv_sem=self.got.at[self.slot(landed or name)],
            device_id=to,
            device_id_type=pl.DeviceIdType.MESH,
        )

    def start(self, name, source, target, to, when=None, landed=None):
        def make():
            return self.copy(name, source, target, to, landed)

        self.started.append((make, when))
        if when is None:
            make().start()
        else:
            pl.when(when)(lambda: make().start())

    def arrive(self, name, target, when=None):
        def wait():
            b = lax.axis_index("blk")
            self.copy(name, target, target, {"blk": b + 1 - 2 * (b % 2)}).wait_recv()

        if when is None:
            wait()
        else:
            pl.when(when)(wait)

    def finish(self):
        for make, when in self.started:
            if when is None:
                make().wait_send()
            else:
                pl.when(when)(lambda make=make: make().wait_send())


def greet(shards, chips):
    f, b = lax.axis_index("fsdp"), lax.axis_index("blk")
    z, c = b // 2, b % 2
    barrier = pltpu.get_barrier_semaphore()

    def signal(to):
        pl.semaphore_signal(barrier, inc=1, device_id=to, device_id_type=pl.DeviceIdType.MESH)

    for k in range(1, shards):
        signal({"fsdp": flip(f, k)})
    signal({"blk": b + 1 - 2 * c})
    pl.when(z > 0)(lambda: signal({"blk": b - 2}))
    pl.when(z < chips - 1)(lambda: signal({"blk": b + 2}))
    ends = (z == 0).astype(I32) + (z == chips - 1).astype(I32)
    pl.semaphore_wait(barrier, shards + 2 - ends)


def greet_all(shards, blocks):
    f, b = lax.axis_index("fsdp"), lax.axis_index("blk")
    barrier = pltpu.get_barrier_semaphore()
    peers = [{"fsdp": flip(f, k)} for k in range(1, shards)]
    peers += [{"blk": flip(b, k)} for k in range(1, blocks)]
    for to in peers:
        pl.semaphore_signal(barrier, inc=1, device_id=to, device_id_type=pl.DeviceIdType.MESH)
    pl.semaphore_wait(barrier, len(peers))


def front_body(
    shards, chips, heads, items_ref, keep_ref, x_ref, c_ref, spec_ref, temb_ref, ada_ref, qkvw_ref,
    outw_ref, fc1w_ref, fc2w_ref, xs_ref, cs_ref, hot_ref, info_ref, mark_ref, perm_ref, mod_ref, cond_ref, low_ref, wave_ref, dm_ref, h_ref,
    qkv_ref, wh_ref, wo_ref, fc2_ref, *refs,
):
    fc_refs, refs = refs[:-18], refs[-18:]
    x_all, spec_all, temb_all, part_own, part_got, hots, dms, wh_all, wo_all = refs[:9]
    h_all, ada_s, qkvw_s, fc1_s, fc_all, local, loads, sent, got = refs[9:]
    f, b = lax.axis_index("fsdp"), lax.axis_index("blk")
    z, c = b // 2, b % 2
    blocks = 2 * chips
    pair = b + 1 - 2 * c
    width = BLOCK // blocks
    count, size = x_ref.shape
    units = count // width
    own = heads // blocks
    head_size = size // heads
    slots = spec_ref.shape[0]
    routes = Routes(sent, got)
    down = fc2_ref.shape[0]
    inside = fetch(
        [
            (ada_ref, ada_s),
            (qkvw_ref, qkvw_s),
            (outw_ref, wo_all.at[f]),
            (fc1w_ref, fc1_s),
            (fc2w_ref.at[pl.ds(pl.multiple_of(c * down, 16), down)], fc2_ref),
        ],
        loads,
    )
    greet(shards, chips)

    spec_all[f] = spec_ref[...]
    temb_all[f] = temb_ref[...]
    for k in range(1, shards):
        to = {"fsdp": flip(f, k)}
        routes.start(("spec", k), spec_ref, spec_all.at[f], to)
        routes.start(("temb", k), temb_ref, temb_all.at[f], to)

    items = items_ref[...]
    slot = lax.broadcasted_iota(I32, (slots, count), 0)
    hot = (items == slot).astype(F32)
    start = jnp.sum((items < slot).astype(F32), axis=1, keepdims=True)
    end = start + jnp.sum(hot, axis=1, keepdims=True)
    row = lax.broadcasted_iota(I32, (count, count), 0)
    col = lax.broadcasted_iota(I32, (count, count), 1)
    rank = nn(hot.astype(BF16), (row <= col).astype(BF16))
    place = jnp.sum(hot * (start + rank), axis=0, keepdims=True) - 1.0
    perm = (row.astype(F32) == place).astype(BF16)
    perm_ref[...] = perm
    x_s = nn(perm, x_ref[...]).astype(BF16)
    xs_ref[...] = x_s
    x_all[b] = x_s

    def line(side, s, send):
        away = s - 1 if send else s
        chip = z - away if side == 0 else z + away
        ahead = z + 1 < chips if side == 0 else z > 0
        known = z >= away if side == 0 else z + away < chips
        when = known & ahead if send else known
        return chip * 2 + c, {"blk": b + 2 if side == 0 else b - 2}, when

    def send_on(s):
        for side in range(2):
            device, to, when = line(side, s, True)
            routes.start(("line", side, s), x_all.at[device], x_all.at[device], to, when)

    send_on(1)
    routes.start("pair", x_all.at[b], x_all.at[b], {"blk": pair})
    cs_ref[...] = nn(perm, c_ref[...]).astype(BF16)
    keep = jnp.broadcast_to(keep_ref[...].astype(F32), (slots, count)).astype(BF16)
    kept = nt(keep, perm)
    at = lax.broadcasted_iota(I32, (slots, count), 1).astype(F32)
    hots[0] = kept * ((at >= start) & (at < end)).astype(F32)
    first = (lax.broadcasted_iota(I32, (slots, LANES), 1) * width).astype(F32)
    mine = ((first >= start) & (first < end)).astype(F32)
    mark_ref[...] = mine
    which = lax.broadcasted_iota(I32, (slots, LANES), 0).astype(F32)
    info_ref[0:1, :] = jnp.sum(mine * which, axis=0, keepdims=True).astype(I32)
    info_ref[1:2, :] = (jnp.sum(mine * start, axis=0, keepdims=True) / width).astype(I32)
    info_ref[2:3, :] = (jnp.sum(mine * end, axis=0, keepdims=True) / width).astype(I32)
    info_ref[3:8, :] = jnp.zeros((5, LANES), I32)

    for k in range(1, shards):
        other = flip(f, k)
        routes.arrive(("spec", k), spec_all.at[other])
        routes.arrive(("temb", k), temb_all.at[other])
    spectra = spec_all[...].reshape(shards * slots, -1).astype(BF16)
    condition = nn(spectra, temb_all[...].reshape(-1, size))
    rows = ada_ref.shape[0]
    for shard in range(shards):

        @pl.when(f == shard)
        def _():
            cond_ref[...] = condition[:, shard * rows : (shard + 1) * rows]
            freqs = temb_ref.shape[0]
            wave_ref[...] = spectra[:, shard * freqs : (shard + 1) * freqs].astype(F32)

    values = cond_ref[...]
    lifted = (values / (1.0 + jnp.exp(-values))).astype(BF16)
    low_ref[...] = lifted
    inside[0].wait()
    part_own[...] = nn(lifted, ada_s[...]).reshape(part_own.shape)
    for k in range(1, shards):
        other = flip(f, k)
        routes.start(("part", k), part_own.at[other], part_got.at[f], {"fsdp": other})

    rows = qkvw_ref.shape[0]
    inside[1].wait()
    narrow = own * head_size
    row = lax.broadcasted_iota(I32, (size, 2 * LANES), 0)
    col = lax.broadcasted_iota(I32, (size, 2 * LANES), 1)
    pick = ((row == b * narrow + col) & (col < narrow)).astype(F32).astype(BF16)
    wh_all[f] = jnp.concatenate(
        [
            nn(qkvw_s[:, part * size : (part + 1) * size], pick)[:, 0:narrow]
            for part in range(3)
        ],
        axis=1,
    ).astype(BF16)
    if shards == 4:
        for k in (1, 2):
            routes.start(("head", k), wh_all.at[f], wh_all.at[f], {"fsdp": flip(f, k)})
    else:
        for k in range(1, shards):
            routes.start(("head", k), wh_all.at[f], wh_all.at[f], {"fsdp": flip(f, k)})

    def take(s):
        for side in range(2):
            device, _, when = line(side, s, False)
            routes.arrive(("line", side, s), x_all.at[device], when)
            if s + 1 < chips:
                device, to, onward = line(side, s + 1, True)
                routes.start(
                    ("line", side, s + 1), x_all.at[device], x_all.at[device], to, onward
                )
            device, _, when = line(side, s, False)
            routes.start(
                ("pair", side, s), x_all.at[device], x_all.at[device], {"blk": pair}, when
            )

    take(1)
    if shards == 4:
        half = rows // 2
        for k, low in ((1, 0), (2, half)):
            routes.arrive(("head", k), wh_all.at[flip(f, k)])
            part = wh_all.at[flip(f, k), low : low + half]
            routes.start(("head", 3, k), part, part, {"fsdp": flip(f, 3 - k)})

    for k in range(1, shards):
        routes.start(("out", k), outw_ref.at[c], wo_all.at[f, c], {"fsdp": flip(f, k)})

    blocks_fc = fc_all.shape[1]
    part = fc1_s.shape[1] // shards // 2
    inside[3].wait()
    for core in range(2):

        @pl.when(c == core)
        def _():
            picked = jnp.concatenate(
                [
                    fc1_s[:, (2 * shard + core) * part : (2 * shard + core + 1) * part]
                    for shard in range(shards)
                ],
                axis=1,
            )
            for block_at in range(blocks_fc):
                fc_all[0, block_at] = picked[:, block_at * size : (block_at + 1) * size]

    for k in range(1, len(fc_refs)):
        routes.start(("fc", k), fc_all.at[0], fc_all.at[k], {"fsdp": flip(f, k)})

    total = part_own[f]
    for k in range(1, shards):
        other = flip(f, k)
        routes.arrive(("part", k), part_got.at[other])
        total = total + part_got[other]
    mod_ref[...] = lax.dot_general(
        mine[:, : mod_ref.shape[0]], total, (((0,), (0,)), ((), ())), precision=HIGH,
        preferred_element_type=F32,
    )

    def early(u):
        rows = pl.ds(pl.multiple_of(u * width, width), width)
        gate = mod_ref[pl.ds(u, 1), 5 * size : 6 * size]
        dms[0, rows, :] = (cs_ref[rows, :].astype(F32) * gate).astype(BF16)

    each(units, early)
    routes.start("dm", dms.at[0], dms.at[1], {"blk": pair})
    routes.start("hot", hots.at[0], hots.at[1], {"blk": pair})

    if shards == 4:
        half = rows // 2
        routes.arrive(("head", 3, 1), wh_all.at[flip(f, 3), 0:half])
        routes.arrive(("head", 3, 2), wh_all.at[flip(f, 3), half:rows])
    else:
        for k in range(1, shards):
            routes.arrive(("head", k), wh_all.at[flip(f, k)])
    packed = wh_all[...].reshape(size, 3 * narrow)
    wh_ref[...] = jnp.zeros_like(wh_ref)
    for i in range(3 * own):
        wh_ref[:, i * LANES : i * LANES + head_size] = packed[
            :, i * head_size : (i + 1) * head_size
        ]

    def block(device):
        at = pl.ds(pl.multiple_of(device * width, width), width)

        def one(u):
            shift = mod_ref[pl.ds(u, 1), 0:size]
            scale = mod_ref[pl.ds(u, 1), size : 2 * size]
            part = x_all[device, pl.ds(pl.multiple_of(u * width, width), width), :]
            normed, _ = normal(part.astype(F32))
            low = (normed * (1.0 + scale) + shift).astype(BF16)
            h_all[pl.ds(pl.multiple_of(u * width, width), width), :] = low

        each(units, one, 3)
        copies = fetch(
            [
                (h_all.at[u * width : (u + 1) * width], h_ref.at[u, at])
                for u in range(units)
            ],
            local,
        )
        found = nn(h_all[...], wh_ref[...]).astype(BF16)
        qkv_ref[:, at, :] = found.reshape(units, width, found.shape[1])
        for copy in copies:
            copy.wait()

    routes.arrive("pair", x_all.at[pair])
    each(2, lambda core: block(z * 2 + core))

    def work(s):
        for side in range(2):
            device, _, when = line(side, s, False)
            routes.arrive(("pair", side, s), x_all.at[device + 1 - 2 * c], when)

        def pick(q):
            chip = z - s + 2 * s * (q // 2)

            @pl.when((chip >= 0) & (chip < chips))
            def _():
                block(chip * 2 + q % 2)

        each(4, pick)

    for s in range(2, chips):
        take(s)
        if s == 2:
            for k in range(1, shards):
                other = flip(f, k)
                routes.arrive(("out", k), wo_all.at[other, c])
                routes.start(
                    ("pair out", k), wo_all.at[other, c], wo_all.at[other, c], {"blk": pair}
                )
        work(s - 1)
    work(chips - 1)
    inside[2].wait()
    for k in range(1, len(fc_refs)):
        routes.arrive(("fc", k), fc_all.at[k])
    inside[4].wait()
    for k in range(1, shards):
        routes.arrive(("pair out", k), wo_all.at[flip(f, k), 1 - c])
    routes.arrive("dm", dms.at[1])
    routes.arrive("hot", hots.at[1])
    routes.finish()
    copies = fetch(
        [(wo_all, wo_ref), (dms, dm_ref), (hots, hot_ref)]
        + [(fc_all.at[k], ref) for k, ref in enumerate(fc_refs)],
        local,
    )
    for copy in copies:
        copy.wait()


def exchange_lanes(tiles, width):
    tiles = list(tiles)
    count = len(tiles)
    group = lax.broadcasted_iota(I32, tiles[0].shape, 1) // width
    half = count // 2
    while half:
        low = (group // half) % 2 == 0
        fresh = list(tiles)
        for i in range(count):
            if (i // half) % 2 == 0:
                a, d = tiles[i], tiles[i + half]
                fresh[i] = jnp.where(low, a, pltpu.roll(d, half * width, 1))
                fresh[i + half] = jnp.where(low, pltpu.roll(a, LANES - half * width, 1), d)
        tiles = fresh
        half //= 2
    return tiles


def in_groups(first, last, sizes, step, carry):
    for size in sizes:
        count = (last - first) // size

        def one(index, carry, first=first, size=size):
            return step(first + index * size, size, carry)

        carry = lax.fori_loop(0, count, one, carry)
        first = first + count * size
    return carry


def attend_body(
    own, size, blocks, ids_ref, info_ref, mask_ref, qkv_ref, o_ref, lse_ref, out_ref, held, turned, placed
):
    units = qkv_ref.shape[0]
    width = BLOCK // blocks
    b = ids_ref[1]
    scale = LOG2E / math.sqrt(size)
    tall = turned.shape[2]

    def turn(j):
        for h in range(own):
            at = (2 * own + h) * LANES
            values = qkv_ref[j, :, at : at + LANES].astype(F32).T
            turned[j, h] = values[0:tall].astype(BF16)

    each(units, turn, 2)

    def one_unit(u):
        queries = [qkv_ref[u, :, h * LANES : (h + 1) * LANES] for h in range(own)]

        def some_blocks(j, count, carry):
            fresh = []
            for h in range(own):
                top, total, acc = carry[h]
                keys = qkv_ref[pl.ds(j, count), :, (own + h) * LANES : (own + h + 1) * LANES]
                scores = nt(keys.reshape(count * BLOCK, LANES), queries[h]) * scale
                new_top = jnp.maximum(top, jnp.max(scores, axis=0, keepdims=True))
                probs = jnp.exp2(scores - new_top)
                decay = jnp.exp2(top - new_top)
                total = total * decay + jnp.sum(probs, axis=0, keepdims=True)
                acc = acc * decay
                low = probs.astype(BF16)
                for i in range(count):
                    acc = acc + nn(turned[j + i, h], low[i * BLOCK : (i + 1) * BLOCK])
                fresh.append((new_top, total, acc))
            return tuple(fresh)

        start = tuple(
            (
                jnp.full((1, BLOCK), NEG, F32),
                jnp.zeros((1, BLOCK), F32),
                jnp.zeros((tall, BLOCK), F32),
            )
            for _ in range(own)
        )
        done = in_groups(info_ref[1, u], info_ref[2, u], (4, 2, 1), some_blocks, start)
        slot = info_ref[0, u]
        rows = []
        for h in range(own):
            top, total, acc = done[h]
            keep = mask_ref[slot, b * own + h].astype(F32)
            rows.append((acc * (keep / total))[0:size])
            lse_ref[u, h : h + 1, :] = top + jnp.log2(total)
        held[u] = jnp.concatenate(rows, axis=0) if own > 1 else rows[0]
        o_ref[u] = held[u].astype(BF16)

    each(units, one_unit)
    groups = LANES // width
    for g in range(units // groups):
        for e in range(blocks // groups):
            tiles = [
                held[groups * g + i, :, e * LANES : (e + 1) * LANES] for i in range(groups)
            ]
            for j, tile in enumerate(exchange_lanes(tiles, width)):
                placed[groups * e + j, :, g * LANES : (g + 1) * LANES] = tile.astype(BF16)
    for k in range(blocks):
        out_ref[k] = placed[lax.bitwise_xor(b, k)]


def attend_back_body(
    own, size, blocks, ids_ref, info_ref, mask_ref, qkv_ref, o_ref, lse_ref, given, d_ref, up, delta, d_q,
    d_k, d_v,
):
    units = qkv_ref.shape[0]
    width = BLOCK // blocks
    b = ids_ref[1]
    factor = 1.0 / math.sqrt(size)
    scale = LOG2E * factor
    up[...] = jnp.zeros_like(up)
    groups = LANES // width
    for g in range(units // groups):
        for e in range(blocks // groups):
            tiles = [
                given[groups * e + j, :, g * LANES : (g + 1) * LANES].astype(F32)
                for j in range(groups)
            ]
            for i, tile in enumerate(exchange_lanes(tiles, width)):
                unit = groups * g + i
                slot = info_ref[0, unit]
                for h in range(own):
                    keep = mask_ref[slot, b * own + h].astype(F32)
                    kept = tile[h * size : (h + 1) * size] * keep
                    up[unit, h, 0:size, e * LANES : (e + 1) * LANES] = kept.astype(BF16)
                    mine = o_ref[unit, h * size : (h + 1) * size, e * LANES : (e + 1) * LANES]
                    delta[unit, h : h + 1, e * LANES : (e + 1) * LANES] = jnp.sum(
                        kept * mine.astype(F32), axis=0, keepdims=True
                    )
    d_q[...] = jnp.zeros_like(d_q)

    def one_unit(j):
        d_k[...] = jnp.zeros_like(d_k)
        d_v[...] = jnp.zeros_like(d_v)
        keys = [qkv_ref[j, :, (own + h) * LANES : (own + h + 1) * LANES] for h in range(own)]
        turned = [keys[h].astype(F32).T.astype(BF16) for h in range(own)]

        def some_blocks(i, count, carry):
            for h in range(own):
                at = (2 * own + h) * LANES
                values = qkv_ref[j, :, at : at + LANES]
                sum_k = sum_v = 0.0
                for n in range(count):
                    queries = qkv_ref[i + n, :, h * LANES : (h + 1) * LANES]
                    scores = nt(keys[h], queries) * scale
                    probs = jnp.exp2(scores - lse_ref[i + n, h : h + 1, :])
                    d_probs = nn(values, up[i + n, h])
                    d_scores = (probs * (d_probs - delta[i + n, h : h + 1, :])).astype(BF16)
                    sum_k = sum_k + nn(d_scores, queries)
                    sum_v = sum_v + nt(probs.astype(BF16), up[i + n, h])
                    d_q[i + n, h] += nn(turned[h], d_scores)
                d_k[h] += sum_k
                d_v[h] += sum_v
            return carry

        in_groups(info_ref[1, j], info_ref[2, j], (4, 2, 1), some_blocks, 0)
        for h in range(own):
            at = (own + h) * LANES
            d_ref[j, :, at : at + LANES] = (d_k[h] * factor).astype(BF16)
            at = (2 * own + h) * LANES
            d_ref[j, :, at : at + LANES] = d_v[h].astype(BF16)

    each(units, one_unit)

    def turn(i):
        for h in range(own):
            d_ref[i, :, h * LANES : (h + 1) * LANES] = (d_q[i, h].T * factor).astype(BF16)

    each(units, turn)


def project_body(shards, blocks, moves, mod_ref, x_ref, w_ref, p_ref, *refs):
    sources, refs = refs[: len(moves)], refs[len(moves) :]
    attn_ref, x1_ref, h_ref, om_ref = refs[:4]
    landed, (om_all, h_all, local, sent, got) = refs[4 : 4 + len(moves)], refs[4 + len(moves) :]
    f, b = lax.axis_index("fsdp"), lax.axis_index("blk")
    width = BLOCK // blocks
    size = x_ref.shape[1]
    routes = Routes(sent, got)
    greet_all(shards, blocks)
    for k in range(blocks - 1, 0, -1):
        routes.start(("om", k), p_ref.at[k], om_all.at[b], {"blk": flip(b, k)})
    for i, (first, high, k) in enumerate(moves):
        routes.start(("move", i), sources[i].at[first:high], landed[i], {"fsdp": flip(f, k)})
    om_all[b] = p_ref[0]
    for k in range(1, blocks):
        routes.arrive(("om", k), om_all.at[flip(b, k)])
    om = om_all[...].reshape(size, x_ref.shape[0])
    om_ref[...] = om
    weight = w_ref[...]
    attn_ref[...] = tn(om, weight)

    def one(u):
        rows = pl.ds(pl.multiple_of(u * width, width), width)
        gate, shift, scale = [mod_ref[pl.ds(u, 1), i * size : (i + 1) * size] for i in (2, 3, 4)]
        middle = x_ref[rows, :].astype(F32) + gate * attn_ref[rows, :]
        x1_ref[rows, :] = middle
        normed, _ = normal(middle)
        h_all[0, rows, :] = (normed * (1.0 + scale) + shift).astype(BF16)

    each(x_ref.shape[0] // width, one, 3)
    routes.start("h", h_all.at[0], h_all.at[1], {"blk": flip(b, 1)})
    routes.arrive("h", h_all.at[1])
    copy = pltpu.make_async_copy(h_all, h_ref, local.at[0])
    copy.start()
    for i in range(len(moves)):
        routes.arrive(("move", i), landed[i])
    routes.finish()
    copy.wait()


def ff_body(shards, step, sides, plan1, plan2, ids_ref, hot_ref, chan_ref, h_ref, dm_ref, *refs):
    w1_refs, refs = refs[: len(plan1)], refs[len(plan1) :]
    w2_refs, refs = refs[: len(plan2)], refs[len(plan2) :]
    f = ids_ref[0]
    mlp_m, mlp_o, dh_m, dh_o, g_ref, w1, w2, h, dm, turned, hid_s, du_s, mlp, dh, g1, g2, sems = refs
    total = h.shape[0]
    count = total // 2
    f_size, size = w2.shape
    blocks = f_size // size
    row1, row2 = size // shards, f_size // shards

    def up_part(ref, shard, low, high):
        block = low // size
        return ref.at[
            shard, block * row1 : (block + 1) * row1, low - block * size : high - block * size
        ]

    def down_part(ref, shard, low, high):
        at = blocks * row1 - shard * row2
        return ref.at[shard, at + low : at + high]

    def chunk(index):
        low, high = index * step, (index + 1) * step
        cols = [
            (max(low, i * size), min(high, (i + 1) * size))
            for i in range(blocks)
            if max(low, i * size) < min(high, (i + 1) * size)
        ]
        rows = [
            (i, max(low, i * row2), min(high, (i + 1) * row2))
            for i in range(shards)
            if max(low, i * row2) < min(high, (i + 1) * row2)
        ]
        return cols, rows

    used = [0]

    def begin(pairs):
        copies = fetch(pairs, sems, used[0])
        used[0] += len(copies)
        return copies

    waits = [
        begin(
            [
                (h_ref.at[0], h.at[0:count]),
                (h_ref.at[1], h.at[count:total]),
                (dm_ref.at[0], dm.at[0:count]),
                (dm_ref.at[1], dm.at[count:total]),
            ]
        )
    ]
    chunks = f_size // step
    pairs = [[] for _ in range(chunks)]
    for ref, (k, first) in zip(w1_refs, plan1):
        at = pl.ds(pl.multiple_of(lax.bitwise_xor(f, k) * row1, 16), row1)
        for i in range(ref.shape[0]):
            low = (first + i) * size
            pairs[low // step].append((ref.at[i], w1.at[at, low : low + size]))
    for ref, (k, first) in zip(w2_refs, plan2):
        at = pl.multiple_of(lax.bitwise_xor(f, k) * row2 + first, 16)
        pairs[0].append((ref, w2.at[pl.ds(at, ref.shape[0])]))
    waits += [begin(some) for some in pairs]
    for copy in waits[0]:
        copy.wait()
    for at in range(0, total, LANES):
        turned[:, at : at + LANES] = h[at : at + LANES, :].astype(F32).T.astype(BF16)
    hots = jnp.concatenate([hot_ref[side] for side in range(2)], axis=1).astype(BF16)
    left = []
    for index in range(chunks):
        for copy in waits[index + 1]:
            copy.wait()
        cols = slice(index * step, (index + 1) * step)
        up = w1[:, cols]
        down = w2[cols, :]
        chan = chan_ref[:, cols].astype(F32).astype(BF16)
        for side in range(sides):
            rows = slice(side * total // sides, (side + 1) * total // sides)
            keep = tn(hots[:, rows], chan)
            pre = nn(h[rows, :], up)
            inner = pre * pre
            bent = jnp.tanh(0.7978845608028654 * (pre + 0.044715 * inner * pre))
            half = 0.5 * (1.0 + bent)
            hid = (pre * half * keep).astype(BF16)
            slope = half + (0.5 * 0.7978845608028654) * pre * (1.0 - bent * bent) * (
                1.0 + (3.0 * 0.044715) * inner
            )
            back = nt(dm[rows, :], down)
            du = (slope * back * keep).astype(BF16)
            hid_s[rows, :] = hid
            du_s[rows, :] = du
            if index:
                mlp[rows, :] += nn(hid, down)
                dh[rows, :] += nt(du, up)
            else:
                mlp[rows, :] = nn(hid, down)
                dh[rows, :] = nt(du, up)
        g1[:, cols] = nn(turned[...], du_s[...]).astype(BF16)
        g2[cols, :] = tn(hid_s[...], dm[...]).astype(BF16)
        parts, rows = chunk(index)
        pairs = [
            (g1.at[shard * row1 : (shard + 1) * row1, lo:hi], up_part(g_ref, shard, lo, hi))
            for shard in range(shards)
            for lo, hi in parts
        ]
        pairs += [(g2.at[lo:hi], down_part(g_ref, shard, lo, hi)) for shard, lo, hi in rows]
        left += begin(pairs)
    mlp_m[...] = mlp[0:count, :]
    mlp_o[...] = mlp[count:total, :].astype(BF16)
    dh_m[...] = dh[0:count, :]
    dh_o[...] = dh[count:total, :].astype(BF16)
    for copy in left:
        copy.wait()


def middle_body(
    shards, blocks, mod_ref, mark_ref, x1_ref, c_ref, dh_ref, dho_ref, mlp_ref, mlpo_ref, attn_ref, om_ref,
    w_ref, perm_ref, up_ref, dx_ref, two_ref, gate_ref, r_ref, mine_ref, other_ref, dh_in, mlp_in, da, leave,
    up_all, held, grad, by_unit, sent, got,
):
    f, b = lax.axis_index("fsdp"), lax.axis_index("blk")
    c = b % 2
    width = BLOCK // blocks
    count, size = x1_ref.shape
    units = count // width
    routes = Routes(sent, got)
    greet_all(shards, blocks)
    routes.start("dh", dho_ref, dh_in, {"blk": flip(b, 1)})
    routes.start("mlp", mlpo_ref, mlp_in, {"blk": flip(b, 1)})
    by_unit[...] = jnp.zeros_like(by_unit)
    routes.arrive("dh", dh_in)

    def one(u):
        rows = pl.ds(pl.multiple_of(u * width, width), width)
        gate = mod_ref[pl.ds(u, 1), 2 * size : 3 * size]
        scale = mod_ref[pl.ds(u, 1), 4 * size : 5 * size]
        normed, spread = normal(x1_ref[rows, :])
        grad = dh_ref[rows, :] + dh_in[rows, :].astype(F32)
        by_unit[pl.ds(u, 1), 0:size] = jnp.sum(grad, axis=0, keepdims=True)
        by_unit[pl.ds(u, 1), size : 2 * size] = jnp.sum(grad * normed, axis=0, keepdims=True)
        dx = c_ref[rows, :].astype(F32) + normal_back(grad * (1.0 + scale), normed, spread)
        dx_ref[rows, :] = dx
        da[rows, :] = (dx * gate).astype(BF16)

    each(units, one, 3)
    for k in range(blocks - 1, -1, -1):
        piece = nt(w_ref[flip(b, k)], da[...]).astype(BF16)
        if k:
            leave[k] = piece
            routes.start(("up", k), leave.at[k], up_all.at[b], {"blk": flip(b, k)})
        else:
            up_all[b] = piece

    def over_slots(target):
        target[...] = lax.dot_general(
            mark_ref[:, : by_unit.shape[0]], by_unit[...], (((1,), (0,)), ((), ())), precision=HIGH,
            preferred_element_type=F32,
        )

    over_slots(two_ref)
    routes.arrive("mlp", mlp_in)

    def two(u):
        rows = pl.ds(pl.multiple_of(u * width, width), width)
        gate = mod_ref[pl.ds(u, 1), 5 * size : 6 * size]
        mlp = mlp_ref[rows, :] + mlp_in[rows, :].astype(F32)
        held[rows, :] = (x1_ref[rows, :] + gate * mlp).astype(BF16)
        by_unit[pl.ds(u, 1), 0:size] = jnp.sum(
            dx_ref[rows, :] * attn_ref[rows, :], axis=0, keepdims=True
        )
        by_unit[pl.ds(u, 1), size : 2 * size] = jnp.sum(
            c_ref[rows, :].astype(F32) * mlp, axis=0, keepdims=True
        )

    each(units, two, 3)
    over_slots(gate_ref)
    r_ref[...] = tn(perm_ref[...], held[...]).astype(BF16)
    grad[...] = nn(om_ref[...], da[...]).astype(BF16).reshape(grad.shape)
    for k in range(shards):
        base = 2 * flip(f, k)
        mine_ref[k] = grad[base + c]
        other_ref[k] = grad[base + 1 - c]
    for k in range(1, blocks):
        routes.arrive(("up", k), up_all.at[flip(b, k)])
    up_ref[...] = up_all[...]
    routes.finish()


def stream_back_body(
    shards, chips, heads, per, h_ref, gs_ref, d_ref, wh_ref, mod_ref, mine_ref, x_ref, dx_ref, perm_ref,
    gm_ref, o_ref, sum_ref, g_ref, go_ref, give, take, keep, came, h_s, acc, low, others, out_in, out_low,
    out_got, total, held, by_unit, local, sent, got,
):
    f, b = lax.axis_index("fsdp"), lax.axis_index("blk")
    z, c = b // 2, b % 2
    pair = b + 1 - 2 * c
    width = BLOCK // (2 * chips)
    units = d_ref.shape[0]
    count, size = x_ref.shape
    wide = wh_ref.shape[1]
    own = heads // (2 * chips)
    head_size = size // heads
    rows = low.shape[1]
    steps = units // per
    routes = Routes(sent, got)

    def load(i):
        return pltpu.make_async_copy(
            h_ref.at[pl.ds(i * per, per)], h_s.at[i % 2], local.at[i % 2]
        )

    load(0).start()
    greet(shards, chips)
    routes.start("out", gs_ref, out_in, {"blk": pair})

    def partial(device, target):
        at = pl.ds(pl.multiple_of(device * width, width), width)
        grads = d_ref[:, at, :].reshape(count, wide)
        for col in range(0, size, 3 * LANES):
            target[:, col : col + 3 * LANES] = nt(
                grads, wh_ref[col : col + 3 * LANES, :]
            ).astype(BF16)

    def route(side, t):
        if side == 0:
            chip = chips - 1 - t
            return chip, z < chip, z > 0
        return t, z > t, z < chips - 1

    def onward(side, t, chip, when):
        if side == 0:
            slot, to = chip, b + 2
        else:
            slot, to = chip + (chips - chip) * (z - 1 == chip).astype(I32), b - 2
        routes.start(("sum", side, t), keep.at[chip], came.at[slot], {"blk": to}, when)

    def join(chip, slot=None):
        value = keep[chip].astype(F32) + take[chip].astype(F32)
        if slot is not None:
            value = value + came[slot].astype(F32)
        keep[chip] = value.astype(BF16)

    for t in range(chips - 1):
        for side in range(2):
            chip, passes, inside = route(side, t)

            @pl.when(passes)
            def _():
                partial(chip * 2 + 1 - c, give.at[chip])

            routes.start(("pair", side, t), give.at[chip], take.at[chip], {"blk": pair}, passes)

            @pl.when(passes)
            def _():
                partial(chip * 2 + c, keep.at[chip])

            first = passes & jnp.logical_not(inside)
            routes.arrive(("pair", side, t), take.at[chip], first)

            pl.when(first)(lambda: join(chip))
            onward(side, t, chip, first)

    partial(z * 2 + 1 - c, give.at[z])
    routes.start(("pair", "own"), give.at[z], take.at[z], {"blk": pair})
    partial(z * 2 + c, keep.at[z])

    def gather(i):
        if i + 1 < steps:
            load(i + 1).start()
        load(i).wait()
        part = tn(
            h_s[i % 2].reshape(per * BLOCK, size),
            d_ref[i * per : (i + 1) * per].reshape(per * BLOCK, wide),
        )
        if i:
            acc[...] += part
        else:
            acc[...] = part

    for t in range(max(chips - 1, steps)):
        if t < steps:
            gather(t)
        if t == steps - 1:
            packed = jnp.concatenate(
                [acc[:, i * LANES : i * LANES + head_size] for i in range(3 * own)], axis=1
            )
            low[...] = packed.astype(BF16).reshape(low.shape)
            for k in range(1, shards):
                other = flip(f, k)
                routes.start(("grad", k), low.at[other], others.at[k], {"fsdp": other})
        if t == 0:
            routes.arrive("out", out_in)
            out_low[...] = (gm_ref[...].astype(F32) + out_in[...].astype(F32)).astype(BF16)
            for k in range(1, shards):
                routes.start(("out", k), out_low.at[k], out_got.at[k], {"fsdp": flip(f, k)})
        if t >= chips - 1:
            continue
        for near, side in ((True, 0), (True, 1), (False, 1), (False, 0)):
            chip, passes, inside = route(side, t)
            when = passes & inside & ((z < chips // 2) == near)
            routes.arrive(("pair", side, t), take.at[chip], when)
            routes.arrive(("sum", side, t), came.at[chip], when)
            pl.when(when)(lambda: join(chip, chip))
            onward(side, t, chip, when)

    grad, grad_out = low[f].astype(F32), out_low[0].astype(F32)
    for k in range(1, shards):
        routes.arrive(("grad", k), others.at[k])
        grad = grad + others[k].astype(F32)
        routes.arrive(("out", k), out_got.at[k])
        grad_out = grad_out + out_got[k].astype(F32)
    g_ref[...] = grad.astype(BF16)
    go_ref[...] = grad_out.astype(BF16)

    routes.arrive(("pair", "own"), take.at[z])
    total[...] = keep[z].astype(F32) + take[z].astype(F32)
    for t in range(chips - 1):
        for side in range(2):
            chip, _, inside = route(side, t)
            slot = chip if side == 0 else chips
            here = (z == chip) & inside
            routes.arrive(("sum", side, t), came.at[slot], here)

            @pl.when(here)
            def _():
                total[...] += came[slot].astype(F32)

    by_unit[...] = jnp.zeros_like(by_unit)

    def one(u):
        rows = pl.ds(pl.multiple_of(u * width, width), width)
        scale = mod_ref[pl.ds(u, 1), size : 2 * size]
        normed, spread = normal(x_ref[rows, :].astype(F32))
        grad = total[rows, :]
        by_unit[pl.ds(u, 1), 0:size] = jnp.sum(grad, axis=0, keepdims=True)
        by_unit[pl.ds(u, 1), size : 2 * size] = jnp.sum(grad * normed, axis=0, keepdims=True)
        dx = dx_ref[rows, :] + normal_back(grad * (1.0 + scale), normed, spread)
        held[rows, :] = dx.astype(BF16)

    each(units, one, 3)
    o_ref[...] = tn(perm_ref[...], held[...]).astype(BF16)
    sum_ref[...] = lax.dot_general(
        mine_ref[:, : by_unit.shape[0]], by_unit[...], (((1,), (0,)), ((), ())), precision=HIGH,
        preferred_element_type=F32,
    )
    routes.finish()


def finish_body(
    shards, chips, fc_ref, ada_ref, go_ref, gq_ref, one_ref, two_ref, gate_ref, cond_ref, tot_ref, gqa_ref,
    dm_ref, dc_ref, mine, up, inner_in, result, other, gq_all, sum_own, sum_pair, small, mods, conds, ada_s,
    local, sent, got,
):
    f, b = lax.axis_index("fsdp"), lax.axis_index("blk")
    z, c = b // 2, b % 2
    pair = b + 1 - 2 * c
    count = mine.shape[0]
    slots, wider = sum_own.shape
    size = wider // 6
    routes = Routes(sent, got)
    loads = fetch([(fc_ref, mine.at[0 : count - 1]), (ada_ref, ada_s)], local)
    greet(shards, chips)

    sum_own[:, 0 : 2 * size] = one_ref[...]
    sum_own[:, 2 * size : 3 * size] = gate_ref[:, 0:size]
    sum_own[:, 3 * size : 5 * size] = two_ref[...]
    sum_own[:, 5 * size : 6 * size] = gate_ref[:, size : 2 * size]
    routes.start("sum", sum_own, sum_pair, {"blk": pair})
    gq_all[b] = gq_ref[...]

    def line(side, s, send):
        away = s - 1 if send else s
        chip = z - away if side == 0 else z + away
        ahead = z + 1 < chips if side == 0 else z > 0
        known = z >= away if side == 0 else z + away < chips
        return chip, {"blk": b + 2 if side == 0 else b - 2}, known & ahead if send else known

    def send(name, s, place):
        for side in range(2):
            chip, to, when = line(side, s, True)
            routes.start((name, side, s), place(chip), place(chip), to, when)

    def take(name, s, place):
        for side in range(2):
            chip, _, when = line(side, s, False)
            routes.arrive((name, side, s), place(chip), when)
        if s + 1 < chips:
            send(name, s + 1, place)

    def head(chip):
        return gq_all.at[chip * 2 + c]

    send("head", 1, head)
    routes.start("head pair", gq_all.at[b], gq_all.at[b], {"blk": pair})

    half = chips // 2
    right = z // half
    inner, outer = {"blk": b + 2 - 4 * right}, {"blk": b - 2 + 4 * right}
    ends = (z > 0) & (z < chips - 1)
    middle = (z == half - 1) | (z == half)
    edge = jnp.logical_not(middle)

    parts = [[small.at[i] for i in range(4)]]
    parts += [[ref.at[i] for ref in (mine, up, inner_in, result)] for i in range(count)]
    count += 1

    def inward(i, when):
        own, above, within, _ = parts[i]
        routes.start(("up", i), own, above, inner, when & edge)
        routes.start(("across", i), own, within, inner, when & middle, ("in", i))

    mine[count - 2] = go_ref[...]
    routes.arrive("sum", sum_pair)
    total = sum_own[...] + sum_pair[...]
    small[0] = jnp.concatenate(
        [total[:, : 3 * size], total[:, 3 * size :]], axis=0
    ).astype(BF16)
    ahead = min(4, count)
    inward(0, jnp.logical_not(ends))
    loads[0].wait()
    for i in range(1, ahead):
        inward(i, jnp.logical_not(ends))

    def combine():
        mods[f, :, : 3 * size] = small[3, 0:slots].astype(F32)
        mods[f, :, 3 * size :] = small[3, slots : 2 * slots].astype(F32)
        for k in range(1, shards):
            routes.start(("mod", k), mods.at[f], mods.at[f], {"fsdp": flip(f, k)})

    def condition():
        for k in range(1, shards):
            routes.arrive(("mod", k), mods.at[flip(f, k)])
        dm_ref[...] = mods[...]
        loads[1].wait()
        grad = nt(mods[...].reshape(shards * slots, wider).astype(BF16), ada_s[...])
        values = cond_ref[...]
        gate = 1.0 / (1.0 + jnp.exp(-values))
        conds[f] = grad * (gate + values * gate * (1.0 - gate))
        for k in range(1, shards):
            routes.start(("cond", k), conds.at[f], conds.at[f], {"fsdp": flip(f, k)})

    def conditions():
        for k in range(1, shards):
            routes.arrive(("cond", k), conds.at[flip(f, k)])
        dc_ref[...] = conds[...]

    jobs = [combine, condition, conditions]
    heads = [lambda s=s: take("head", s, head) for s in range(1, chips)]

    def forward(i):
        own, above, _, _ = parts[i]
        routes.arrive(("up", i), above, ends)

        @pl.when(ends)
        def _():
            own[...] = (own[...].astype(F32) + above[...].astype(F32)).astype(BF16)

        inward(i, ends)
        if i + ahead < count:
            inward(i + ahead, jnp.logical_not(ends))

    def back(i):
        own, _, within, full = parts[i]
        routes.arrive(("in", i), within)

        @pl.when(middle)
        def _():
            full[...] = (own[...].astype(F32) + within[...].astype(F32)).astype(BF16)

        @pl.when(edge)
        def _():
            full[...] = within[...]

        routes.start(("down", i), full, within, outer, ends, ("in", i))
        if i:
            routes.start(("pair", i - 1), full, other.at[i - 1], {"blk": pair})

    for i in range(count + 1):
        if i < count:
            forward(i)
        if i:
            back(i - 1)
            if jobs and i % 2 == 1:
                jobs.pop(0)()
            if heads and i % 2 == 0 and i > 2:
                heads.pop(0)()
    for job in jobs + heads:
        job()
    for s in range(1, chips):
        for side in range(2):
            chip, _, when = line(side, s, False)
            routes.start(("head pair", side, s), head(chip), head(chip), {"blk": pair}, when)
    copies = fetch([(result, tot_ref.at[c])], local)
    for i in range(count - 1):
        routes.arrive(("pair", i), other.at[i])
    copies += fetch([(other, tot_ref.at[1 - c])], local, 1)
    routes.arrive("head pair", gq_all.at[pair])
    for s in range(1, chips):
        for side in range(2):
            chip, _, when = line(side, s, False)
            routes.arrive(("head pair", side, s), gq_all.at[chip * 2 + 1 - c], when)
    copies += fetch([(gq_all, gqa_ref)], local, 2)
    routes.finish()
    for copy in copies:
        copy.wait()


def unfold_body(
    shards, low_ref, wave_ref, dm_ref, dc_ref, tot_ref, gq_ref, temb_ref, ada_ref, qkv_ref, out_ref,
    fc1_ref, fc2_ref, ada_s, qkv_s, out_s, fc1_s, fc2_s, sems,
):
    _, count, rows, size = tot_ref.shape
    slots = dm_ref.shape[1]
    copies = []

    def leave(source, target):
        copy = pltpu.make_async_copy(source, target, sems.at[len(copies)])
        copy.start()
        copies.append(copy)

    hidden = fc1_s.shape[1]
    part = hidden // shards // 2
    height = fc1_s.shape[0]
    blocks = hidden // 2 // size
    per = height // rows
    for core in range(2):
        for i in range(blocks * per):
            piece = tot_ref[core, i].astype(F32)
            block, at = i // per, (i % per) * rows
            for j in range(size // part):
                column = (block * (size // part) + j) * 2 * part + core * part
                fc1_s[at : at + rows, column : column + part] = piece[:, j * part : (j + 1) * part]
        rest = count - 1 - blocks * per
        for i in range(rest):
            at = (core * rest + i) * rows
            fc2_s[at : at + rows, :] = tot_ref[core, blocks * per + i].astype(F32)
        out_s[core * rows : (core + 1) * rows, :] = tot_ref[core, count - 1].astype(F32)
    leave(fc1_s, fc1_ref)
    leave(fc2_s, fc2_ref)
    leave(out_s, out_ref)
    devices, _, packed = gq_ref.shape
    narrow = packed // 3
    for p in range(3):
        for i in range(devices):
            at = p * size + i * narrow
            qkv_s[:, at : at + narrow] = gq_ref[i, :, p * narrow : (p + 1) * narrow].astype(F32)
    leave(qkv_s, qkv_ref)
    grads = dm_ref[...].reshape(shards * slots, -1).astype(BF16)
    ada_s[...] = tn(low_ref[...], grads)
    leave(ada_s, ada_ref)
    step = dc_ref.shape[2]
    for i in range(shards):
        temb_ref[:, i * step : (i + 1) * step] = lax.dot_general(
            wave_ref[...], dc_ref[i], (((0,), (0,)), ((), ())), precision=HIGH,
            preferred_element_type=F32,
        )
    for copy in copies:
        copy.wait()


def on_device(
    tokens,
    timesteps,
    segment_ids,
    head_mask,
    chan_mask,
    token_mask,
    w_temb,
    w_ada,
    w_qkv,
    w_out,
    w_fc1,
    w_fc2,
    cotangent,
):
    count, size = tokens.shape
    slots, heads = head_mask.shape[1:]
    head_size = size // heads
    shards, blocks = lax.axis_size("fsdp"), lax.axis_size("blk")
    chips = blocks // 2
    f, b = lax.axis_index("fsdp"), lax.axis_index("blk")
    c = b % 2
    width = BLOCK // blocks
    units = count // width
    own = heads // blocks
    wide = 3 * own * LANES
    hidden = w_fc1.shape[1]
    half = hidden // 2
    ids = jnp.stack([f, b, c]).astype(I32)

    near = 3 if shards == 4 else shards
    row1, row2 = w_fc1.shape[0], w_fc2.shape[0] // 2
    fc_blocks = half // size
    fc_rows = fc_blocks * row1 + row2

    items = lax.dynamic_slice_in_dim(segment_ids, b * count, count, axis=1)
    rows = w_temb.shape[0]
    entries = rows * shards
    spectrum = frequencies(timesteps[0], entries).astype(BF16).astype(F32)
    out_rows = w_out.shape[0] // 2
    ada_rows, wider = w_ada.shape
    padded = -(-units // 8) * 8
    n_copies = 9 * shards + 4 * chips + 8
    outs = run(
        "front",
        functools.partial(front_body, shards, chips, heads),
        [
            (VMEM, a)
            for a in (items, token_mask[None, :], tokens, cotangent, spectrum, w_temb)
        ]
        + [(ANY, a) for a in (w_ada, w_qkv, w_out.reshape(2, out_rows, size), w_fc1, w_fc2)],
        [
            (VMEM, shape((count, size))),
            (VMEM, shape((count, size))),
            (ANY, shape((2, slots, count), F32)),
            (VMEM, shape((8, LANES), I32)),
            (VMEM, shape((slots, LANES), F32)),
            (VMEM, shape((count, count))),
            (VMEM, shape((padded, wider), F32)),
            (VMEM, shape((shards * slots, ada_rows), F32)),
            (VMEM, shape((shards * slots, ada_rows))),
            (VMEM, shape((shards * slots, rows), F32)),
            (ANY, shape((2, count, size))),
            (ANY, shape((units, BLOCK, size))),
            (VMEM, shape((units, BLOCK, wide))),
            (VMEM, shape((size, wide))),
            (ANY, shape((shards, 2, out_rows, size))),
            (ANY, shape((row2, size))),
        ]
        + [(ANY, shape((fc_blocks, row1, size)))] * near,
        [
            pltpu.VMEM((blocks, count, size), BF16),
            pltpu.VMEM((shards, slots, entries), F32),
            pltpu.VMEM((shards, rows, size), BF16),
            pltpu.VMEM((shards, slots, wider), F32),
            pltpu.VMEM((shards, slots, wider), F32),
            pltpu.VMEM((2, slots, count), F32),
            pltpu.VMEM((2, count, size), BF16),
            pltpu.VMEM((shards, w_qkv.shape[0], 3 * own * head_size), BF16),
            pltpu.VMEM((shards, 2, out_rows, size), BF16),
            pltpu.VMEM((count, size), BF16),
            pltpu.VMEM(w_ada.shape, BF16),
            pltpu.VMEM(w_qkv.shape, BF16),
            pltpu.VMEM(w_fc1.shape, BF16),
            pltpu.VMEM((near, fc_blocks, row1, size), BF16),
            pltpu.SemaphoreType.DMA((units + 4 + near,)),
            pltpu.SemaphoreType.DMA((5,)),
            pltpu.SemaphoreType.DMA((n_copies,)),
            pltpu.SemaphoreType.DMA((n_copies,)),
        ],
        flops=2 * units * BLOCK * size * wide,
        vmem=60,
        collective=0,
    )
    x_s, c_s, hots, info, mark, perm, mod, condition, lifted, waves, dms = outs[:11]
    normed, qkv, w_heads, w_out_all, fc2_own = outs[11:16]
    fc1_near = outs[16:]
    fc1_parts = [(a, k, 0) for k, a in enumerate(fc1_near)]
    if shards == 4 and fc_blocks == 2:
        one, two = swap(fc2_own, "fsdp", 1), swap(fc2_own, "fsdp", 2)
        cut = row2 // 2
        fc2_parts = [(fc2_own, 0, 0), (one, 1, 0), (two, 2, 0)]
        moves = [
            (fc1_near[1], (0, 1, 2)),
            (fc1_near[2], (1, 2, 1)),
            (one, (0, cut, 2)),
            (two, (cut, row2, 1)),
        ]
    else:
        fc1_parts += [
            (swap(fc1_near[0], "fsdp", k), k, 0) for k in range(len(fc1_near), shards)
        ]
        moves = []
        fc2_parts = [(fc2_own, 0, 0)] + [(swap(fc2_own, "fsdp", k), k, 0) for k in range(1, shards)]
    w_out_all = w_out_all.reshape(size, size)

    mask = head_mask[0]
    narrow = own * head_size
    held, lse, pieces = run(
        "attend",
        functools.partial(attend_body, own, head_size, blocks),
        [(SMEM, ids), (SMEM, info), (SMEM, mask), (VMEM, qkv)],
        [
            (VMEM, shape((units, narrow, BLOCK))),
            (VMEM, shape((units, 8, BLOCK), F32)),
            (VMEM, shape((blocks, narrow, count))),
        ],
        [
            pltpu.VMEM((units, narrow, BLOCK), F32),
            pltpu.VMEM((units, own, -(-head_size // 16) * 16, BLOCK), BF16),
            pltpu.VMEM((blocks, narrow, count), BF16),
        ],
        flops=2 * units * units * BLOCK * BLOCK * wide // 3,
    )
    if moves:
        moved = lax.optimization_barrier(tuple(a for a, _ in moves) + (lse,))[:-1]
    else:
        moved = ()
    plan = [move for _, move in moves]
    n_copies = blocks + len(moves) + 1
    outs = run(
        "project",
        functools.partial(project_body, shards, blocks, plan),
        [(VMEM, a) for a in (mod, x_s, w_out_all, pieces)] + [(ANY, a) for a in moved],
        [
            (VMEM, shape((count, size), F32)),
            (VMEM, shape((count, size), F32)),
            (ANY, shape((2, count, size))),
            (VMEM, shape((size, count))),
        ]
        + [(ANY, shape((high - low,) + a.shape[1:])) for a, (low, high, _) in moves],
        [
            pltpu.VMEM((blocks, narrow, count), BF16),
            pltpu.VMEM((2, count, size), BF16),
            pltpu.SemaphoreType.DMA((1,)),
            pltpu.SemaphoreType.DMA((n_copies,)),
            pltpu.SemaphoreType.DMA((n_copies,)),
        ],
        flops=2 * count * size * size,
        collective=3,
    )
    attn, x1, h2, om = outs[:4]
    if moves:
        fc1_parts += [(outs[4], 3, 0), (outs[5], 3, 1)]
        fc2_parts += [(outs[6], 3, 0), (outs[7], 3, cut)]

    chan = chan_mask[0].reshape(slots, shards, 2, half // shards)
    chan = lax.dynamic_slice_in_dim(chan, c, 1, axis=2).reshape(slots, half)
    ff_step = 768
    n_sems = 4 + 4 * shards * (half // ff_step + 1)
    mlp, mlp_send, dh2, dh2_send, g_fc = run(
        "feed_forward",
        functools.partial(
            ff_body,
            shards,
            ff_step,
            2,
            [(k, first) for _, k, first in fc1_parts],
            [(k, first) for _, k, first in fc2_parts],
        ),
        [(SMEM, ids), (VMEM, hots), (VMEM, chan)]
        + [(ANY, a) for a in (h2, dms)]
        + [(ANY, a) for a, _, _ in fc1_parts + fc2_parts],
        [
            (VMEM, shape((count, size), F32)),
            (VMEM, shape((count, size))),
            (VMEM, shape((count, size), F32)),
            (VMEM, shape((count, size))),
            (ANY, shape((shards, fc_rows, size))),
        ],
        [
            pltpu.VMEM((size, half), BF16),
            pltpu.VMEM((half, size), BF16),
            pltpu.VMEM((2 * count, size), BF16),
            pltpu.VMEM((2 * count, size), BF16),
            pltpu.VMEM((size, 2 * count), BF16),
            pltpu.VMEM((2 * count, ff_step), BF16),
            pltpu.VMEM((2 * count, ff_step), BF16),
            pltpu.VMEM((2 * count, size), F32),
            pltpu.VMEM((2 * count, size), F32),
            pltpu.VMEM((size, half), BF16),
            pltpu.VMEM((half, size), BF16),
            pltpu.SemaphoreType.DMA((n_sems,)),
        ],
        flops=6 * 2 * 2 * count * size * half,
        vmem=60,
    )
    g_fc = lax.psum_scatter(
        g_fc.reshape(shards * fc_rows, size), "fsdp", scatter_dimension=0, tiled=True
    )

    n_copies = blocks + 2
    up_parts, dx1, sums_two, sums_gate, result, g_out, g_out_send = run(
        "middle_back",
        functools.partial(middle_body, shards, blocks),
        [
            (VMEM, a)
            for a in (
                mod, mark, x1, c_s, dh2, dh2_send, mlp, mlp_send, attn, om,
                w_out_all.reshape(blocks, narrow, size), perm,
            )
        ],
        [
            (VMEM, shape((blocks, narrow, count))),
            (VMEM, shape((count, size), F32)),
            (VMEM, shape((slots, 2 * size), F32)),
            (VMEM, shape((slots, 2 * size), F32)),
            (VMEM, shape((count, size))),
            (VMEM, shape((shards, out_rows, size))),
            (VMEM, shape((shards, out_rows, size))),
        ],
        [
            pltpu.VMEM((count, size), BF16),
            pltpu.VMEM((count, size), BF16),
            pltpu.VMEM((count, size), BF16),
            pltpu.VMEM((blocks, narrow, count), BF16),
            pltpu.VMEM((blocks, narrow, count), BF16),
            pltpu.VMEM((count, size), BF16),
            pltpu.VMEM((2 * shards, out_rows, size), BF16),
            pltpu.VMEM((padded, 2 * size), F32),
            pltpu.SemaphoreType.DMA((n_copies,)),
            pltpu.SemaphoreType.DMA((n_copies,)),
        ],
        flops=4 * count * size * size,
        collective=4,
    )

    (d_qkv,) = run(
        "attend_back",
        functools.partial(attend_back_body, own, head_size, blocks),
        [(SMEM, ids), (SMEM, info), (SMEM, mask)]
        + [(VMEM, a) for a in (qkv, held, lse, up_parts)],
        [(VMEM, shape((units, BLOCK, wide)))],
        [
            pltpu.VMEM((units, own, LANES, BLOCK), BF16),
            pltpu.VMEM((units, 8, BLOCK), F32),
            pltpu.VMEM((units, own, LANES, BLOCK), F32),
            pltpu.VMEM((own, BLOCK, LANES), F32),
            pltpu.VMEM((own, BLOCK, LANES), F32),
        ],
        flops=5 * units * units * BLOCK * BLOCK * wide // 3,
    )
    per = 4 if units % 4 == 0 else 1
    rows_qkv = w_qkv.shape[0]
    n_copies = 4 * chips + 2 * shards + 4
    grad_tokens, sums_one, g_qkv, g_out = run(
        "stream_back",
        functools.partial(stream_back_body, shards, chips, heads, per),
        [(ANY, normed), (ANY, g_out_send)]
        + [(VMEM, a) for a in (d_qkv, w_heads, mod, mark, x_s, dx1, perm, g_out)],
        [
            (VMEM, shape((count, size))),
            (VMEM, shape((slots, 2 * size), F32)),
            (VMEM, shape((rows_qkv, 3 * narrow))),
            (VMEM, shape((out_rows, size))),
        ],
        [
            pltpu.VMEM((chips, count, size), BF16),
            pltpu.VMEM((chips, count, size), BF16),
            pltpu.VMEM((chips, count, size), BF16),
            pltpu.VMEM((chips + 1, count, size), BF16),
            pltpu.VMEM((2, per, BLOCK, size), BF16),
            pltpu.VMEM((size, wide), F32),
            pltpu.VMEM((shards, rows_qkv, 3 * narrow), BF16),
            pltpu.VMEM((shards, rows_qkv, 3 * narrow), BF16),
            pltpu.VMEM((shards, out_rows, size), BF16),
            pltpu.VMEM((shards, out_rows, size), BF16),
            pltpu.VMEM((shards, out_rows, size), BF16),
            pltpu.VMEM((count, size), F32),
            pltpu.VMEM((count, size), BF16),
            pltpu.VMEM((padded, 2 * size), F32),
            pltpu.SemaphoreType.DMA((2,)),
            pltpu.SemaphoreType.DMA((n_copies,)),
            pltpu.SemaphoreType.DMA((n_copies,)),
        ],
        flops=4 * units * BLOCK * size * wide,
        vmem=60,
        collective=1,
    )

    pieces = fc_rows // out_rows
    n_copies = 5 * pieces + 16 + 4 * chips + 2 * shards
    totals, g_qkv, d_mod, d_cond = run(
        "finish",
        functools.partial(finish_body, shards, chips),
        [(ANY, g_fc.reshape(pieces, out_rows, size)), (ANY, w_ada)]
        + [(VMEM, a) for a in (g_out, g_qkv, sums_one, sums_two, sums_gate, condition)],
        [
            (ANY, shape((2, pieces + 1, out_rows, size))),
            (ANY, shape((blocks, rows_qkv, 3 * narrow))),
            (VMEM, shape((shards, slots, wider), F32)),
            (VMEM, shape((shards, shards * slots, ada_rows), F32)),
        ],
        [pltpu.VMEM((pieces + 1, out_rows, size), BF16)] * 5
        + [
            pltpu.VMEM((blocks, rows_qkv, 3 * narrow), BF16),
            pltpu.VMEM((slots, wider), F32),
            pltpu.VMEM((slots, wider), F32),
            pltpu.VMEM((4, 2 * slots, wider // 2), BF16),
            pltpu.VMEM((shards, slots, wider), F32),
            pltpu.VMEM((shards, shards * slots, ada_rows), F32),
            pltpu.VMEM(w_ada.shape, BF16),
            pltpu.SemaphoreType.DMA((3,)),
            pltpu.SemaphoreType.DMA((n_copies,)),
            pltpu.SemaphoreType.DMA((n_copies,)),
        ],
        vmem=60,
        collective=2,
    )
    grad_temb, grad_ada, grad_qkv, grad_out, grad_fc1, grad_fc2 = run(
        "unfold",
        functools.partial(unfold_body, shards),
        [(VMEM, a) for a in (lifted, waves, d_mod, d_cond, totals, g_qkv)],
        [
            (VMEM, shape(w_temb.shape, F32)),
            (ANY, shape(w_ada.shape, F32)),
            (ANY, shape(w_qkv.shape, F32)),
            (ANY, shape(w_out.shape, F32)),
            (ANY, shape(w_fc1.shape, F32)),
            (ANY, shape(w_fc2.shape, F32)),
        ],
        [
            pltpu.VMEM(a.shape, F32) for a in (w_ada, w_qkv, w_out, w_fc1, w_fc2)
        ]
        + [pltpu.SemaphoreType.DMA((5,))],
        vmem=60,
    )
    return (
        result,
        grad_tokens,
        grad_temb,
        grad_ada,
        grad_qkv,
        grad_out,
        grad_fc1,
        grad_fc2,
    )


def solution(mesh):
    placed = (
        P(("fsdp", "blk"), None),
        P("fsdp", None),
        P("fsdp", None),
        P("fsdp", None, None),
        P("fsdp", None, None),
        P(("fsdp", "blk")),
        P("fsdp", None),
        P("fsdp", None),
        P("fsdp", None),
        P("fsdp", None),
        P("fsdp", None),
        P("fsdp", None),
        P(("fsdp", "blk"), None),
    )
    return jax.shard_map(
        on_device,
        mesh=mesh,
        in_specs=placed,
        out_specs=(
            P(("fsdp", "blk"), None),
            P(("fsdp", "blk"), None),
            P("fsdp", None),
            P("fsdp", None),
            P("fsdp", None),
            P("fsdp", None),
            P("fsdp", None),
            P("fsdp", None),
        ),
        check_vma=False,
    )
```

```python
import functools
import math

import jax
import jax.numpy as jnp
from jax import lax
from jax.experimental import pallas as pl
from jax.experimental.pallas import tpu as pltpu
from jax.sharding import PartitionSpec as P

HIGH = lax.Precision.HIGHEST
BF16 = jnp.bfloat16
F32 = jnp.float32
I32 = jnp.int32
LANES = 128
BLOCK = 256
NEG = -1e30
LOG2E = 1.4426950408889634

VMEM = pl.BlockSpec(memory_space=pltpu.VMEM)
SMEM = pl.BlockSpec(memory_space=pltpu.SMEM)
ANY = pl.BlockSpec(memory_space=pl.ANY)


def shape(dims, kind=BF16):
    return jax.ShapeDtypeStruct(tuple(dims), kind)


def run(name, body, ins, outs, scratch=(), flops=0, vmem=62, collective=None, **more):
    moved = sum(a.size * a.dtype.itemsize for _, a in ins)
    moved += sum(math.prod(o.shape) * jnp.dtype(o.dtype).itemsize for _, o in outs)
    return pl.pallas_call(
        body,
        out_shape=[o for _, o in outs],
        in_specs=[s for s, _ in ins],
        out_specs=[s for s, _ in outs],
        scratch_shapes=list(scratch),
        compiler_params=pltpu.CompilerParams(
            vmem_limit_bytes=vmem << 20,
            collective_id=collective,
            has_side_effects=collective is not None,
        ),
        cost_estimate=pl.CostEstimate(flops=flops, bytes_accessed=moved, transcendentals=0),
        name=name,
        **more,
    )(*[a for _, a in ins])


def swap(array, axis, by):
    size = lax.axis_size(axis)
    return lax.ppermute(array, axis, [(i, i ^ by) for i in range(size)])


def frequencies(steps, entries):
    half = entries // 2
    ladder = jnp.exp(-math.log(10000.0) * lax.iota(jnp.int32, half) / half)
    angles = steps.astype(F32)[:, None] * ladder[None, :]
    return jnp.concatenate([jnp.cos(angles), jnp.sin(angles)], axis=1)


def nn(left, right):
    return lax.dot_general(left, right, (((1,), (0,)), ((), ())), preferred_element_type=F32)


def nt(left, right):
    return lax.dot_general(left, right, (((1,), (1,)), ((), ())), preferred_element_type=F32)


def tn(left, right):
    return lax.dot_general(left, right, (((0,), (0,)), ((), ())), preferred_element_type=F32)


def each(count, step, group=1):
    if count % group:
        group = 1

    def one(index, carry):
        for i in range(group):
            step(index * group + i)
        return carry

    lax.fori_loop(0, count // group, one, 0)


def normal(values):
    center = values - jnp.mean(values, axis=-1, keepdims=True)
    scale = lax.rsqrt(jnp.mean(center * center, axis=-1, keepdims=True) + 1e-06)
    return center * scale, scale


def normal_back(grad, normed, scale):
    along = jnp.mean(grad * normed, axis=-1, keepdims=True)
    return scale * (grad - jnp.mean(grad, axis=-1, keepdims=True) - normed * along)


def flip(index, by):
    bit = 1
    while bit <= by:
        if by & bit:
            index = index + bit * (1 - 2 * ((index // bit) % 2))
        bit *= 2
    return index


def fetch(pairs, sems, first=0):
    copies = []
    for index, (source, target) in enumerate(pairs, first):
        copy = pltpu.make_async_copy(source, target, sems.at[index])
        copy.start()
        copies.append(copy)
    return copies


class Routes:
    def __init__(self, sent, got):
        self.sent, self.got, self.known, self.started = sent, got, {}, []

    def slot(self, name):
        return self.known.setdefault(name, len(self.known))

    def copy(self, name, source, target, to, landed=None):
        return pltpu.make_async_remote_copy(
            src_ref=source,
            dst_ref=target,
            send_sem=self.sent.at[self.slot(name)],
            recv_sem=self.got.at[self.slot(landed or name)],
            device_id=to,
            device_id_type=pl.DeviceIdType.MESH,
        )

    def start(self, name, source, target, to, when=None, landed=None):
        def make():
            return self.copy(name, source, target, to, landed)

        self.started.append((make, when))
        if when is None:
            make().start()
        else:
            pl.when(when)(lambda: make().start())

    def arrive(self, name, target, when=None):
        def wait():
            b = lax.axis_index("blk")
            self.copy(name, target, target, {"blk": b + 1 - 2 * (b % 2)}).wait_recv()

        if when is None:
            wait()
        else:
            pl.when(when)(wait)

    def finish(self):
        for make, when in self.started:
            if when is None:
                make().wait_send()
            else:
                pl.when(when)(lambda make=make: make().wait_send())


def greet(shards, chips):
    f, b = lax.axis_index("fsdp"), lax.axis_index("blk")
    z, c = b // 2, b % 2
    barrier = pltpu.get_barrier_semaphore()

    def signal(to):
        pl.semaphore_signal(barrier, inc=1, device_id=to, device_id_type=pl.DeviceIdType.MESH)

    for k in range(1, shards):
        signal({"fsdp": flip(f, k)})
    signal({"blk": b + 1 - 2 * c})
    pl.when(z > 0)(lambda: signal({"blk": b - 2}))
    pl.when(z < chips - 1)(lambda: signal({"blk": b + 2}))
    ends = (z == 0).astype(I32) + (z == chips - 1).astype(I32)
    pl.semaphore_wait(barrier, shards + 2 - ends)


def greet_all(shards, blocks):
    f, b = lax.axis_index("fsdp"), lax.axis_index("blk")
    barrier = pltpu.get_barrier_semaphore()
    peers = [{"fsdp": flip(f, k)} for k in range(1, shards)]
    peers += [{"blk": flip(b, k)} for k in range(1, blocks)]
    for to in peers:
        pl.semaphore_signal(barrier, inc=1, device_id=to, device_id_type=pl.DeviceIdType.MESH)
    pl.semaphore_wait(barrier, len(peers))


def front_body(
    shards, chips, heads, items_ref, keep_ref, x_ref, c_ref, spec_ref, temb_ref, ada_ref, qkvw_ref,
    outw_ref, fc1w_ref, fc2w_ref, xs_ref, cs_ref, hot_ref, info_ref, mark_ref, perm_ref, mod_ref, cond_ref, low_ref, wave_ref, dm_ref, h_ref,
    qkv_ref, wh_ref, wo_ref, fc2_ref, *refs,
):
    fc_refs, refs = refs[:-18], refs[-18:]
    x_all, spec_all, temb_all, part_own, part_got, hots, dms, wh_all, wo_all = refs[:9]
    h_all, ada_s, qkvw_s, fc1_s, fc_all, local, loads, sent, got = refs[9:]
    f, b = lax.axis_index("fsdp"), lax.axis_index("blk")
    z, c = b // 2, b % 2
    blocks = 2 * chips
    pair = b + 1 - 2 * c
    width = BLOCK // blocks
    count, size = x_ref.shape
    units = count // width
    own = heads // blocks
    head_size = size // heads
    slots = spec_ref.shape[0]
    routes = Routes(sent, got)
    down = fc2_ref.shape[0]
    inside = fetch(
        [
            (ada_ref, ada_s),
            (qkvw_ref, qkvw_s),
            (outw_ref, wo_all.at[f]),
            (fc1w_ref, fc1_s),
            (fc2w_ref.at[pl.ds(pl.multiple_of(c * down, 16), down)], fc2_ref),
        ],
        loads,
    )
    greet(shards, chips)

    spec_all[f] = spec_ref[...]
    temb_all[f] = temb_ref[...]
    for k in range(1, shards):
        to = {"fsdp": flip(f, k)}
        routes.start(("spec", k), spec_ref, spec_all.at[f], to)
        routes.start(("temb", k), temb_ref, temb_all.at[f], to)

    items = items_ref[...]
    slot = lax.broadcasted_iota(I32, (slots, count), 0)
    hot = (items == slot).astype(F32)
    start = jnp.sum((items < slot).astype(F32), axis=1, keepdims=True)
    end = start + jnp.sum(hot, axis=1, keepdims=True)
    row = lax.broadcasted_iota(I32, (count, count), 0)
    col = lax.broadcasted_iota(I32, (count, count), 1)
    rank = nn(hot.astype(BF16), (row <= col).astype(BF16))
    place = jnp.sum(hot * (start + rank), axis=0, keepdims=True) - 1.0
    perm = (row.astype(F32) == place).astype(BF16)
    perm_ref[...] = perm
    x_s = nn(perm, x_ref[...]).astype(BF16)
    xs_ref[...] = x_s
    x_all[b] = x_s

    def line(side, s, send):
        away = s - 1 if send else s
        chip = z - away if side == 0 else z + away
        ahead = z + 1 < chips if side == 0 else z > 0
        known = z >= away if side == 0 else z + away < chips
        when = known & ahead if send else known
        return chip * 2 + c, {"blk": b + 2 if side == 0 else b - 2}, when

    def send_on(s):
        for side in range(2):
            device, to, when = line(side, s, True)
            routes.start(("line", side, s), x_all.at[device], x_all.at[device], to, when)

    send_on(1)
    routes.start("pair", x_all.at[b], x_all.at[b], {"blk": pair})
    cs_ref[...] = nn(perm, c_ref[...]).astype(BF16)
    keep = jnp.broadcast_to(keep_ref[...].astype(F32), (slots, count)).astype(BF16)
    kept = nt(keep, perm)
    at = lax.broadcasted_iota(I32, (slots, count), 1).astype(F32)
    hots[0] = kept * ((at >= start) & (at < end)).astype(F32)
    first = (lax.broadcasted_iota(I32, (slots, LANES), 1) * width).astype(F32)
    mine = ((first >= start) & (first < end)).astype(F32)
    mark_ref[...] = mine
    which = lax.broadcasted_iota(I32, (slots, LANES), 0).astype(F32)
    info_ref[0:1, :] = jnp.sum(mine * which, axis=0, keepdims=True).astype(I32)
    info_ref[1:2, :] = (jnp.sum(mine * start, axis=0, keepdims=True) / width).astype(I32)
    info_ref[2:3, :] = (jnp.sum(mine * end, axis=0, keepdims=True) / width).astype(I32)
    info_ref[3:8, :] = jnp.zeros((5, LANES), I32)

    for k in range(1, shards):
        other = flip(f, k)
        routes.arrive(("spec", k), spec_all.at[other])
        routes.arrive(("temb", k), temb_all.at[other])
    spectra = spec_all[...].reshape(shards * slots, -1).astype(BF16)
    condition = nn(spectra, temb_all[...].reshape(-1, size))
    rows = ada_ref.shape[0]
    for shard in range(shards):

        @pl.when(f == shard)
        def _():
            cond_ref[...] = condition[:, shard * rows : (shard + 1) * rows]
            freqs = temb_ref.shape[0]
            wave_ref[...] = spectra[:, shard * freqs : (shard + 1) * freqs].astype(F32)

    values = cond_ref[...]
    lifted = (values / (1.0 + jnp.exp(-values))).astype(BF16)
    low_ref[...] = lifted
    inside[0].wait()
    part_own[...] = nn(lifted, ada_s[...]).reshape(part_own.shape)
    for k in range(1, shards):
        other = flip(f, k)
        routes.start(("part", k), part_own.at[other], part_got.at[f], {"fsdp": other})

    rows = qkvw_ref.shape[0]
    inside[1].wait()
    narrow = own * head_size
    row = lax.broadcasted_iota(I32, (size, 2 * LANES), 0)
    col = lax.broadcasted_iota(I32, (size, 2 * LANES), 1)
    pick = ((row == b * narrow + col) & (col < narrow)).astype(F32).astype(BF16)
    wh_all[f] = jnp.concatenate(
        [
            nn(qkvw_s[:, part * size : (part + 1) * size], pick)[:, 0:narrow]
            for part in range(3)
        ],
        axis=1,
    ).astype(BF16)
    if shards == 4:
        for k in (1, 2):
            routes.start(("head", k), wh_all.at[f], wh_all.at[f], {"fsdp": flip(f, k)})
    else:
        for k in range(1, shards):
            routes.start(("head", k), wh_all.at[f], wh_all.at[f], {"fsdp": flip(f, k)})

    def take(s):
        for side in range(2):
            device, _, when = line(side, s, False)
            routes.arrive(("line", side, s), x_all.at[device], when)
            if s + 1 < chips:
                device, to, onward = line(side, s + 1, True)
                routes.start(
                    ("line", side, s + 1), x_all.at[device], x_all.at[device], to, onward
                )
            device, _, when = line(side, s, False)
            routes.start(
                ("pair", side, s), x_all.at[device], x_all.at[device], {"blk": pair}, when
            )

    take(1)
    if shards == 4:
        half = rows // 2
        for k, low in ((1, 0), (2, half)):
            routes.arrive(("head", k), wh_all.at[flip(f, k)])
            part = wh_all.at[flip(f, k), low : low + half]
            routes.start(("head", 3, k), part, part, {"fsdp": flip(f, 3 - k)})

    for k in range(1, shards):
        routes.start(("out", k), outw_ref.at[c], wo_all.at[f, c], {"fsdp": flip(f, k)})

    blocks_fc = fc_all.shape[1]
    part = fc1_s.shape[1] // shards // 2
    inside[3].wait()
    for core in range(2):

        @pl.when(c == core)
        def _():
            picked = jnp.concatenate(
                [
                    fc1_s[:, (2 * shard + core) * part : (2 * shard + core + 1) * part]
                    for shard in range(shards)
                ],
                axis=1,
            )
            for block_at in range(blocks_fc):
                fc_all[0, block_at] = picked[:, block_at * size : (block_at + 1) * size]

    for k in range(1, len(fc_refs)):
        routes.start(("fc", k), fc_all.at[0], fc_all.at[k], {"fsdp": flip(f, k)})

    total = part_own[f]
    for k in range(1, shards):
        other = flip(f, k)
        routes.arrive(("part", k), part_got.at[other])
        total = total + part_got[other]
    mod_ref[...] = lax.dot_general(
        mine[:, : mod_ref.shape[0]], total, (((0,), (0,)), ((), ())), precision=HIGH,
        preferred_element_type=F32,
    )

    def early(u):
        rows = pl.ds(pl.multiple_of(u * width, width), width)
        gate = mod_ref[pl.ds(u, 1), 5 * size : 6 * size]
        dms[0, rows, :] = (cs_ref[rows, :].astype(F32) * gate).astype(BF16)

    each(units, early)
    routes.start("dm", dms.at[0], dms.at[1], {"blk": pair})
    routes.start("hot", hots.at[0], hots.at[1], {"blk": pair})

    if shards == 4:
        half = rows // 2
        routes.arrive(("head", 3, 1), wh_all.at[flip(f, 3), 0:half])
        routes.arrive(("head", 3, 2), wh_all.at[flip(f, 3), half:rows])
    else:
        for k in range(1, shards):
            routes.arrive(("head", k), wh_all.at[flip(f, k)])
    packed = wh_all[...].reshape(size, 3 * narrow)
    wh_ref[...] = jnp.zeros_like(wh_ref)
    for i in range(3 * own):
        wh_ref[:, i * LANES : i * LANES + head_size] = packed[
            :, i * head_size : (i + 1) * head_size
        ]

    def block(device):
        at = pl.ds(pl.multiple_of(device * width, width), width)

        def one(u):
            shift = mod_ref[pl.ds(u, 1), 0:size]
            scale = mod_ref[pl.ds(u, 1), size : 2 * size]
            part = x_all[device, pl.ds(pl.multiple_of(u * width, width), width), :]
            normed, _ = normal(part.astype(F32))
            low = (normed * (1.0 + scale) + shift).astype(BF16)
            h_all[pl.ds(pl.multiple_of(u * width, width), width), :] = low

        each(units, one, 3)
        copies = fetch(
            [
                (h_all.at[u * width : (u + 1) * width], h_ref.at[u, at])
                for u in range(units)
            ],
            local,
        )
        found = nn(h_all[...], wh_ref[...]).astype(BF16)
        qkv_ref[:, at, :] = found.reshape(units, width, found.shape[1])
        for copy in copies:
            copy.wait()

    routes.arrive("pair", x_all.at[pair])
    each(2, lambda core: block(z * 2 + core))

    def work(s):
        for side in range(2):
            device, _, when = line(side, s, False)
            routes.arrive(("pair", side, s), x_all.at[device + 1 - 2 * c], when)

        def pick(q):
            chip = z - s + 2 * s * (q // 2)

            @pl.when((chip >= 0) & (chip < chips))
            def _():
                block(chip * 2 + q % 2)

        each(4, pick)

    for s in range(2, chips):
        take(s)
        if s == 2:
            for k in range(1, shards):
                other = flip(f, k)
                routes.arrive(("out", k), wo_all.at[other, c])
                routes.start(
                    ("pair out", k), wo_all.at[other, c], wo_all.at[other, c], {"blk": pair}
                )
        work(s - 1)
    work(chips - 1)
    inside[2].wait()
    for k in range(1, len(fc_refs)):
        routes.arrive(("fc", k), fc_all.at[k])
    inside[4].wait()
    for k in range(1, shards):
        routes.arrive(("pair out", k), wo_all.at[flip(f, k), 1 - c])
    routes.arrive("dm", dms.at[1])
    routes.arrive("hot", hots.at[1])
    routes.finish()
    copies = fetch(
        [(wo_all, wo_ref), (dms, dm_ref), (hots, hot_ref)]
        + [(fc_all.at[k], ref) for k, ref in enumerate(fc_refs)],
        local,
    )
    for copy in copies:
        copy.wait()


def exchange_lanes(tiles, width):
    tiles = list(tiles)
    count = len(tiles)
    group = lax.broadcasted_iota(I32, tiles[0].shape, 1) // width
    half = count // 2
    while half:
        low = (group // half) % 2 == 0
        fresh = list(tiles)
        for i in range(count):
            if (i // half) % 2 == 0:
                a, d = tiles[i], tiles[i + half]
                fresh[i] = jnp.where(low, a, pltpu.roll(d, half * width, 1))
                fresh[i + half] = jnp.where(low, pltpu.roll(a, LANES - half * width, 1), d)
        tiles = fresh
        half //= 2
    return tiles


def in_groups(first, last, sizes, step, carry):
    for size in sizes:
        count = (last - first) // size

        def one(index, carry, first=first, size=size):
            return step(first + index * size, size, carry)

        carry = lax.fori_loop(0, count, one, carry)
        first = first + count * size
    return carry


def attend_body(
    own, size, blocks, ids_ref, info_ref, mask_ref, qkv_ref, o_ref, lse_ref, out_ref, held, turned, placed
):
    units = qkv_ref.shape[0]
    width = BLOCK // blocks
    b = ids_ref[1]
    scale = LOG2E / math.sqrt(size)
    tall = turned.shape[2]

    def turn(j):
        for h in range(own):
            at = (2 * own + h) * LANES
            values = qkv_ref[j, :, at : at + LANES].astype(F32).T
            turned[j, h] = values[0:tall].astype(BF16)

    each(units, turn, 2)

    def one_unit(u):
        queries = [qkv_ref[u, :, h * LANES : (h + 1) * LANES] for h in range(own)]

        def some_blocks(j, count, carry):
            fresh = []
            for h in range(own):
                top, total, acc = carry[h]
                keys = qkv_ref[pl.ds(j, count), :, (own + h) * LANES : (own + h + 1) * LANES]
                scores = nt(keys.reshape(count * BLOCK, LANES), queries[h]) * scale
                new_top = jnp.maximum(top, jnp.max(scores, axis=0, keepdims=True))
                probs = jnp.exp2(scores - new_top)
                decay = jnp.exp2(top - new_top)
                total = total * decay + jnp.sum(probs, axis=0, keepdims=True)
                acc = acc * decay
                low = probs.astype(BF16)
                for i in range(count):
                    acc = acc + nn(turned[j + i, h], low[i * BLOCK : (i + 1) * BLOCK])
                fresh.append((new_top, total, acc))
            return tuple(fresh)

        start = tuple(
            (
                jnp.full((1, BLOCK), NEG, F32),
                jnp.zeros((1, BLOCK), F32),
                jnp.zeros((tall, BLOCK), F32),
            )
            for _ in range(own)
        )
        done = in_groups(info_ref[1, u], info_ref[2, u], (4, 2, 1), some_blocks, start)
        slot = info_ref[0, u]
        rows = []
        for h in range(own):
            top, total, acc = done[h]
            keep = mask_ref[slot, b * own + h].astype(F32)
            rows.append((acc * (keep / total))[0:size])
            lse_ref[u, h : h + 1, :] = top + jnp.log2(total)
        held[u] = jnp.concatenate(rows, axis=0) if own > 1 else rows[0]
        o_ref[u] = held[u].astype(BF16)

    each(units, one_unit)
    groups = LANES // width
    for g in range(units // groups):
        for e in range(blocks // groups):
            tiles = [
                held[groups * g + i, :, e * LANES : (e + 1) * LANES] for i in range(groups)
            ]
            for j, tile in enumerate(exchange_lanes(tiles, width)):
                placed[groups * e + j, :, g * LANES : (g + 1) * LANES] = tile.astype(BF16)
    for k in range(blocks):
        out_ref[k] = placed[lax.bitwise_xor(b, k)]


def attend_back_body(
    own, size, blocks, ids_ref, info_ref, mask_ref, qkv_ref, o_ref, lse_ref, given, d_ref, up, delta, d_q,
    d_k, d_v,
):
    units = qkv_ref.shape[0]
    width = BLOCK // blocks
    b = ids_ref[1]
    factor = 1.0 / math.sqrt(size)
    scale = LOG2E * factor
    up[...] = jnp.zeros_like(up)
    groups = LANES // width
    for g in range(units // groups):
        for e in range(blocks // groups):
            tiles = [
                given[groups * e + j, :, g * LANES : (g + 1) * LANES].astype(F32)
                for j in range(groups)
            ]
            for i, tile in enumerate(exchange_lanes(tiles, width)):
                unit = groups * g + i
                slot = info_ref[0, unit]
                for h in range(own):
                    keep = mask_ref[slot, b * own + h].astype(F32)
                    kept = tile[h * size : (h + 1) * size] * keep
                    up[unit, h, 0:size, e * LANES : (e + 1) * LANES] = kept.astype(BF16)
                    mine = o_ref[unit, h * size : (h + 1) * size, e * LANES : (e + 1) * LANES]
                    delta[unit, h : h + 1, e * LANES : (e + 1) * LANES] = jnp.sum(
                        kept * mine.astype(F32), axis=0, keepdims=True
                    )
    d_q[...] = jnp.zeros_like(d_q)

    def one_unit(j):
        d_k[...] = jnp.zeros_like(d_k)
        d_v[...] = jnp.zeros_like(d_v)
        keys = [qkv_ref[j, :, (own + h) * LANES : (own + h + 1) * LANES] for h in range(own)]
        turned = [keys[h].astype(F32).T.astype(BF16) for h in range(own)]

        def some_blocks(i, count, carry):
            for h in range(own):
                at = (2 * own + h) * LANES
                values = qkv_ref[j, :, at : at + LANES]
                sum_k = sum_v = 0.0
                for n in range(count):
                    queries = qkv_ref[i + n, :, h * LANES : (h + 1) * LANES]
                    scores = nt(keys[h], queries) * scale
                    probs = jnp.exp2(scores - lse_ref[i + n, h : h + 1, :])
                    d_probs = nn(values, up[i + n, h])
                    d_scores = (probs * (d_probs - delta[i + n, h : h + 1, :])).astype(BF16)
                    sum_k = sum_k + nn(d_scores, queries)
                    sum_v = sum_v + nt(probs.astype(BF16), up[i + n, h])
                    d_q[i + n, h] += nn(turned[h], d_scores)
                d_k[h] += sum_k
                d_v[h] += sum_v
            return carry

        in_groups(info_ref[1, j], info_ref[2, j], (4, 2, 1), some_blocks, 0)
        for h in range(own):
            at = (own + h) * LANES
            d_ref[j, :, at : at + LANES] = (d_k[h] * factor).astype(BF16)
            at = (2 * own + h) * LANES
            d_ref[j, :, at : at + LANES] = d_v[h].astype(BF16)

    each(units, one_unit)

    def turn(i):
        for h in range(own):
            d_ref[i, :, h * LANES : (h + 1) * LANES] = (d_q[i, h].T * factor).astype(BF16)

    each(units, turn)


def project_body(shards, blocks, moves, mod_ref, x_ref, w_ref, p_ref, *refs):
    sources, refs = refs[: len(moves)], refs[len(moves) :]
    attn_ref, x1_ref, h_ref, om_ref = refs[:4]
    landed, (om_all, h_all, local, sent, got) = refs[4 : 4 + len(moves)], refs[4 + len(moves) :]
    f, b = lax.axis_index("fsdp"), lax.axis_index("blk")
    width = BLOCK // blocks
    size = x_ref.shape[1]
    routes = Routes(sent, got)
    greet_all(shards, blocks)
    for k in range(blocks - 1, 0, -1):
        routes.start(("om", k), p_ref.at[k], om_all.at[b], {"blk": flip(b, k)})
    for i, (first, high, k) in enumerate(moves):
        routes.start(("move", i), sources[i].at[first:high], landed[i], {"fsdp": flip(f, k)})
    om_all[b] = p_ref[0]
    for k in range(1, blocks):
        routes.arrive(("om", k), om_all.at[flip(b, k)])
    om = om_all[...].reshape(size, x_ref.shape[0])
    om_ref[...] = om
    weight = w_ref[...]
    attn_ref[...] = tn(om, weight)

    def one(u):
        rows = pl.ds(pl.multiple_of(u * width, width), width)
        gate, shift, scale = [mod_ref[pl.ds(u, 1), i * size : (i + 1) * size] for i in (2, 3, 4)]
        middle = x_ref[rows, :].astype(F32) + gate * attn_ref[rows, :]
        x1_ref[rows, :] = middle
        normed, _ = normal(middle)
        h_all[0, rows, :] = (normed * (1.0 + scale) + shift).astype(BF16)

    each(x_ref.shape[0] // width, one, 3)
    routes.start("h", h_all.at[0], h_all.at[1], {"blk": flip(b, 1)})
    routes.arrive("h", h_all.at[1])
    copy = pltpu.make_async_copy(h_all, h_ref, local.at[0])
    copy.start()
    for i in range(len(moves)):
        routes.arrive(("move", i), landed[i])
    routes.finish()
    copy.wait()


def ff_body(shards, step, sides, plan1, plan2, ids_ref, hot_ref, chan_ref, h_ref, dm_ref, *refs):
    w1_refs, refs = refs[: len(plan1)], refs[len(plan1) :]
    w2_refs, refs = refs[: len(plan2)], refs[len(plan2) :]
    f = ids_ref[0]
    mlp_m, mlp_o, dh_m, dh_o, g_ref, w1, w2, h, dm, turned, hid_s, du_s, mlp, dh, g1, g2, sems = refs
    total = h.shape[0]
    count = total // 2
    f_size, size = w2.shape
    blocks = f_size // size
    row1, row2 = size // shards, f_size // shards

    def up_part(ref, shard, low, high):
        block = low // size
        return ref.at[
            shard, block * row1 : (block + 1) * row1, low - block * size : high - block * size
        ]

    def down_part(ref, shard, low, high):
        at = blocks * row1 - shard * row2
        return ref.at[shard, at + low : at + high]

    def chunk(index):
        low, high = index * step, (index + 1) * step
        cols = [
            (max(low, i * size), min(high, (i + 1) * size))
            for i in range(blocks)
            if max(low, i * size) < min(high, (i + 1) * size)
        ]
        rows = [
            (i, max(low, i * row2), min(high, (i + 1) * row2))
            for i in range(shards)
            if max(low, i * row2) < min(high, (i + 1) * row2)
        ]
        return cols, rows

    used = [0]

    def begin(pairs):
        copies = fetch(pairs, sems, used[0])
        used[0] += len(copies)
        return copies

    waits = [
        begin(
            [
                (h_ref.at[0], h.at[0:count]),
                (h_ref.at[1], h.at[count:total]),
                (dm_ref.at[0], dm.at[0:count]),
                (dm_ref.at[1], dm.at[count:total]),
            ]
        )
    ]
    chunks = f_size // step
    pairs = [[] for _ in range(chunks)]
    for ref, (k, first) in zip(w1_refs, plan1):
        at = pl.ds(pl.multiple_of(lax.bitwise_xor(f, k) * row1, 16), row1)
        for i in range(ref.shape[0]):
            low = (first + i) * size
            pairs[low // step].append((ref.at[i], w1.at[at, low : low + size]))
    for ref, (k, first) in zip(w2_refs, plan2):
        at = pl.multiple_of(lax.bitwise_xor(f, k) * row2 + first, 16)
        pairs[0].append((ref, w2.at[pl.ds(at, ref.shape[0])]))
    waits += [begin(some) for some in pairs]
    for copy in waits[0]:
        copy.wait()
    for at in range(0, total, LANES):
        turned[:, at : at + LANES] = h[at : at + LANES, :].astype(F32).T.astype(BF16)
    hots = jnp.concatenate([hot_ref[side] for side in range(2)], axis=1).astype(BF16)
    left = []
    for index in range(chunks):
        for copy in waits[index + 1]:
            copy.wait()
        cols = slice(index * step, (index + 1) * step)
        up = w1[:, cols]
        down = w2[cols, :]
        chan = chan_ref[:, cols].astype(F32).astype(BF16)
        for side in range(sides):
            rows = slice(side * total // sides, (side + 1) * total // sides)
            keep = tn(hots[:, rows], chan)
            pre = nn(h[rows, :], up)
            inner = pre * pre
            bent = jnp.tanh(0.7978845608028654 * (pre + 0.044715 * inner * pre))
            half = 0.5 * (1.0 + bent)
            hid = (pre * half * keep).astype(BF16)
            slope = half + (0.5 * 0.7978845608028654) * pre * (1.0 - bent * bent) * (
                1.0 + (3.0 * 0.044715) * inner
            )
            back = nt(dm[rows, :], down)
            du = (slope * back * keep).astype(BF16)
            hid_s[rows, :] = hid
            du_s[rows, :] = du
            if index:
                mlp[rows, :] += nn(hid, down)
                dh[rows, :] += nt(du, up)
            else:
                mlp[rows, :] = nn(hid, down)
                dh[rows, :] = nt(du, up)
        g1[:, cols] = nn(turned[...], du_s[...]).astype(BF16)
        g2[cols, :] = tn(hid_s[...], dm[...]).astype(BF16)
        parts, rows = chunk(index)
        pairs = [
            (g1.at[shard * row1 : (shard + 1) * row1, lo:hi], up_part(g_ref, shard, lo, hi))
            for shard in range(shards)
            for lo, hi in parts
        ]
        pairs += [(g2.at[lo:hi], down_part(g_ref, shard, lo, hi)) for shard, lo, hi in rows]
        left += begin(pairs)
    mlp_m[...] = mlp[0:count, :]
    mlp_o[...] = mlp[count:total, :].astype(BF16)
    dh_m[...] = dh[0:count, :]
    dh_o[...] = dh[count:total, :].astype(BF16)
    for copy in left:
        copy.wait()


def middle_body(
    shards, blocks, mod_ref, mark_ref, x1_ref, c_ref, dh_ref, dho_ref, mlp_ref, mlpo_ref, attn_ref, om_ref,
    w_ref, perm_ref, up_ref, dx_ref, two_ref, gate_ref, r_ref, mine_ref, other_ref, dh_in, mlp_in, da, leave,
    up_all, held, grad, by_unit, w_s, mlp_s, attn_s, om_s, local, sent, got,
):
    f, b = lax.axis_index("fsdp"), lax.axis_index("blk")
    c = b % 2
    width = BLOCK // blocks
    count, size = x1_ref.shape
    units = count // width
    routes = Routes(sent, got)
    inside = fetch([(w_ref, w_s), (mlp_ref, mlp_s), (attn_ref, attn_s), (om_ref, om_s)], local)
    greet_all(shards, blocks)
    routes.start("dh", dho_ref, dh_in, {"blk": flip(b, 1)})
    routes.start("mlp", mlpo_ref, mlp_in, {"blk": flip(b, 1)})
    by_unit[...] = jnp.zeros_like(by_unit)
    routes.arrive("dh", dh_in)

    def one(u):
        rows = pl.ds(pl.multiple_of(u * width, width), width)
        gate = mod_ref[pl.ds(u, 1), 2 * size : 3 * size]
        scale = mod_ref[pl.ds(u, 1), 4 * size : 5 * size]
        normed, spread = normal(x1_ref[rows, :])
        grad = dh_ref[rows, :] + dh_in[rows, :].astype(F32)
        by_unit[pl.ds(u, 1), 0:size] = jnp.sum(grad, axis=0, keepdims=True)
        by_unit[pl.ds(u, 1), size : 2 * size] = jnp.sum(grad * normed, axis=0, keepdims=True)
        dx = c_ref[rows, :].astype(F32) + normal_back(grad * (1.0 + scale), normed, spread)
        dx_ref[rows, :] = dx
        da[rows, :] = (dx * gate).astype(BF16)

    each(units, one, 3)
    inside[0].wait()
    for k in range(blocks - 1, -1, -1):
        piece = nt(w_s[flip(b, k)], da[...]).astype(BF16)
        if k:
            leave[k] = piece
            routes.start(("up", k), leave.at[k], up_all.at[b], {"blk": flip(b, k)})
        else:
            up_all[b] = piece

    def over_slots(target):
        target[...] = lax.dot_general(
            mark_ref[:, : by_unit.shape[0]], by_unit[...], (((1,), (0,)), ((), ())), precision=HIGH,
            preferred_element_type=F32,
        )

    over_slots(two_ref)
    routes.arrive("mlp", mlp_in)
    for copy in inside[1:]:
        copy.wait()

    def two(u):
        rows = pl.ds(pl.multiple_of(u * width, width), width)
        gate = mod_ref[pl.ds(u, 1), 5 * size : 6 * size]
        mlp = mlp_s[rows, :] + mlp_in[rows, :].astype(F32)
        held[rows, :] = (x1_ref[rows, :] + gate * mlp).astype(BF16)
        by_unit[pl.ds(u, 1), 0:size] = jnp.sum(
            dx_ref[rows, :] * attn_s[rows, :], axis=0, keepdims=True
        )
        by_unit[pl.ds(u, 1), size : 2 * size] = jnp.sum(
            c_ref[rows, :].astype(F32) * mlp, axis=0, keepdims=True
        )

    each(units, two, 3)
    over_slots(gate_ref)
    r_ref[...] = tn(perm_ref[...], held[...]).astype(BF16)
    grad[...] = nn(om_s[...], da[...]).astype(BF16).reshape(grad.shape)
    for k in range(shards):
        base = 2 * flip(f, k)
        mine_ref[k] = grad[base + c]
        other_ref[k] = grad[base + 1 - c]
    for k in range(1, blocks):
        routes.arrive(("up", k), up_all.at[flip(b, k)])
    up_ref[...] = up_all[...]
    routes.finish()


def stream_back_body(
    shards, chips, heads, per, h_ref, gs_ref, d_ref, wh_ref, mod_ref, mine_ref, x_ref, dx_ref, perm_ref,
    gm_ref, o_ref, sum_ref, g_ref, go_ref, give, take, keep, came, h_s, acc, low, others, out_in, out_low,
    out_got, total, held, by_unit, local, sent, got,
):
    f, b = lax.axis_index("fsdp"), lax.axis_index("blk")
    z, c = b // 2, b % 2
    pair = b + 1 - 2 * c
    width = BLOCK // (2 * chips)
    units = d_ref.shape[0]
    count, size = x_ref.shape
    wide = wh_ref.shape[1]
    own = heads // (2 * chips)
    head_size = size // heads
    rows = low.shape[1]
    steps = units // per
    routes = Routes(sent, got)

    def load(i):
        return pltpu.make_async_copy(
            h_ref.at[pl.ds(i * per, per)], h_s.at[i % 2], local.at[i % 2]
        )

    load(0).start()
    greet(shards, chips)
    routes.start("out", gs_ref, out_in, {"blk": pair})

    def partial(device, target):
        at = pl.ds(pl.multiple_of(device * width, width), width)
        grads = d_ref[:, at, :].reshape(count, wide)
        for col in range(0, size, 3 * LANES):
            target[:, col : col + 3 * LANES] = nt(
                grads, wh_ref[col : col + 3 * LANES, :]
            ).astype(BF16)

    def route(side, t):
        if side == 0:
            chip = chips - 1 - t
            return chip, z < chip, z > 0
        return t, z > t, z < chips - 1

    def onward(side, t, chip, when):
        if side == 0:
            slot, to = chip, b + 2
        else:
            slot, to = chip + (chips - chip) * (z - 1 == chip).astype(I32), b - 2
        routes.start(("sum", side, t), keep.at[chip], came.at[slot], {"blk": to}, when)

    def join(chip, slot=None):
        value = keep[chip].astype(F32) + take[chip].astype(F32)
        if slot is not None:
            value = value + came[slot].astype(F32)
        keep[chip] = value.astype(BF16)

    for t in range(chips - 1):
        for side in range(2):
            chip, passes, inside = route(side, t)

            @pl.when(passes)
            def _():
                partial(chip * 2 + 1 - c, give.at[chip])

            routes.start(("pair", side, t), give.at[chip], take.at[chip], {"blk": pair}, passes)

            @pl.when(passes)
            def _():
                partial(chip * 2 + c, keep.at[chip])

            first = passes & jnp.logical_not(inside)
            routes.arrive(("pair", side, t), take.at[chip], first)

            pl.when(first)(lambda: join(chip))
            onward(side, t, chip, first)

    partial(z * 2 + 1 - c, give.at[z])
    routes.start(("pair", "own"), give.at[z], take.at[z], {"blk": pair})
    partial(z * 2 + c, keep.at[z])

    def gather(i):
        if i + 1 < steps:
            load(i + 1).start()
        load(i).wait()
        part = tn(
            h_s[i % 2].reshape(per * BLOCK, size),
            d_ref[i * per : (i + 1) * per].reshape(per * BLOCK, wide),
        )
        if i:
            acc[...] += part
        else:
            acc[...] = part

    for t in range(max(chips - 1, steps)):
        if t < steps:
            gather(t)
        if t == steps - 1:
            packed = jnp.concatenate(
                [acc[:, i * LANES : i * LANES + head_size] for i in range(3 * own)], axis=1
            )
            low[...] = packed.astype(BF16).reshape(low.shape)
            for k in range(1, shards):
                other = flip(f, k)
                routes.start(("grad", k), low.at[other], others.at[k], {"fsdp": other})
        if t == 0:
            routes.arrive("out", out_in)
            out_low[...] = (gm_ref[...].astype(F32) + out_in[...].astype(F32)).astype(BF16)
            for k in range(1, shards):
                routes.start(("out", k), out_low.at[k], out_got.at[k], {"fsdp": flip(f, k)})
        if t >= chips - 1:
            continue
        for near, side in ((True, 0), (True, 1), (False, 1), (False, 0)):
            chip, passes, inside = route(side, t)
            when = passes & inside & ((z < chips // 2) == near)
            routes.arrive(("pair", side, t), take.at[chip], when)
            routes.arrive(("sum", side, t), came.at[chip], when)
            pl.when(when)(lambda: join(chip, chip))
            onward(side, t, chip, when)

    grad, grad_out = low[f].astype(F32), out_low[0].astype(F32)
    for k in range(1, shards):
        routes.arrive(("grad", k), others.at[k])
        grad = grad + others[k].astype(F32)
        routes.arrive(("out", k), out_got.at[k])
        grad_out = grad_out + out_got[k].astype(F32)
    g_ref[...] = grad.astype(BF16)
    go_ref[...] = grad_out.astype(BF16)

    routes.arrive(("pair", "own"), take.at[z])
    total[...] = keep[z].astype(F32) + take[z].astype(F32)
    for t in range(chips - 1):
        for side in range(2):
            chip, _, inside = route(side, t)
            slot = chip if side == 0 else chips
            here = (z == chip) & inside
            routes.arrive(("sum", side, t), came.at[slot], here)

            @pl.when(here)
            def _():
                total[...] += came[slot].astype(F32)

    by_unit[...] = jnp.zeros_like(by_unit)

    def one(u):
        rows = pl.ds(pl.multiple_of(u * width, width), width)
        scale = mod_ref[pl.ds(u, 1), size : 2 * size]
        normed, spread = normal(x_ref[rows, :].astype(F32))
        grad = total[rows, :]
        by_unit[pl.ds(u, 1), 0:size] = jnp.sum(grad, axis=0, keepdims=True)
        by_unit[pl.ds(u, 1), size : 2 * size] = jnp.sum(grad * normed, axis=0, keepdims=True)
        dx = dx_ref[rows, :] + normal_back(grad * (1.0 + scale), normed, spread)
        held[rows, :] = dx.astype(BF16)

    each(units, one, 3)
    o_ref[...] = tn(perm_ref[...], held[...]).astype(BF16)
    sum_ref[...] = lax.dot_general(
        mine_ref[:, : by_unit.shape[0]], by_unit[...], (((1,), (0,)), ((), ())), precision=HIGH,
        preferred_element_type=F32,
    )
    routes.finish()


def finish_body(
    shards, chips, fc_ref, ada_ref, go_ref, gq_ref, one_ref, two_ref, gate_ref, cond_ref, tot_ref, gqa_ref,
    dm_ref, dc_ref, mine, up, inner_in, result, other, gq_all, sum_own, sum_pair, small, mods, conds, ada_s,
    local, sent, got,
):
    f, b = lax.axis_index("fsdp"), lax.axis_index("blk")
    z, c = b // 2, b % 2
    pair = b + 1 - 2 * c
    count = mine.shape[0]
    slots, wider = sum_own.shape
    size = wider // 6
    routes = Routes(sent, got)
    loads = fetch([(fc_ref, mine.at[0 : count - 1]), (ada_ref, ada_s)], local)
    greet(shards, chips)

    sum_own[:, 0 : 2 * size] = one_ref[...]
    sum_own[:, 2 * size : 3 * size] = gate_ref[:, 0:size]
    sum_own[:, 3 * size : 5 * size] = two_ref[...]
    sum_own[:, 5 * size : 6 * size] = gate_ref[:, size : 2 * size]
    routes.start("sum", sum_own, sum_pair, {"blk": pair})
    gq_all[b] = gq_ref[...]

    def line(side, s, send):
        away = s - 1 if send else s
        chip = z - away if side == 0 else z + away
        ahead = z + 1 < chips if side == 0 else z > 0
        known = z >= away if side == 0 else z + away < chips
        return chip, {"blk": b + 2 if side == 0 else b - 2}, known & ahead if send else known

    def send(name, s, place):
        for side in range(2):
            chip, to, when = line(side, s, True)
            routes.start((name, side, s), place(chip), place(chip), to, when)

    def take(name, s, place):
        for side in range(2):
            chip, _, when = line(side, s, False)
            routes.arrive((name, side, s), place(chip), when)
        if s + 1 < chips:
            send(name, s + 1, place)

    def head(chip):
        return gq_all.at[chip * 2 + c]

    send("head", 1, head)
    routes.start("head pair", gq_all.at[b], gq_all.at[b], {"blk": pair})

    half = chips // 2
    right = z // half
    inner, outer = {"blk": b + 2 - 4 * right}, {"blk": b - 2 + 4 * right}
    ends = (z > 0) & (z < chips - 1)
    middle = (z == half - 1) | (z == half)
    edge = jnp.logical_not(middle)

    parts = [[small.at[i] for i in range(4)]]
    parts += [[ref.at[i] for ref in (mine, up, inner_in, result)] for i in range(count)]
    count += 1

    def inward(i, when):
        own, above, within, _ = parts[i]
        routes.start(("up", i), own, above, inner, when & edge)
        routes.start(("across", i), own, within, inner, when & middle, ("in", i))

    mine[count - 2] = go_ref[...]
    routes.arrive("sum", sum_pair)
    total = sum_own[...] + sum_pair[...]
    small[0] = jnp.concatenate(
        [total[:, : 3 * size], total[:, 3 * size :]], axis=0
    ).astype(BF16)
    ahead = min(4, count)
    inward(0, jnp.logical_not(ends))
    loads[0].wait()
    for i in range(1, ahead):
        inward(i, jnp.logical_not(ends))

    def combine():
        mods[f, :, : 3 * size] = small[3, 0:slots].astype(F32)
        mods[f, :, 3 * size :] = small[3, slots : 2 * slots].astype(F32)
        for k in range(1, shards):
            routes.start(("mod", k), mods.at[f], mods.at[f], {"fsdp": flip(f, k)})

    def condition():
        for k in range(1, shards):
            routes.arrive(("mod", k), mods.at[flip(f, k)])
        dm_ref[...] = mods[...]
        loads[1].wait()
        grad = nt(mods[...].reshape(shards * slots, wider).astype(BF16), ada_s[...])
        values = cond_ref[...]
        gate = 1.0 / (1.0 + jnp.exp(-values))
        conds[f] = grad * (gate + values * gate * (1.0 - gate))
        for k in range(1, shards):
            routes.start(("cond", k), conds.at[f], conds.at[f], {"fsdp": flip(f, k)})

    def conditions():
        for k in range(1, shards):
            routes.arrive(("cond", k), conds.at[flip(f, k)])
        dc_ref[...] = conds[...]

    jobs = [combine, condition, conditions]
    heads = [lambda s=s: take("head", s, head) for s in range(1, chips)]

    def forward(i):
        own, above, _, _ = parts[i]
        routes.arrive(("up", i), above, ends)

        @pl.when(ends)
        def _():
            own[...] = (own[...].astype(F32) + above[...].astype(F32)).astype(BF16)

        inward(i, ends)
        if i + ahead < count:
            inward(i + ahead, jnp.logical_not(ends))

    def back(i):
        own, _, within, full = parts[i]
        routes.arrive(("in", i), within)

        @pl.when(middle)
        def _():
            full[...] = (own[...].astype(F32) + within[...].astype(F32)).astype(BF16)

        @pl.when(edge)
        def _():
            full[...] = within[...]

        routes.start(("down", i), full, within, outer, ends, ("in", i))
        if i:
            routes.start(("pair", i - 1), full, other.at[i - 1], {"blk": pair})

    for i in range(count + 1):
        if i < count:
            forward(i)
        if i:
            back(i - 1)
            if jobs and i % 2 == 1:
                jobs.pop(0)()
            if heads and i % 2 == 0 and i > 2:
                heads.pop(0)()
    for job in jobs + heads:
        job()
    for s in range(1, chips):
        for side in range(2):
            chip, _, when = line(side, s, False)
            routes.start(("head pair", side, s), head(chip), head(chip), {"blk": pair}, when)
    copies = fetch([(result, tot_ref.at[c])], local)
    for i in range(count - 1):
        routes.arrive(("pair", i), other.at[i])
    copies += fetch([(other, tot_ref.at[1 - c])], local, 1)
    routes.arrive("head pair", gq_all.at[pair])
    for s in range(1, chips):
        for side in range(2):
            chip, _, when = line(side, s, False)
            routes.arrive(("head pair", side, s), gq_all.at[chip * 2 + 1 - c], when)
    copies += fetch([(gq_all, gqa_ref)], local, 2)
    routes.finish()
    for copy in copies:
        copy.wait()


def unfold_body(
    shards, low_ref, wave_ref, dm_ref, dc_ref, tot_ref, gq_ref, temb_ref, ada_ref, qkv_ref, out_ref,
    fc1_ref, fc2_ref, tot_s, gq_s, ada_s, qkv_s, out_s, fc1_s, fc2_s, loads, sems,
):
    _, count, rows, size = tot_ref.shape
    slots = dm_ref.shape[1]
    inside = fetch([(tot_ref, tot_s), (gq_ref, gq_s)], loads)
    copies = []

    def leave(source, target):
        copy = pltpu.make_async_copy(source, target, sems.at[len(copies)])
        copy.start()
        copies.append(copy)

    grads = dm_ref[...].reshape(shards * slots, -1).astype(BF16)
    ada_s[...] = tn(low_ref[...], grads)
    leave(ada_s, ada_ref)
    inside[0].wait()
    hidden = fc1_s.shape[1]
    part = hidden // shards // 2
    height = fc1_s.shape[0]
    blocks = hidden // 2 // size
    per = height // rows
    for core in range(2):
        for i in range(blocks * per):
            piece = tot_s[core, i].astype(F32)
            block, at = i // per, (i % per) * rows
            for j in range(size // part):
                column = (block * (size // part) + j) * 2 * part + core * part
                fc1_s[at : at + rows, column : column + part] = piece[:, j * part : (j + 1) * part]
        rest = count - 1 - blocks * per
        for i in range(rest):
            at = (core * rest + i) * rows
            fc2_s[at : at + rows, :] = tot_s[core, blocks * per + i].astype(F32)
        out_s[core * rows : (core + 1) * rows, :] = tot_s[core, count - 1].astype(F32)
    leave(fc1_s, fc1_ref)
    leave(fc2_s, fc2_ref)
    leave(out_s, out_ref)
    inside[1].wait()
    devices, _, packed = gq_ref.shape
    narrow = packed // 3
    for p in range(3):
        for i in range(devices):
            at = p * size + i * narrow
            qkv_s[:, at : at + narrow] = gq_s[i, :, p * narrow : (p + 1) * narrow].astype(F32)
    leave(qkv_s, qkv_ref)
    step = dc_ref.shape[2]
    for i in range(shards):
        temb_ref[:, i * step : (i + 1) * step] = lax.dot_general(
            wave_ref[...], dc_ref[i], (((0,), (0,)), ((), ())), precision=HIGH,
            preferred_element_type=F32,
        )
    for copy in copies:
        copy.wait()


def on_device(
    tokens,
    timesteps,
    segment_ids,
    head_mask,
    chan_mask,
    token_mask,
    w_temb,
    w_ada,
    w_qkv,
    w_out,
    w_fc1,
    w_fc2,
    cotangent,
):
    count, size = tokens.shape
    slots, heads = head_mask.shape[1:]
    head_size = size // heads
    shards, blocks = lax.axis_size("fsdp"), lax.axis_size("blk")
    chips = blocks // 2
    f, b = lax.axis_index("fsdp"), lax.axis_index("blk")
    c = b % 2
    width = BLOCK // blocks
    units = count // width
    own = heads // blocks
    wide = 3 * own * LANES
    hidden = w_fc1.shape[1]
    half = hidden // 2
    ids = jnp.stack([f, b, c]).astype(I32)

    near = 3 if shards == 4 else shards
    row1, row2 = w_fc1.shape[0], w_fc2.shape[0] // 2
    fc_blocks = half // size
    fc_rows = fc_blocks * row1 + row2

    items = lax.dynamic_slice_in_dim(segment_ids, b * count, count, axis=1)
    rows = w_temb.shape[0]
    entries = rows * shards
    spectrum = frequencies(timesteps[0], entries).astype(BF16).astype(F32)
    out_rows = w_out.shape[0] // 2
    ada_rows, wider = w_ada.shape
    padded = -(-units // 8) * 8
    n_copies = 9 * shards + 4 * chips + 8
    outs = run(
        "front",
        functools.partial(front_body, shards, chips, heads),
        [
            (VMEM, a)
            for a in (items, token_mask[None, :], tokens, cotangent, spectrum, w_temb)
        ]
        + [(ANY, a) for a in (w_ada, w_qkv, w_out.reshape(2, out_rows, size), w_fc1, w_fc2)],
        [
            (VMEM, shape((count, size))),
            (VMEM, shape((count, size))),
            (ANY, shape((2, slots, count), F32)),
            (VMEM, shape((8, LANES), I32)),
            (VMEM, shape((slots, LANES), F32)),
            (VMEM, shape((count, count))),
            (VMEM, shape((padded, wider), F32)),
            (VMEM, shape((shards * slots, ada_rows), F32)),
            (VMEM, shape((shards * slots, ada_rows))),
            (VMEM, shape((shards * slots, rows), F32)),
            (ANY, shape((2, count, size))),
            (ANY, shape((units, BLOCK, size))),
            (VMEM, shape((units, BLOCK, wide))),
            (VMEM, shape((size, wide))),
            (ANY, shape((shards, 2, out_rows, size))),
            (ANY, shape((row2, size))),
        ]
        + [(ANY, shape((fc_blocks, row1, size)))] * near,
        [
            pltpu.VMEM((blocks, count, size), BF16),
            pltpu.VMEM((shards, slots, entries), F32),
            pltpu.VMEM((shards, rows, size), BF16),
            pltpu.VMEM((shards, slots, wider), F32),
            pltpu.VMEM((shards, slots, wider), F32),
            pltpu.VMEM((2, slots, count), F32),
            pltpu.VMEM((2, count, size), BF16),
            pltpu.VMEM((shards, w_qkv.shape[0], 3 * own * head_size), BF16),
            pltpu.VMEM((shards, 2, out_rows, size), BF16),
            pltpu.VMEM((count, size), BF16),
            pltpu.VMEM(w_ada.shape, BF16),
            pltpu.VMEM(w_qkv.shape, BF16),
            pltpu.VMEM(w_fc1.shape, BF16),
            pltpu.VMEM((near, fc_blocks, row1, size), BF16),
            pltpu.SemaphoreType.DMA((units + 4 + near,)),
            pltpu.SemaphoreType.DMA((5,)),
            pltpu.SemaphoreType.DMA((n_copies,)),
            pltpu.SemaphoreType.DMA((n_copies,)),
        ],
        flops=2 * units * BLOCK * size * wide,
        collective=0,
    )
    x_s, c_s, hots, info, mark, perm, mod, condition, lifted, waves, dms = outs[:11]
    normed, qkv, w_heads, w_out_all, fc2_own = outs[11:16]
    fc1_near = outs[16:]
    fc1_parts = [(a, k, 0) for k, a in enumerate(fc1_near)]
    if shards == 4 and fc_blocks == 2:
        one, two = swap(fc2_own, "fsdp", 1), swap(fc2_own, "fsdp", 2)
        cut = row2 // 2
        fc2_parts = [(fc2_own, 0, 0), (one, 1, 0), (two, 2, 0)]
        moves = [
            (fc1_near[1], (0, 1, 2)),
            (fc1_near[2], (1, 2, 1)),
            (one, (0, cut, 2)),
            (two, (cut, row2, 1)),
        ]
    else:
        fc1_parts += [
            (swap(fc1_near[0], "fsdp", k), k, 0) for k in range(len(fc1_near), shards)
        ]
        moves = []
        fc2_parts = [(fc2_own, 0, 0)] + [(swap(fc2_own, "fsdp", k), k, 0) for k in range(1, shards)]
    w_out_all = w_out_all.reshape(size, size)

    mask = head_mask[0]
    narrow = own * head_size
    held, lse, pieces = run(
        "attend",
        functools.partial(attend_body, own, head_size, blocks),
        [(SMEM, ids), (SMEM, info), (SMEM, mask), (VMEM, qkv)],
        [
            (VMEM, shape((units, narrow, BLOCK))),
            (VMEM, shape((units, 8, BLOCK), F32)),
            (VMEM, shape((blocks, narrow, count))),
        ],
        [
            pltpu.VMEM((units, narrow, BLOCK), F32),
            pltpu.VMEM((units, own, -(-head_size // 16) * 16, BLOCK), BF16),
            pltpu.VMEM((blocks, narrow, count), BF16),
        ],
        flops=2 * units * units * BLOCK * BLOCK * wide // 3,
    )
    if moves:
        moved = lax.optimization_barrier(tuple(a for a, _ in moves) + (lse,))[:-1]
    else:
        moved = ()
    plan = [move for _, move in moves]
    n_copies = blocks + len(moves) + 1
    outs = run(
        "project",
        functools.partial(project_body, shards, blocks, plan),
        [(VMEM, a) for a in (mod, x_s, w_out_all, pieces)] + [(ANY, a) for a in moved],
        [
            (VMEM, shape((count, size), F32)),
            (VMEM, shape((count, size), F32)),
            (ANY, shape((2, count, size))),
            (VMEM, shape((size, count))),
        ]
        + [(ANY, shape((high - low,) + a.shape[1:])) for a, (low, high, _) in moves],
        [
            pltpu.VMEM((blocks, narrow, count), BF16),
            pltpu.VMEM((2, count, size), BF16),
            pltpu.SemaphoreType.DMA((1,)),
            pltpu.SemaphoreType.DMA((n_copies,)),
            pltpu.SemaphoreType.DMA((n_copies,)),
        ],
        flops=2 * count * size * size,
        collective=3,
    )
    attn, x1, h2, om = outs[:4]
    if moves:
        fc1_parts += [(outs[4], 3, 0), (outs[5], 3, 1)]
        fc2_parts += [(outs[6], 3, 0), (outs[7], 3, cut)]

    chan = chan_mask[0].reshape(slots, shards, 2, half // shards)
    chan = lax.dynamic_slice_in_dim(chan, c, 1, axis=2).reshape(slots, half)
    ff_step = 768
    n_sems = 4 + 4 * shards * (half // ff_step + 1)
    mlp, mlp_send, dh2, dh2_send, g_fc = run(
        "feed_forward",
        functools.partial(
            ff_body,
            shards,
            ff_step,
            2,
            [(k, first) for _, k, first in fc1_parts],
            [(k, first) for _, k, first in fc2_parts],
        ),
        [(SMEM, ids), (VMEM, hots), (VMEM, chan)]
        + [(ANY, a) for a in (h2, dms)]
        + [(ANY, a) for a, _, _ in fc1_parts + fc2_parts],
        [
            (VMEM, shape((count, size), F32)),
            (VMEM, shape((count, size))),
            (VMEM, shape((count, size), F32)),
            (VMEM, shape((count, size))),
            (ANY, shape((shards, fc_rows, size))),
        ],
        [
            pltpu.VMEM((size, half), BF16),
            pltpu.VMEM((half, size), BF16),
            pltpu.VMEM((2 * count, size), BF16),
            pltpu.VMEM((2 * count, size), BF16),
            pltpu.VMEM((size, 2 * count), BF16),
            pltpu.VMEM((2 * count, ff_step), BF16),
            pltpu.VMEM((2 * count, ff_step), BF16),
            pltpu.VMEM((2 * count, size), F32),
            pltpu.VMEM((2 * count, size), F32),
            pltpu.VMEM((size, half), BF16),
            pltpu.VMEM((half, size), BF16),
            pltpu.SemaphoreType.DMA((n_sems,)),
        ],
        flops=6 * 2 * 2 * count * size * half,
    )
    g_fc = lax.psum_scatter(
        g_fc.reshape(shards * fc_rows, size), "fsdp", scatter_dimension=0, tiled=True
    )

    n_copies = blocks + 2
    up_parts, dx1, sums_two, sums_gate, result, g_out, g_out_send = run(
        "middle_back",
        functools.partial(middle_body, shards, blocks),
        [(VMEM, a) for a in (mod, mark, x1, c_s, dh2)]
        + [(ANY, a) for a in (dh2_send, mlp, mlp_send, attn, om)]
        + [(ANY, w_out_all.reshape(blocks, narrow, size)), (VMEM, perm)],
        [
            (VMEM, shape((blocks, narrow, count))),
            (VMEM, shape((count, size), F32)),
            (VMEM, shape((slots, 2 * size), F32)),
            (VMEM, shape((slots, 2 * size), F32)),
            (VMEM, shape((count, size))),
            (VMEM, shape((shards, out_rows, size))),
            (VMEM, shape((shards, out_rows, size))),
        ],
        [
            pltpu.VMEM((count, size), BF16),
            pltpu.VMEM((count, size), BF16),
            pltpu.VMEM((count, size), BF16),
            pltpu.VMEM((blocks, narrow, count), BF16),
            pltpu.VMEM((blocks, narrow, count), BF16),
            pltpu.VMEM((count, size), BF16),
            pltpu.VMEM((2 * shards, out_rows, size), BF16),
            pltpu.VMEM((padded, 2 * size), F32),
            pltpu.VMEM((blocks, narrow, size), BF16),
            pltpu.VMEM((count, size), F32),
            pltpu.VMEM((count, size), F32),
            pltpu.VMEM((size, count), BF16),
            pltpu.SemaphoreType.DMA((4,)),
            pltpu.SemaphoreType.DMA((n_copies,)),
            pltpu.SemaphoreType.DMA((n_copies,)),
        ],
        flops=4 * count * size * size,
        collective=4,
    )

    (d_qkv,) = run(
        "attend_back",
        functools.partial(attend_back_body, own, head_size, blocks),
        [(SMEM, ids), (SMEM, info), (SMEM, mask)]
        + [(VMEM, a) for a in (qkv, held, lse, up_parts)],
        [(VMEM, shape((units, BLOCK, wide)))],
        [
            pltpu.VMEM((units, own, LANES, BLOCK), BF16),
            pltpu.VMEM((units, 8, BLOCK), F32),
            pltpu.VMEM((units, own, LANES, BLOCK), F32),
            pltpu.VMEM((own, BLOCK, LANES), F32),
            pltpu.VMEM((own, BLOCK, LANES), F32),
        ],
        flops=5 * units * units * BLOCK * BLOCK * wide // 3,
    )
    per = 4 if units % 4 == 0 else 1
    rows_qkv = w_qkv.shape[0]
    n_copies = 4 * chips + 2 * shards + 4
    grad_tokens, sums_one, g_qkv, g_out = run(
        "stream_back",
        functools.partial(stream_back_body, shards, chips, heads, per),
        [(ANY, normed), (ANY, g_out_send)]
        + [(VMEM, a) for a in (d_qkv, w_heads, mod, mark, x_s, dx1, perm, g_out)],
        [
            (VMEM, shape((count, size))),
            (VMEM, shape((slots, 2 * size), F32)),
            (VMEM, shape((rows_qkv, 3 * narrow))),
            (VMEM, shape((out_rows, size))),
        ],
        [
            pltpu.VMEM((chips, count, size), BF16),
            pltpu.VMEM((chips, count, size), BF16),
            pltpu.VMEM((chips, count, size), BF16),
            pltpu.VMEM((chips + 1, count, size), BF16),
            pltpu.VMEM((2, per, BLOCK, size), BF16),
            pltpu.VMEM((size, wide), F32),
            pltpu.VMEM((shards, rows_qkv, 3 * narrow), BF16),
            pltpu.VMEM((shards, rows_qkv, 3 * narrow), BF16),
            pltpu.VMEM((shards, out_rows, size), BF16),
            pltpu.VMEM((shards, out_rows, size), BF16),
            pltpu.VMEM((shards, out_rows, size), BF16),
            pltpu.VMEM((count, size), F32),
            pltpu.VMEM((count, size), BF16),
            pltpu.VMEM((padded, 2 * size), F32),
            pltpu.SemaphoreType.DMA((2,)),
            pltpu.SemaphoreType.DMA((n_copies,)),
            pltpu.SemaphoreType.DMA((n_copies,)),
        ],
        flops=4 * units * BLOCK * size * wide,
        collective=1,
    )

    pieces = fc_rows // out_rows
    n_copies = 5 * pieces + 16 + 4 * chips + 2 * shards
    totals, g_qkv, d_mod, d_cond = run(
        "finish",
        functools.partial(finish_body, shards, chips),
        [(ANY, g_fc.reshape(pieces, out_rows, size)), (ANY, w_ada)]
        + [(VMEM, a) for a in (g_out, g_qkv, sums_one, sums_two, sums_gate, condition)],
        [
            (ANY, shape((2, pieces + 1, out_rows, size))),
            (ANY, shape((blocks, rows_qkv, 3 * narrow))),
            (VMEM, shape((shards, slots, wider), F32)),
            (VMEM, shape((shards, shards * slots, ada_rows), F32)),
        ],
        [pltpu.VMEM((pieces + 1, out_rows, size), BF16)] * 5
        + [
            pltpu.VMEM((blocks, rows_qkv, 3 * narrow), BF16),
            pltpu.VMEM((slots, wider), F32),
            pltpu.VMEM((slots, wider), F32),
            pltpu.VMEM((4, 2 * slots, wider // 2), BF16),
            pltpu.VMEM((shards, slots, wider), F32),
            pltpu.VMEM((shards, shards * slots, ada_rows), F32),
            pltpu.VMEM(w_ada.shape, BF16),
            pltpu.SemaphoreType.DMA((3,)),
            pltpu.SemaphoreType.DMA((n_copies,)),
            pltpu.SemaphoreType.DMA((n_copies,)),
        ],
        collective=2,
    )
    grad_temb, grad_ada, grad_qkv, grad_out, grad_fc1, grad_fc2 = run(
        "unfold",
        functools.partial(unfold_body, shards),
        [(VMEM, a) for a in (lifted, waves, d_mod, d_cond)] + [(ANY, totals), (ANY, g_qkv)],
        [
            (VMEM, shape(w_temb.shape, F32)),
            (ANY, shape(w_ada.shape, F32)),
            (ANY, shape(w_qkv.shape, F32)),
            (ANY, shape(w_out.shape, F32)),
            (ANY, shape(w_fc1.shape, F32)),
            (ANY, shape(w_fc2.shape, F32)),
        ],
        [pltpu.VMEM(a.shape, BF16) for a in (totals, g_qkv)]
        + [pltpu.VMEM(a.shape, F32) for a in (w_ada, w_qkv, w_out, w_fc1, w_fc2)]
        + [pltpu.SemaphoreType.DMA((2,)), pltpu.SemaphoreType.DMA((5,))],
    )
    return (
        result,
        grad_tokens,
        grad_temb,
        grad_ada,
        grad_qkv,
        grad_out,
        grad_fc1,
        grad_fc2,
    )


def solution(mesh):
    placed = (
        P(("fsdp", "blk"), None),
        P("fsdp", None),
        P("fsdp", None),
        P("fsdp", None, None),
        P("fsdp", None, None),
        P(("fsdp", "blk")),
        P("fsdp", None),
        P("fsdp", None),
        P("fsdp", None),
        P("fsdp", None),
        P("fsdp", None),
        P("fsdp", None),
        P(("fsdp", "blk"), None),
    )
    return jax.shard_map(
        on_device,
        mesh=mesh,
        in_specs=placed,
        out_specs=(
            P(("fsdp", "blk"), None),
            P(("fsdp", "blk"), None),
            P("fsdp", None),
            P("fsdp", None),
            P("fsdp", None),
            P("fsdp", None),
            P("fsdp", None),
            P("fsdp", None),
        ),
        check_vma=False,
    )
```

```python
import functools
import math

import jax
import jax.numpy as jnp
from jax import lax
from jax.experimental import pallas as pl
from jax.experimental.pallas import tpu as pltpu
from jax.sharding import PartitionSpec as P

HIGH = lax.Precision.HIGHEST
BF16 = jnp.bfloat16
F32 = jnp.float32
I32 = jnp.int32
LANES = 128
BLOCK = 256
NEG = -1e30
LOG2E = 1.4426950408889634

VMEM = pl.BlockSpec(memory_space=pltpu.VMEM)
SMEM = pl.BlockSpec(memory_space=pltpu.SMEM)
ANY = pl.BlockSpec(memory_space=pl.ANY)


def shape(dims, kind=BF16):
    return jax.ShapeDtypeStruct(tuple(dims), kind)


def run(name, body, ins, outs, scratch=(), flops=0, vmem=62, collective=None, **more):
    moved = sum(a.size * a.dtype.itemsize for _, a in ins)
    moved += sum(math.prod(o.shape) * jnp.dtype(o.dtype).itemsize for _, o in outs)
    return pl.pallas_call(
        body,
        out_shape=[o for _, o in outs],
        in_specs=[s for s, _ in ins],
        out_specs=[s for s, _ in outs],
        scratch_shapes=list(scratch),
        compiler_params=pltpu.CompilerParams(
            vmem_limit_bytes=vmem << 20,
            collective_id=collective,
            has_side_effects=collective is not None,
        ),
        cost_estimate=pl.CostEstimate(flops=flops, bytes_accessed=moved, transcendentals=0),
        name=name,
        **more,
    )(*[a for _, a in ins])


def swap(array, axis, by):
    size = lax.axis_size(axis)
    return lax.ppermute(array, axis, [(i, i ^ by) for i in range(size)])


def frequencies(steps, entries):
    half = entries // 2
    ladder = jnp.exp(-math.log(10000.0) * lax.iota(jnp.int32, half) / half)
    angles = steps.astype(F32)[:, None] * ladder[None, :]
    return jnp.concatenate([jnp.cos(angles), jnp.sin(angles)], axis=1)


def nn(left, right):
    return lax.dot_general(left, right, (((1,), (0,)), ((), ())), preferred_element_type=F32)


def nt(left, right):
    return lax.dot_general(left, right, (((1,), (1,)), ((), ())), preferred_element_type=F32)


def tn(left, right):
    return lax.dot_general(left, right, (((0,), (0,)), ((), ())), preferred_element_type=F32)


def each(count, step, group=1):
    if count % group:
        group = 1

    def one(index, carry):
        for i in range(group):
            step(index * group + i)
        return carry

    lax.fori_loop(0, count // group, one, 0)


def normal(values):
    center = values - jnp.mean(values, axis=-1, keepdims=True)
    scale = lax.rsqrt(jnp.mean(center * center, axis=-1, keepdims=True) + 1e-06)
    return center * scale, scale


def normal_back(grad, normed, scale):
    along = jnp.mean(grad * normed, axis=-1, keepdims=True)
    return scale * (grad - jnp.mean(grad, axis=-1, keepdims=True) - normed * along)


def flip(index, by):
    bit = 1
    while bit <= by:
        if by & bit:
            index = index + bit * (1 - 2 * ((index // bit) % 2))
        bit *= 2
    return index


def fetch(pairs, sems, first=0):
    copies = []
    for index, (source, target) in enumerate(pairs, first):
        copy = pltpu.make_async_copy(source, target, sems.at[index])
        copy.start()
        copies.append(copy)
    return copies


class Routes:
    def __init__(self, sent, got):
        self.sent, self.got, self.known, self.started = sent, got, {}, []

    def slot(self, name):
        return self.known.setdefault(name, len(self.known))

    def copy(self, name, source, target, to, landed=None):
        return pltpu.make_async_remote_copy(
            src_ref=source,
            dst_ref=target,
            send_sem=self.sent.at[self.slot(name)],
            recv_sem=self.got.at[self.slot(landed or name)],
            device_id=to,
            device_id_type=pl.DeviceIdType.MESH,
        )

    def start(self, name, source, target, to, when=None, landed=None):
        def make():
            return self.copy(name, source, target, to, landed)

        self.started.append((make, when))
        if when is None:
            make().start()
        else:
            pl.when(when)(lambda: make().start())

    def arrive(self, name, target, when=None):
        def wait():
            b = lax.axis_index("blk")
            self.copy(name, target, target, {"blk": b + 1 - 2 * (b % 2)}).wait_recv()

        if when is None:
            wait()
        else:
            pl.when(when)(wait)

    def finish(self):
        for make, when in self.started:
            if when is None:
                make().wait_send()
            else:
                pl.when(when)(lambda make=make: make().wait_send())


def greet(shards, chips):
    f, b = lax.axis_index("fsdp"), lax.axis_index("blk")
    z, c = b // 2, b % 2
    barrier = pltpu.get_barrier_semaphore()

    def signal(to):
        pl.semaphore_signal(barrier, inc=1, device_id=to, device_id_type=pl.DeviceIdType.MESH)

    for k in range(1, shards):
        signal({"fsdp": flip(f, k)})
    signal({"blk": b + 1 - 2 * c})
    pl.when(z > 0)(lambda: signal({"blk": b - 2}))
    pl.when(z < chips - 1)(lambda: signal({"blk": b + 2}))
    ends = (z == 0).astype(I32) + (z == chips - 1).astype(I32)
    pl.semaphore_wait(barrier, shards + 2 - ends)


def greet_all(shards, blocks):
    f, b = lax.axis_index("fsdp"), lax.axis_index("blk")
    barrier = pltpu.get_barrier_semaphore()
    peers = [{"fsdp": flip(f, k)} for k in range(1, shards)]
    peers += [{"blk": flip(b, k)} for k in range(1, blocks)]
    for to in peers:
        pl.semaphore_signal(barrier, inc=1, device_id=to, device_id_type=pl.DeviceIdType.MESH)
    pl.semaphore_wait(barrier, len(peers))


def front_body(
    shards, chips, heads, items_ref, keep_ref, x_ref, c_ref, spec_ref, temb_ref, ada_ref, qkvw_ref,
    outw_ref, fc1w_ref, fc2w_ref, xs_ref, cs_ref, hot_ref, info_ref, mark_ref, perm_ref, mod_ref, cond_ref, low_ref, wave_ref, dm_ref, h_ref,
    qkv_ref, wh_ref, wo_ref, fc2_ref, *refs,
):
    fc_refs, refs = refs[:-19], refs[-19:]
    x_all, spec_all, temb_all, part_own, part_got, mod_all, hots, dms, wh_all, wo_all = refs[:10]
    h_all, ada_s, qkvw_s, fc1_s, fc_all, local, loads, sent, got = refs[10:]
    f, b = lax.axis_index("fsdp"), lax.axis_index("blk")
    z, c = b // 2, b % 2
    blocks = 2 * chips
    pair = b + 1 - 2 * c
    width = BLOCK // blocks
    count, size = x_ref.shape
    units = count // width
    own = heads // blocks
    head_size = size // heads
    slots = spec_ref.shape[0]
    routes = Routes(sent, got)
    down = fc2_ref.shape[0]
    inside = fetch(
        [
            (ada_ref, ada_s),
            (qkvw_ref, qkvw_s),
            (outw_ref, wo_all.at[f]),
            (fc1w_ref, fc1_s),
            (fc2w_ref.at[pl.ds(pl.multiple_of(c * down, 16), down)], fc2_ref),
        ],
        loads,
    )
    greet(shards, chips)

    spec_all[f] = spec_ref[...]
    temb_all[f] = temb_ref[...]
    for k in range(1, shards):
        to = {"fsdp": flip(f, k)}
        routes.start(("spec", k), spec_ref, spec_all.at[f], to)
        routes.start(("temb", k), temb_ref, temb_all.at[f], to)

    items = items_ref[...]
    slot = lax.broadcasted_iota(I32, (slots, count), 0)
    hot = (items == slot).astype(F32)
    start = jnp.sum((items < slot).astype(F32), axis=1, keepdims=True)
    end = start + jnp.sum(hot, axis=1, keepdims=True)
    row = lax.broadcasted_iota(I32, (count, count), 0)
    col = lax.broadcasted_iota(I32, (count, count), 1)
    rank = nn(hot.astype(BF16), (row <= col).astype(BF16))
    place = jnp.sum(hot * (start + rank), axis=0, keepdims=True) - 1.0
    perm = (row.astype(F32) == place).astype(BF16)
    perm_ref[...] = perm
    x_s = nn(perm, x_ref[...]).astype(BF16)
    xs_ref[...] = x_s
    x_all[b] = x_s

    def line(side, s, send):
        away = s - 1 if send else s
        chip = z - away if side == 0 else z + away
        ahead = z + 1 < chips if side == 0 else z > 0
        known = z >= away if side == 0 else z + away < chips
        when = known & ahead if send else known
        return chip * 2 + c, {"blk": b + 2 if side == 0 else b - 2}, when

    def send_on(s):
        for side in range(2):
            device, to, when = line(side, s, True)
            routes.start(("line", side, s), x_all.at[device], x_all.at[device], to, when)

    send_on(1)
    routes.start("pair", x_all.at[b], x_all.at[b], {"blk": pair})
    cs_ref[...] = nn(perm, c_ref[...]).astype(BF16)
    keep = jnp.broadcast_to(keep_ref[...].astype(F32), (slots, count)).astype(BF16)
    kept = nt(keep, perm)
    at = lax.broadcasted_iota(I32, (slots, count), 1).astype(F32)
    hots[0] = kept * ((at >= start) & (at < end)).astype(F32)
    first = (lax.broadcasted_iota(I32, (slots, LANES), 1) * width).astype(F32)
    mine = ((first >= start) & (first < end)).astype(F32)
    mark_ref[...] = mine
    which = lax.broadcasted_iota(I32, (slots, LANES), 0).astype(F32)
    info_ref[0:1, :] = jnp.sum(mine * which, axis=0, keepdims=True).astype(I32)
    info_ref[1:2, :] = (jnp.sum(mine * start, axis=0, keepdims=True) / width).astype(I32)
    info_ref[2:3, :] = (jnp.sum(mine * end, axis=0, keepdims=True) / width).astype(I32)
    info_ref[3:8, :] = jnp.zeros((5, LANES), I32)

    for k in range(1, shards):
        other = flip(f, k)
        routes.arrive(("spec", k), spec_all.at[other])
        routes.arrive(("temb", k), temb_all.at[other])
    spectra = spec_all[...].reshape(shards * slots, -1).astype(BF16)
    condition = nn(spectra, temb_all[...].reshape(-1, size))
    rows = ada_ref.shape[0]
    for shard in range(shards):

        @pl.when(f == shard)
        def _():
            cond_ref[...] = condition[:, shard * rows : (shard + 1) * rows]
            freqs = temb_ref.shape[0]
            wave_ref[...] = spectra[:, shard * freqs : (shard + 1) * freqs].astype(F32)

    values = cond_ref[...]
    lifted = (values / (1.0 + jnp.exp(-values))).astype(BF16)
    low_ref[...] = lifted
    inside[0].wait()
    for side in range(2):
        columns = slice(side * 3 * size, (side + 1) * 3 * size)
        found = nn(lifted, ada_s[:, columns])
        part_own[:, side] = found.reshape(shards, slots, 3 * size)
    for k in range(1, shards):
        other = flip(f, k)
        routes.start(("part", k), part_own.at[other, c], part_got.at[k], {"fsdp": other})

    rows = qkvw_ref.shape[0]
    inside[1].wait()
    narrow = own * head_size
    row = lax.broadcasted_iota(I32, (size, 2 * LANES), 0)
    col = lax.broadcasted_iota(I32, (size, 2 * LANES), 1)
    pick = ((row == b * narrow + col) & (col < narrow)).astype(F32).astype(BF16)
    wh_all[f] = jnp.concatenate(
        [
            nn(qkvw_s[:, part * size : (part + 1) * size], pick)[:, 0:narrow]
            for part in range(3)
        ],
        axis=1,
    ).astype(BF16)
    if shards == 4:
        for k in (1, 2):
            routes.start(("head", k), wh_all.at[f], wh_all.at[f], {"fsdp": flip(f, k)})
    else:
        for k in range(1, shards):
            routes.start(("head", k), wh_all.at[f], wh_all.at[f], {"fsdp": flip(f, k)})

    def take(s):
        for side in range(2):
            device, _, when = line(side, s, False)
            routes.arrive(("line", side, s), x_all.at[device], when)
            if s + 1 < chips:
                device, to, onward = line(side, s + 1, True)
                routes.start(
                    ("line", side, s + 1), x_all.at[device], x_all.at[device], to, onward
                )
            device, _, when = line(side, s, False)
            routes.start(
                ("pair", side, s), x_all.at[device], x_all.at[device], {"blk": pair}, when
            )

    take(1)
    if shards == 4:
        half = rows // 2
        for k, low in ((1, 0), (2, half)):
            routes.arrive(("head", k), wh_all.at[flip(f, k)])
            part = wh_all.at[flip(f, k), low : low + half]
            routes.start(("head", 3, k), part, part, {"fsdp": flip(f, 3 - k)})

    cut = size // (2 * LANES) * LANES
    for k in range(1, 3 if shards == 4 else shards):
        routes.start(("out", k), outw_ref.at[c], wo_all.at[f, c], {"fsdp": flip(f, k)})

    blocks_fc = fc_all.shape[1]
    part = fc1_s.shape[1] // shards // 2
    inside[3].wait()
    for core in range(2):

        @pl.when(c == core)
        def _():
            picked = jnp.concatenate(
                [
                    fc1_s[:, (2 * shard + core) * part : (2 * shard + core + 1) * part]
                    for shard in range(shards)
                ],
                axis=1,
            )
            for block_at in range(blocks_fc):
                fc_all[0, block_at] = picked[:, block_at * size : (block_at + 1) * size]

    for k in range(1, len(fc_refs)):
        routes.start(("fc", k), fc_all.at[0], fc_all.at[k], {"fsdp": flip(f, k)})

    total = part_own[f, c]
    for k in range(1, shards):
        routes.arrive(("part", k), part_got.at[k])
        total = total + part_got[k]
    mod_all[c] = total
    routes.start("mod", mod_all.at[c], mod_all.at[c], {"blk": pair})
    routes.arrive("mod", mod_all.at[1 - c])
    total = jnp.concatenate([mod_all[0], mod_all[1]], axis=1)
    mod_ref[...] = lax.dot_general(
        mine[:, : mod_ref.shape[0]], total, (((0,), (0,)), ((), ())), precision=HIGH,
        preferred_element_type=F32,
    )

    def early(u):
        rows = pl.ds(pl.multiple_of(u * width, width), width)
        gate = mod_ref[pl.ds(u, 1), 5 * size : 6 * size]
        dms[0, rows, :] = (cs_ref[rows, :].astype(F32) * gate).astype(BF16)

    each(units, early)
    routes.start("dm", dms.at[0], dms.at[1], {"blk": pair})
    routes.start("hot", hots.at[0], hots.at[1], {"blk": pair})

    if shards == 4:
        half = rows // 2
        routes.arrive(("head", 3, 1), wh_all.at[flip(f, 3), 0:half])
        routes.arrive(("head", 3, 2), wh_all.at[flip(f, 3), half:rows])
    else:
        for k in range(1, shards):
            routes.arrive(("head", k), wh_all.at[flip(f, k)])
    packed = wh_all[...].reshape(size, 3 * narrow)
    wh_ref[...] = jnp.zeros_like(wh_ref)
    for i in range(3 * own):
        wh_ref[:, i * LANES : i * LANES + head_size] = packed[
            :, i * head_size : (i + 1) * head_size
        ]

    def block(device):
        at = pl.ds(pl.multiple_of(device * width, width), width)

        def one(u):
            shift = mod_ref[pl.ds(u, 1), 0:size]
            scale = mod_ref[pl.ds(u, 1), size : 2 * size]
            part = x_all[device, pl.ds(pl.multiple_of(u * width, width), width), :]
            normed, _ = normal(part.astype(F32))
            low = (normed * (1.0 + scale) + shift).astype(BF16)
            h_all[pl.ds(pl.multiple_of(u * width, width), width), :] = low

        each(units, one, 3)
        copies = fetch(
            [
                (h_all.at[u * width : (u + 1) * width], h_ref.at[u, at])
                for u in range(units)
            ],
            local,
        )
        found = nn(h_all[...], wh_ref[...]).astype(BF16)
        qkv_ref[:, at, :] = found.reshape(units, width, found.shape[1])
        for copy in copies:
            copy.wait()

    routes.arrive("pair", x_all.at[pair])
    each(2, lambda core: block(z * 2 + core))

    def work(s):
        for side in range(2):
            device, _, when = line(side, s, False)
            routes.arrive(("pair", side, s), x_all.at[device + 1 - 2 * c], when)

        def pick(q):
            chip = z - s + 2 * s * (q // 2)

            @pl.when((chip >= 0) & (chip < chips))
            def _():
                block(chip * 2 + q % 2)

        each(4, pick)

    for s in range(2, chips):
        take(s)
        if s == 2:
            for k in range(1, 3 if shards == 4 else shards):
                other = flip(f, k)
                routes.arrive(("out", k), wo_all.at[other, c])
                if shards == 4:
                    columns = slice(0, cut) if k == 1 else slice(cut, size)
                    piece = wo_all.at[other, c, :, columns]
                    routes.start(("out", 3, k), piece, piece, {"fsdp": flip(f, 3 - k)})
                routes.start(
                    ("pair out", k), wo_all.at[other, c], wo_all.at[other, c], {"blk": pair}
                )
        work(s - 1)
    if shards == 4:
        other = flip(f, 3)
        routes.arrive(("out", 3, 1), wo_all.at[other, c, :, 0:cut])
        routes.arrive(("out", 3, 2), wo_all.at[other, c, :, cut:size])
        routes.start(("pair out", 3), wo_all.at[other, c], wo_all.at[other, c], {"blk": pair})
    work(chips - 1)
    inside[2].wait()
    for k in range(1, len(fc_refs)):
        routes.arrive(("fc", k), fc_all.at[k])
    inside[4].wait()
    for k in range(1, shards):
        routes.arrive(("pair out", k), wo_all.at[flip(f, k), 1 - c])
    routes.arrive("dm", dms.at[1])
    routes.arrive("hot", hots.at[1])
    routes.finish()
    copies = fetch(
        [(wo_all, wo_ref), (dms, dm_ref), (hots, hot_ref)]
        + [(fc_all.at[k], ref) for k, ref in enumerate(fc_refs)],
        local,
    )
    for copy in copies:
        copy.wait()


def exchange_lanes(tiles, width):
    tiles = list(tiles)
    count = len(tiles)
    group = lax.broadcasted_iota(I32, tiles[0].shape, 1) // width
    half = count // 2
    while half:
        low = (group // half) % 2 == 0
        fresh = list(tiles)
        for i in range(count):
            if (i // half) % 2 == 0:
                a, d = tiles[i], tiles[i + half]
                fresh[i] = jnp.where(low, a, pltpu.roll(d, half * width, 1))
                fresh[i + half] = jnp.where(low, pltpu.roll(a, LANES - half * width, 1), d)
        tiles = fresh
        half //= 2
    return tiles


def in_groups(first, last, sizes, step, carry):
    for size in sizes:
        count = (last - first) // size

        def one(index, carry, first=first, size=size):
            return step(first + index * size, size, carry)

        carry = lax.fori_loop(0, count, one, carry)
        first = first + count * size
    return carry


def attend_body(
    own, size, blocks, ids_ref, info_ref, mask_ref, qkv_ref, o_ref, lse_ref, out_ref, held, turned, placed
):
    units = qkv_ref.shape[0]
    width = BLOCK // blocks
    b = ids_ref[1]
    scale = LOG2E / math.sqrt(size)
    tall = turned.shape[2]

    def turn(j):
        for h in range(own):
            at = (2 * own + h) * LANES
            values = qkv_ref[j, :, at : at + LANES].astype(F32).T
            turned[j, h] = values[0:tall].astype(BF16)

    each(units, turn, 2)

    def one_unit(u):
        queries = [qkv_ref[u, :, h * LANES : (h + 1) * LANES] for h in range(own)]

        def some_blocks(j, count, carry):
            fresh = []
            for h in range(own):
                top, total, acc = carry[h]
                keys = qkv_ref[pl.ds(j, count), :, (own + h) * LANES : (own + h + 1) * LANES]
                scores = nt(keys.reshape(count * BLOCK, LANES), queries[h]) * scale
                new_top = jnp.maximum(top, jnp.max(scores, axis=0, keepdims=True))
                probs = jnp.exp2(scores - new_top)
                decay = jnp.exp2(top - new_top)
                total = total * decay + jnp.sum(probs, axis=0, keepdims=True)
                acc = acc * decay
                low = probs.astype(BF16)
                for i in range(count):
                    acc = acc + nn(turned[j + i, h], low[i * BLOCK : (i + 1) * BLOCK])
                fresh.append((new_top, total, acc))
            return tuple(fresh)

        start = tuple(
            (
                jnp.full((1, BLOCK), NEG, F32),
                jnp.zeros((1, BLOCK), F32),
                jnp.zeros((tall, BLOCK), F32),
            )
            for _ in range(own)
        )
        done = in_groups(info_ref[1, u], info_ref[2, u], (4, 2, 1), some_blocks, start)
        slot = info_ref[0, u]
        rows = []
        for h in range(own):
            top, total, acc = done[h]
            keep = mask_ref[slot, b * own + h].astype(F32)
            rows.append((acc * (keep / total))[0:size])
            lse_ref[u, h : h + 1, :] = top + jnp.log2(total)
        held[u] = jnp.concatenate(rows, axis=0) if own > 1 else rows[0]
        o_ref[u] = held[u].astype(BF16)

    each(units, one_unit)
    groups = LANES // width
    for g in range(units // groups):
        for e in range(blocks // groups):
            tiles = [
                held[groups * g + i, :, e * LANES : (e + 1) * LANES] for i in range(groups)
            ]
            for j, tile in enumerate(exchange_lanes(tiles, width)):
                placed[groups * e + j, :, g * LANES : (g + 1) * LANES] = tile.astype(BF16)
    for k in range(blocks):
        out_ref[k] = placed[lax.bitwise_xor(b, k)]


def attend_back_body(
    own, size, blocks, ids_ref, info_ref, mask_ref, qkv_ref, o_ref, lse_ref, given, d_ref, up, delta, d_q,
    d_k, d_v,
):
    units = qkv_ref.shape[0]
    width = BLOCK // blocks
    b = ids_ref[1]
    factor = 1.0 / math.sqrt(size)
    scale = LOG2E * factor
    up[...] = jnp.zeros_like(up)
    groups = LANES // width
    for g in range(units // groups):
        for e in range(blocks // groups):
            tiles = [
                given[groups * e + j, :, g * LANES : (g + 1) * LANES].astype(F32)
                for j in range(groups)
            ]
            for i, tile in enumerate(exchange_lanes(tiles, width)):
                unit = groups * g + i
                slot = info_ref[0, unit]
                for h in range(own):
                    keep = mask_ref[slot, b * own + h].astype(F32)
                    kept = tile[h * size : (h + 1) * size] * keep
                    up[unit, h, 0:size, e * LANES : (e + 1) * LANES] = kept.astype(BF16)
                    mine = o_ref[unit, h * size : (h + 1) * size, e * LANES : (e + 1) * LANES]
                    delta[unit, h : h + 1, e * LANES : (e + 1) * LANES] = jnp.sum(
                        kept * mine.astype(F32), axis=0, keepdims=True
                    )
    d_q[...] = jnp.zeros_like(d_q)

    def one_unit(j):
        d_k[...] = jnp.zeros_like(d_k)
        d_v[...] = jnp.zeros_like(d_v)
        keys = [qkv_ref[j, :, (own + h) * LANES : (own + h + 1) * LANES] for h in range(own)]
        turned = [keys[h].astype(F32).T.astype(BF16) for h in range(own)]

        def some_blocks(i, count, carry):
            for h in range(own):
                at = (2 * own + h) * LANES
                values = qkv_ref[j, :, at : at + LANES]
                sum_k = sum_v = 0.0
                for n in range(count):
                    queries = qkv_ref[i + n, :, h * LANES : (h + 1) * LANES]
                    scores = nt(keys[h], queries) * scale
                    probs = jnp.exp2(scores - lse_ref[i + n, h : h + 1, :])
                    d_probs = nn(values, up[i + n, h])
                    d_scores = (probs * (d_probs - delta[i + n, h : h + 1, :])).astype(BF16)
                    sum_k = sum_k + nn(d_scores, queries)
                    sum_v = sum_v + nt(probs.astype(BF16), up[i + n, h])
                    d_q[i + n, h] += nn(turned[h], d_scores)
                d_k[h] += sum_k
                d_v[h] += sum_v
            return carry

        in_groups(info_ref[1, j], info_ref[2, j], (4, 2, 1), some_blocks, 0)
        for h in range(own):
            at = (own + h) * LANES
            d_ref[j, :, at : at + LANES] = (d_k[h] * factor).astype(BF16)
            at = (2 * own + h) * LANES
            d_ref[j, :, at : at + LANES] = d_v[h].astype(BF16)

    each(units, one_unit)

    def turn(i):
        for h in range(own):
            d_ref[i, :, h * LANES : (h + 1) * LANES] = (d_q[i, h].T * factor).astype(BF16)

    each(units, turn)


def project_body(shards, blocks, moves, mod_ref, x_ref, w_ref, p_ref, *refs):
    sources, refs = refs[: len(moves)], refs[len(moves) :]
    attn_ref, x1_ref, h_ref, om_ref = refs[:4]
    landed, (om_all, h_all, local, sent, got) = refs[4 : 4 + len(moves)], refs[4 + len(moves) :]
    f, b = lax.axis_index("fsdp"), lax.axis_index("blk")
    width = BLOCK // blocks
    size = x_ref.shape[1]
    routes = Routes(sent, got)
    greet_all(shards, blocks)
    for k in range(blocks - 1, 0, -1):
        routes.start(("om", k), p_ref.at[k], om_all.at[b], {"blk": flip(b, k)})
    for i, (first, high, k) in enumerate(moves):
        routes.start(("move", i), sources[i].at[first:high], landed[i], {"fsdp": flip(f, k)})
    om_all[b] = p_ref[0]
    for k in range(1, blocks):
        routes.arrive(("om", k), om_all.at[flip(b, k)])
    om = om_all[...].reshape(size, x_ref.shape[0])
    om_ref[...] = om
    weight = w_ref[...]
    attn_ref[...] = tn(om, weight)

    def one(u):
        rows = pl.ds(pl.multiple_of(u * width, width), width)
        gate, shift, scale = [mod_ref[pl.ds(u, 1), i * size : (i + 1) * size] for i in (2, 3, 4)]
        middle = x_ref[rows, :].astype(F32) + gate * attn_ref[rows, :]
        x1_ref[rows, :] = middle
        normed, _ = normal(middle)
        h_all[0, rows, :] = (normed * (1.0 + scale) + shift).astype(BF16)

    each(x_ref.shape[0] // width, one, 3)
    routes.start("h", h_all.at[0], h_all.at[1], {"blk": flip(b, 1)})
    routes.arrive("h", h_all.at[1])
    copy = pltpu.make_async_copy(h_all, h_ref, local.at[0])
    copy.start()
    for i in range(len(moves)):
        routes.arrive(("move", i), landed[i])
    routes.finish()
    copy.wait()


def ff_body(shards, step, sides, plan1, plan2, ids_ref, hot_ref, chan_ref, h_ref, dm_ref, *refs):
    w1_refs, refs = refs[: len(plan1)], refs[len(plan1) :]
    w2_refs, refs = refs[: len(plan2)], refs[len(plan2) :]
    f = ids_ref[0]
    mlp_m, mlp_o, dh_m, dh_o, g_ref, w1, w2, h, dm, turned, hid_s, du_s, mlp, dh, g1, g2, sems = refs
    total = h.shape[0]
    count = total // 2
    f_size, size = w2.shape
    blocks = f_size // size
    row1, row2 = size // shards, f_size // shards

    def up_part(ref, shard, low, high):
        block = low // size
        return ref.at[
            shard, block * row1 : (block + 1) * row1, low - block * size : high - block * size
        ]

    def down_part(ref, shard, low, high):
        at = blocks * row1 - shard * row2
        return ref.at[shard, at + low : at + high]

    def chunk(index):
        low, high = index * step, (index + 1) * step
        cols = [
            (max(low, i * size), min(high, (i + 1) * size))
            for i in range(blocks)
            if max(low, i * size) < min(high, (i + 1) * size)
        ]
        rows = [
            (i, max(low, i * row2), min(high, (i + 1) * row2))
            for i in range(shards)
            if max(low, i * row2) < min(high, (i + 1) * row2)
        ]
        return cols, rows

    used = [0]

    def begin(pairs):
        copies = fetch(pairs, sems, used[0])
        used[0] += len(copies)
        return copies

    waits = [
        begin(
            [
                (h_ref.at[0], h.at[0:count]),
                (h_ref.at[1], h.at[count:total]),
                (dm_ref.at[0], dm.at[0:count]),
                (dm_ref.at[1], dm.at[count:total]),
            ]
        )
    ]
    chunks = f_size // step
    pairs = [[] for _ in range(chunks)]
    for ref, (k, first) in zip(w1_refs, plan1):
        at = pl.ds(pl.multiple_of(lax.bitwise_xor(f, k) * row1, 16), row1)
        for i in range(ref.shape[0]):
            low = (first + i) * size
            pairs[low // step].append((ref.at[i], w1.at[at, low : low + size]))
    for ref, (k, first) in zip(w2_refs, plan2):
        at = pl.multiple_of(lax.bitwise_xor(f, k) * row2 + first, 16)
        pairs[0].append((ref, w2.at[pl.ds(at, ref.shape[0])]))
    waits += [begin(some) for some in pairs]
    for copy in waits[0]:
        copy.wait()
    for at in range(0, total, LANES):
        turned[:, at : at + LANES] = h[at : at + LANES, :].astype(F32).T.astype(BF16)
    hots = jnp.concatenate([hot_ref[side] for side in range(2)], axis=1).astype(BF16)
    left = []
    for index in range(chunks):
        for copy in waits[index + 1]:
            copy.wait()
        cols = slice(index * step, (index + 1) * step)
        up = w1[:, cols]
        down = w2[cols, :]
        chan = chan_ref[:, cols].astype(F32).astype(BF16)
        for side in range(sides):
            rows = slice(side * total // sides, (side + 1) * total // sides)
            keep = tn(hots[:, rows], chan)
            pre = nn(h[rows, :], up)
            inner = pre * pre
            bent = jnp.tanh(0.7978845608028654 * (pre + 0.044715 * inner * pre))
            half = 0.5 * (1.0 + bent)
            hid = (pre * half * keep).astype(BF16)
            slope = half + (0.5 * 0.7978845608028654) * pre * (1.0 - bent * bent) * (
                1.0 + (3.0 * 0.044715) * inner
            )
            back = nt(dm[rows, :], down)
            du = (slope * back * keep).astype(BF16)
            hid_s[rows, :] = hid
            du_s[rows, :] = du
            if index:
                mlp[rows, :] += nn(hid, down)
                dh[rows, :] += nt(du, up)
            else:
                mlp[rows, :] = nn(hid, down)
                dh[rows, :] = nt(du, up)
        g1[:, cols] = nn(turned[...], du_s[...]).astype(BF16)
        g2[cols, :] = tn(hid_s[...], dm[...]).astype(BF16)
        parts, rows = chunk(index)
        pairs = [
            (g1.at[shard * row1 : (shard + 1) * row1, lo:hi], up_part(g_ref, shard, lo, hi))
            for shard in range(shards)
            for lo, hi in parts
        ]
        pairs += [(g2.at[lo:hi], down_part(g_ref, shard, lo, hi)) for shard, lo, hi in rows]
        left += begin(pairs)
    mlp_m[...] = mlp[0:count, :]
    mlp_o[...] = mlp[count:total, :].astype(BF16)
    dh_m[...] = dh[0:count, :]
    dh_o[...] = dh[count:total, :].astype(BF16)
    for copy in left:
        copy.wait()


def middle_body(
    shards, blocks, mod_ref, mark_ref, x1_ref, c_ref, dh_ref, dho_ref, mlp_ref, mlpo_ref, attn_ref, om_ref,
    w_ref, perm_ref, up_ref, dx_ref, two_ref, gate_ref, r_ref, mine_ref, other_ref, dh_in, mlp_in, da, leave,
    up_all, held, grad, by_unit, w_s, mlp_s, attn_s, om_s, local, sent, got,
):
    f, b = lax.axis_index("fsdp"), lax.axis_index("blk")
    c = b % 2
    width = BLOCK // blocks
    count, size = x1_ref.shape
    units = count // width
    routes = Routes(sent, got)
    inside = fetch([(w_ref, w_s), (mlp_ref, mlp_s), (attn_ref, attn_s), (om_ref, om_s)], local)
    greet_all(shards, blocks)
    routes.start("dh", dho_ref, dh_in, {"blk": flip(b, 1)})
    routes.start("mlp", mlpo_ref, mlp_in, {"blk": flip(b, 1)})
    by_unit[...] = jnp.zeros_like(by_unit)
    routes.arrive("dh", dh_in)

    def one(u):
        rows = pl.ds(pl.multiple_of(u * width, width), width)
        gate = mod_ref[pl.ds(u, 1), 2 * size : 3 * size]
        scale = mod_ref[pl.ds(u, 1), 4 * size : 5 * size]
        normed, spread = normal(x1_ref[rows, :])
        grad = dh_ref[rows, :] + dh_in[rows, :].astype(F32)
        by_unit[pl.ds(u, 1), 0:size] = jnp.sum(grad, axis=0, keepdims=True)
        by_unit[pl.ds(u, 1), size : 2 * size] = jnp.sum(grad * normed, axis=0, keepdims=True)
        dx = c_ref[rows, :].astype(F32) + normal_back(grad * (1.0 + scale), normed, spread)
        dx_ref[rows, :] = dx
        da[rows, :] = (dx * gate).astype(BF16)

    each(units, one, 3)
    inside[0].wait()
    for k in range(blocks - 1, -1, -1):
        piece = nt(w_s[flip(b, k)], da[...]).astype(BF16)
        if k:
            leave[k] = piece
            routes.start(("up", k), leave.at[k], up_all.at[b], {"blk": flip(b, k)})
        else:
            up_all[b] = piece

    def over_slots(target):
        target[...] = lax.dot_general(
            mark_ref[:, : by_unit.shape[0]], by_unit[...], (((1,), (0,)), ((), ())), precision=HIGH,
            preferred_element_type=F32,
        )

    over_slots(two_ref)
    routes.arrive("mlp", mlp_in)
    for copy in inside[1:]:
        copy.wait()

    def two(u):
        rows = pl.ds(pl.multiple_of(u * width, width), width)
        gate = mod_ref[pl.ds(u, 1), 5 * size : 6 * size]
        mlp = mlp_s[rows, :] + mlp_in[rows, :].astype(F32)
        held[rows, :] = (x1_ref[rows, :] + gate * mlp).astype(BF16)
        by_unit[pl.ds(u, 1), 0:size] = jnp.sum(
            dx_ref[rows, :] * attn_s[rows, :], axis=0, keepdims=True
        )
        by_unit[pl.ds(u, 1), size : 2 * size] = jnp.sum(
            c_ref[rows, :].astype(F32) * mlp, axis=0, keepdims=True
        )

    each(units, two, 3)
    over_slots(gate_ref)
    r_ref[...] = tn(perm_ref[...], held[...]).astype(BF16)
    grad[...] = nn(om_s[...], da[...]).astype(BF16).reshape(grad.shape)
    for k in range(shards):
        base = 2 * flip(f, k)
        mine_ref[k] = grad[base + c]
        other_ref[k] = grad[base + 1 - c]
    for k in range(1, blocks):
        routes.arrive(("up", k), up_all.at[flip(b, k)])
    up_ref[...] = up_all[...]
    routes.finish()


def stream_back_body(
    shards, chips, heads, per, h_ref, gs_ref, d_ref, wh_ref, mod_ref, mine_ref, x_ref, dx_ref, perm_ref,
    gm_ref, o_ref, sum_ref, g_ref, go_ref, give, take, keep, came, h_s, acc, low, others, out_in, out_low,
    out_got, total, held, by_unit, local, sent, got,
):
    f, b = lax.axis_index("fsdp"), lax.axis_index("blk")
    z, c = b // 2, b % 2
    pair = b + 1 - 2 * c
    width = BLOCK // (2 * chips)
    units = d_ref.shape[0]
    count, size = x_ref.shape
    wide = wh_ref.shape[1]
    own = heads // (2 * chips)
    head_size = size // heads
    rows = low.shape[1]
    steps = units // per
    routes = Routes(sent, got)

    def load(i):
        return pltpu.make_async_copy(
            h_ref.at[pl.ds(i * per, per)], h_s.at[i % 2], local.at[i % 2]
        )

    load(0).start()
    greet(shards, chips)
    routes.start("out", gs_ref, out_in, {"blk": pair})

    def partial(device, target):
        at = pl.ds(pl.multiple_of(device * width, width), width)
        grads = d_ref[:, at, :].reshape(count, wide)
        for col in range(0, size, 3 * LANES):
            target[:, col : col + 3 * LANES] = nt(
                grads, wh_ref[col : col + 3 * LANES, :]
            ).astype(BF16)

    def route(side, t):
        if side == 0:
            chip = chips - 1 - t
            return chip, z < chip, z > 0
        return t, z > t, z < chips - 1

    def onward(side, t, chip, when):
        if side == 0:
            slot, to = chip, b + 2
        else:
            slot, to = chip + (chips - chip) * (z - 1 == chip).astype(I32), b - 2
        routes.start(("sum", side, t), keep.at[chip], came.at[slot], {"blk": to}, when)

    def join(chip, slot=None):
        value = keep[chip].astype(F32) + take[chip].astype(F32)
        if slot is not None:
            value = value + came[slot].astype(F32)
        keep[chip] = value.astype(BF16)

    for t in range(chips - 1):
        for side in range(2):
            chip, passes, inside = route(side, t)

            @pl.when(passes)
            def _():
                partial(chip * 2 + 1 - c, give.at[chip])

            routes.start(("pair", side, t), give.at[chip], take.at[chip], {"blk": pair}, passes)

            @pl.when(passes)
            def _():
                partial(chip * 2 + c, keep.at[chip])

            first = passes & jnp.logical_not(inside)
            routes.arrive(("pair", side, t), take.at[chip], first)

            pl.when(first)(lambda: join(chip))
            onward(side, t, chip, first)

    partial(z * 2 + 1 - c, give.at[z])
    routes.start(("pair", "own"), give.at[z], take.at[z], {"blk": pair})
    partial(z * 2 + c, keep.at[z])

    def gather(i):
        if i + 1 < steps:
            load(i + 1).start()
        load(i).wait()
        part = tn(
            h_s[i % 2].reshape(per * BLOCK, size),
            d_ref[i * per : (i + 1) * per].reshape(per * BLOCK, wide),
        )
        if i:
            acc[...] += part
        else:
            acc[...] = part

    for t in range(max(chips - 1, steps)):
        if t < steps:
            gather(t)
        if t == steps - 1:
            packed = jnp.concatenate(
                [acc[:, i * LANES : i * LANES + head_size] for i in range(3 * own)], axis=1
            )
            low[...] = packed.astype(BF16).reshape(low.shape)
            for k in range(1, shards):
                other = flip(f, k)
                routes.start(("grad", k), low.at[other], others.at[k], {"fsdp": other})
        if t == 0:
            routes.arrive("out", out_in)
            out_low[...] = (gm_ref[...].astype(F32) + out_in[...].astype(F32)).astype(BF16)
            for k in range(1, shards):
                routes.start(("out", k), out_low.at[k], out_got.at[k], {"fsdp": flip(f, k)})
        if t >= chips - 1:
            continue
        for near, side in ((True, 0), (True, 1), (False, 1), (False, 0)):
            chip, passes, inside = route(side, t)
            when = passes & inside & ((z < chips // 2) == near)
            routes.arrive(("pair", side, t), take.at[chip], when)
            routes.arrive(("sum", side, t), came.at[chip], when)
            pl.when(when)(lambda: join(chip, chip))
            onward(side, t, chip, when)

    grad, grad_out = low[f].astype(F32), out_low[0].astype(F32)
    for k in range(1, shards):
        routes.arrive(("grad", k), others.at[k])
        grad = grad + others[k].astype(F32)
        routes.arrive(("out", k), out_got.at[k])
        grad_out = grad_out + out_got[k].astype(F32)
    g_ref[...] = grad.astype(BF16)
    go_ref[...] = grad_out.astype(BF16)

    routes.arrive(("pair", "own"), take.at[z])
    total[...] = keep[z].astype(F32) + take[z].astype(F32)
    for t in range(chips - 1):
        for side in range(2):
            chip, _, inside = route(side, t)
            slot = chip if side == 0 else chips
            here = (z == chip) & inside
            routes.arrive(("sum", side, t), came.at[slot], here)

            @pl.when(here)
            def _():
                total[...] += came[slot].astype(F32)

    by_unit[...] = jnp.zeros_like(by_unit)

    def one(u):
        rows = pl.ds(pl.multiple_of(u * width, width), width)
        scale = mod_ref[pl.ds(u, 1), size : 2 * size]
        normed, spread = normal(x_ref[rows, :].astype(F32))
        grad = total[rows, :]
        by_unit[pl.ds(u, 1), 0:size] = jnp.sum(grad, axis=0, keepdims=True)
        by_unit[pl.ds(u, 1), size : 2 * size] = jnp.sum(grad * normed, axis=0, keepdims=True)
        dx = dx_ref[rows, :] + normal_back(grad * (1.0 + scale), normed, spread)
        held[rows, :] = dx.astype(BF16)

    each(units, one, 3)
    o_ref[...] = tn(perm_ref[...], held[...]).astype(BF16)
    sum_ref[...] = lax.dot_general(
        mine_ref[:, : by_unit.shape[0]], by_unit[...], (((1,), (0,)), ((), ())), precision=HIGH,
        preferred_element_type=F32,
    )
    routes.finish()


def finish_body(
    shards, chips, fc_ref, ada_ref, go_ref, gq_ref, one_ref, two_ref, gate_ref, cond_ref, tot_ref, gqa_ref,
    dm_ref, dc_ref, mine, up, inner_in, result, other, gq_all, sum_own, sum_pair, small, mods, conds, ada_s,
    local, sent, got,
):
    f, b = lax.axis_index("fsdp"), lax.axis_index("blk")
    z, c = b // 2, b % 2
    pair = b + 1 - 2 * c
    count = mine.shape[0]
    slots, wider = sum_own.shape
    size = wider // 6
    routes = Routes(sent, got)
    loads = fetch([(fc_ref, mine.at[0 : count - 1]), (ada_ref, ada_s)], local)
    greet(shards, chips)

    sum_own[:, 0 : 2 * size] = one_ref[...]
    sum_own[:, 2 * size : 3 * size] = gate_ref[:, 0:size]
    sum_own[:, 3 * size : 5 * size] = two_ref[...]
    sum_own[:, 5 * size : 6 * size] = gate_ref[:, size : 2 * size]
    routes.start("sum", sum_own, sum_pair, {"blk": pair})
    gq_all[b] = gq_ref[...]

    def line(side, s, send):
        away = s - 1 if send else s
        chip = z - away if side == 0 else z + away
        ahead = z + 1 < chips if side == 0 else z > 0
        known = z >= away if side == 0 else z + away < chips
        return chip, {"blk": b + 2 if side == 0 else b - 2}, known & ahead if send else known

    def send(name, s, place):
        for side in range(2):
            chip, to, when = line(side, s, True)
            routes.start((name, side, s), place(chip), place(chip), to, when)

    def take(name, s, place):
        for side in range(2):
            chip, _, when = line(side, s, False)
            routes.arrive((name, side, s), place(chip), when)
        if s + 1 < chips:
            send(name, s + 1, place)

    def head(chip):
        return gq_all.at[chip * 2 + c]

    send("head", 1, head)
    routes.start("head pair", gq_all.at[b], gq_all.at[b], {"blk": pair})

    half = chips // 2
    right = z // half
    inner, outer = {"blk": b + 2 - 4 * right}, {"blk": b - 2 + 4 * right}
    ends = (z > 0) & (z < chips - 1)
    middle = (z == half - 1) | (z == half)
    edge = jnp.logical_not(middle)

    parts = [[small.at[i] for i in range(4)]]
    parts += [[ref.at[i] for ref in (mine, up, inner_in, result)] for i in range(count)]
    count += 1

    def inward(i, when):
        own, above, within, _ = parts[i]
        routes.start(("up", i), own, above, inner, when & edge)
        routes.start(("across", i), own, within, inner, when & middle, ("in", i))

    mine[count - 2] = go_ref[...]
    routes.arrive("sum", sum_pair)
    total = sum_own[...] + sum_pair[...]
    small[0] = jnp.concatenate(
        [total[:, : 3 * size], total[:, 3 * size :]], axis=0
    ).astype(BF16)
    ahead = min(4, count)
    inward(0, jnp.logical_not(ends))
    loads[0].wait()
    for i in range(1, ahead):
        inward(i, jnp.logical_not(ends))

    def combine():
        mods[f, :, : 3 * size] = small[3, 0:slots].astype(F32)
        mods[f, :, 3 * size :] = small[3, slots : 2 * slots].astype(F32)
        for k in range(1, shards):
            routes.start(("mod", k), mods.at[f], mods.at[f], {"fsdp": flip(f, k)})

    def condition():
        for k in range(1, shards):
            routes.arrive(("mod", k), mods.at[flip(f, k)])
        dm_ref[...] = mods[...]
        loads[1].wait()
        grad = nt(mods[...].reshape(shards * slots, wider).astype(BF16), ada_s[...])
        values = cond_ref[...]
        gate = 1.0 / (1.0 + jnp.exp(-values))
        conds[f] = grad * (gate + values * gate * (1.0 - gate))
        for k in range(1, shards):
            routes.start(("cond", k), conds.at[f], conds.at[f], {"fsdp": flip(f, k)})

    def conditions():
        for k in range(1, shards):
            routes.arrive(("cond", k), conds.at[flip(f, k)])
        dc_ref[...] = conds[...]

    jobs = [combine, condition, conditions]
    heads = [lambda s=s: take("head", s, head) for s in range(1, chips)]

    def forward(i):
        own, above, _, _ = parts[i]
        routes.arrive(("up", i), above, ends)

        @pl.when(ends)
        def _():
            own[...] = (own[...].astype(F32) + above[...].astype(F32)).astype(BF16)

        inward(i, ends)
        if i + ahead < count:
            inward(i + ahead, jnp.logical_not(ends))

    def back(i):
        own, _, within, full = parts[i]
        routes.arrive(("in", i), within)

        @pl.when(middle)
        def _():
            full[...] = (own[...].astype(F32) + within[...].astype(F32)).astype(BF16)

        @pl.when(edge)
        def _():
            full[...] = within[...]

        routes.start(("down", i), full, within, outer, ends, ("in", i))
        if i:
            routes.start(("pair", i - 1), full, other.at[i - 1], {"blk": pair})

    for i in range(count + 1):
        if i < count:
            forward(i)
        if i:
            back(i - 1)
            if jobs and i % 2 == 1:
                jobs.pop(0)()
            if heads and i % 2 == 0 and i > 2:
                heads.pop(0)()
    for job in jobs + heads:
        job()
    for s in range(1, chips):
        for side in range(2):
            chip, _, when = line(side, s, False)
            routes.start(("head pair", side, s), head(chip), head(chip), {"blk": pair}, when)
    copies = fetch([(result, tot_ref.at[c])], local)
    for i in range(count - 1):
        routes.arrive(("pair", i), other.at[i])
    copies += fetch([(other, tot_ref.at[1 - c])], local, 1)
    routes.arrive("head pair", gq_all.at[pair])
    for s in range(1, chips):
        for side in range(2):
            chip, _, when = line(side, s, False)
            routes.arrive(("head pair", side, s), gq_all.at[chip * 2 + 1 - c], when)
    copies += fetch([(gq_all, gqa_ref)], local, 2)
    routes.finish()
    for copy in copies:
        copy.wait()


def unfold_body(
    shards, low_ref, wave_ref, dm_ref, dc_ref, tot_ref, gq_ref, temb_ref, ada_ref, qkv_ref, out_ref,
    fc1_ref, fc2_ref, tot_s, gq_s, ada_s, qkv_s, out_s, fc1_s, fc2_s, loads, sems,
):
    _, count, rows, size = tot_ref.shape
    slots = dm_ref.shape[1]
    inside = fetch([(tot_ref, tot_s), (gq_ref, gq_s)], loads)
    copies = []

    def leave(source, target):
        copy = pltpu.make_async_copy(source, target, sems.at[len(copies)])
        copy.start()
        copies.append(copy)

    grads = dm_ref[...].reshape(shards * slots, -1).astype(BF16)
    ada_s[...] = tn(low_ref[...], grads)
    leave(ada_s, ada_ref)
    inside[0].wait()
    hidden = fc1_s.shape[1]
    part = hidden // shards // 2
    height = fc1_s.shape[0]
    blocks = hidden // 2 // size
    per = height // rows
    for core in range(2):
        for i in range(blocks * per):
            piece = tot_s[core, i].astype(F32)
            block, at = i // per, (i % per) * rows
            for j in range(size // part):
                column = (block * (size // part) + j) * 2 * part + core * part
                fc1_s[at : at + rows, column : column + part] = piece[:, j * part : (j + 1) * part]
        rest = count - 1 - blocks * per
        for i in range(rest):
            at = (core * rest + i) * rows
            fc2_s[at : at + rows, :] = tot_s[core, blocks * per + i].astype(F32)
        out_s[core * rows : (core + 1) * rows, :] = tot_s[core, count - 1].astype(F32)
    leave(fc1_s, fc1_ref)
    leave(fc2_s, fc2_ref)
    leave(out_s, out_ref)
    inside[1].wait()
    devices, _, packed = gq_ref.shape
    narrow = packed // 3
    for p in range(3):
        for i in range(devices):
            at = p * size + i * narrow
            qkv_s[:, at : at + narrow] = gq_s[i, :, p * narrow : (p + 1) * narrow].astype(F32)
    leave(qkv_s, qkv_ref)
    step = dc_ref.shape[2]
    for i in range(shards):
        temb_ref[:, i * step : (i + 1) * step] = lax.dot_general(
            wave_ref[...], dc_ref[i], (((0,), (0,)), ((), ())), precision=HIGH,
            preferred_element_type=F32,
        )
    for copy in copies:
        copy.wait()


def on_device(
    tokens,
    timesteps,
    segment_ids,
    head_mask,
    chan_mask,
    token_mask,
    w_temb,
    w_ada,
    w_qkv,
    w_out,
    w_fc1,
    w_fc2,
    cotangent,
):
    count, size = tokens.shape
    slots, heads = head_mask.shape[1:]
    head_size = size // heads
    shards, blocks = lax.axis_size("fsdp"), lax.axis_size("blk")
    chips = blocks // 2
    f, b = lax.axis_index("fsdp"), lax.axis_index("blk")
    c = b % 2
    width = BLOCK // blocks
    units = count // width
    own = heads // blocks
    wide = 3 * own * LANES
    hidden = w_fc1.shape[1]
    half = hidden // 2
    ids = jnp.stack([f, b, c]).astype(I32)

    near = 3 if shards == 4 else shards
    row1, row2 = w_fc1.shape[0], w_fc2.shape[0] // 2
    fc_blocks = half // size
    fc_rows = fc_blocks * row1 + row2

    items = lax.dynamic_slice_in_dim(segment_ids, b * count, count, axis=1)
    rows = w_temb.shape[0]
    entries = rows * shards
    spectrum = frequencies(timesteps[0], entries).astype(BF16).astype(F32)
    out_rows = w_out.shape[0] // 2
    ada_rows, wider = w_ada.shape
    padded = -(-units // 8) * 8
    n_copies = 9 * shards + 4 * chips + 12
    outs = run(
        "front",
        functools.partial(front_body, shards, chips, heads),
        [
            (VMEM, a)
            for a in (items, token_mask[None, :], tokens, cotangent, spectrum, w_temb)
        ]
        + [(ANY, a) for a in (w_ada, w_qkv, w_out.reshape(2, out_rows, size), w_fc1, w_fc2)],
        [
            (VMEM, shape((count, size))),
            (VMEM, shape((count, size))),
            (ANY, shape((2, slots, count), F32)),
            (VMEM, shape((8, LANES), I32)),
            (VMEM, shape((slots, LANES), F32)),
            (VMEM, shape((count, count))),
            (VMEM, shape((padded, wider), F32)),
            (VMEM, shape((shards * slots, ada_rows), F32)),
            (VMEM, shape((shards * slots, ada_rows))),
            (VMEM, shape((shards * slots, rows), F32)),
            (ANY, shape((2, count, size))),
            (ANY, shape((units, BLOCK, size))),
            (VMEM, shape((units, BLOCK, wide))),
            (VMEM, shape((size, wide))),
            (ANY, shape((shards, 2, out_rows, size))),
            (ANY, shape((row2, size))),
        ]
        + [(ANY, shape((fc_blocks, row1, size)))] * near,
        [
            pltpu.VMEM((blocks, count, size), BF16),
            pltpu.VMEM((shards, slots, entries), F32),
            pltpu.VMEM((shards, rows, size), BF16),
            pltpu.VMEM((shards, 2, slots, wider // 2), F32),
            pltpu.VMEM((shards, slots, wider // 2), F32),
            pltpu.VMEM((2, slots, wider // 2), F32),
            pltpu.VMEM((2, slots, count), F32),
            pltpu.VMEM((2, count, size), BF16),
            pltpu.VMEM((shards, w_qkv.shape[0], 3 * own * head_size), BF16),
            pltpu.VMEM((shards, 2, out_rows, size), BF16),
            pltpu.VMEM((count, size), BF16),
            pltpu.VMEM(w_ada.shape, BF16),
            pltpu.VMEM(w_qkv.shape, BF16),
            pltpu.VMEM(w_fc1.shape, BF16),
            pltpu.VMEM((near, fc_blocks, row1, size), BF16),
            pltpu.SemaphoreType.DMA((units + 4 + near,)),
            pltpu.SemaphoreType.DMA((5,)),
            pltpu.SemaphoreType.DMA((n_copies,)),
            pltpu.SemaphoreType.DMA((n_copies,)),
        ],
        flops=2 * units * BLOCK * size * wide,
        collective=0,
    )
    x_s, c_s, hots, info, mark, perm, mod, condition, lifted, waves, dms = outs[:11]
    normed, qkv, w_heads, w_out_all, fc2_own = outs[11:16]
    fc1_near = outs[16:]
    fc1_parts = [(a, k, 0) for k, a in enumerate(fc1_near)]
    if shards == 4 and fc_blocks == 2:
        one, two = swap(fc2_own, "fsdp", 1), swap(fc2_own, "fsdp", 2)
        cut = row2 // 2
        fc2_parts = [(fc2_own, 0, 0), (one, 1, 0), (two, 2, 0)]
        moves = [
            (fc1_near[1], (0, 1, 2)),
            (fc1_near[2], (1, 2, 1)),
            (one, (0, cut, 2)),
            (two, (cut, row2, 1)),
        ]
    else:
        fc1_parts += [
            (swap(fc1_near[0], "fsdp", k), k, 0) for k in range(len(fc1_near), shards)
        ]
        moves = []
        fc2_parts = [(fc2_own, 0, 0)] + [(swap(fc2_own, "fsdp", k), k, 0) for k in range(1, shards)]
    w_out_all = w_out_all.reshape(size, size)

    mask = head_mask[0]
    narrow = own * head_size
    held, lse, pieces = run(
        "attend",
        functools.partial(attend_body, own, head_size, blocks),
        [(SMEM, ids), (SMEM, info), (SMEM, mask), (VMEM, qkv)],
        [
            (VMEM, shape((units, narrow, BLOCK))),
            (VMEM, shape((units, 8, BLOCK), F32)),
            (VMEM, shape((blocks, narrow, count))),
        ],
        [
            pltpu.VMEM((units, narrow, BLOCK), F32),
            pltpu.VMEM((units, own, -(-head_size // 16) * 16, BLOCK), BF16),
            pltpu.VMEM((blocks, narrow, count), BF16),
        ],
        flops=2 * units * units * BLOCK * BLOCK * wide // 3,
    )
    if moves:
        moved = lax.optimization_barrier(tuple(a for a, _ in moves) + (lse,))[:-1]
    else:
        moved = ()
    plan = [move for _, move in moves]
    n_copies = blocks + len(moves) + 1
    outs = run(
        "project",
        functools.partial(project_body, shards, blocks, plan),
        [(VMEM, a) for a in (mod, x_s, w_out_all, pieces)] + [(ANY, a) for a in moved],
        [
            (VMEM, shape((count, size), F32)),
            (VMEM, shape((count, size), F32)),
            (ANY, shape((2, count, size))),
            (VMEM, shape((size, count))),
        ]
        + [(ANY, shape((high - low,) + a.shape[1:])) for a, (low, high, _) in moves],
        [
            pltpu.VMEM((blocks, narrow, count), BF16),
            pltpu.VMEM((2, count, size), BF16),
            pltpu.SemaphoreType.DMA((1,)),
            pltpu.SemaphoreType.DMA((n_copies,)),
            pltpu.SemaphoreType.DMA((n_copies,)),
        ],
        flops=2 * count * size * size,
        collective=3,
    )
    attn, x1, h2, om = outs[:4]
    if moves:
        fc1_parts += [(outs[4], 3, 0), (outs[5], 3, 1)]
        fc2_parts += [(outs[6], 3, 0), (outs[7], 3, cut)]

    chan = chan_mask[0].reshape(slots, shards, 2, half // shards)
    chan = lax.dynamic_slice_in_dim(chan, c, 1, axis=2).reshape(slots, half)
    ff_step = 768
    n_sems = 4 + 4 * shards * (half // ff_step + 1)
    mlp, mlp_send, dh2, dh2_send, g_fc = run(
        "feed_forward",
        functools.partial(
            ff_body,
            shards,
            ff_step,
            2,
            [(k, first) for _, k, first in fc1_parts],
            [(k, first) for _, k, first in fc2_parts],
        ),
        [(SMEM, ids), (VMEM, hots), (VMEM, chan)]
        + [(ANY, a) for a in (h2, dms)]
        + [(ANY, a) for a, _, _ in fc1_parts + fc2_parts],
        [
            (VMEM, shape((count, size), F32)),
            (VMEM, shape((count, size))),
            (VMEM, shape((count, size), F32)),
            (VMEM, shape((count, size))),
            (ANY, shape((shards, fc_rows, size))),
        ],
        [
            pltpu.VMEM((size, half), BF16),
            pltpu.VMEM((half, size), BF16),
            pltpu.VMEM((2 * count, size), BF16),
            pltpu.VMEM((2 * count, size), BF16),
            pltpu.VMEM((size, 2 * count), BF16),
            pltpu.VMEM((2 * count, ff_step), BF16),
            pltpu.VMEM((2 * count, ff_step), BF16),
            pltpu.VMEM((2 * count, size), F32),
            pltpu.VMEM((2 * count, size), F32),
            pltpu.VMEM((size, half), BF16),
            pltpu.VMEM((half, size), BF16),
            pltpu.SemaphoreType.DMA((n_sems,)),
        ],
        flops=6 * 2 * 2 * count * size * half,
    )
    g_fc = lax.psum_scatter(
        g_fc.reshape(shards * fc_rows, size), "fsdp", scatter_dimension=0, tiled=True
    )

    n_copies = blocks + 2
    up_parts, dx1, sums_two, sums_gate, result, g_out, g_out_send = run(
        "middle_back",
        functools.partial(middle_body, shards, blocks),
        [(VMEM, a) for a in (mod, mark, x1, c_s, dh2)]
        + [(ANY, a) for a in (dh2_send, mlp, mlp_send, attn, om)]
        + [(ANY, w_out_all.reshape(blocks, narrow, size)), (VMEM, perm)],
        [
            (VMEM, shape((blocks, narrow, count))),
            (VMEM, shape((count, size), F32)),
            (VMEM, shape((slots, 2 * size), F32)),
            (VMEM, shape((slots, 2 * size), F32)),
            (VMEM, shape((count, size))),
            (VMEM, shape((shards, out_rows, size))),
            (VMEM, shape((shards, out_rows, size))),
        ],
        [
            pltpu.VMEM((count, size), BF16),
            pltpu.VMEM((count, size), BF16),
            pltpu.VMEM((count, size), BF16),
            pltpu.VMEM((blocks, narrow, count), BF16),
            pltpu.VMEM((blocks, narrow, count), BF16),
            pltpu.VMEM((count, size), BF16),
            pltpu.VMEM((2 * shards, out_rows, size), BF16),
            pltpu.VMEM((padded, 2 * size), F32),
            pltpu.VMEM((blocks, narrow, size), BF16),
            pltpu.VMEM((count, size), F32),
            pltpu.VMEM((count, size), F32),
            pltpu.VMEM((size, count), BF16),
            pltpu.SemaphoreType.DMA((4,)),
            pltpu.SemaphoreType.DMA((n_copies,)),
            pltpu.SemaphoreType.DMA((n_copies,)),
        ],
        flops=4 * count * size * size,
        collective=4,
    )

    (d_qkv,) = run(
        "attend_back",
        functools.partial(attend_back_body, own, head_size, blocks),
        [(SMEM, ids), (SMEM, info), (SMEM, mask)]
        + [(VMEM, a) for a in (qkv, held, lse, up_parts)],
        [(VMEM, shape((units, BLOCK, wide)))],
        [
            pltpu.VMEM((units, own, LANES, BLOCK), BF16),
            pltpu.VMEM((units, 8, BLOCK), F32),
            pltpu.VMEM((units, own, LANES, BLOCK), F32),
            pltpu.VMEM((own, BLOCK, LANES), F32),
            pltpu.VMEM((own, BLOCK, LANES), F32),
        ],
        flops=5 * units * units * BLOCK * BLOCK * wide // 3,
    )
    per = 4 if units % 4 == 0 else 1
    rows_qkv = w_qkv.shape[0]
    n_copies = 4 * chips + 2 * shards + 4
    grad_tokens, sums_one, g_qkv, g_out = run(
        "stream_back",
        functools.partial(stream_back_body, shards, chips, heads, per),
        [(ANY, normed), (ANY, g_out_send)]
        + [(VMEM, a) for a in (d_qkv, w_heads, mod, mark, x_s, dx1, perm, g_out)],
        [
            (VMEM, shape((count, size))),
            (VMEM, shape((slots, 2 * size), F32)),
            (VMEM, shape((rows_qkv, 3 * narrow))),
            (VMEM, shape((out_rows, size))),
        ],
        [
            pltpu.VMEM((chips, count, size), BF16),
            pltpu.VMEM((chips, count, size), BF16),
            pltpu.VMEM((chips, count, size), BF16),
            pltpu.VMEM((chips + 1, count, size), BF16),
            pltpu.VMEM((2, per, BLOCK, size), BF16),
            pltpu.VMEM((size, wide), F32),
            pltpu.VMEM((shards, rows_qkv, 3 * narrow), BF16),
            pltpu.VMEM((shards, rows_qkv, 3 * narrow), BF16),
            pltpu.VMEM((shards, out_rows, size), BF16),
            pltpu.VMEM((shards, out_rows, size), BF16),
            pltpu.VMEM((shards, out_rows, size), BF16),
            pltpu.VMEM((count, size), F32),
            pltpu.VMEM((count, size), BF16),
            pltpu.VMEM((padded, 2 * size), F32),
            pltpu.SemaphoreType.DMA((2,)),
            pltpu.SemaphoreType.DMA((n_copies,)),
            pltpu.SemaphoreType.DMA((n_copies,)),
        ],
        flops=4 * units * BLOCK * size * wide,
        collective=1,
    )

    pieces = fc_rows // out_rows
    n_copies = 5 * pieces + 16 + 4 * chips + 2 * shards
    totals, g_qkv, d_mod, d_cond = run(
        "finish",
        functools.partial(finish_body, shards, chips),
        [(ANY, g_fc.reshape(pieces, out_rows, size)), (ANY, w_ada)]
        + [(VMEM, a) for a in (g_out, g_qkv, sums_one, sums_two, sums_gate, condition)],
        [
            (ANY, shape((2, pieces + 1, out_rows, size))),
            (ANY, shape((blocks, rows_qkv, 3 * narrow))),
            (VMEM, shape((shards, slots, wider), F32)),
            (VMEM, shape((shards, shards * slots, ada_rows), F32)),
        ],
        [pltpu.VMEM((pieces + 1, out_rows, size), BF16)] * 5
        + [
            pltpu.VMEM((blocks, rows_qkv, 3 * narrow), BF16),
            pltpu.VMEM((slots, wider), F32),
            pltpu.VMEM((slots, wider), F32),
            pltpu.VMEM((4, 2 * slots, wider // 2), BF16),
            pltpu.VMEM((shards, slots, wider), F32),
            pltpu.VMEM((shards, shards * slots, ada_rows), F32),
            pltpu.VMEM(w_ada.shape, BF16),
            pltpu.SemaphoreType.DMA((3,)),
            pltpu.SemaphoreType.DMA((n_copies,)),
            pltpu.SemaphoreType.DMA((n_copies,)),
        ],
        collective=2,
    )
    grad_temb, grad_ada, grad_qkv, grad_out, grad_fc1, grad_fc2 = run(
        "unfold",
        functools.partial(unfold_body, shards),
        [(VMEM, a) for a in (lifted, waves, d_mod, d_cond)] + [(ANY, totals), (ANY, g_qkv)],
        [
            (VMEM, shape(w_temb.shape, F32)),
            (ANY, shape(w_ada.shape, F32)),
            (ANY, shape(w_qkv.shape, F32)),
            (ANY, shape(w_out.shape, F32)),
            (ANY, shape(w_fc1.shape, F32)),
            (ANY, shape(w_fc2.shape, F32)),
        ],
        [pltpu.VMEM(a.shape, BF16) for a in (totals, g_qkv)]
        + [pltpu.VMEM(a.shape, F32) for a in (w_ada, w_qkv, w_out, w_fc1, w_fc2)]
        + [pltpu.SemaphoreType.DMA((2,)), pltpu.SemaphoreType.DMA((5,))],
    )
    return (
        result,
        grad_tokens,
        grad_temb,
        grad_ada,
        grad_qkv,
        grad_out,
        grad_fc1,
        grad_fc2,
    )


def solution(mesh):
    placed = (
        P(("fsdp", "blk"), None),
        P("fsdp", None),
        P("fsdp", None),
        P("fsdp", None, None),
        P("fsdp", None, None),
        P(("fsdp", "blk")),
        P("fsdp", None),
        P("fsdp", None),
        P("fsdp", None),
        P("fsdp", None),
        P("fsdp", None),
        P("fsdp", None),
        P(("fsdp", "blk"), None),
    )
    return jax.shard_map(
        on_device,
        mesh=mesh,
        in_specs=placed,
        out_specs=(
            P(("fsdp", "blk"), None),
            P(("fsdp", "blk"), None),
            P("fsdp", None),
            P("fsdp", None),
            P("fsdp", None),
            P("fsdp", None),
            P("fsdp", None),
            P("fsdp", None),
        ),
        check_vma=False,
    )
```

```python
import functools
import math

import jax
import jax.numpy as jnp
from jax import lax
from jax.experimental import pallas as pl
from jax.experimental.pallas import tpu as pltpu
from jax.sharding import PartitionSpec as P

HIGH = lax.Precision.HIGHEST
BF16 = jnp.bfloat16
F32 = jnp.float32
I32 = jnp.int32
LANES = 128
BLOCK = 256
NEG = -1e30
LOG2E = 1.4426950408889634

VMEM = pl.BlockSpec(memory_space=pltpu.VMEM)
SMEM = pl.BlockSpec(memory_space=pltpu.SMEM)
ANY = pl.BlockSpec(memory_space=pl.ANY)


def shape(dims, kind=BF16):
    return jax.ShapeDtypeStruct(tuple(dims), kind)


def run(name, body, ins, outs, scratch=(), flops=0, vmem=62, collective=None, **more):
    moved = sum(a.size * a.dtype.itemsize for _, a in ins)
    moved += sum(math.prod(o.shape) * jnp.dtype(o.dtype).itemsize for _, o in outs)
    return pl.pallas_call(
        body,
        out_shape=[o for _, o in outs],
        in_specs=[s for s, _ in ins],
        out_specs=[s for s, _ in outs],
        scratch_shapes=list(scratch),
        compiler_params=pltpu.CompilerParams(
            vmem_limit_bytes=vmem << 20,
            collective_id=collective,
            has_side_effects=collective is not None,
        ),
        cost_estimate=pl.CostEstimate(flops=flops, bytes_accessed=moved, transcendentals=0),
        name=name,
        **more,
    )(*[a for _, a in ins])


def swap(array, axis, by):
    size = lax.axis_size(axis)
    return lax.ppermute(array, axis, [(i, i ^ by) for i in range(size)])


def frequencies(steps, entries):
    half = entries // 2
    ladder = jnp.exp(-math.log(10000.0) * lax.iota(jnp.int32, half) / half)
    angles = steps.astype(F32)[:, None] * ladder[None, :]
    return jnp.concatenate([jnp.cos(angles), jnp.sin(angles)], axis=1)


def nn(left, right):
    return lax.dot_general(left, right, (((1,), (0,)), ((), ())), preferred_element_type=F32)


def nt(left, right):
    return lax.dot_general(left, right, (((1,), (1,)), ((), ())), preferred_element_type=F32)


def tn(left, right):
    return lax.dot_general(left, right, (((0,), (0,)), ((), ())), preferred_element_type=F32)


def each(count, step, group=1):
    if count % group:
        group = 1

    def one(index, carry):
        for i in range(group):
            step(index * group + i)
        return carry

    lax.fori_loop(0, count // group, one, 0)


def normal(values):
    center = values - jnp.mean(values, axis=-1, keepdims=True)
    scale = lax.rsqrt(jnp.mean(center * center, axis=-1, keepdims=True) + 1e-06)
    return center * scale, scale


def normal_back(grad, normed, scale):
    along = jnp.mean(grad * normed, axis=-1, keepdims=True)
    return scale * (grad - jnp.mean(grad, axis=-1, keepdims=True) - normed * along)


def flip(index, by):
    bit = 1
    while bit <= by:
        if by & bit:
            index = index + bit * (1 - 2 * ((index // bit) % 2))
        bit *= 2
    return index


def fetch(pairs, sems, first=0):
    copies = []
    for index, (source, target) in enumerate(pairs, first):
        copy = pltpu.make_async_copy(source, target, sems.at[index])
        copy.start()
        copies.append(copy)
    return copies


class Routes:
    def __init__(self, sent, got):
        self.sent, self.got, self.known, self.started = sent, got, {}, []

    def slot(self, name):
        return self.known.setdefault(name, len(self.known))

    def copy(self, name, source, target, to, landed=None):
        return pltpu.make_async_remote_copy(
            src_ref=source,
            dst_ref=target,
            send_sem=self.sent.at[self.slot(name)],
            recv_sem=self.got.at[self.slot(landed or name)],
            device_id=to,
            device_id_type=pl.DeviceIdType.MESH,
        )

    def start(self, name, source, target, to, when=None, landed=None):
        def make():
            return self.copy(name, source, target, to, landed)

        self.started.append((make, when))
        if when is None:
            make().start()
        else:
            pl.when(when)(lambda: make().start())

    def arrive(self, name, target, when=None):
        def wait():
            b = lax.axis_index("blk")
            self.copy(name, target, target, {"blk": b + 1 - 2 * (b % 2)}).wait_recv()

        if when is None:
            wait()
        else:
            pl.when(when)(wait)

    def finish(self):
        for make, when in self.started:
            if when is None:
                make().wait_send()
            else:
                pl.when(when)(lambda make=make: make().wait_send())


def greet(shards, chips):
    f, b = lax.axis_index("fsdp"), lax.axis_index("blk")
    z, c = b // 2, b % 2
    barrier = pltpu.get_barrier_semaphore()

    def signal(to):
        pl.semaphore_signal(barrier, inc=1, device_id=to, device_id_type=pl.DeviceIdType.MESH)

    for k in range(1, shards):
        signal({"fsdp": flip(f, k)})
    signal({"blk": b + 1 - 2 * c})
    pl.when(z > 0)(lambda: signal({"blk": b - 2}))
    pl.when(z < chips - 1)(lambda: signal({"blk": b + 2}))
    ends = (z == 0).astype(I32) + (z == chips - 1).astype(I32)
    pl.semaphore_wait(barrier, shards + 2 - ends)


def greet_all(shards, blocks):
    f, b = lax.axis_index("fsdp"), lax.axis_index("blk")
    barrier = pltpu.get_barrier_semaphore()
    peers = [{"fsdp": flip(f, k)} for k in range(1, shards)]
    peers += [{"blk": flip(b, k)} for k in range(1, blocks)]
    for to in peers:
        pl.semaphore_signal(barrier, inc=1, device_id=to, device_id_type=pl.DeviceIdType.MESH)
    pl.semaphore_wait(barrier, len(peers))


def front_body(
    shards, chips, heads, items_ref, keep_ref, x_ref, c_ref, spec_ref, temb_ref, ada_ref, qkvw_ref,
    outw_ref, fc1w_ref, fc2w_ref, xs_ref, cs_ref, hot_ref, info_ref, mark_ref, perm_ref, mod_ref, cond_ref, low_ref, wave_ref, dm_ref, h_ref,
    qkv_ref, wh_ref, wo_ref, fc2_ref, *refs,
):
    fc_refs, refs = refs[:-19], refs[-19:]
    x_all, spec_all, temb_all, part_own, part_got, mod_all, hots, dms, wh_all, wo_all = refs[:10]
    h_all, ada_s, qkvw_s, fc1_s, fc_all, local, loads, sent, got = refs[10:]
    f, b = lax.axis_index("fsdp"), lax.axis_index("blk")
    z, c = b // 2, b % 2
    blocks = 2 * chips
    pair = b + 1 - 2 * c
    width = BLOCK // blocks
    count, size = x_ref.shape
    units = count // width
    own = heads // blocks
    head_size = size // heads
    slots = spec_ref.shape[0]
    routes = Routes(sent, got)
    down = fc2_ref.shape[0]
    inside = fetch(
        [
            (ada_ref, ada_s),
            (qkvw_ref, qkvw_s),
            (outw_ref, wo_all.at[f]),
            (fc1w_ref, fc1_s),
            (fc2w_ref.at[pl.ds(pl.multiple_of(c * down, 16), down)], fc2_ref),
        ],
        loads,
    )
    greet(shards, chips)

    spec_all[f] = spec_ref[...]
    temb_all[f] = temb_ref[...]
    for k in range(1, shards):
        to = {"fsdp": flip(f, k)}
        routes.start(("spec", k), spec_ref, spec_all.at[f], to)
        routes.start(("temb", k), temb_ref, temb_all.at[f], to)

    items = items_ref[...]
    slot = lax.broadcasted_iota(I32, (slots, count), 0)
    hot = (items == slot).astype(F32)
    start = jnp.sum((items < slot).astype(F32), axis=1, keepdims=True)
    end = start + jnp.sum(hot, axis=1, keepdims=True)
    row = lax.broadcasted_iota(I32, (count, count), 0)
    col = lax.broadcasted_iota(I32, (count, count), 1)
    rank = nn(hot.astype(BF16), (row <= col).astype(BF16))
    place = jnp.sum(hot * (start + rank), axis=0, keepdims=True) - 1.0
    perm = (row.astype(F32) == place).astype(BF16)
    perm_ref[...] = perm
    x_s = nn(perm, x_ref[...]).astype(BF16)
    xs_ref[...] = x_s
    x_all[b] = x_s

    def line(side, s, send):
        away = s - 1 if send else s
        chip = z - away if side == 0 else z + away
        ahead = z + 1 < chips if side == 0 else z > 0
        known = z >= away if side == 0 else z + away < chips
        when = known & ahead if send else known
        return chip * 2 + c, {"blk": b + 2 if side == 0 else b - 2}, when

    def send_on(s):
        for side in range(2):
            device, to, when = line(side, s, True)
            routes.start(("line", side, s), x_all.at[device], x_all.at[device], to, when)

    send_on(1)
    routes.start("pair", x_all.at[b], x_all.at[b], {"blk": pair})
    cs_ref[...] = nn(perm, c_ref[...]).astype(BF16)
    keep = jnp.broadcast_to(keep_ref[...].astype(F32), (slots, count)).astype(BF16)
    kept = nt(keep, perm)
    at = lax.broadcasted_iota(I32, (slots, count), 1).astype(F32)
    hots[0] = kept * ((at >= start) & (at < end)).astype(F32)
    first = (lax.broadcasted_iota(I32, (slots, LANES), 1) * width).astype(F32)
    mine = ((first >= start) & (first < end)).astype(F32)
    mark_ref[...] = mine
    which = lax.broadcasted_iota(I32, (slots, LANES), 0).astype(F32)
    info_ref[0:1, :] = jnp.sum(mine * which, axis=0, keepdims=True).astype(I32)
    info_ref[1:2, :] = (jnp.sum(mine * start, axis=0, keepdims=True) / width).astype(I32)
    info_ref[2:3, :] = (jnp.sum(mine * end, axis=0, keepdims=True) / width).astype(I32)
    info_ref[3:8, :] = jnp.zeros((5, LANES), I32)

    for k in range(1, shards):
        other = flip(f, k)
        routes.arrive(("spec", k), spec_all.at[other])
        routes.arrive(("temb", k), temb_all.at[other])
    spectra = spec_all[...].reshape(shards * slots, -1).astype(BF16)
    condition = nn(spectra, temb_all[...].reshape(-1, size))
    rows = ada_ref.shape[0]
    for shard in range(shards):

        @pl.when(f == shard)
        def _():
            cond_ref[...] = condition[:, shard * rows : (shard + 1) * rows]
            freqs = temb_ref.shape[0]
            wave_ref[...] = spectra[:, shard * freqs : (shard + 1) * freqs].astype(F32)

    values = cond_ref[...]
    lifted = (values / (1.0 + jnp.exp(-values))).astype(BF16)
    low_ref[...] = lifted
    inside[0].wait()
    for side in range(2):
        columns = slice(side * 3 * size, (side + 1) * 3 * size)
        found = nn(lifted, ada_s[:, columns])
        part_own[:, side] = found.reshape(shards, slots, 3 * size)
    for k in range(1, shards):
        other = flip(f, k)
        routes.start(("part", k), part_own.at[other, c], part_got.at[k], {"fsdp": other})

    rows = qkvw_ref.shape[0]
    inside[1].wait()
    narrow = own * head_size
    row = lax.broadcasted_iota(I32, (size, 2 * LANES), 0)
    col = lax.broadcasted_iota(I32, (size, 2 * LANES), 1)
    pick = ((row == b * narrow + col) & (col < narrow)).astype(F32).astype(BF16)
    wh_all[f] = jnp.concatenate(
        [
            nn(qkvw_s[:, part * size : (part + 1) * size], pick)[:, 0:narrow]
            for part in range(3)
        ],
        axis=1,
    ).astype(BF16)
    if shards == 4:
        for k in (1, 2):
            routes.start(("head", k), wh_all.at[f], wh_all.at[f], {"fsdp": flip(f, k)})
    else:
        for k in range(1, shards):
            routes.start(("head", k), wh_all.at[f], wh_all.at[f], {"fsdp": flip(f, k)})

    def take(s):
        for side in range(2):
            device, _, when = line(side, s, False)
            routes.arrive(("line", side, s), x_all.at[device], when)
            if s + 1 < chips:
                device, to, onward = line(side, s + 1, True)
                routes.start(
                    ("line", side, s + 1), x_all.at[device], x_all.at[device], to, onward
                )
            device, _, when = line(side, s, False)
            routes.start(
                ("pair", side, s), x_all.at[device], x_all.at[device], {"blk": pair}, when
            )

    take(1)
    if shards == 4:
        half = rows // 2
        for k, low in ((1, 0), (2, half)):
            routes.arrive(("head", k), wh_all.at[flip(f, k)])
            part = wh_all.at[flip(f, k), low : low + half]
            routes.start(("head", 3, k), part, part, {"fsdp": flip(f, 3 - k)})

    cut = size // (2 * LANES) * LANES
    for k in range(1, 3 if shards == 4 else shards):
        routes.start(("out", k), outw_ref.at[c], wo_all.at[f, c], {"fsdp": flip(f, k)})

    blocks_fc = fc_all.shape[1]
    part = fc1_s.shape[1] // shards // 2
    inside[3].wait()
    for core in range(2):

        @pl.when(c == core)
        def _():
            picked = jnp.concatenate(
                [
                    fc1_s[:, (2 * shard + core) * part : (2 * shard + core + 1) * part]
                    for shard in range(shards)
                ],
                axis=1,
            )
            for block_at in range(blocks_fc):
                fc_all[0, block_at] = picked[:, block_at * size : (block_at + 1) * size]

    for k in range(1, len(fc_refs)):
        routes.start(("fc", k), fc_all.at[0], fc_all.at[k], {"fsdp": flip(f, k)})

    total = part_own[f, c]
    for k in range(1, shards):
        routes.arrive(("part", k), part_got.at[k])
        total = total + part_got[k]
    mod_all[c] = total
    routes.start("mod", mod_all.at[c], mod_all.at[c], {"blk": pair})
    routes.arrive("mod", mod_all.at[1 - c])
    total = jnp.concatenate([mod_all[0], mod_all[1]], axis=1)
    mod_ref[...] = lax.dot_general(
        mine[:, : mod_ref.shape[0]], total, (((0,), (0,)), ((), ())), precision=HIGH,
        preferred_element_type=F32,
    )

    def early(u):
        rows = pl.ds(pl.multiple_of(u * width, width), width)
        gate = mod_ref[pl.ds(u, 1), 5 * size : 6 * size]
        dms[0, rows, :] = (cs_ref[rows, :].astype(F32) * gate).astype(BF16)

    each(units, early)
    routes.start("dm", dms.at[0], dms.at[1], {"blk": pair})
    routes.start("hot", hots.at[0], hots.at[1], {"blk": pair})

    if shards == 4:
        half = rows // 2
        routes.arrive(("head", 3, 1), wh_all.at[flip(f, 3), 0:half])
        routes.arrive(("head", 3, 2), wh_all.at[flip(f, 3), half:rows])
    else:
        for k in range(1, shards):
            routes.arrive(("head", k), wh_all.at[flip(f, k)])
    packed = wh_all[...].reshape(size, 3 * narrow)
    wh_ref[...] = jnp.zeros_like(wh_ref)
    for i in range(3 * own):
        wh_ref[:, i * LANES : i * LANES + head_size] = packed[
            :, i * head_size : (i + 1) * head_size
        ]

    def block(device):
        at = pl.ds(pl.multiple_of(device * width, width), width)

        def one(u):
            shift = mod_ref[pl.ds(u, 1), 0:size]
            scale = mod_ref[pl.ds(u, 1), size : 2 * size]
            part = x_all[device, pl.ds(pl.multiple_of(u * width, width), width), :]
            normed, _ = normal(part.astype(F32))
            low = (normed * (1.0 + scale) + shift).astype(BF16)
            h_all[pl.ds(pl.multiple_of(u * width, width), width), :] = low

        each(units, one, 3)
        copies = fetch(
            [
                (h_all.at[u * width : (u + 1) * width], h_ref.at[u, at])
                for u in range(units)
            ],
            local,
        )
        found = nn(h_all[...], wh_ref[...]).astype(BF16)
        qkv_ref[:, at, :] = found.reshape(units, width, found.shape[1])
        for copy in copies:
            copy.wait()

    routes.arrive("pair", x_all.at[pair])
    each(2, lambda core: block(z * 2 + core))

    def work(s):
        for side in range(2):
            device, _, when = line(side, s, False)
            routes.arrive(("pair", side, s), x_all.at[device + 1 - 2 * c], when)

        def pick(q):
            chip = z - s + 2 * s * (q // 2)

            @pl.when((chip >= 0) & (chip < chips))
            def _():
                block(chip * 2 + q % 2)

        each(4, pick)

    for s in range(2, chips):
        take(s)
        if s == 2:
            for k in range(1, 3 if shards == 4 else shards):
                other = flip(f, k)
                routes.arrive(("out", k), wo_all.at[other, c])
                if shards == 4:
                    columns = slice(0, cut) if k == 1 else slice(cut, size)
                    piece = wo_all.at[other, c, :, columns]
                    routes.start(("out", 3, k), piece, piece, {"fsdp": flip(f, 3 - k)})
                routes.start(
                    ("pair out", k), wo_all.at[other, c], wo_all.at[other, c], {"blk": pair}
                )
        work(s - 1)
    if shards == 4:
        other = flip(f, 3)
        routes.arrive(("out", 3, 1), wo_all.at[other, c, :, 0:cut])
        routes.arrive(("out", 3, 2), wo_all.at[other, c, :, cut:size])
        routes.start(("pair out", 3), wo_all.at[other, c], wo_all.at[other, c], {"blk": pair})
    inside[2].wait()
    for k in range(1, shards):
        routes.arrive(("pair out", k), wo_all.at[flip(f, k), 1 - c])
    routes.arrive("dm", dms.at[1])
    routes.arrive("hot", hots.at[1])
    done = fetch([(wo_all, wo_ref), (dms, dm_ref), (hots, hot_ref)], local, units)
    work(chips - 1)
    for k in range(1, len(fc_refs)):
        routes.arrive(("fc", k), fc_all.at[k])
    inside[4].wait()
    done += fetch([(fc_all.at[k], ref) for k, ref in enumerate(fc_refs)], local, units + 3)
    routes.finish()
    for copy in done:
        copy.wait()


def exchange_lanes(tiles, width):
    tiles = list(tiles)
    count = len(tiles)
    group = lax.broadcasted_iota(I32, tiles[0].shape, 1) // width
    half = count // 2
    while half:
        low = (group // half) % 2 == 0
        fresh = list(tiles)
        for i in range(count):
            if (i // half) % 2 == 0:
                a, d = tiles[i], tiles[i + half]
                fresh[i] = jnp.where(low, a, pltpu.roll(d, half * width, 1))
                fresh[i + half] = jnp.where(low, pltpu.roll(a, LANES - half * width, 1), d)
        tiles = fresh
        half //= 2
    return tiles


def in_groups(first, last, sizes, step, carry):
    for size in sizes:
        count = (last - first) // size

        def one(index, carry, first=first, size=size):
            return step(first + index * size, size, carry)

        carry = lax.fori_loop(0, count, one, carry)
        first = first + count * size
    return carry


def attend_body(
    own, size, blocks, ids_ref, info_ref, mask_ref, qkv_ref, o_ref, lse_ref, out_ref, held, turned, placed
):
    units = qkv_ref.shape[0]
    width = BLOCK // blocks
    b = ids_ref[1]
    scale = LOG2E / math.sqrt(size)
    tall = turned.shape[2]

    def turn(j):
        for h in range(own):
            at = (2 * own + h) * LANES
            values = qkv_ref[j, :, at : at + LANES].astype(F32).T
            turned[j, h] = values[0:tall].astype(BF16)

    each(units, turn, 2)

    def one_unit(u):
        queries = [qkv_ref[u, :, h * LANES : (h + 1) * LANES] for h in range(own)]

        def some_blocks(j, count, carry):
            fresh = []
            for h in range(own):
                top, total, acc = carry[h]
                keys = qkv_ref[pl.ds(j, count), :, (own + h) * LANES : (own + h + 1) * LANES]
                scores = nt(keys.reshape(count * BLOCK, LANES), queries[h]) * scale
                new_top = jnp.maximum(top, jnp.max(scores, axis=0, keepdims=True))
                probs = jnp.exp2(scores - new_top)
                decay = jnp.exp2(top - new_top)
                total = total * decay + jnp.sum(probs, axis=0, keepdims=True)
                acc = acc * decay
                low = probs.astype(BF16)
                for i in range(count):
                    acc = acc + nn(turned[j + i, h], low[i * BLOCK : (i + 1) * BLOCK])
                fresh.append((new_top, total, acc))
            return tuple(fresh)

        start = tuple(
            (
                jnp.full((1, BLOCK), NEG, F32),
                jnp.zeros((1, BLOCK), F32),
                jnp.zeros((tall, BLOCK), F32),
            )
            for _ in range(own)
        )
        done = in_groups(info_ref[1, u], info_ref[2, u], (4, 2, 1), some_blocks, start)
        slot = info_ref[0, u]
        rows = []
        for h in range(own):
            top, total, acc = done[h]
            keep = mask_ref[slot, b * own + h].astype(F32)
            rows.append((acc * (keep / total))[0:size])
            lse_ref[u, h : h + 1, :] = top + jnp.log2(total)
        held[u] = jnp.concatenate(rows, axis=0) if own > 1 else rows[0]
        o_ref[u] = held[u].astype(BF16)

    each(units, one_unit)
    groups = LANES // width
    for g in range(units // groups):
        for e in range(blocks // groups):
            tiles = [
                held[groups * g + i, :, e * LANES : (e + 1) * LANES] for i in range(groups)
            ]
            for j, tile in enumerate(exchange_lanes(tiles, width)):
                placed[groups * e + j, :, g * LANES : (g + 1) * LANES] = tile.astype(BF16)
    for k in range(blocks):
        out_ref[k] = placed[lax.bitwise_xor(b, k)]


def attend_back_body(
    own, size, blocks, ids_ref, info_ref, mask_ref, qkv_ref, o_ref, lse_ref, given, d_ref, up, delta, d_q,
    d_k, d_v,
):
    units = qkv_ref.shape[0]
    width = BLOCK // blocks
    b = ids_ref[1]
    factor = 1.0 / math.sqrt(size)
    scale = LOG2E * factor
    up[...] = jnp.zeros_like(up)
    groups = LANES // width
    for g in range(units // groups):
        for e in range(blocks // groups):
            tiles = [
                given[groups * e + j, :, g * LANES : (g + 1) * LANES].astype(F32)
                for j in range(groups)
            ]
            for i, tile in enumerate(exchange_lanes(tiles, width)):
                unit = groups * g + i
                slot = info_ref[0, unit]
                for h in range(own):
                    keep = mask_ref[slot, b * own + h].astype(F32)
                    kept = tile[h * size : (h + 1) * size] * keep
                    up[unit, h, 0:size, e * LANES : (e + 1) * LANES] = kept.astype(BF16)
                    mine = o_ref[unit, h * size : (h + 1) * size, e * LANES : (e + 1) * LANES]
                    delta[unit, h : h + 1, e * LANES : (e + 1) * LANES] = jnp.sum(
                        kept * mine.astype(F32), axis=0, keepdims=True
                    )
    d_q[...] = jnp.zeros_like(d_q)

    def one_unit(j):
        d_k[...] = jnp.zeros_like(d_k)
        d_v[...] = jnp.zeros_like(d_v)
        keys = [qkv_ref[j, :, (own + h) * LANES : (own + h + 1) * LANES] for h in range(own)]
        turned = [keys[h].astype(F32).T.astype(BF16) for h in range(own)]

        def some_blocks(i, count, carry):
            for h in range(own):
                at = (2 * own + h) * LANES
                values = qkv_ref[j, :, at : at + LANES]
                sum_k = sum_v = 0.0
                for n in range(count):
                    queries = qkv_ref[i + n, :, h * LANES : (h + 1) * LANES]
                    scores = nt(keys[h], queries) * scale
                    probs = jnp.exp2(scores - lse_ref[i + n, h : h + 1, :])
                    d_probs = nn(values, up[i + n, h])
                    d_scores = (probs * (d_probs - delta[i + n, h : h + 1, :])).astype(BF16)
                    sum_k = sum_k + nn(d_scores, queries)
                    sum_v = sum_v + nt(probs.astype(BF16), up[i + n, h])
                    d_q[i + n, h] += nn(turned[h], d_scores)
                d_k[h] += sum_k
                d_v[h] += sum_v
            return carry

        in_groups(info_ref[1, j], info_ref[2, j], (4, 2, 1), some_blocks, 0)
        for h in range(own):
            at = (own + h) * LANES
            d_ref[j, :, at : at + LANES] = (d_k[h] * factor).astype(BF16)
            at = (2 * own + h) * LANES
            d_ref[j, :, at : at + LANES] = d_v[h].astype(BF16)

    each(units, one_unit)

    def turn(i):
        for h in range(own):
            d_ref[i, :, h * LANES : (h + 1) * LANES] = (d_q[i, h].T * factor).astype(BF16)

    each(units, turn)


def project_body(shards, blocks, moves, mod_ref, x_ref, w_ref, p_ref, *refs):
    sources, refs = refs[: len(moves)], refs[len(moves) :]
    attn_ref, x1_ref, h_ref, om_ref = refs[:4]
    landed, (om_all, h_all, local, sent, got) = refs[4 : 4 + len(moves)], refs[4 + len(moves) :]
    f, b = lax.axis_index("fsdp"), lax.axis_index("blk")
    width = BLOCK // blocks
    size = x_ref.shape[1]
    routes = Routes(sent, got)
    greet_all(shards, blocks)
    for k in range(blocks - 1, 0, -1):
        routes.start(("om", k), p_ref.at[k], om_all.at[b], {"blk": flip(b, k)})
    for i, (first, high, k) in enumerate(moves):
        routes.start(("move", i), sources[i].at[first:high], landed[i], {"fsdp": flip(f, k)})
    om_all[b] = p_ref[0]
    for k in range(1, blocks):
        routes.arrive(("om", k), om_all.at[flip(b, k)])
    om = om_all[...].reshape(size, x_ref.shape[0])
    om_ref[...] = om
    weight = w_ref[...]
    attn_ref[...] = tn(om, weight)

    def one(u):
        rows = pl.ds(pl.multiple_of(u * width, width), width)
        gate, shift, scale = [mod_ref[pl.ds(u, 1), i * size : (i + 1) * size] for i in (2, 3, 4)]
        middle = x_ref[rows, :].astype(F32) + gate * attn_ref[rows, :]
        x1_ref[rows, :] = middle
        normed, _ = normal(middle)
        h_all[0, rows, :] = (normed * (1.0 + scale) + shift).astype(BF16)

    each(x_ref.shape[0] // width, one, 3)
    routes.start("h", h_all.at[0], h_all.at[1], {"blk": flip(b, 1)})
    routes.arrive("h", h_all.at[1])
    copy = pltpu.make_async_copy(h_all, h_ref, local.at[0])
    copy.start()
    for i in range(len(moves)):
        routes.arrive(("move", i), landed[i])
    routes.finish()
    copy.wait()


def ff_body(shards, step, sides, plan1, plan2, ids_ref, hot_ref, chan_ref, h_ref, dm_ref, *refs):
    w1_refs, refs = refs[: len(plan1)], refs[len(plan1) :]
    w2_refs, refs = refs[: len(plan2)], refs[len(plan2) :]
    f = ids_ref[0]
    mlp_m, mlp_o, dh_m, dh_o, g_ref, w1, w2, h, dm, turned, hid_s, du_s, mlp, dh, g1, g2, sems = refs
    total = h.shape[0]
    count = total // 2
    f_size, size = w2.shape
    blocks = f_size // size
    row1, row2 = size // shards, f_size // shards

    def up_part(ref, shard, low, high):
        block = low // size
        return ref.at[
            shard, block * row1 : (block + 1) * row1, low - block * size : high - block * size
        ]

    def down_part(ref, shard, low, high):
        at = blocks * row1 - shard * row2
        return ref.at[shard, at + low : at + high]

    def chunk(index):
        low, high = index * step, (index + 1) * step
        cols = [
            (max(low, i * size), min(high, (i + 1) * size))
            for i in range(blocks)
            if max(low, i * size) < min(high, (i + 1) * size)
        ]
        rows = [
            (i, max(low, i * row2), min(high, (i + 1) * row2))
            for i in range(shards)
            if max(low, i * row2) < min(high, (i + 1) * row2)
        ]
        return cols, rows

    used = [0]

    def begin(pairs):
        copies = fetch(pairs, sems, used[0])
        used[0] += len(copies)
        return copies

    waits = [
        begin(
            [
                (h_ref.at[0], h.at[0:count]),
                (h_ref.at[1], h.at[count:total]),
                (dm_ref.at[0], dm.at[0:count]),
                (dm_ref.at[1], dm.at[count:total]),
            ]
        )
    ]
    chunks = f_size // step
    pairs = [[] for _ in range(chunks)]
    for ref, (k, first) in zip(w1_refs, plan1):
        at = pl.ds(pl.multiple_of(lax.bitwise_xor(f, k) * row1, 16), row1)
        for i in range(ref.shape[0]):
            low = (first + i) * size
            pairs[low // step].append((ref.at[i], w1.at[at, low : low + size]))
    for ref, (k, first) in zip(w2_refs, plan2):
        at = pl.multiple_of(lax.bitwise_xor(f, k) * row2 + first, 16)
        pairs[0].append((ref, w2.at[pl.ds(at, ref.shape[0])]))
    waits += [begin(some) for some in pairs]
    for copy in waits[0]:
        copy.wait()
    for at in range(0, total, LANES):
        turned[:, at : at + LANES] = h[at : at + LANES, :].astype(F32).T.astype(BF16)
    hots = jnp.concatenate([hot_ref[side] for side in range(2)], axis=1).astype(BF16)
    left = []
    for index in range(chunks):
        for copy in waits[index + 1]:
            copy.wait()
        cols = slice(index * step, (index + 1) * step)
        up = w1[:, cols]
        down = w2[cols, :]
        chan = chan_ref[:, cols].astype(F32).astype(BF16)
        for side in range(sides):
            rows = slice(side * total // sides, (side + 1) * total // sides)
            keep = tn(hots[:, rows], chan)
            pre = nn(h[rows, :], up)
            inner = pre * pre
            bent = jnp.tanh(0.7978845608028654 * (pre + 0.044715 * inner * pre))
            half = 0.5 * (1.0 + bent)
            hid = (pre * half * keep).astype(BF16)
            slope = half + (0.5 * 0.7978845608028654) * pre * (1.0 - bent * bent) * (
                1.0 + (3.0 * 0.044715) * inner
            )
            back = nt(dm[rows, :], down)
            du = (slope * back * keep).astype(BF16)
            hid_s[rows, :] = hid
            du_s[rows, :] = du
            if index:
                mlp[rows, :] += nn(hid, down)
                dh[rows, :] += nt(du, up)
            else:
                mlp[rows, :] = nn(hid, down)
                dh[rows, :] = nt(du, up)
        g1[:, cols] = nn(turned[...], du_s[...]).astype(BF16)
        g2[cols, :] = tn(hid_s[...], dm[...]).astype(BF16)
        parts, rows = chunk(index)
        pairs = [
            (g1.at[shard * row1 : (shard + 1) * row1, lo:hi], up_part(g_ref, shard, lo, hi))
            for shard in range(shards)
            for lo, hi in parts
        ]
        pairs += [(g2.at[lo:hi], down_part(g_ref, shard, lo, hi)) for shard, lo, hi in rows]
        left += begin(pairs)
    mlp_m[...] = mlp[0:count, :]
    mlp_o[...] = mlp[count:total, :].astype(BF16)
    dh_m[...] = dh[0:count, :]
    dh_o[...] = dh[count:total, :].astype(BF16)
    for copy in left:
        copy.wait()


def middle_body(
    shards, blocks, mod_ref, mark_ref, x1_ref, c_ref, dh_ref, dho_ref, mlp_ref, mlpo_ref, attn_ref, om_ref,
    w_ref, perm_ref, up_ref, dx_ref, two_ref, gate_ref, r_ref, mine_ref, other_ref, dh_in, mlp_in, da, leave,
    up_all, held, grad, by_unit, w_s, mlp_s, attn_s, om_s, local, sent, got,
):
    f, b = lax.axis_index("fsdp"), lax.axis_index("blk")
    c = b % 2
    width = BLOCK // blocks
    count, size = x1_ref.shape
    units = count // width
    routes = Routes(sent, got)
    inside = fetch([(w_ref, w_s), (mlp_ref, mlp_s), (attn_ref, attn_s), (om_ref, om_s)], local)
    greet_all(shards, blocks)
    routes.start("dh", dho_ref, dh_in, {"blk": flip(b, 1)})
    routes.start("mlp", mlpo_ref, mlp_in, {"blk": flip(b, 1)})
    by_unit[...] = jnp.zeros_like(by_unit)
    routes.arrive("dh", dh_in)

    def one(u):
        rows = pl.ds(pl.multiple_of(u * width, width), width)
        gate = mod_ref[pl.ds(u, 1), 2 * size : 3 * size]
        scale = mod_ref[pl.ds(u, 1), 4 * size : 5 * size]
        normed, spread = normal(x1_ref[rows, :])
        grad = dh_ref[rows, :] + dh_in[rows, :].astype(F32)
        by_unit[pl.ds(u, 1), 0:size] = jnp.sum(grad, axis=0, keepdims=True)
        by_unit[pl.ds(u, 1), size : 2 * size] = jnp.sum(grad * normed, axis=0, keepdims=True)
        dx = c_ref[rows, :].astype(F32) + normal_back(grad * (1.0 + scale), normed, spread)
        dx_ref[rows, :] = dx
        da[rows, :] = (dx * gate).astype(BF16)

    each(units, one, 3)
    inside[0].wait()
    for k in range(blocks - 1, -1, -1):
        piece = nt(w_s[flip(b, k)], da[...]).astype(BF16)
        if k:
            leave[k] = piece
            routes.start(("up", k), leave.at[k], up_all.at[b], {"blk": flip(b, k)})
        else:
            up_all[b] = piece

    def over_slots(target):
        target[...] = lax.dot_general(
            mark_ref[:, : by_unit.shape[0]], by_unit[...], (((1,), (0,)), ((), ())), precision=HIGH,
            preferred_element_type=F32,
        )

    over_slots(two_ref)
    routes.arrive("mlp", mlp_in)
    for copy in inside[1:]:
        copy.wait()

    def two(u):
        rows = pl.ds(pl.multiple_of(u * width, width), width)
        gate = mod_ref[pl.ds(u, 1), 5 * size : 6 * size]
        mlp = mlp_s[rows, :] + mlp_in[rows, :].astype(F32)
        held[rows, :] = (x1_ref[rows, :] + gate * mlp).astype(BF16)
        by_unit[pl.ds(u, 1), 0:size] = jnp.sum(
            dx_ref[rows, :] * attn_s[rows, :], axis=0, keepdims=True
        )
        by_unit[pl.ds(u, 1), size : 2 * size] = jnp.sum(
            c_ref[rows, :].astype(F32) * mlp, axis=0, keepdims=True
        )

    each(units, two, 3)
    over_slots(gate_ref)
    r_ref[...] = tn(perm_ref[...], held[...]).astype(BF16)
    grad[...] = nn(om_s[...], da[...]).astype(BF16).reshape(grad.shape)
    for k in range(shards):
        base = 2 * flip(f, k)
        mine_ref[k] = grad[base + c]
        other_ref[k] = grad[base + 1 - c]
    for k in range(1, blocks):
        routes.arrive(("up", k), up_all.at[flip(b, k)])
    up_ref[...] = up_all[...]
    routes.finish()


def stream_back_body(
    shards, chips, heads, per, h_ref, gs_ref, d_ref, wh_ref, mod_ref, mine_ref, x_ref, dx_ref, perm_ref,
    gm_ref, o_ref, sum_ref, g_ref, go_ref, give, take, keep, came, h_s, acc, low, others, out_in, out_low,
    out_got, total, held, x_s, dx_s, perm_s, late, by_unit, local, sent, got,
):
    f, b = lax.axis_index("fsdp"), lax.axis_index("blk")
    z, c = b // 2, b % 2
    pair = b + 1 - 2 * c
    width = BLOCK // (2 * chips)
    units = d_ref.shape[0]
    count, size = x_ref.shape
    wide = wh_ref.shape[1]
    own = heads // (2 * chips)
    head_size = size // heads
    rows = low.shape[1]
    steps = units // per
    routes = Routes(sent, got)

    def load(i):
        return pltpu.make_async_copy(
            h_ref.at[pl.ds(i * per, per)], h_s.at[i % 2], local.at[i % 2]
        )

    load(0).start()
    loaded = fetch([(x_ref, x_s), (dx_ref, dx_s), (perm_ref, perm_s)], late)
    greet(shards, chips)
    routes.start("out", gs_ref, out_in, {"blk": pair})

    def partial(device, target):
        at = pl.ds(pl.multiple_of(device * width, width), width)
        grads = d_ref[:, at, :].reshape(count, wide)
        for col in range(0, size, 3 * LANES):
            target[:, col : col + 3 * LANES] = nt(
                grads, wh_ref[col : col + 3 * LANES, :]
            ).astype(BF16)

    def route(side, t):
        if side == 0:
            chip = chips - 1 - t
            return chip, z < chip, z > 0
        return t, z > t, z < chips - 1

    def onward(side, t, chip, when):
        if side == 0:
            slot, to = chip, b + 2
        else:
            slot, to = chip + (chips - chip) * (z - 1 == chip).astype(I32), b - 2
        routes.start(("sum", side, t), keep.at[chip], came.at[slot], {"blk": to}, when)

    def join(chip, slot=None):
        value = keep[chip].astype(F32) + take[chip].astype(F32)
        if slot is not None:
            value = value + came[slot].astype(F32)
        keep[chip] = value.astype(BF16)

    for t in range(chips - 1):
        for side in range(2):
            chip, passes, inside = route(side, t)

            @pl.when(passes)
            def _():
                partial(chip * 2 + 1 - c, give.at[chip])

            routes.start(("pair", side, t), give.at[chip], take.at[chip], {"blk": pair}, passes)

            @pl.when(passes)
            def _():
                partial(chip * 2 + c, keep.at[chip])

            first = passes & jnp.logical_not(inside)
            routes.arrive(("pair", side, t), take.at[chip], first)

            pl.when(first)(lambda: join(chip))
            onward(side, t, chip, first)

    partial(z * 2 + 1 - c, give.at[z])
    routes.start(("pair", "own"), give.at[z], take.at[z], {"blk": pair})
    partial(z * 2 + c, keep.at[z])

    def gather(i):
        if i + 1 < steps:
            load(i + 1).start()
        load(i).wait()
        part = tn(
            h_s[i % 2].reshape(per * BLOCK, size),
            d_ref[i * per : (i + 1) * per].reshape(per * BLOCK, wide),
        )
        if i:
            acc[...] += part
        else:
            acc[...] = part

    for t in range(max(chips - 1, steps)):
        if t < steps:
            gather(t)
        if t == steps - 1:
            packed = jnp.concatenate(
                [acc[:, i * LANES : i * LANES + head_size] for i in range(3 * own)], axis=1
            )
            low[...] = packed.astype(BF16).reshape(low.shape)
            for k in range(1, shards):
                other = flip(f, k)
                routes.start(("grad", k), low.at[other], others.at[k], {"fsdp": other})
        if t == 0:
            routes.arrive("out", out_in)
            out_low[...] = (gm_ref[...].astype(F32) + out_in[...].astype(F32)).astype(BF16)
            for k in range(1, shards):
                routes.start(("out", k), out_low.at[k], out_got.at[k], {"fsdp": flip(f, k)})
        if t >= chips - 1:
            continue
        for near, side in ((True, 0), (True, 1), (False, 1), (False, 0)):
            chip, passes, inside = route(side, t)
            when = passes & inside & ((z < chips // 2) == near)
            routes.arrive(("pair", side, t), take.at[chip], when)
            routes.arrive(("sum", side, t), came.at[chip], when)
            pl.when(when)(lambda: join(chip, chip))
            onward(side, t, chip, when)

    grad, grad_out = low[f].astype(F32), out_low[0].astype(F32)
    for k in range(1, shards):
        routes.arrive(("grad", k), others.at[k])
        grad = grad + others[k].astype(F32)
        routes.arrive(("out", k), out_got.at[k])
        grad_out = grad_out + out_got[k].astype(F32)
    g_ref[...] = grad.astype(BF16)
    go_ref[...] = grad_out.astype(BF16)

    routes.arrive(("pair", "own"), take.at[z])
    total[...] = keep[z].astype(F32) + take[z].astype(F32)
    for t in range(chips - 1):
        for side in range(2):
            chip, _, inside = route(side, t)
            slot = chip if side == 0 else chips
            here = (z == chip) & inside
            routes.arrive(("sum", side, t), came.at[slot], here)

            @pl.when(here)
            def _():
                total[...] += came[slot].astype(F32)

    by_unit[...] = jnp.zeros_like(by_unit)
    for copy in loaded:
        copy.wait()

    def one(u):
        rows = pl.ds(pl.multiple_of(u * width, width), width)
        scale = mod_ref[pl.ds(u, 1), size : 2 * size]
        normed, spread = normal(x_s[rows, :].astype(F32))
        grad = total[rows, :]
        by_unit[pl.ds(u, 1), 0:size] = jnp.sum(grad, axis=0, keepdims=True)
        by_unit[pl.ds(u, 1), size : 2 * size] = jnp.sum(grad * normed, axis=0, keepdims=True)
        dx = dx_s[rows, :] + normal_back(grad * (1.0 + scale), normed, spread)
        held[rows, :] = dx.astype(BF16)

    each(units, one, 3)
    o_ref[...] = tn(perm_s[...], held[...]).astype(BF16)
    sum_ref[...] = lax.dot_general(
        mine_ref[:, : by_unit.shape[0]], by_unit[...], (((1,), (0,)), ((), ())), precision=HIGH,
        preferred_element_type=F32,
    )
    routes.finish()


def finish_body(
    shards, chips, fc_ref, ada_ref, go_ref, gq_ref, one_ref, two_ref, gate_ref, cond_ref, tot_ref, gqa_ref,
    dm_ref, dc_ref, mine, up, inner_in, result, other, gq_all, sum_own, sum_pair, small, mods, conds, ada_s,
    local, sent, got,
):
    f, b = lax.axis_index("fsdp"), lax.axis_index("blk")
    z, c = b // 2, b % 2
    pair = b + 1 - 2 * c
    count = mine.shape[0]
    slots, wider = sum_own.shape
    size = wider // 6
    routes = Routes(sent, got)
    loads = fetch([(fc_ref, mine.at[0 : count - 1]), (ada_ref, ada_s)], local)
    greet(shards, chips)

    sum_own[:, 0 : 2 * size] = one_ref[...]
    sum_own[:, 2 * size : 3 * size] = gate_ref[:, 0:size]
    sum_own[:, 3 * size : 5 * size] = two_ref[...]
    sum_own[:, 5 * size : 6 * size] = gate_ref[:, size : 2 * size]
    routes.start("sum", sum_own, sum_pair, {"blk": pair})
    gq_all[b] = gq_ref[...]

    def line(side, s, send):
        away = s - 1 if send else s
        chip = z - away if side == 0 else z + away
        ahead = z + 1 < chips if side == 0 else z > 0
        known = z >= away if side == 0 else z + away < chips
        return chip, {"blk": b + 2 if side == 0 else b - 2}, known & ahead if send else known

    def send(name, s, place):
        for side in range(2):
            chip, to, when = line(side, s, True)
            routes.start((name, side, s), place(chip), place(chip), to, when)

    def take(name, s, place):
        for side in range(2):
            chip, _, when = line(side, s, False)
            routes.arrive((name, side, s), place(chip), when)
        if s + 1 < chips:
            send(name, s + 1, place)

    def head(chip):
        return gq_all.at[chip * 2 + c]

    send("head", 1, head)
    routes.start("head pair", gq_all.at[b], gq_all.at[b], {"blk": pair})

    half = chips // 2
    right = z // half
    inner, outer = {"blk": b + 2 - 4 * right}, {"blk": b - 2 + 4 * right}
    ends = (z > 0) & (z < chips - 1)
    middle = (z == half - 1) | (z == half)
    edge = jnp.logical_not(middle)

    parts = [[small.at[i] for i in range(4)]]
    parts += [[ref.at[i] for ref in (mine, up, inner_in, result)] for i in range(count)]
    count += 1

    def inward(i, when):
        own, above, within, _ = parts[i]
        routes.start(("up", i), own, above, inner, when & edge)
        routes.start(("across", i), own, within, inner, when & middle, ("in", i))

    mine[count - 2] = go_ref[...]
    routes.arrive("sum", sum_pair)
    total = sum_own[...] + sum_pair[...]
    small[0] = jnp.concatenate(
        [total[:, : 3 * size], total[:, 3 * size :]], axis=0
    ).astype(BF16)
    ahead = min(4, count)
    inward(0, jnp.logical_not(ends))
    loads[0].wait()
    for i in range(1, ahead):
        inward(i, jnp.logical_not(ends))

    def combine():
        mods[f, :, : 3 * size] = small[3, 0:slots].astype(F32)
        mods[f, :, 3 * size :] = small[3, slots : 2 * slots].astype(F32)
        for k in range(1, shards):
            routes.start(("mod", k), mods.at[f], mods.at[f], {"fsdp": flip(f, k)})

    def condition():
        for k in range(1, shards):
            routes.arrive(("mod", k), mods.at[flip(f, k)])
        dm_ref[...] = mods[...]
        loads[1].wait()
        grad = nt(mods[...].reshape(shards * slots, wider).astype(BF16), ada_s[...])
        values = cond_ref[...]
        gate = 1.0 / (1.0 + jnp.exp(-values))
        conds[f] = grad * (gate + values * gate * (1.0 - gate))
        for k in range(1, shards):
            routes.start(("cond", k), conds.at[f], conds.at[f], {"fsdp": flip(f, k)})

    def conditions():
        for k in range(1, shards):
            routes.arrive(("cond", k), conds.at[flip(f, k)])
        dc_ref[...] = conds[...]

    jobs = [combine, condition, conditions]
    heads = [lambda s=s: take("head", s, head) for s in range(1, chips)]

    def forward(i):
        own, above, _, _ = parts[i]
        routes.arrive(("up", i), above, ends)

        @pl.when(ends)
        def _():
            own[...] = (own[...].astype(F32) + above[...].astype(F32)).astype(BF16)

        inward(i, ends)
        if i + ahead < count:
            inward(i + ahead, jnp.logical_not(ends))

    def back(i):
        own, _, within, full = parts[i]
        routes.arrive(("in", i), within)

        @pl.when(middle)
        def _():
            full[...] = (own[...].astype(F32) + within[...].astype(F32)).astype(BF16)

        @pl.when(edge)
        def _():
            full[...] = within[...]

        routes.start(("down", i), full, within, outer, ends, ("in", i))
        if i:
            routes.start(("pair", i - 1), full, other.at[i - 1], {"blk": pair})

    for i in range(count + 1):
        if i < count:
            forward(i)
        if i:
            back(i - 1)
            if jobs and i % 2 == 1:
                jobs.pop(0)()
            if heads and i % 2 == 0 and i > 2:
                heads.pop(0)()
    for job in jobs + heads:
        job()
    for s in range(1, chips):
        for side in range(2):
            chip, _, when = line(side, s, False)
            routes.start(("head pair", side, s), head(chip), head(chip), {"blk": pair}, when)
    copies = fetch([(result, tot_ref.at[c])], local)
    for i in range(count - 1):
        routes.arrive(("pair", i), other.at[i])
    copies += fetch([(other, tot_ref.at[1 - c])], local, 1)
    routes.arrive("head pair", gq_all.at[pair])
    for s in range(1, chips):
        for side in range(2):
            chip, _, when = line(side, s, False)
            routes.arrive(("head pair", side, s), gq_all.at[chip * 2 + 1 - c], when)
    copies += fetch([(gq_all, gqa_ref)], local, 2)
    routes.finish()
    for copy in copies:
        copy.wait()


def unfold_body(
    shards, low_ref, wave_ref, dm_ref, dc_ref, tot_ref, gq_ref, temb_ref, ada_ref, qkv_ref, out_ref,
    fc1_ref, fc2_ref, tot_s, gq_s, ada_s, qkv_s, out_s, fc1_s, fc2_s, loads, sems,
):
    _, count, rows, size = tot_ref.shape
    slots = dm_ref.shape[1]
    inside = fetch([(tot_ref, tot_s), (gq_ref, gq_s)], loads)
    copies = []

    def leave(source, target):
        copy = pltpu.make_async_copy(source, target, sems.at[len(copies)])
        copy.start()
        copies.append(copy)

    grads = dm_ref[...].reshape(shards * slots, -1).astype(BF16)
    ada_s[...] = tn(low_ref[...], grads)
    leave(ada_s, ada_ref)
    inside[0].wait()
    hidden = fc1_s.shape[1]
    part = hidden // shards // 2
    height = fc1_s.shape[0]
    blocks = hidden // 2 // size
    per = height // rows
    for core in range(2):
        for i in range(blocks * per):
            piece = tot_s[core, i].astype(F32)
            block, at = i // per, (i % per) * rows
            for j in range(size // part):
                column = (block * (size // part) + j) * 2 * part + core * part
                fc1_s[at : at + rows, column : column + part] = piece[:, j * part : (j + 1) * part]
        rest = count - 1 - blocks * per
        for i in range(rest):
            at = (core * rest + i) * rows
            fc2_s[at : at + rows, :] = tot_s[core, blocks * per + i].astype(F32)
        out_s[core * rows : (core + 1) * rows, :] = tot_s[core, count - 1].astype(F32)
    leave(fc1_s, fc1_ref)
    leave(fc2_s, fc2_ref)
    leave(out_s, out_ref)
    inside[1].wait()
    devices, _, packed = gq_ref.shape
    narrow = packed // 3
    for p in range(3):
        for i in range(devices):
            at = p * size + i * narrow
            qkv_s[:, at : at + narrow] = gq_s[i, :, p * narrow : (p + 1) * narrow].astype(F32)
    leave(qkv_s, qkv_ref)
    step = dc_ref.shape[2]
    for i in range(shards):
        temb_ref[:, i * step : (i + 1) * step] = lax.dot_general(
            wave_ref[...], dc_ref[i], (((0,), (0,)), ((), ())), precision=HIGH,
            preferred_element_type=F32,
        )
    for copy in copies:
        copy.wait()


def on_device(
    tokens,
    timesteps,
    segment_ids,
    head_mask,
    chan_mask,
    token_mask,
    w_temb,
    w_ada,
    w_qkv,
    w_out,
    w_fc1,
    w_fc2,
    cotangent,
):
    count, size = tokens.shape
    slots, heads = head_mask.shape[1:]
    head_size = size // heads
    shards, blocks = lax.axis_size("fsdp"), lax.axis_size("blk")
    chips = blocks // 2
    f, b = lax.axis_index("fsdp"), lax.axis_index("blk")
    c = b % 2
    width = BLOCK // blocks
    units = count // width
    own = heads // blocks
    wide = 3 * own * LANES
    hidden = w_fc1.shape[1]
    half = hidden // 2
    ids = jnp.stack([f, b, c]).astype(I32)

    near = 3 if shards == 4 else shards
    row1, row2 = w_fc1.shape[0], w_fc2.shape[0] // 2
    fc_blocks = half // size
    fc_rows = fc_blocks * row1 + row2

    items = lax.dynamic_slice_in_dim(segment_ids, b * count, count, axis=1)
    rows = w_temb.shape[0]
    entries = rows * shards
    spectrum = frequencies(timesteps[0], entries).astype(BF16).astype(F32)
    out_rows = w_out.shape[0] // 2
    ada_rows, wider = w_ada.shape
    padded = -(-units // 8) * 8
    n_copies = 9 * shards + 4 * chips + 12
    outs = run(
        "front",
        functools.partial(front_body, shards, chips, heads),
        [
            (VMEM, a)
            for a in (items, token_mask[None, :], tokens, cotangent, spectrum, w_temb)
        ]
        + [(ANY, a) for a in (w_ada, w_qkv, w_out.reshape(2, out_rows, size), w_fc1, w_fc2)],
        [
            (VMEM, shape((count, size))),
            (VMEM, shape((count, size))),
            (ANY, shape((2, slots, count), F32)),
            (VMEM, shape((8, LANES), I32)),
            (VMEM, shape((slots, LANES), F32)),
            (VMEM, shape((count, count))),
            (VMEM, shape((padded, wider), F32)),
            (VMEM, shape((shards * slots, ada_rows), F32)),
            (VMEM, shape((shards * slots, ada_rows))),
            (VMEM, shape((shards * slots, rows), F32)),
            (ANY, shape((2, count, size))),
            (ANY, shape((units, BLOCK, size))),
            (VMEM, shape((units, BLOCK, wide))),
            (VMEM, shape((size, wide))),
            (ANY, shape((shards, 2, out_rows, size))),
            (ANY, shape((row2, size))),
        ]
        + [(ANY, shape((fc_blocks, row1, size)))] * near,
        [
            pltpu.VMEM((blocks, count, size), BF16),
            pltpu.VMEM((shards, slots, entries), F32),
            pltpu.VMEM((shards, rows, size), BF16),
            pltpu.VMEM((shards, 2, slots, wider // 2), F32),
            pltpu.VMEM((shards, slots, wider // 2), F32),
            pltpu.VMEM((2, slots, wider // 2), F32),
            pltpu.VMEM((2, slots, count), F32),
            pltpu.VMEM((2, count, size), BF16),
            pltpu.VMEM((shards, w_qkv.shape[0], 3 * own * head_size), BF16),
            pltpu.VMEM((shards, 2, out_rows, size), BF16),
            pltpu.VMEM((count, size), BF16),
            pltpu.VMEM(w_ada.shape, BF16),
            pltpu.VMEM(w_qkv.shape, BF16),
            pltpu.VMEM(w_fc1.shape, BF16),
            pltpu.VMEM((near, fc_blocks, row1, size), BF16),
            pltpu.SemaphoreType.DMA((units + 4 + near,)),
            pltpu.SemaphoreType.DMA((5,)),
            pltpu.SemaphoreType.DMA((n_copies,)),
            pltpu.SemaphoreType.DMA((n_copies,)),
        ],
        flops=2 * units * BLOCK * size * wide,
        collective=0,
    )
    x_s, c_s, hots, info, mark, perm, mod, condition, lifted, waves, dms = outs[:11]
    normed, qkv, w_heads, w_out_all, fc2_own = outs[11:16]
    fc1_near = outs[16:]
    fc1_parts = [(a, k, 0) for k, a in enumerate(fc1_near)]
    if shards == 4 and fc_blocks == 2:
        one, two = swap(fc2_own, "fsdp", 1), swap(fc2_own, "fsdp", 2)
        cut = row2 // 2
        fc2_parts = [(fc2_own, 0, 0), (one, 1, 0), (two, 2, 0)]
        moves = [
            (fc1_near[1], (0, 1, 2)),
            (fc1_near[2], (1, 2, 1)),
            (one, (0, cut, 2)),
            (two, (cut, row2, 1)),
        ]
    else:
        fc1_parts += [
            (swap(fc1_near[0], "fsdp", k), k, 0) for k in range(len(fc1_near), shards)
        ]
        moves = []
        fc2_parts = [(fc2_own, 0, 0)] + [(swap(fc2_own, "fsdp", k), k, 0) for k in range(1, shards)]
    w_out_all = w_out_all.reshape(size, size)

    mask = head_mask[0]
    narrow = own * head_size
    held, lse, pieces = run(
        "attend",
        functools.partial(attend_body, own, head_size, blocks),
        [(SMEM, ids), (SMEM, info), (SMEM, mask), (VMEM, qkv)],
        [
            (VMEM, shape((units, narrow, BLOCK))),
            (VMEM, shape((units, 8, BLOCK), F32)),
            (VMEM, shape((blocks, narrow, count))),
        ],
        [
            pltpu.VMEM((units, narrow, BLOCK), F32),
            pltpu.VMEM((units, own, -(-head_size // 16) * 16, BLOCK), BF16),
            pltpu.VMEM((blocks, narrow, count), BF16),
        ],
        flops=2 * units * units * BLOCK * BLOCK * wide // 3,
    )
    if moves:
        moved = lax.optimization_barrier(tuple(a for a, _ in moves) + (lse,))[:-1]
    else:
        moved = ()
    plan = [move for _, move in moves]
    n_copies = blocks + len(moves) + 1
    outs = run(
        "project",
        functools.partial(project_body, shards, blocks, plan),
        [(VMEM, a) for a in (mod, x_s, w_out_all, pieces)] + [(ANY, a) for a in moved],
        [
            (VMEM, shape((count, size), F32)),
            (VMEM, shape((count, size), F32)),
            (ANY, shape((2, count, size))),
            (VMEM, shape((size, count))),
        ]
        + [(ANY, shape((high - low,) + a.shape[1:])) for a, (low, high, _) in moves],
        [
            pltpu.VMEM((blocks, narrow, count), BF16),
            pltpu.VMEM((2, count, size), BF16),
            pltpu.SemaphoreType.DMA((1,)),
            pltpu.SemaphoreType.DMA((n_copies,)),
            pltpu.SemaphoreType.DMA((n_copies,)),
        ],
        flops=2 * count * size * size,
        collective=3,
    )
    attn, x1, h2, om = outs[:4]
    if moves:
        fc1_parts += [(outs[4], 3, 0), (outs[5], 3, 1)]
        fc2_parts += [(outs[6], 3, 0), (outs[7], 3, cut)]

    chan = chan_mask[0].reshape(slots, shards, 2, half // shards)
    chan = lax.dynamic_slice_in_dim(chan, c, 1, axis=2).reshape(slots, half)
    ff_step = 768
    n_sems = 4 + 4 * shards * (half // ff_step + 1)
    mlp, mlp_send, dh2, dh2_send, g_fc = run(
        "feed_forward",
        functools.partial(
            ff_body,
            shards,
            ff_step,
            2,
            [(k, first) for _, k, first in fc1_parts],
            [(k, first) for _, k, first in fc2_parts],
        ),
        [(SMEM, ids), (VMEM, hots), (VMEM, chan)]
        + [(ANY, a) for a in (h2, dms)]
        + [(ANY, a) for a, _, _ in fc1_parts + fc2_parts],
        [
            (VMEM, shape((count, size), F32)),
            (VMEM, shape((count, size))),
            (VMEM, shape((count, size), F32)),
            (VMEM, shape((count, size))),
            (ANY, shape((shards, fc_rows, size))),
        ],
        [
            pltpu.VMEM((size, half), BF16),
            pltpu.VMEM((half, size), BF16),
            pltpu.VMEM((2 * count, size), BF16),
            pltpu.VMEM((2 * count, size), BF16),
            pltpu.VMEM((size, 2 * count), BF16),
            pltpu.VMEM((2 * count, ff_step), BF16),
            pltpu.VMEM((2 * count, ff_step), BF16),
            pltpu.VMEM((2 * count, size), F32),
            pltpu.VMEM((2 * count, size), F32),
            pltpu.VMEM((size, half), BF16),
            pltpu.VMEM((half, size), BF16),
            pltpu.SemaphoreType.DMA((n_sems,)),
        ],
        flops=6 * 2 * 2 * count * size * half,
    )
    g_fc = lax.psum_scatter(
        g_fc.reshape(shards * fc_rows, size), "fsdp", scatter_dimension=0, tiled=True
    )

    n_copies = blocks + 2
    up_parts, dx1, sums_two, sums_gate, result, g_out, g_out_send = run(
        "middle_back",
        functools.partial(middle_body, shards, blocks),
        [(VMEM, a) for a in (mod, mark, x1, c_s, dh2)]
        + [(ANY, a) for a in (dh2_send, mlp, mlp_send, attn, om)]
        + [(ANY, w_out_all.reshape(blocks, narrow, size)), (VMEM, perm)],
        [
            (VMEM, shape((blocks, narrow, count))),
            (VMEM, shape((count, size), F32)),
            (VMEM, shape((slots, 2 * size), F32)),
            (VMEM, shape((slots, 2 * size), F32)),
            (VMEM, shape((count, size))),
            (VMEM, shape((shards, out_rows, size))),
            (VMEM, shape((shards, out_rows, size))),
        ],
        [
            pltpu.VMEM((count, size), BF16),
            pltpu.VMEM((count, size), BF16),
            pltpu.VMEM((count, size), BF16),
            pltpu.VMEM((blocks, narrow, count), BF16),
            pltpu.VMEM((blocks, narrow, count), BF16),
            pltpu.VMEM((count, size), BF16),
            pltpu.VMEM((2 * shards, out_rows, size), BF16),
            pltpu.VMEM((padded, 2 * size), F32),
            pltpu.VMEM((blocks, narrow, size), BF16),
            pltpu.VMEM((count, size), F32),
            pltpu.VMEM((count, size), F32),
            pltpu.VMEM((size, count), BF16),
            pltpu.SemaphoreType.DMA((4,)),
            pltpu.SemaphoreType.DMA((n_copies,)),
            pltpu.SemaphoreType.DMA((n_copies,)),
        ],
        flops=4 * count * size * size,
        collective=4,
    )

    (d_qkv,) = run(
        "attend_back",
        functools.partial(attend_back_body, own, head_size, blocks),
        [(SMEM, ids), (SMEM, info), (SMEM, mask)]
        + [(VMEM, a) for a in (qkv, held, lse, up_parts)],
        [(VMEM, shape((units, BLOCK, wide)))],
        [
            pltpu.VMEM((units, own, LANES, BLOCK), BF16),
            pltpu.VMEM((units, 8, BLOCK), F32),
            pltpu.VMEM((units, own, LANES, BLOCK), F32),
            pltpu.VMEM((own, BLOCK, LANES), F32),
            pltpu.VMEM((own, BLOCK, LANES), F32),
        ],
        flops=5 * units * units * BLOCK * BLOCK * wide // 3,
    )
    per = 4 if units % 4 == 0 else 1
    rows_qkv = w_qkv.shape[0]
    n_copies = 4 * chips + 2 * shards + 4
    grad_tokens, sums_one, g_qkv, g_out = run(
        "stream_back",
        functools.partial(stream_back_body, shards, chips, heads, per),
        [(ANY, normed), (ANY, g_out_send)]
        + [(VMEM, a) for a in (d_qkv, w_heads, mod, mark)]
        + [(ANY, a) for a in (x_s, dx1, perm)]
        + [(VMEM, g_out)],
        [
            (VMEM, shape((count, size))),
            (VMEM, shape((slots, 2 * size), F32)),
            (VMEM, shape((rows_qkv, 3 * narrow))),
            (VMEM, shape((out_rows, size))),
        ],
        [
            pltpu.VMEM((chips, count, size), BF16),
            pltpu.VMEM((chips, count, size), BF16),
            pltpu.VMEM((chips, count, size), BF16),
            pltpu.VMEM((chips + 1, count, size), BF16),
            pltpu.VMEM((2, per, BLOCK, size), BF16),
            pltpu.VMEM((size, wide), F32),
            pltpu.VMEM((shards, rows_qkv, 3 * narrow), BF16),
            pltpu.VMEM((shards, rows_qkv, 3 * narrow), BF16),
            pltpu.VMEM((shards, out_rows, size), BF16),
            pltpu.VMEM((shards, out_rows, size), BF16),
            pltpu.VMEM((shards, out_rows, size), BF16),
            pltpu.VMEM((count, size), F32),
            pltpu.VMEM((count, size), BF16),
            pltpu.VMEM((count, size), BF16),
            pltpu.VMEM((count, size), F32),
            pltpu.VMEM((count, count), BF16),
            pltpu.SemaphoreType.DMA((3,)),
            pltpu.VMEM((padded, 2 * size), F32),
            pltpu.SemaphoreType.DMA((2,)),
            pltpu.SemaphoreType.DMA((n_copies,)),
            pltpu.SemaphoreType.DMA((n_copies,)),
        ],
        flops=4 * units * BLOCK * size * wide,
        collective=1,
    )

    pieces = fc_rows // out_rows
    n_copies = 5 * pieces + 16 + 4 * chips + 2 * shards
    totals, g_qkv, d_mod, d_cond = run(
        "finish",
        functools.partial(finish_body, shards, chips),
        [(ANY, g_fc.reshape(pieces, out_rows, size)), (ANY, w_ada)]
        + [(VMEM, a) for a in (g_out, g_qkv, sums_one, sums_two, sums_gate, condition)],
        [
            (ANY, shape((2, pieces + 1, out_rows, size))),
            (ANY, shape((blocks, rows_qkv, 3 * narrow))),
            (VMEM, shape((shards, slots, wider), F32)),
            (VMEM, shape((shards, shards * slots, ada_rows), F32)),
        ],
        [pltpu.VMEM((pieces + 1, out_rows, size), BF16)] * 5
        + [
            pltpu.VMEM((blocks, rows_qkv, 3 * narrow), BF16),
            pltpu.VMEM((slots, wider), F32),
            pltpu.VMEM((slots, wider), F32),
            pltpu.VMEM((4, 2 * slots, wider // 2), BF16),
            pltpu.VMEM((shards, slots, wider), F32),
            pltpu.VMEM((shards, shards * slots, ada_rows), F32),
            pltpu.VMEM(w_ada.shape, BF16),
            pltpu.SemaphoreType.DMA((3,)),
            pltpu.SemaphoreType.DMA((n_copies,)),
            pltpu.SemaphoreType.DMA((n_copies,)),
        ],
        collective=2,
    )
    grad_temb, grad_ada, grad_qkv, grad_out, grad_fc1, grad_fc2 = run(
        "unfold",
        functools.partial(unfold_body, shards),
        [(VMEM, a) for a in (lifted, waves, d_mod, d_cond)] + [(ANY, totals), (ANY, g_qkv)],
        [
            (VMEM, shape(w_temb.shape, F32)),
            (ANY, shape(w_ada.shape, F32)),
            (ANY, shape(w_qkv.shape, F32)),
            (ANY, shape(w_out.shape, F32)),
            (ANY, shape(w_fc1.shape, F32)),
            (ANY, shape(w_fc2.shape, F32)),
        ],
        [pltpu.VMEM(a.shape, BF16) for a in (totals, g_qkv)]
        + [pltpu.VMEM(a.shape, F32) for a in (w_ada, w_qkv, w_out, w_fc1, w_fc2)]
        + [pltpu.SemaphoreType.DMA((2,)), pltpu.SemaphoreType.DMA((5,))],
    )
    return (
        result,
        grad_tokens,
        grad_temb,
        grad_ada,
        grad_qkv,
        grad_out,
        grad_fc1,
        grad_fc2,
    )


def solution(mesh):
    placed = (
        P(("fsdp", "blk"), None),
        P("fsdp", None),
        P("fsdp", None),
        P("fsdp", None, None),
        P("fsdp", None, None),
        P(("fsdp", "blk")),
        P("fsdp", None),
        P("fsdp", None),
        P("fsdp", None),
        P("fsdp", None),
        P("fsdp", None),
        P("fsdp", None),
        P(("fsdp", "blk"), None),
    )
    return jax.shard_map(
        on_device,
        mesh=mesh,
        in_specs=placed,
        out_specs=(
            P(("fsdp", "blk"), None),
            P(("fsdp", "blk"), None),
            P("fsdp", None),
            P("fsdp", None),
            P("fsdp", None),
            P("fsdp", None),
            P("fsdp", None),
            P("fsdp", None),
        ),
        check_vma=False,
    )
```
